32 devices in a mesh: dp: 8 (over z, x), mp: 4 (over y, core).
Axes of the slice: x: 2, y: 2, z: 4, core: 2. Of those that a mesh axis runs over, the one named last changes fastest.
Arguments:
- token_ids: int32 [32, 512], P('dp'), may hold values from 0 to 50303
- mlm_targets: int32 [32, 32], P('dp'), may hold values from 0 to 50303
- page_lengths: int32 [32], P(('dp', 'mp')), may hold values from 1 to 512, as said below
- box_coords: int32 [4, 32, 512], P(None, ('dp', 'mp')), may hold values from 0 to 1023
- mlm_positions: int32 [32, 32], P(('dp', 'mp')), may hold values from 0 to 511, as said below
- align_pairs: int32 [32, 32, 2], P(('dp', 'mp')), may hold values from 0 to 511, as said below
- align_labels: int32 [32, 32], P(('dp', 'mp')), may hold values 0 or 1
- table: float32 [50304, 768], P(('mp', 'dp'))
- text_mats: float32 [2, 768, 3072], P(None, 'dp')
- layout_mats: float32 [2, 192, 768], P(None, 'dp')
- text_ffn: float32 [2, 3072, 1536], P(None, ('mp', 'dp')), may hold values from -0.21875 to 0.21875
- layout_ffn: float32 [2, 768, 384], P(None, ('mp', 'dp')), may hold values from -0.4375 to 0.4375
- small_params: float32 [762240], P('dp')
- table_momentum: float32 [50304, 768], P(('mp', 'dp')), may hold values from -1.9073486e-05 to 1.9073486e-05
- text_mats_momentum: float32 [2, 768, 3072], P(None, 'dp'), may hold values from -1.9073486e-05 to 1.9073486e-05
- layout_mats_momentum: float32 [2, 192, 768], P(None, 'dp'), may hold values from -1.9073486e-05 to 1.9073486e-05
- text_ffn_momentum: float32 [2, 3072, 1536], P(None, ('mp', 'dp')), may hold values from -1.9073486e-05 to 1.9073486e-05
- layout_ffn_momentum: float32 [2, 768, 384], P(None, ('mp', 'dp')), may hold values from -1.9073486e-05 to 1.9073486e-05
- small_momentum: float32 [762240], P('dp'), may hold values from -6.1035156e-05 to 6.1035156e-05
- table_average: float32 [50304, 768], P(('mp', 'dp')), may hold values from -0.21875 to 0.21875
- text_mats_average: float32 [2, 768, 3072], P(None, 'dp'), may hold values from -0.21875 to 0.21875
- layout_mats_average: float32 [2, 192, 768], P(None, 'dp'), may hold values from -0.4375 to 0.4375
- text_ffn_average: float32 [2, 3072, 1536], P(None, ('mp', 'dp')), may hold values from -0.21875 to 0.21875
- layout_ffn_average: float32 [2, 768, 384], P(None, ('mp', 'dp')), may hold values from -0.4375 to 0.4375
- small_average: float32 [762240], P('dp'), may hold values from -6 to 6
Outputs:
- loss_sum: float32 [], replicated
- loss_count: float32 [], replicated
- grad_norm: float32 [], replicated
- new_table: float32 [50304, 768], P(('mp', 'dp'))
- new_text_mats: float32 [2, 768, 3072], P(None, 'dp')
- new_layout_mats: float32 [2, 192, 768], P(None, 'dp')
- new_text_ffn: float32 [2, 3072, 1536], P(None, ('mp', 'dp'))
- new_layout_ffn: float32 [2, 768, 384], P(None, ('mp', 'dp'))
- new_small: float32 [762240], P('dp')
- table_copy: bfloat16 [50304, 768], P(('mp', 'dp'))
- text_mats_copy: bfloat16 [2, 768, 3072], P(None, 'dp')
- layout_mats_copy: bfloat16 [2, 192, 768], P(None, 'dp')
- text_ffn_copy: bfloat16 [2, 3072, 1536], P(None, ('mp', 'dp'))
- layout_ffn_copy: bfloat16 [2, 768, 384], P(None, ('mp', 'dp'))
- table_momentum_new: float32 [50304, 768], P(('mp', 'dp'))
- text_mats_momentum_new: float32 [2, 768, 3072], P(None, 'dp')
- layout_mats_momentum_new: float32 [2, 192, 768], P(None, 'dp')
- text_ffn_momentum_new: float32 [2, 3072, 1536], P(None, ('mp', 'dp'))
- layout_ffn_momentum_new: float32 [2, 768, 384], P(None, ('mp', 'dp'))
- small_momentum_new: float32 [762240], P('dp')
- table_average_new: float32 [50304, 768], P(('mp', 'dp'))
- text_mats_average_new: float32 [2, 768, 3072], P(None, 'dp')
- layout_mats_average_new: float32 [2, 192, 768], P(None, 'dp')
- text_ffn_average_new: float32 [2, 3072, 1536], P(None, ('mp', 'dp'))
- layout_ffn_average_new: float32 [2, 768, 384], P(None, ('mp', 'dp'))
- small_average_new: float32 [762240], P('dp')
The draws below stay inside these ranges and needn't reach their ends.
Inputs may be any that keep to these rules, and one draw needn't show every extreme that they name: `page_lengths`: the live tokens of each page; slots beyond are padding. Some page has 512. `mlm_positions`: every slot lies below its page's length. `align_pairs`: both slots of a pair lie below their page's length.
All inputs are finite; a program needn't handle non-finite values. No bound on the sum of `align_labels` on one device may be relied on, other than what follows from the above.
Results may differ from the reference program's by a relative error of at most 0.011.
Values may be sent and summed in bfloat16 or wider, within the bound.
No kernel may reach another device: no remote copies, remote signals or barrier semaphores. Data moves between devices by JAX's collectives and lax.ppermute only.
A program may use at most 320 MiB of HBM per device.

```python
import math
import jax
import jax.numpy as jnp
import numpy as np
from jax import lax

WIDTH = 768
HEADS = 12
FFN_UNITS = 3072
LAYOUT_WIDTH = 192
LAYOUT_UNITS = 768
BOXES = 1024
VOCAB = 50304
PAGE_SLOTS = 512
MASK_SLOTS = 32
PAIRS = 32
LAYERS = 2
PAGES_DEV = 1
PAGES = 32
GROUPS = 8
LANES = 4
SMALL = 762240
PARAM_TOTAL = 54436224


def small_shapes_drawn():
    return [(LAYERS, 8, WIDTH), (LAYERS, 8, LAYOUT_WIDTH), (LAYERS, FFN_UNITS), (LAYERS, LAYOUT_UNITS), (2, WIDTH), (2, LAYOUT_WIDTH), (PAGE_SLOTS, WIDTH), (PAGE_SLOTS, LAYOUT_WIDTH), (2, BOXES, LAYOUT_WIDTH // 4), (LAYOUT_WIDTH, WIDTH)]


def page_lengths_of(key):
    page_index = jnp.arange(PAGES)
    device_no = page_index // PAGES_DEV
    across = 1000 + 2000 * (device_no // LANES) // (GROUPS - 1)
    along_lane = 1000 + 2000 * (device_no % LANES) // (LANES - 1)
    ceiling = jnp.maximum(PAGE_SLOTS * across // 3000 * along_lane // 3000, 2)
    jitter = jax.random.randint(jax.random.fold_in(key, 101), (PAGES,), 0, 1 << 20)
    lengths = ceiling - jitter % (ceiling // 2 + 1)
    return jnp.where(page_index == PAGES - 1, PAGE_SLOTS, lengths).astype(jnp.int32)


def draw_page_lengths(key, part):
    return page_lengths_of(key)


def draw_mlm_positions(key, part):
    lengths = page_lengths_of(key)
    key = jax.random.fold_in(key, 3)
    drawn_ints = jax.random.randint(key, (PAGES, MASK_SLOTS), 0, 1 << 20)
    positions = drawn_ints % lengths[:, None]
    return positions.at[:, 0].set(lengths - 1).astype(jnp.int32)


def draw_align_pairs(key, part):
    lengths = page_lengths_of(key)
    key = jax.random.fold_in(key, 4)
    drawn_ints = jax.random.randint(key, (PAGES, PAIRS, 2), 0, 1 << 20)
    return (drawn_ints % lengths[:, None, None]).astype(jnp.int32)


def sample_of(key, piece_dims):
    return jax.random.normal(key, piece_dims, jnp.float32)


def draw_table(key, part):
    key = jax.random.fold_in(key, 11)
    rows_up = jnp.arange(VOCAB, dtype=jnp.float32)[:, None] / VOCAB
    rise = 1.0 + 2.0 * rows_up
    return sample_of(key, (VOCAB, WIDTH)) * rise * WIDTH ** (-0.5)


def mats_of(key, width):
    column_scale = jnp.where(jnp.arange(4 * width) >= 3 * width, 2.0, 1.0)
    return sample_of(key, (LAYERS, width, 4 * width)) * column_scale * width ** (-0.5)


def draw_text_mats(key, part):
    key = jax.random.fold_in(key, 12)
    return mats_of(key, WIDTH)


def draw_layout_mats(key, part):
    key = jax.random.fold_in(key, 13)
    return mats_of(key, LAYOUT_WIDTH)


def draw_small_params(key, part):
    key = jax.random.fold_in(key, 14)
    row_scale = jnp.array([0.3, 0.3, 0.3, 0.1, 0.3, 0.3, 0.1, 0.3], jnp.float32)[:, None]
    row_base = jnp.array([0.0, 0.0, 0.0, 1.0, 0.0, 0.0, 1.0, 0.0], jnp.float32)[:, None]
    emb_scale = jnp.array([0.1, 0.3], jnp.float32)[:, None]
    emb_base = jnp.array([1.0, 0.0], jnp.float32)[:, None]
    layout_scale = LAYOUT_WIDTH ** (-0.5)
    settings = [(row_scale, row_base), (row_scale, row_base), (0.3, 0.0), (0.3, 0.0), (emb_scale, emb_base), (emb_scale, emb_base), (0.5, 0.0), (0.5, 0.0), (0.5, 0.0), (layout_scale, 0.0)]
    pieces = []
    for number, piece_dims in enumerate(small_shapes_drawn()):
        scale_of, base_of = settings[number]
        sample = sample_of(jax.random.fold_in(key, number), piece_dims)
        pieces.append((sample * scale_of + base_of).reshape(-1))
    return jnp.concatenate(pieces)


def set_ends(values, key, low, high):
    place = [jax.random.randint(jax.random.fold_in(key, axis), (), 0, length) for axis, length in enumerate(values.shape)]
    main_axis = values.shape.index(max(values.shape))
    neighbour = place[:main_axis] + [(place[main_axis] + 1) % values.shape[main_axis]] + place[main_axis + 1:]
    return values.at[tuple(place)].set(low).at[tuple(neighbour)].set(high)


def shard_levels(stream_key, extent, shards, low, high):
    def one(axis_at, blocks):
        steps = jax.random.uniform(jax.random.fold_in(jax.random.fold_in(stream_key, 6), axis_at), (blocks,), jnp.float32, low / len(shards), high / len(shards))
        return jnp.repeat(jnp.exp(steps), extent[axis_at] // blocks).reshape((-1,) + (1,) * (len(extent) - axis_at - 1))

    level = one(*shards[0])
    for cut in shards[1:]:
        level = level * one(*cut)
    return level


def rank_bounds(count, slope):
    loads = [(1 << 20) // math.isqrt(standing ** slope) + 1 for standing in range(1, count + 1)]
    scale = 1 + sum(loads) // (1 << 30)
    return np.cumsum(np.array([max(1, weight // scale) for weight in loads]))


def skewed_ids(key, dims, count, skew):
    listing = rank_bounds(count, skew)
    lot = jax.random.randint(jax.random.fold_in(key, 1), dims, 0, int(listing[count - 1]))
    rank = jnp.searchsorted(jnp.asarray(listing, jnp.int32), lot, side="right")
    return jax.random.permutation(jax.random.fold_in(key, 2), count)[rank].astype(jnp.int32)


def centred(rng, shape, scale, bound, shards=(), held_as=jnp.bfloat16):
    drawn = scale * jax.random.normal(rng, shape, jnp.float32)
    if shards:
        drawn = drawn * shard_levels(rng, shape, shards, -0.22, 0.18)
    return jnp.clip(drawn, -bound, bound).astype(held_as)


def setup_inputs(seed: int = 0) -> dict:
    streams_of = jax.random.split(jax.random.key(seed), 26)
    return {
        "token_ids": set_ends(skewed_ids(streams_of[0], (PAGES, PAGE_SLOTS), VOCAB, 2), jax.random.fold_in(streams_of[0], 3), 0, VOCAB - 1).astype(jnp.int32),
        "mlm_targets": set_ends(skewed_ids(streams_of[1], (PAGES, MASK_SLOTS), VOCAB, 2), jax.random.fold_in(streams_of[1], 3), 0, VOCAB - 1).astype(jnp.int32),
        "page_lengths": draw_page_lengths(jax.random.fold_in(streams_of[25], 71), 0),
        "box_coords": set_ends(jax.random.randint(streams_of[3], (4, PAGES, PAGE_SLOTS), 0, BOXES), jax.random.fold_in(streams_of[3], 1), 0, BOXES - 1).astype(jnp.int32),
        "mlm_positions": draw_mlm_positions(jax.random.fold_in(streams_of[25], 71), 0),
        "align_pairs": draw_align_pairs(jax.random.fold_in(streams_of[25], 71), 0),
        "align_labels": set_ends((jax.random.randint(streams_of[6], (PAGES, PAIRS), 0, 2) < 1).astype(jnp.int32), jax.random.fold_in(streams_of[6], 1), 0, 1),
        "table": draw_table(jax.random.fold_in(streams_of[25], 71), 0),
        "text_mats": draw_text_mats(jax.random.fold_in(streams_of[25], 71), 0),
        "layout_mats": draw_layout_mats(jax.random.fold_in(streams_of[25], 71), 0),
        "text_ffn": centred(streams_of[10], (LAYERS, FFN_UNITS, 2 * WIDTH), WIDTH ** -0.5, 0.21875, ((1, 32),), jnp.float32),
        "layout_ffn": centred(streams_of[11], (LAYERS, LAYOUT_UNITS, 2 * LAYOUT_WIDTH), LAYOUT_WIDTH ** -0.5, 0.4375, ((1, 32),), jnp.float32),
        "small_params": draw_small_params(jax.random.fold_in(streams_of[25], 71), 0),
        "table_momentum": centred(streams_of[13], (VOCAB, WIDTH), (0.01 * PARAM_TOTAL ** -0.5), 1.9073486328125e-05, ((0, 32),), jnp.float32),
        "text_mats_momentum": centred(streams_of[14], (LAYERS, WIDTH, 4 * WIDTH), (0.01 * PARAM_TOTAL ** -0.5), 1.9073486328125e-05, ((1, 8),), jnp.float32),
        "layout_mats_momentum": centred(streams_of[15], (LAYERS, LAYOUT_WIDTH, 4 * LAYOUT_WIDTH), (0.01 * PARAM_TOTAL ** -0.5), 1.9073486328125e-05, ((1, 8),), jnp.float32),
        "text_ffn_momentum": centred(streams_of[16], (LAYERS, FFN_UNITS, 2 * WIDTH), (0.01 * PARAM_TOTAL ** -0.5), 1.9073486328125e-05, ((1, 32),), jnp.float32),
        "layout_ffn_momentum": centred(streams_of[17], (LAYERS, LAYOUT_UNITS, 2 * LAYOUT_WIDTH), (0.01 * PARAM_TOTAL ** -0.5), 1.9073486328125e-05, ((1, 32),), jnp.float32),
        "small_momentum": centred(streams_of[18], (SMALL,), (0.03 * PARAM_TOTAL ** -0.5), 6.103515625e-05, ((0, 8),), jnp.float32),
        "table_average": centred(streams_of[19], (VOCAB, WIDTH), WIDTH ** -0.5, 0.21875, ((0, 32),), jnp.float32),
        "text_mats_average": centred(streams_of[20], (LAYERS, WIDTH, 4 * WIDTH), WIDTH ** -0.5, 0.21875, ((1, 8),), jnp.float32),
        "layout_mats_average": centred(streams_of[21], (LAYERS, LAYOUT_WIDTH, 4 * LAYOUT_WIDTH), LAYOUT_WIDTH ** -0.5, 0.4375, ((1, 8),), jnp.float32),
        "text_ffn_average": centred(streams_of[22], (LAYERS, FFN_UNITS, 2 * WIDTH), WIDTH ** -0.5, 0.21875, ((1, 32),), jnp.float32),
        "layout_ffn_average": centred(streams_of[23], (LAYERS, LAYOUT_UNITS, 2 * LAYOUT_WIDTH), LAYOUT_WIDTH ** -0.5, 0.4375, ((1, 32),), jnp.float32),
        "small_average": centred(streams_of[24], (SMALL,), 0.5, 6.0, ((0, 8),), jnp.float32),
    }


EPSILON = 1e-05
CLIP_NORM = 0.01
LEARN_RATE = 10000.0
MOMENTUM = 0.5
AVERAGE_DECAY = 0.5
MASK_FILL = -1e+30
BLOCK_PAGES = 8
PRECISE = lax.Precision.HIGHEST

@jax.custom_vjp
def low(v):
    return lax.optimization_barrier(v.astype(jnp.bfloat16)).astype(jnp.float32)

@jax.custom_vjp
def low_back(v):
    return v

def low_keep(v):
    return (low(v), None)

def low_pass(kept, grad):
    return (grad,)

def back_keep(v):
    return (v, None)

def back_low(kept, grad):
    return (low(grad),)
low.defvjp(low_keep, low_pass)
low_back.defvjp(back_keep, back_low)

def small_shapes():
    return [(LAYERS, 8, WIDTH), (LAYERS, 8, LAYOUT_WIDTH), (LAYERS, FFN_UNITS), (LAYERS, LAYOUT_UNITS), (2, WIDTH), (2, LAYOUT_WIDTH), (PAGE_SLOTS, WIDTH), (PAGE_SLOTS, LAYOUT_WIDTH), (2, BOXES, LAYOUT_WIDTH // 4), (LAYOUT_WIDTH, WIDTH)]

def unpack_small(flat_vec):
    pieces = []
    offset = 0
    for piece_dims in small_shapes():
        amount = math.prod(piece_dims)
        pieces.append(flat_vec[offset:offset + amount].reshape(piece_dims))
        offset = offset + amount
    return pieces

def layer_norm(values, gain_row, bias_row):
    centre = values - lax.optimization_barrier(jnp.mean(values, axis=-1, keepdims=True))
    spread = lax.optimization_barrier(jnp.mean(centre * centre, axis=-1, keepdims=True))
    return centre * lax.rsqrt(spread + EPSILON) * gain_row + bias_row

def product(left, right):
    return jnp.dot(left, right, precision=PRECISE)

def heads_view(values, pages):
    return values.reshape(pages, PAGE_SLOTS, HEADS, values.shape[-1] // HEADS)

def slot_live(lengths):
    live = jnp.arange(MASK_SLOTS)[None, :] * PAGE_SLOTS < MASK_SLOTS * lengths[:, None]
    return live.astype(jnp.float32).reshape(-1)

def stream_qkv(rows, mats, vectors, width):
    joined = product(low(rows), mats[:, :3 * width])
    query = low_back(low(joined[:, :width] + vectors[0]))
    keys = low_back(low(joined[:, width:2 * width]))
    values = low_back(low(joined[:, 2 * width:] + vectors[1]))
    return (query, keys, values)

def attention(text_qkv, layout_qkv, key_live, pages):
    text_q, text_k, text_v = [heads_view(item, pages) for item in text_qkv]
    layout_q, layout_k, layout_v = [heads_view(item, pages) for item in layout_qkv]
    scores = jnp.einsum('pqhd,pkhd->phqk', text_q, text_k, precision=PRECISE) * (1.0 / math.sqrt(WIDTH // HEADS))
    scores = scores + jnp.einsum('pqhd,pkhd->phqk', layout_q, layout_k, precision=PRECISE) * (1.0 / math.sqrt(LAYOUT_WIDTH // HEADS))
    scores = jnp.where(key_live[:, None, None, :], low_back(scores), MASK_FILL)
    peak = lax.optimization_barrier(jnp.max(scores, axis=-1, keepdims=True))
    expo = jnp.exp(scores - peak)
    probs = low(expo / lax.optimization_barrier(jnp.sum(expo, axis=-1, keepdims=True)))
    text_out = jnp.einsum('phqk,pkhd->pqhd', probs, text_v, precision=PRECISE).reshape(-1, WIDTH)
    layout_out = jnp.einsum('phqk,pkhd->pqhd', probs, layout_v, precision=PRECISE).reshape(-1, LAYOUT_WIDTH)
    return (low_back(low(text_out)), low_back(low(layout_out)))

def feed_forward(rows, unit_mats, bias_in, width):
    pre_act = low_back(product(low(rows), unit_mats[:, :width].T) + bias_in)
    hidden = low(jax.nn.gelu(pre_act, approximate=False))
    return low_back(product(hidden, unit_mats[:, width:]))

def layer_forward(text, layout, weights, key_live, pages):
    text_mats, layout_mats, text_units, layout_units, text_bias, layout_bias, text_vec, layout_vec = weights
    text_att, layout_att = attention(stream_qkv(text, text_mats, text_vec, WIDTH), stream_qkv(layout, layout_mats, layout_vec, LAYOUT_WIDTH), key_live, pages)
    text = layer_norm(text + low_back(product(text_att, text_mats[:, 3 * WIDTH:])) + text_vec[2], text_vec[3], text_vec[4])
    layout = layer_norm(layout + low_back(product(layout_att, layout_mats[:, 3 * LAYOUT_WIDTH:])) + layout_vec[2], layout_vec[3], layout_vec[4])
    text = layer_norm(text + feed_forward(text, text_units, text_bias, WIDTH) + text_vec[5], text_vec[6], text_vec[7])
    layout = layer_norm(layout + feed_forward(layout, layout_units, layout_bias, LAYOUT_WIDTH) + layout_vec[5], layout_vec[6], layout_vec[7])
    return (text, layout)

def block_loss(lowed, block):
    table_low, text_mats, layout_mats, text_ffn, layout_ffn, small_low = lowed
    ids, targets, lengths, boxes, positions, pairs, labels = block
    text_vec, layout_vec, text_bias, layout_bias, text_emb, layout_emb, text_pos, layout_pos, box_table, align_mat = unpack_small(small_low)
    pages = ids.shape[0]
    key_live = jnp.arange(PAGE_SLOTS)[None, :] < lengths[:, None]
    embedded = low_back(table_low[ids.reshape(-1)])
    text = layer_norm(embedded + jnp.tile(text_pos, (pages, 1)), text_emb[0], text_emb[1])
    looked = [box_table[number % 2][boxes[:, number]] for number in range(4)]
    layout_pre = jnp.concatenate(looked, -1).reshape(-1, LAYOUT_WIDTH) + jnp.tile(layout_pos, (pages, 1))
    layout = layer_norm(layout_pre, layout_emb[0], layout_emb[1])
    for layer_no in range(LAYERS):
        weights = (text_mats[layer_no], layout_mats[layer_no], text_ffn[layer_no], layout_ffn[layer_no], text_bias[layer_no], layout_bias[layer_no], text_vec[layer_no], layout_vec[layer_no])
        text, layout = layer_forward(text, layout, weights, key_live, pages)
    page_base = jnp.arange(pages)[:, None] * PAGE_SLOTS
    rows = (page_base + positions).reshape(-1)
    logits = low_back(jnp.dot(low(text[rows]), table_low.T, precision=PRECISE))
    peak = lax.optimization_barrier(jnp.max(logits, axis=1, keepdims=True))
    log_total = peak[:, 0] + jnp.log(lax.optimization_barrier(jnp.sum(jnp.exp(logits - peak), axis=1)))
    picked = jnp.take_along_axis(logits, targets.reshape(-1, 1), axis=1)[:, 0]
    masked_loss = jnp.sum((log_total - picked) * slot_live(lengths))
    first_rows = (page_base + pairs[:, :, 0]).reshape(-1)
    second_rows = (page_base + pairs[:, :, 1]).reshape(-1)
    right = product(layout[second_rows], align_mat)
    logit = lax.optimization_barrier(jnp.sum(text[first_rows] * right, axis=-1)) / math.sqrt(WIDTH)
    answer = labels.reshape(-1).astype(jnp.float32)
    return masked_loss + jnp.sum(jax.nn.softplus(logit) - answer * logit)

def reference(token_ids, mlm_targets, page_lengths, box_coords, mlm_positions, align_pairs, align_labels, table, text_mats, layout_mats, text_ffn, layout_ffn, small_params, table_momentum, text_mats_momentum, layout_mats_momentum, text_ffn_momentum, layout_ffn_momentum, small_momentum, table_average, text_mats_average, layout_mats_average, text_ffn_average, layout_ffn_average, small_average):
    masters = (table, text_mats, layout_mats, text_ffn, layout_ffn, small_params)
    moments = (table_momentum, text_mats_momentum, layout_mats_momentum, text_ffn_momentum, layout_ffn_momentum, small_momentum)
    averages = (table_average, text_mats_average, layout_mats_average, text_ffn_average, layout_ffn_average, small_average)
    blocks = PAGES // BLOCK_PAGES

    def split_pages(values):
        return values.reshape((blocks, BLOCK_PAGES) + values.shape[1:])
    data = (split_pages(token_ids), split_pages(mlm_targets), split_pages(page_lengths), split_pages(jnp.transpose(box_coords, (1, 0, 2))), split_pages(mlm_positions), split_pages(align_pairs), split_pages(align_labels))
    checked = jax.checkpoint(block_loss)

    def loss_of(weights):
        lowed = tuple((low(item) for item in weights))

        def one_step(carry, block):
            return (carry + checked(lowed, block), None)
        total, unused = lax.scan(one_step, jnp.zeros((), jnp.float32), data)
        return total
    loss_sum, pullback = jax.vjp(loss_of, masters)
    grads = pullback(jnp.ones((), jnp.float32))[0]
    loss_count = jnp.sum(slot_live(page_lengths)) + jnp.float32(PAGES * PAIRS)
    scaled = [item / loss_count for item in grads]
    grad_norm = jnp.sqrt(sum((jnp.sum(item * item) for item in scaled)))
    factor = jnp.minimum(1.0, CLIP_NORM / grad_norm)
    new_masters, new_moments, new_averages = ([], [], [])
    for master, grad, moment, average in zip(masters, scaled, moments, averages):
        clipped = grad * factor
        moment_new = MOMENTUM * moment + clipped
        master_new = master - LEARN_RATE * (clipped + MOMENTUM * moment_new)
        new_masters.append(master_new)
        new_moments.append(moment_new)
        new_averages.append(AVERAGE_DECAY * average + (1.0 - AVERAGE_DECAY) * master_new)
    copies = [item.astype(jnp.bfloat16) for item in new_masters[:5]]
    return (loss_sum, loss_count, grad_norm, new_masters[0], new_masters[1], new_masters[2], new_masters[3], new_masters[4], new_masters[5], copies[0], copies[1], copies[2], copies[3], copies[4], new_moments[0], new_moments[1], new_moments[2], new_moments[3], new_moments[4], new_moments[5], new_averages[0], new_averages[1], new_averages[2], new_averages[3], new_averages[4], new_averages[5])
```

```python
import math

import jax
import jax.numpy as jnp
from jax import lax
from jax.experimental import pallas as pl
from jax.experimental.pallas import tpu as pltpu
from jax.sharding import PartitionSpec as P

WIDTH = 768
HEADS = 12
FFN_UNITS = 3072
LAYOUT_WIDTH = 192
LAYOUT_UNITS = 768
BOXES = 1024
PAGE_SLOTS = 512
PAIRS = 32
LAYERS = 2


EPSILON = 1e-05
CLIP_NORM = 0.01
LEARN_RATE = 10000.0
MOMENTUM = 0.5
AVERAGE_DECAY = 0.5
MASK_FILL = -1e30
PRECISE = lax.Precision.HIGHEST


def small_shapes():
    return [
        (LAYERS, 8, WIDTH),
        (LAYERS, 8, LAYOUT_WIDTH),
        (LAYERS, FFN_UNITS),
        (LAYERS, LAYOUT_UNITS),
        (2, WIDTH),
        (2, LAYOUT_WIDTH),
        (PAGE_SLOTS, WIDTH),
        (PAGE_SLOTS, LAYOUT_WIDTH),
        (2, BOXES, LAYOUT_WIDTH // 4),
        (LAYOUT_WIDTH, WIDTH),
    ]


def unpack_small(flat_vec):
    pieces = []
    offset = 0
    for piece_dims in small_shapes():
        amount = math.prod(piece_dims)
        pieces.append(flat_vec[offset : offset + amount].reshape(piece_dims))
        offset = offset + amount
    return pieces


def norm_apply(values, gain_row, bias_row):
    centre = values - jnp.mean(values, axis=-1, keepdims=True)
    spread = jnp.mean(centre * centre, axis=-1, keepdims=True)
    return centre * lax.rsqrt(spread + EPSILON) * gain_row + bias_row


def norm_back(values, gain_row, bias_row, grad_out):
    unused, pullback = jax.vjp(norm_apply, values, gain_row, bias_row)
    return pullback(grad_out)


def gelu_exact(values):
    return jax.nn.gelu(values, approximate=False)


def contract_rows(left, right):
    return lax.dot_general(
        left, right, (((0,), (0,)), ((), ())), preferred_element_type=jnp.float32
    )


def contract_cols(left, right):
    return lax.dot_general(
        left, right, (((1,), (1,)), ((), ())), preferred_element_type=jnp.float32
    )


def heads_view(values, pages):
    return values.reshape(pages, PAGE_SLOTS, HEADS, values.shape[-1] // HEADS)


ROUND_ROWS = 32


def bits_of(size):
    return list(reversed(range(size.bit_length() - 1)))


def hop(values, axis, bit):
    pairs = [(spot, spot ^ (1 << bit)) for spot in range(lax.axis_size(axis))]
    return lax.ppermute(values, axis, pairs)


def own_bit(axis, bit):
    return (lax.axis_index(axis) >> bit) & 1


def routes():
    far = [("dp", bit) for bit in bits_of(lax.axis_size("dp"))]
    high = [("mp", bit) for bit in bits_of(lax.axis_size("mp"))[:-1]]
    core = ("mp", 0)
    return (far[:-1], far[-1], high, core)


def add_low(kept, came):
    return (kept.astype(jnp.float32) + came.astype(jnp.float32)).astype(jnp.bfloat16)


def tie(value, *waits):
    def kernel(*refs):
        pass

    spec = pl.BlockSpec(memory_space=pl.ANY)
    return pl.pallas_call(
        kernel,
        out_shape=jax.ShapeDtypeStruct(value.shape, value.dtype),
        in_specs=[spec] * (1 + len(waits)),
        out_specs=spec,
        input_output_aliases={0: 0},
        cost_estimate=pl.CostEstimate(flops=0, bytes_accessed=0, transcendentals=0),
    )(value, *waits)


def put_in_order(own, came, places):
    slots, rows, width = own.shape

    def kernel(place_ref, own_ref, came_ref, out_ref):
        mine = place_ref[slots] == pl.program_id(0)

        @pl.when(mine)
        def _():
            out_ref[...] = own_ref[...]

        @pl.when(jnp.logical_not(mine))
        def _():
            out_ref[...] = came_ref[...]

    piece = pl.BlockSpec((1, rows, width), lambda half, spot, place: (place[spot], 0, 0))
    return pl.pallas_call(
        kernel,
        out_shape=jax.ShapeDtypeStruct((2, slots * rows, width), own.dtype),
        grid_spec=pltpu.PrefetchScalarGridSpec(
            num_scalar_prefetch=1,
            grid=(2, slots),
            in_specs=[piece, piece],
            out_specs=pl.BlockSpec((1, rows, width), lambda half, spot, place: (half, spot, 0)),
        ),
        cost_estimate=pl.CostEstimate(
            flops=0, bytes_accessed=12 * slots * rows * width, transcendentals=0
        ),
    )(places, own, came)


HEAD_PAIRS = HEADS // 2
TEXT_HEAD = WIDTH // HEADS
LAYOUT_HEAD = LAYOUT_WIDTH // HEADS


def pair_split(values):
    return values.reshape(PAGE_SLOTS, HEAD_PAIRS, 2 * LAYOUT_HEAD).transpose(1, 0, 2)


def pair_join(values):
    return values.transpose(1, 0, 2).reshape(PAGE_SLOTS, LAYOUT_WIDTH)


def head_of(text_ref, layout_ref, head, scaled=False):
    text = text_ref[:, head * TEXT_HEAD : (head + 1) * TEXT_HEAD]
    layout = layout_ref[0, :, head * LAYOUT_HEAD : (head + 1) * LAYOUT_HEAD]
    if scaled:
        text_scale, layout_scale = scale_pair()
        text = (text.astype(jnp.float32) * text_scale).astype(text.dtype)
        layout = (layout.astype(jnp.float32) * layout_scale).astype(layout.dtype)
    return jnp.concatenate([text, layout], 1)


def store_heads(text_ref, layout_ref, both):
    text_ref[...] = jnp.concatenate([item[:, :TEXT_HEAD] for item in both], 1).astype(
        text_ref.dtype
    )
    layout_ref[0] = jnp.concatenate([item[:, TEXT_HEAD:] for item in both], 1).astype(
        layout_ref.dtype
    )


def attend_kernel(length, qt, kt, vt, ql, kl, vl, out_t, out_l, lse):
    live = lax.broadcasted_iota(jnp.int32, (PAGE_SLOTS, PAGE_SLOTS), 1) < length[0]
    outs = []
    for head in range(2):
        query, keys = head_of(qt, ql, head, True), head_of(kt, kl, head)
        scores = jnp.where(live, contract_cols(query, keys), MASK_FILL)
        peak = jnp.max(scores, 1, keepdims=True)
        expo = jnp.exp(scores - peak)
        total = jnp.sum(expo, 1, keepdims=True)
        probs = (expo * (1.0 / total)).astype(jnp.bfloat16)
        outs.append(
            jnp.dot(probs, head_of(vt, vl, head), preferred_element_type=jnp.float32)
        )
        lse[0, :, head : head + 1] = peak + jnp.log(total)
    store_heads(out_t, out_l, outs)


def attend_back_kernel(length, qt, kt, vt, ql, kl, vl, got, gol, lse, *outs):
    dqt, dkt, dvt, dql, dkl, dvl = outs
    text_scale, layout_scale = scale_pair()
    live = lax.broadcasted_iota(jnp.int32, (PAGE_SLOTS, PAGE_SLOTS), 0) < length[0]
    column = lax.broadcasted_iota(jnp.int32, (1, TEXT_HEAD + LAYOUT_HEAD), 1)
    scales = jnp.where(column < TEXT_HEAD, text_scale, layout_scale)
    grads_q, grads_k, grads_v = [], [], []
    for head in range(2):
        query, keys = head_of(qt, ql, head, True), head_of(kt, kl, head)
        values, grad = head_of(vt, vl, head), head_of(got, gol, head)
        scores = jnp.where(live, contract_cols(keys, query), MASK_FILL)
        probs = jnp.exp(scores - lse[0, head : head + 1, :])
        grad_probs = contract_cols(values, grad)
        shift = jnp.sum(probs * grad_probs, 0, keepdims=True)
        grad_scores = (probs * (grad_probs - shift)).astype(jnp.bfloat16)
        grads_v.append(
            jnp.dot(probs.astype(jnp.bfloat16), grad, preferred_element_type=jnp.float32)
        )
        grads_k.append(jnp.dot(grad_scores, query, preferred_element_type=jnp.float32))
        grads_q.append(contract_rows(grad_scores, keys) * scales)
    store_heads(dqt, dql, grads_q)
    store_heads(dkt, dkl, grads_k)
    store_heads(dvt, dvl, grads_v)


def pair_specs():
    text = pl.BlockSpec((PAGE_SLOTS, 2 * TEXT_HEAD), lambda step: (0, step))
    layout = pl.BlockSpec((1, PAGE_SLOTS, 2 * LAYOUT_HEAD), lambda step: (step, 0, 0))
    return text, layout


def attend(text_qkv, layout_qkv, lengths):
    text, layout = pair_specs()
    low = jnp.bfloat16
    out_t, out_l, lse = pl.pallas_call(
        attend_kernel,
        grid=(HEAD_PAIRS,),
        in_specs=[pl.BlockSpec(memory_space=pltpu.SMEM)] + [text] * 3 + [layout] * 3,
        out_specs=[text, layout, pl.BlockSpec((1, PAGE_SLOTS, 2), lambda step: (step, 0, 0))],
        out_shape=[
            jax.ShapeDtypeStruct((PAGE_SLOTS, WIDTH), low),
            jax.ShapeDtypeStruct((HEAD_PAIRS, PAGE_SLOTS, 2 * LAYOUT_HEAD), low),
            jax.ShapeDtypeStruct((HEAD_PAIRS, PAGE_SLOTS, 2), jnp.float32),
        ],
        cost_estimate=pl.CostEstimate(
            flops=12000000000, bytes_accessed=8000000, transcendentals=3200000
        ),
        compiler_params=pltpu.CompilerParams(vmem_limit_bytes=24 * 1024 * 1024),
    )(lengths, *text_qkv, *[pair_split(item) for item in layout_qkv])
    return (out_t, pair_join(out_l), lse.transpose(0, 2, 1))


def attend_back(text_qkv, layout_qkv, lengths, lse, text_grad, layout_grad):
    text, layout = pair_specs()
    low = jnp.bfloat16
    text_out = jax.ShapeDtypeStruct((PAGE_SLOTS, WIDTH), low)
    layout_out = jax.ShapeDtypeStruct((HEAD_PAIRS, PAGE_SLOTS, 2 * LAYOUT_HEAD), low)
    outs = pl.pallas_call(
        attend_back_kernel,
        grid=(HEAD_PAIRS,),
        in_specs=[pl.BlockSpec(memory_space=pltpu.SMEM)]
        + [text] * 3
        + [layout] * 3
        + [text, layout, pl.BlockSpec((1, 2, PAGE_SLOTS), lambda step: (step, 0, 0))],
        out_specs=[text] * 3 + [layout] * 3,
        out_shape=[text_out] * 3 + [layout_out] * 3,
        cost_estimate=pl.CostEstimate(
            flops=20000000000, bytes_accessed=14000000, transcendentals=3200000
        ),
        compiler_params=pltpu.CompilerParams(vmem_limit_bytes=32 * 1024 * 1024),
    )(
        lengths,
        *text_qkv,
        *[pair_split(item) for item in layout_qkv],
        text_grad,
        pair_split(layout_grad),
        lse,
    )
    return (list(outs[:3]), [pair_join(item) for item in outs[3:]])


ERF_TERMS = (0.254829592, -0.284496736, 1.421413741, -1.453152027, 1.061405429)


def gelu_pair(values):
    size = jnp.abs(values)
    base = 1.0 / (1.0 + (0.3275911 / math.sqrt(2.0)) * size)
    series = ERF_TERMS[4]
    for term in reversed(ERF_TERMS[:4]):
        series = series * base + term
    bell = jnp.exp(values * values * -0.5)
    tail = 0.5 * series * base * bell
    share = jnp.where(values < 0.0, tail, 1.0 - tail)
    return (values * share, share + values * bell * (1.0 / math.sqrt(2.0 * math.pi)))


def ffn_kernel(rows_ref, in_ref, out_ref, bias_ref, hidden_ref, slope_ref, part_ref):
    width = rows_ref.shape[1]
    units_in, units_out = in_ref[...], out_ref[...]

    @pl.when(pl.program_id(0) == 0)
    def _():
        part_ref[...] = jnp.zeros_like(part_ref)

    step = PAGE_SLOTS // 2
    for number in range(2):
        rows = pl.ds(number * step, step)
        pre_act = contract_cols(rows_ref[rows, :], units_in) + bias_ref[...]
        hidden, slope = gelu_pair(pre_act)
        hidden = hidden.astype(jnp.bfloat16)
        hidden_ref[rows, :] = hidden
        slope_ref[rows, :] = slope.astype(jnp.bfloat16)
        part_ref[rows, :] += jnp.dot(hidden, units_out, preferred_element_type=jnp.float32)


def ffn_front(rows_in, units, bias_in, chunks):
    slots, width = rows_in.shape
    total = bias_in.shape[0]
    chunk = total // chunks
    whole = pl.BlockSpec((slots, width), lambda step: (0, 0))
    piece = pl.BlockSpec((slots, chunk), lambda step: (0, step))
    unit = pl.BlockSpec((chunk, width), lambda step: (step, 0))
    return pl.pallas_call(
        ffn_kernel,
        grid=(chunks,),
        in_specs=[whole, unit, unit, pl.BlockSpec((1, chunk), lambda step: (0, step))],
        out_specs=[piece, piece, whole],
        out_shape=[
            jax.ShapeDtypeStruct((slots, total), jnp.bfloat16),
            jax.ShapeDtypeStruct((slots, total), jnp.bfloat16),
            jax.ShapeDtypeStruct((slots, width), jnp.float32),
        ],
        cost_estimate=pl.CostEstimate(
            flops=4 * slots * width * total,
            bytes_accessed=4 * total * (width + slots),
            transcendentals=2 * slots * total,
        ),
        compiler_params=pltpu.CompilerParams(vmem_limit_bytes=40 * 1024 * 1024),
    )(rows_in, *units, bias_in[None])


def tail_route(flip):
    far, near, high, core = routes()
    return (high + [near] if flip else [near] + high) + [core]


def key_mask(key, axis):
    return sum(1 << bit for name, bit in key if name == axis)


class Spread:
    def __init__(self, block, joined, apart):
        self.joined, self.apart = list(joined), list(apart)
        self.masks = [frozenset()]
        self.pieces = {frozenset(): block[None]}

    def advance(self, wait=None):
        if self.joined:
            step = self.joined.pop(0)
            (held,) = self.pieces.values()
            came = hop(held if wait is None else tie(held, wait), *step)
            self.pieces = {frozenset(): jnp.concatenate([held, came], 0)}
            self.masks = self.masks + [mask | {step} for mask in self.masks]
            return came
        step = self.apart.pop(0)
        for key, piece in list(self.pieces.items()):
            came = hop(piece if wait is None else tie(piece, wait), *step)
            self.pieces[key | {step}] = came
        return came


def half_spread(own, near_first=False):
    far, near, high, core = routes()
    return Spread(own, [near] + far if near_first else far + [near], [core])


def half_result(chain):
    core = routes()[3]
    spot = lax.axis_index("dp")
    masks = [key_mask(mask, "dp") for mask in chain.masks]
    slot_of = {mask: number for number, mask in enumerate(masks)}
    table = jnp.array([slot_of[number] for number in range(len(masks))], jnp.int32)
    numbers = jnp.arange(len(masks))
    marks = (spot ^ numbers)[:, None] == numbers[None, :]
    places = jnp.sum(jnp.where(marks, table[None, :], 0), 1, dtype=jnp.int32)
    places = jnp.concatenate([places, own_bit(*core).astype(jnp.int32)[None]])
    own, came = chain.pieces[frozenset()], chain.pieces[frozenset([core])]
    return put_in_order(own, came, places)


def unit_spread(block, flip):
    return Spread(block, routes()[0], tail_route(flip))


def unit_keys():
    far, near, high, core = routes()
    keys = [frozenset()]
    for step in [near] + list(reversed(high)) + [core]:
        keys = keys + [key | {step} for key in keys]
    return keys


def unit_result(chain, rows):
    pieces = [chain.pieces[key] for key in unit_keys()]
    main = jnp.concatenate([piece[:, :rows] for piece in pieces], 0)
    extra = jnp.concatenate([piece[:, rows:] for piece in pieces], 0)
    return (main.reshape(-1, main.shape[-1]), extra)


def unit_blocks():
    far = [frozenset()]
    for step in routes()[0]:
        far = far + [mask | {step} for mask in far]
    masks = [key | mask for key in unit_keys() for mask in far]
    spots = jnp.array([key_mask(mask, "dp") for mask in masks], jnp.int32)
    lanes = jnp.array([key_mask(mask, "mp") for mask in masks], jnp.int32)
    lanes, spots = lanes ^ lax.axis_index("mp"), spots ^ lax.axis_index("dp")
    return lanes * lax.axis_size("dp") + spots


class UnitSum:
    def __init__(self, kept, sent, flip):
        far, near, high, core = routes()
        self.order = high + [near]
        self.left = list(reversed(tail_route(flip)[:-1])) + list(reversed(far))
        shape = (2,) * len(self.order) + (lax.axis_size("dp") // 2,) + kept.shape[1:]
        self.kept, self.came = kept.reshape(shape), hop(sent, *core).reshape(shape)

    def half(self, values, side, where):
        if where is not None:
            return lax.index_in_dim(values, side, where, keepdims=False)
        size = values.shape[0] // 2
        return values[side * size : (side + 1) * size]

    def advance(self):
        step = self.left.pop(0)
        where = self.order.index(step) if step in self.order else None
        if where is not None:
            self.order.remove(step)
        sent, kept = [
            add_low(self.half(self.kept, side, where), self.half(self.came, side, where))
            for side in (1, 0)
        ]
        self.kept, self.came = kept, hop(sent, *step)
        return self.came

    def finish(self):
        while self.left:
            self.advance()
        return (self.kept.astype(jnp.float32) + self.came.astype(jnp.float32))[0]


def to_rows(values):
    flat = values.reshape(values.shape[0], -1)
    flat = jnp.pad(flat, ((0, 0), (0, -flat.shape[1] % WIDTH)))
    return flat.reshape(values.shape[0], -1, WIDTH)


def from_rows(values, rows):
    flat = values.reshape(values.shape[0], -1)[:, : rows * LAYOUT_WIDTH]
    return flat.reshape(-1, LAYOUT_WIDTH)


class HalfSum:
    def __init__(self, halves):
        far, near, high, core = routes()
        self.order = far + [near]
        self.left = [near] + list(reversed(far))
        first = own_bit(*core) == 0
        shape = (2,) * len(self.order) + halves[0].shape[1:]
        sent = jnp.where(first, halves[1], halves[0]).reshape(shape)
        self.kept = jnp.where(first, halves[0], halves[1]).reshape(shape)
        self.came = hop(sent, *core)

    def advance(self):
        step = self.left.pop(0)
        where = self.order.index(step)
        self.order.remove(step)
        mine = own_bit(*step)

        def side(values, number):
            return lax.dynamic_index_in_dim(values, number, where, keepdims=False)

        sent = add_low(side(self.kept, 1 - mine), side(self.came, 1 - mine))
        kept = add_low(side(self.kept, mine), side(self.came, mine))
        self.kept, self.came = kept, hop(sent, *step)
        return self.came

    def finish(self):
        while self.left:
            self.advance()
        far, near, high, core = routes()
        held = add_low(self.kept, self.came)
        for step in high:
            held = add_low(held, hop(held, *step))
        other = hop(held, *core)
        first = own_bit(*core) == 0
        return jnp.stack([jnp.where(first, held, other), jnp.where(first, other, held)]).astype(
            jnp.float32
        )


def own_half(values):
    half = values.shape[-1] // 2
    return jnp.where(own_bit("mp", 0) == 0, values[..., :half], values[..., half:])


def sum_everywhere(values):
    far, near, high, core = routes()
    for step in [core] + high + [near] + far:
        values = values + hop(values, *step)
    return values


def show_all(values):
    everywhere = ("dp", "mp")
    count = lax.axis_size("dp") * lax.axis_size("mp")
    return lax.all_to_all(
        jnp.broadcast_to(values[None], (count,) + values.shape), everywhere, 0, 0, tiled=True
    )


def trade(values):
    return lax.all_to_all(values, ("dp", "mp"), 0, 0, tiled=True)


def project_qkv(rows_low, mats, vectors, width):
    joined = jnp.dot(rows_low, mats[0], preferred_element_type=jnp.float32)
    query = (joined[:, :width] + vectors[0]).astype(jnp.bfloat16)
    keys = joined[:, width:].astype(jnp.bfloat16)
    values = jnp.dot(rows_low, mats[1][:, :width], preferred_element_type=jnp.float32)
    return (query, keys, (values + vectors[1]).astype(jnp.bfloat16))


def scale_pair():
    return (1.0 / math.sqrt(WIDTH // HEADS), 1.0 / math.sqrt(LAYOUT_WIDTH // HEADS))


def project_back(rows_low, mats, grads, width):
    first = jnp.concatenate(grads[:2], 1)
    rows_grad = contract_cols(first, mats[0]) + contract_cols(grads[2], mats[1][:, :width])
    return (
        rows_grad,
        contract_rows(rows_low, first).astype(jnp.bfloat16),
        contract_rows(rows_low, grads[2]).astype(jnp.bfloat16),
        jnp.sum(grads[0], 0, dtype=jnp.float32),
        jnp.sum(grads[2], 0, dtype=jnp.float32),
    )


def ffn_back_kernel(
    rows_ref, grad_ref, in_ref, out_ref, hidden_ref, slope_ref, part_ref, bias_ref, *sums
):
    step, last = pl.program_id(0), pl.num_programs(0) // 2
    rows, grad = rows_ref[...], grad_ref[...]
    grad_hidden = contract_cols(grad, out_ref[...])
    grad_pre = grad_hidden * slope_ref[...].astype(jnp.float32)
    grad_low = grad_pre.astype(jnp.bfloat16)
    bias_ref[...] = jnp.sum(grad_low.astype(jnp.float32), 0, keepdims=True)

    @pl.when(step == 0)
    def _():
        part_ref[...] = jnp.zeros_like(part_ref)

    part_ref[...] += jnp.dot(grad_low, in_ref[...], preferred_element_type=jnp.float32)
    results = [contract_rows(grad_low, rows), contract_rows(hidden_ref[...], grad)]

    def store(targets):
        for target, result in zip(targets, results):
            if len(target.shape) == 2:
                target[...] = result.astype(target.dtype)
            else:
                blocks = result.astype(target.dtype).reshape(target.shape[0], -1, rows.shape[1])
                target[:, : blocks.shape[1], :] = blocks

    @pl.when(step < last)
    def _():
        store(sums[:2])

    @pl.when(step >= last)
    def _():
        store(sums[2:])


def ffn_back(rows_in, units, slope, hidden, grad_rows, chunks, slot_rows):
    slots, width = rows_in.shape
    total = hidden.shape[1]
    chunk, half = total // chunks, chunks // 2
    whole = pl.BlockSpec((slots, width), lambda step: (0, 0))
    piece = pl.BlockSpec((slots, chunk), lambda step: (0, step))
    unit = pl.BlockSpec((chunk, width), lambda step: (step, 0))

    def first(step):
        return jnp.minimum(step, half - 1)

    def second(step):
        return jnp.maximum(step - half, 0)

    if slot_rows is None:
        shape = (total // 2, width)
        sum_specs = [
            pl.BlockSpec((chunk, width), lambda step, turn=turn: (turn(step), 0))
            for turn in (first, first, second, second)
        ]
    else:
        rows, padded = slot_rows
        shape = (total // (2 * rows), padded, width)
        sum_specs = [
            pl.BlockSpec((chunk // rows, padded, width), lambda step, turn=turn: (turn(step), 0, 0))
            for turn in (first, first, second, second)
        ]
    return pl.pallas_call(
        ffn_back_kernel,
        grid=(chunks,),
        in_specs=[whole, whole, unit, unit, piece, piece],
        out_specs=[whole, pl.BlockSpec((1, chunk), lambda step: (0, step))] + sum_specs,
        out_shape=[
            jax.ShapeDtypeStruct((slots, width), jnp.float32),
            jax.ShapeDtypeStruct((1, total), jnp.float32),
        ]
        + [jax.ShapeDtypeStruct(shape, jnp.bfloat16)] * 4,
        cost_estimate=pl.CostEstimate(
            flops=8 * slots * width * total,
            bytes_accessed=8 * total * (width + slots),
            transcendentals=0,
        ),
        compiler_params=pltpu.CompilerParams(vmem_limit_bytes=48 * 1024 * 1024),
    )(rows_in, grad_rows, *units, hidden, slope)


def stream_forward(rows, att, mats, units, bias_in, vec):
    width = rows.shape[1]
    first = (
        rows + jnp.dot(att, mats[1][:, width:], preferred_element_type=jnp.float32) + vec[2]
    )
    mid = norm_apply(first, vec[3], vec[4])
    mid_low = mid.astype(jnp.bfloat16)
    hidden, slope, part = ffn_front(mid_low, units, bias_in, 4 if width == WIDTH else 1)
    last = mid + part + vec[5]
    return (norm_apply(last, vec[6], vec[7]), (first, mid_low, slope, hidden, last))


def layer_forward(text, layout, weights, lengths):
    (tm, lm, tu, lu, tb, lb, tv, lv) = weights[:8]
    text_low = text.astype(jnp.bfloat16)
    layout_low = layout.astype(jnp.bfloat16)
    text_qkv = project_qkv(text_low, tm, tv, WIDTH)
    layout_qkv = project_qkv(layout_low, lm, lv, LAYOUT_WIDTH)
    text_att, layout_att, log_total = attend(text_qkv, layout_qkv, lengths)
    text_new, text_kept = stream_forward(text, text_att, tm, tu, tb, tv)
    layout_new, layout_kept = stream_forward(layout, layout_att, lm, lu, lb, lv)
    cache = (
        text_low,
        layout_low,
        text_qkv,
        layout_qkv,
        log_total,
        text_att,
        layout_att,
        text_kept,
        layout_kept,
    )
    return (text_new, layout_new, cache)


def stream_back(kept, att, mats, units, vec, grad, slot_rows):
    first, mid_low, slope, hidden, last = kept
    width = first.shape[1]
    last_g, gain2, bias2 = norm_back(last, vec[6], vec[7], grad)
    in_grad, bias_in_g, *unit_grads = ffn_back(
        mid_low,
        units,
        slope,
        hidden,
        last_g.astype(jnp.bfloat16),
        4 if width == WIDTH else 2,
        slot_rows,
    )
    first_g, gain1, bias1 = norm_back(first, vec[3], vec[4], last_g + in_grad)
    first_low = first_g.astype(jnp.bfloat16)
    out_proj = contract_rows(att, first_low).astype(jnp.bfloat16)
    att_grad = contract_cols(first_low, mats[1][:, width:]).astype(jnp.bfloat16)
    vec_tail = [jnp.sum(first_g, 0), gain1, bias1, jnp.sum(last_g, 0), gain2, bias2]
    return (first_g, att_grad, out_proj, unit_grads, bias_in_g[0], vec_tail)


def layer_backward(cache, grad_text, grad_layout, weights, lengths, plan):
    (
        text_low,
        layout_low,
        text_qkv,
        layout_qkv,
        log_total,
        text_att,
        layout_att,
        text_kept,
        layout_kept,
    ) = cache
    (tm, lm, tu, lu, tb, lb, tv, lv) = weights
    count = lax.axis_size("dp") * lax.axis_size("mp")
    rows = FFN_UNITS // count
    layout_rows = -(-(LAYOUT_UNITS // count * LAYOUT_WIDTH) // WIDTH)
    padded = -(-(rows + layout_rows) // 8) * 8
    first_l, att_l, out_l, lu_g, lb_g, tail_l = stream_back(
        layout_kept, layout_att, lm, lu, lv, grad_layout, None
    )
    first_t, att_t, out_t, tu_g, tb_g, tail_t = stream_back(
        text_kept, text_att, tm, tu, tv, grad_text, (rows, padded)
    )
    joined = []
    for text_g, layout_g in zip(tu_g, lu_g):
        extra = jnp.pad(
            to_rows(layout_g.reshape(count // 2, -1, LAYOUT_WIDTH)),
            ((0, 0), (0, padded - rows - layout_rows), (0, 0)),
        )
        joined.append(lax.dynamic_update_slice(text_g, extra, (0, rows, 0)))
    att_t = plan.after_units(att_t, joined)
    text_dqkv, layout_dqkv = attend_back(
        text_qkv, layout_qkv, lengths, log_total, att_t, att_l
    )
    text_dqkv[0] = plan.after_attend(text_dqkv[0])
    rows_t, qk_t, v_t, q_bias_t, v_bias_t = project_back(text_low, tm, text_dqkv, WIDTH)
    rows_l, qk_l, v_l, q_bias_l, v_bias_l = project_back(
        layout_low, lm, layout_dqkv, LAYOUT_WIDTH
    )
    grads = (
        tb_g,
        lb_g,
        jnp.stack([q_bias_t, v_bias_t] + tail_t),
        jnp.stack([q_bias_l, v_bias_l] + tail_l),
    )
    plan.after_mats(
        (qk_t, jnp.concatenate([v_t, out_t], 1)), (qk_l, jnp.concatenate([v_l, out_l], 1))
    )
    return (first_t + rows_t, first_l + rows_l, grads)


class Plan:
    def __init__(self):
        self.units = []
        self.mats = []

    def step(self, value, items):
        return tie(value, *[item.advance() for item in items]) if items else value

    def after_units(self, value, grads):
        keep_in, keep_out, send_in, send_out = grads
        self.units.append([UnitSum(keep_in, send_in, False), UnitSum(keep_out, send_out, True)])
        if self.mats:
            return self.step(value, self.units[0] + self.mats[0][:1])
        return tie(value, *[item.came for item in self.units[0]])

    def after_attend(self, value):
        if self.mats:
            return self.step(value, self.units[0] + self.mats[0][:1] + self.units[1])
        return value

    def after_mats(self, text_halves, layout_halves):
        dp = lax.axis_size("dp")

        def blocks(halves):
            return [item.reshape(dp, -1, item.shape[-1]) for item in halves]

        self.mats.append([HalfSum(blocks(text_halves)), HalfSum(blocks(layout_halves))])

    def between(self, value):
        return self.step(value, self.units[0])


def split_high(values):
    high = values.astype(jnp.bfloat16)
    return (high, (values - high.astype(jnp.float32)).astype(jnp.bfloat16))


def add_rows(marks, values):
    high, low = split_high(values)
    return contract_rows(marks, high) + contract_rows(marks, low)


def apply_update(master, grad, moment, average, loss_count, factor):
    clipped = grad / loss_count * factor
    moment_new = MOMENTUM * moment + clipped
    master_new = master - LEARN_RATE * (clipped + MOMENTUM * moment_new)
    return (master_new, moment_new, AVERAGE_DECAY * average + (1.0 - AVERAGE_DECAY) * master_new)


def on_device(
    token_ids,
    mlm_targets,
    page_lengths,
    box_coords,
    mlm_positions,
    align_pairs,
    align_labels,
    table,
    text_mats,
    layout_mats,
    text_ffn,
    layout_ffn,
    small_params,
    table_momentum,
    text_mats_momentum,
    layout_mats_momentum,
    text_ffn_momentum,
    layout_ffn_momentum,
    small_momentum,
    table_average,
    text_mats_average,
    layout_mats_average,
    text_ffn_average,
    layout_ffn_average,
    small_average,
):
    lane, spot = lax.axis_index("mp"), lax.axis_index("dp")
    dp, mp = lax.axis_size("dp"), lax.axis_size("mp")
    count = dp * mp
    slots = PAGE_SLOTS
    mask_slots = mlm_positions.shape[1]
    pages = 1
    vocab_rows = table.shape[0]
    low = jnp.bfloat16

    own_ids = lax.dynamic_index_in_dim(token_ids, lane, 0, keepdims=False)
    own_targets = lax.dynamic_index_in_dim(mlm_targets, lane, 0, keepdims=False)
    shown = show_all(
        jnp.concatenate([own_ids, own_targets, jnp.broadcast_to(page_lengths, (mask_slots,))])
    )
    all_ids = shown[:, :slots]
    all_targets = shown[:, slots : slots + mask_slots].reshape(-1)
    all_lengths = shown[:, slots + mask_slots]
    table_low = table.astype(low)
    share = small_params.shape[0]
    line = 2 * WIDTH
    layout_rows = layout_mats.shape[1] * LAYOUT_WIDTH * 2 * LAYERS // line
    small_rows = -(-share // (16 * line)) * 8
    pad_rows = -(layout_rows + small_rows) % 16
    small_pad = jnp.pad(small_params.astype(low), (0, 2 * small_rows * line - share))
    small_half = lax.dynamic_slice_in_dim(
        small_pad, (lane & 1) * small_rows * line, small_rows * line
    ).reshape(small_rows, line)
    tmats_half = own_half(text_mats.astype(low))
    extra = jnp.concatenate(
        [
            small_half,
            own_half(layout_mats.astype(low)).reshape(layout_rows, line),
            jnp.zeros((pad_rows, line), low),
        ],
        0,
    )
    unit_rows = text_ffn.shape[1]
    layout_units = layout_ffn.shape[1]
    layout_unit_rows = -(-(layout_units * LAYOUT_WIDTH) // WIDTH)
    unit_pad = -(unit_rows + layout_unit_rows) % 8

    def unit_block(layer_no, part):
        return jnp.concatenate(
            [
                text_ffn[layer_no, :, part * WIDTH : (part + 1) * WIDTH].astype(low),
                to_rows(
                    layout_ffn[
                        layer_no : layer_no + 1, :, part * LAYOUT_WIDTH : (part + 1) * LAYOUT_WIDTH
                    ].astype(low)
                )[0],
                jnp.zeros((unit_pad, WIDTH), low),
            ],
            0,
        )

    mats_chains = [half_spread(tmats_half[layer_no]) for layer_no in range(LAYERS)]
    extra_chain = half_spread(extra, True)
    unit_chains = [
        [unit_spread(unit_block(layer_no, part), part == 1) for part in range(2)]
        for layer_no in range(LAYERS)
    ]
    far_steps = len(routes()[0])
    extra_chain.advance()
    wait = None
    for number in range(far_steps):
        wait = mats_chains[0].advance(wait)
    for number in range(far_steps):
        wait = extra_chain.advance(wait)
    for layer_no in range(LAYERS):
        if layer_no:
            for number in range(far_steps):
                wait = mats_chains[layer_no].advance(wait)
        for number in range(far_steps):
            waits = [chain.advance(wait) for chain in unit_chains[layer_no]]
            wait = waits[1]
    while extra_chain.apart:
        extra_chain.advance()
    for layer_no in range(LAYERS):
        for chain in [mats_chains[layer_no]] + unit_chains[layer_no]:
            while chain.joined or chain.apart:
                chain.advance()
    tmats_all = [half_result(chain) for chain in mats_chains]
    extra_all = half_result(extra_chain).reshape(2, dp, extra.shape[0], line)
    small_all = (
        extra_all[:, :, :small_rows]
        .transpose(1, 0, 2, 3)
        .reshape(dp, 2 * small_rows * line)[:, :share]
        .reshape(-1)
    )
    lmats_all = extra_all[:, :, small_rows : small_rows + layout_rows].reshape(
        2, dp, LAYERS, -1, 2 * LAYOUT_WIDTH
    )
    (
        text_vec,
        layout_vec,
        text_bias,
        layout_bias,
        text_emb,
        layout_emb,
        text_pos,
        layout_pos,
        box_table,
        align_mat,
    ) = unpack_small(small_all.astype(jnp.float32))

    own_block = lane * dp + spot
    steps = jnp.arange(slots)
    earlier = steps[None, :] < steps[:, None]
    all_first = ~jnp.any((all_ids[:, :, None] == all_ids[:, None, :]) & earlier[None], -1)
    all_blocks = all_ids // vocab_rows
    counts = jnp.sum(
        (all_blocks[:, None, :] == jnp.arange(count)[None, :, None]) & all_first[:, None, :],
        -1,
        dtype=jnp.int32,
    )
    rounds = (jnp.max(counts) + ROUND_ROWS - 1) // ROUND_ROWS
    mine = all_first & (all_blocks == own_block)
    order = contract_cols(mine.astype(low), earlier.astype(low)).astype(jnp.int32)
    local = all_ids - own_block * vocab_rows
    page_first = lax.dynamic_index_in_dim(all_first, spot * mp + lane, 0, keepdims=False)
    same = own_ids[:, None] == own_ids[None, :]
    first_at = jnp.min(jnp.where(same, steps[None, :], slots), 1)
    block_own = own_ids // vocab_rows
    rank = jnp.sum(
        page_first[None, :]
        & (block_own[:, None] == block_own[None, :])
        & (steps[None, :] < first_at[:, None]),
        1,
        dtype=jnp.int32,
    )
    source = (block_own % dp) * mp + block_own // dp

    def asked_marks(turn):
        turn_rank = order - turn * ROUND_ROWS
        chosen = mine[:, None, :] & (turn_rank[:, None, :] == jnp.arange(ROUND_ROWS)[None, :, None])
        rows = jnp.sum(jnp.where(chosen, local[:, None, :] + 1, 0), -1).reshape(-1) - 1
        return (rows[:, None] == jnp.arange(vocab_rows)[None, :]).astype(low)

    def held_marks(turn):
        turn_rank = rank - turn * ROUND_ROWS
        inside = (turn_rank >= 0) & (turn_rank < ROUND_ROWS)
        place = jnp.where(inside, source * ROUND_ROWS + turn_rank, -1)
        return (place[:, None] == jnp.arange(count * ROUND_ROWS)[None, :]).astype(low)

    def fetch(turn, so_far):
        rows = jnp.dot(asked_marks(turn), table_low, preferred_element_type=jnp.float32)
        came = trade(rows.astype(low))
        return so_far + jnp.dot(held_marks(turn), came, preferred_element_type=jnp.float32)

    embedded = lax.fori_loop(
        1, rounds, fetch, fetch(0, jnp.zeros((slots, WIDTH), jnp.float32))
    )

    def text_embed_fn(embed_vals, pos_table, emb_rows):
        return norm_apply(embed_vals + pos_table, emb_rows[0], emb_rows[1])

    box_marks = [
        (box_coords[number, 0][:, None] == jnp.arange(BOXES)[None, :]).astype(low)
        for number in range(4)
    ]
    box_low = box_table.astype(low)
    looked = jnp.concatenate(
        [
            jnp.dot(box_marks[number], box_low[number % 2], preferred_element_type=jnp.float32)
            for number in range(4)
        ],
        1,
    )

    text, text_pull = jax.vjp(text_embed_fn, embedded, text_pos, text_emb)
    layout, layout_pull = jax.vjp(text_embed_fn, looked, layout_pos, layout_emb)
    caches = []
    layer_weights = []
    slot_marks = (unit_blocks()[:, None] == jnp.arange(count)[None, :]).astype(jnp.float32)
    for layer_no in range(LAYERS):
        results = [unit_result(chain, unit_rows) for chain in unit_chains[layer_no]]
        weights = (
            tmats_all[layer_no],
            lmats_all[:, :, layer_no].reshape(2, LAYOUT_WIDTH, -1),
            [item[0] for item in results],
            [
                from_rows(item[1][:, :layout_unit_rows], layout_units)
                for item in results
            ],
            jnp.dot(
                slot_marks, text_bias[layer_no].reshape(count, -1), precision=PRECISE
            ).reshape(-1),
            jnp.dot(
                slot_marks, layout_bias[layer_no].reshape(count, -1), precision=PRECISE
            ).reshape(-1),
            text_vec[layer_no],
            layout_vec[layer_no],
        )
        text, layout, cache = layer_forward(text, layout, weights, page_lengths)
        caches.append(cache)
        layer_weights.append(weights)

    row_index = mlm_positions.reshape(-1)
    live_all = (
        (jnp.arange(mask_slots)[None, :] * slots < mask_slots * all_lengths[:, None])
        .astype(jnp.float32)
        .reshape(-1)
    )
    chosen_marks = (row_index[:, None] == steps[None, :]).astype(low)
    chosen_own = jnp.dot(
        chosen_marks, text.astype(low), preferred_element_type=jnp.float32
    ).astype(low)
    chosen_all = show_all(chosen_own).reshape(count * mask_slots, WIDTH)
    logits = contract_cols(chosen_all, table_low)
    target_local = all_targets - own_block * vocab_rows
    target_in = target_local[:, None] == jnp.arange(vocab_rows)[None, :]
    target_logit = jnp.sum(jnp.where(target_in, logits, 0.0), 1)
    row_peak = jnp.max(logits, axis=1)
    row_total = jnp.sum(jnp.exp(logits - row_peak[:, None]), axis=1)
    stats = show_all(jnp.stack([row_peak, row_total, target_logit]))
    all_peak = jnp.max(stats[:, 0], 0)
    all_total = jnp.sum(stats[:, 1] * jnp.exp(stats[:, 0] - all_peak[None]), 0)
    all_target = jnp.sum(stats[:, 2], 0)
    log_total = all_peak + jnp.log(all_total)
    own_start = (spot * mp + lane) * mask_slots
    live_own = lax.dynamic_slice_in_dim(live_all, own_start, mask_slots)
    own_loss = jnp.sum(
        lax.dynamic_slice_in_dim((log_total - all_target) * live_all, own_start, mask_slots)
    )
    grad_low = (
        (jnp.exp(logits - log_total[:, None]) - target_in.astype(jnp.float32)) * live_all[:, None]
    ).astype(low)
    table_grad = contract_rows(grad_low, chosen_all)
    chosen_parts = trade(jnp.dot(grad_low, table_low, preferred_element_type=jnp.float32).astype(low))
    chosen_grad = jnp.sum(
        chosen_parts.reshape(count, mask_slots, WIDTH).astype(jnp.float32), 0
    )

    first_marks = (align_pairs[0, :, 0][:, None] == steps[None, :]).astype(jnp.float32)
    second_marks = (align_pairs[0, :, 1][:, None] == steps[None, :]).astype(jnp.float32)
    answer = align_labels.reshape(-1).astype(jnp.float32)
    first_rows = jnp.dot(first_marks, text, precision=PRECISE)
    second_rows = jnp.dot(second_marks, layout, precision=PRECISE)

    def pair_loss(text_rows, layout_rows, align_weight):
        right = jnp.dot(layout_rows, align_weight, precision=PRECISE)
        logit = jnp.sum(text_rows * right, axis=-1) / math.sqrt(WIDTH)
        return jnp.sum(jax.nn.softplus(logit) - answer * logit)

    align_part, align_pull = jax.vjp(pair_loss, first_rows, second_rows, align_mat)
    first_back, second_back, align_grad = align_pull(jnp.ones((), jnp.float32))
    grad_text = add_rows(
        jnp.concatenate([first_marks.astype(low), chosen_marks], 0),
        jnp.concatenate([first_back, chosen_grad], 0),
    )
    grad_layout = add_rows(second_marks.astype(low), second_back)

    plan = Plan()
    layer_grads = [None] * LAYERS
    for layer_no in reversed(range(LAYERS)):
        grad_text, grad_layout, layer_grads[layer_no] = layer_backward(
            caches[layer_no], grad_text, grad_layout, layer_weights[layer_no], page_lengths, plan
        )
        if layer_no:
            grad_text = plan.between(grad_text)

    embed_grad, text_pos_grad, text_emb_grad = text_pull(grad_text)
    looked_grad, layout_pos_grad, layout_emb_grad = layout_pull(grad_layout)
    quarter = LAYOUT_WIDTH // 4
    box_parts = [
        add_rows(box_marks[number], looked_grad[:, number * quarter : (number + 1) * quarter])
        for number in range(4)
    ]
    box_grad = jnp.stack([box_parts[0] + box_parts[2], box_parts[1] + box_parts[3]])
    embed_low = embed_grad.astype(low)

    def give(turn, so_far):
        came = trade(contract_rows(held_marks(turn), embed_low).astype(low))
        return so_far + contract_rows(asked_marks(turn), came)

    table_sum = lax.fori_loop(1, rounds, give, give(0, table_grad))

    def stacked(member):
        return jnp.stack([layer_grads[layer_no][member] for layer_no in range(LAYERS)])

    def in_order(member):
        return jnp.stack(
            [
                lax.dot_general(
                    slot_marks,
                    layer_grads[layer_no][member].reshape(count, -1),
                    (((0,), (0,)), ((), ())),
                    precision=PRECISE,
                )
                for layer_no in range(LAYERS)
            ]
        )

    small_grad = jnp.concatenate(
        [
            item.reshape(-1)
            for item in (
                stacked(2),
                stacked(3),
                in_order(0),
                in_order(1),
                text_emb_grad,
                layout_emb_grad,
                text_pos_grad,
                layout_pos_grad,
                box_grad,
                align_grad,
            )
        ]
    )
    small_blocks = jnp.pad(
        small_grad.astype(low).reshape(dp, share), ((0, 0), (0, 2 * small_rows * line - share))
    ).reshape(dp, 2, small_rows, line)
    small_total = HalfSum([small_blocks[:, 0], small_blocks[:, 1]])
    small_sum = small_total.finish().reshape(-1)[:share]
    plan.units.reverse()
    plan.mats.reverse()

    def whole_mats(number):
        halves = [plan.mats[layer_no][number].finish() for layer_no in range(LAYERS)]
        return jnp.stack([jnp.concatenate([item[0], item[1]], 1) for item in halves])

    tmats_sum = whole_mats(0)
    lmats_sum = whole_mats(1)
    unit_sums = [
        [item.finish() for item in plan.units[layer_no]] for layer_no in range(LAYERS)
    ]
    tffn_sum = jnp.stack(
        [jnp.concatenate([item[:unit_rows] for item in pair], 1) for pair in unit_sums]
    )
    lffn_sum = jnp.stack(
        [
            jnp.concatenate(
                [
                    from_rows(item[None, unit_rows : unit_rows + layout_unit_rows], layout_units)
                    for item in pair
                ],
                1,
            )
            for pair in unit_sums
        ]
    )
    final_grads = (table_sum, tmats_sum, lmats_sum, tffn_sum, lffn_sum, small_sum)
    lane_first = (lane == 0).astype(jnp.float32)
    squares = (
        jnp.sum(table_sum * table_sum) + jnp.sum(tffn_sum * tffn_sum) + jnp.sum(lffn_sum * lffn_sum)
    )
    squares = squares + lane_first * (
        jnp.sum(tmats_sum * tmats_sum)
        + jnp.sum(lmats_sum * lmats_sum)
        + jnp.sum(small_sum * small_sum)
    )
    count_part = jnp.sum(live_own) + jnp.float32(pages * PAIRS)
    sums = sum_everywhere(
        jnp.broadcast_to(
            jnp.stack([squares, own_loss + align_part, count_part, squares])[:, None], (4, 128)
        )
    )
    total_squares, loss_sum, loss_count = sums[0, 0], sums[1, 0], sums[2, 0]
    grad_norm = jnp.sqrt(total_squares) / loss_count
    factor = jnp.minimum(1.0, CLIP_NORM / grad_norm)
    masters = (table, text_mats, layout_mats, text_ffn, layout_ffn, small_params)
    moments = (
        table_momentum,
        text_mats_momentum,
        layout_mats_momentum,
        text_ffn_momentum,
        layout_ffn_momentum,
        small_momentum,
    )
    averages = (
        table_average,
        text_mats_average,
        layout_mats_average,
        text_ffn_average,
        layout_ffn_average,
        small_average,
    )
    updated = [
        apply_update(
            masters[number],
            final_grads[number],
            moments[number],
            averages[number],
            loss_count,
            factor,
        )
        for number in range(6)
    ]
    new_masters = [item[0] for item in updated]
    new_moments = [item[1] for item in updated]
    new_averages = [item[2] for item in updated]
    copies = [item.astype(jnp.bfloat16) for item in new_masters[:5]]
    return (
        loss_sum,
        loss_count,
        grad_norm,
        new_masters[0],
        new_masters[1],
        new_masters[2],
        new_masters[3],
        new_masters[4],
        new_masters[5],
        copies[0],
        copies[1],
        copies[2],
        copies[3],
        copies[4],
        new_moments[0],
        new_moments[1],
        new_moments[2],
        new_moments[3],
        new_moments[4],
        new_moments[5],
        new_averages[0],
        new_averages[1],
        new_averages[2],
        new_averages[3],
        new_averages[4],
        new_averages[5],
    )


def solution(mesh):
    return jax.shard_map(
        on_device,
        mesh=mesh,
        in_specs=(
            P("dp", None),
            P("dp", None),
            P(("dp", "mp")),
            P(None, ("dp", "mp"), None),
            P(("dp", "mp"), None),
            P(("dp", "mp"), None, None),
            P(("dp", "mp"), None),
            P(("mp", "dp"), None),
            P(None, "dp", None),
            P(None, "dp", None),
            P(None, ("mp", "dp"), None),
            P(None, ("mp", "dp"), None),
            P("dp"),
            P(("mp", "dp"), None),
            P(None, "dp", None),
            P(None, "dp", None),
            P(None, ("mp", "dp"), None),
            P(None, ("mp", "dp"), None),
            P("dp"),
            P(("mp", "dp"), None),
            P(None, "dp", None),
            P(None, "dp", None),
            P(None, ("mp", "dp"), None),
            P(None, ("mp", "dp"), None),
            P("dp"),
        ),
        out_specs=(
            P(),
            P(),
            P(),
            P(("mp", "dp"), None),
            P(None, "dp", None),
            P(None, "dp", None),
            P(None, ("mp", "dp"), None),
            P(None, ("mp", "dp"), None),
            P("dp"),
            P(("mp", "dp"), None),
            P(None, "dp", None),
            P(None, "dp", None),
            P(None, ("mp", "dp"), None),
            P(None, ("mp", "dp"), None),
            P(("mp", "dp"), None),
            P(None, "dp", None),
            P(None, "dp", None),
            P(None, ("mp", "dp"), None),
            P(None, ("mp", "dp"), None),
            P("dp"),
            P(("mp", "dp"), None),
            P(None, "dp", None),
            P(None, "dp", None),
            P(None, ("mp", "dp"), None),
            P(None, ("mp", "dp"), None),
            P("dp"),
        ),
        check_vma=False,
    )
```

```python
import functools
import math

import jax
import jax.numpy as jnp
from jax import lax
from jax.experimental import pallas as pl
from jax.experimental.pallas import tpu as pltpu
from jax.sharding import PartitionSpec as P

WIDTH = 768
HEADS = 12
FFN_UNITS = 3072
LAYOUT_WIDTH = 192
LAYOUT_UNITS = 768
BOXES = 1024
PAGE_SLOTS = 512
PAIRS = 32
LAYERS = 2


EPSILON = 1e-05
CLIP_NORM = 0.01
LEARN_RATE = 10000.0
MOMENTUM = 0.5
AVERAGE_DECAY = 0.5
MASK_FILL = -1e30
PRECISE = lax.Precision.HIGHEST


def small_shapes():
    return [
        (LAYERS, 8, WIDTH),
        (LAYERS, 8, LAYOUT_WIDTH),
        (LAYERS, FFN_UNITS),
        (LAYERS, LAYOUT_UNITS),
        (2, WIDTH),
        (2, LAYOUT_WIDTH),
        (PAGE_SLOTS, WIDTH),
        (PAGE_SLOTS, LAYOUT_WIDTH),
        (2, BOXES // 8, 2 * LAYOUT_WIDTH),
        (LAYOUT_WIDTH, WIDTH),
    ]


def small_views():
    views = []
    offset = 0
    for piece_dims in small_shapes():
        amount = math.prod(piece_dims)
        width = piece_dims[-1] if piece_dims[-1] % 128 == 0 else 2 * piece_dims[-1]
        views.append((offset // 128, amount // width, width))
        offset = offset + amount
    return views, offset // 128


def small_half_rows(share):
    return -(-share // (128 * 32)) * 16


def pack_small(items, dp):
    views, total = small_views()
    share = total * 128 // dp
    rows = 2 * small_half_rows(share)

    def kernel(*refs):
        sources, out_ref, flat = refs[: len(items)], refs[len(items)], refs[len(items) + 1]
        flat[total:, :] = jnp.zeros((flat.shape[0] - total, 128), jnp.float32)
        for source, (start, count, width) in zip(sources, views):
            per = width // 128
            for part in range(per):
                flat[pl.ds(start + part, count, stride=per), :] = source[
                    :, part * 128 : (part + 1) * 128
                ]
        column = lax.broadcasted_iota(jnp.int32, (rows, 128), 1)
        for number in range(dp):
            start, shift = number * share // 128, number * share % 128
            block = flat[pl.ds(start, rows), :]
            if shift:
                after = flat[pl.ds(start + 1, rows), :]
                block = jnp.where(
                    column < 128 - shift,
                    pltpu.roll(block, 128 - shift, 1),
                    pltpu.roll(after, 128 - shift, 1),
                )
            out_ref[number] = block.astype(out_ref.dtype)

    whole = pl.BlockSpec(memory_space=pltpu.VMEM)
    return pl.pallas_call(
        kernel,
        out_shape=jax.ShapeDtypeStruct((dp, rows, 128), jnp.bfloat16),
        in_specs=[whole] * len(items),
        out_specs=whole,
        scratch_shapes=[pltpu.VMEM((total + rows + 8, 128), jnp.float32)],
        cost_estimate=pl.CostEstimate(flops=0, bytes_accessed=2000000, transcendentals=0),
        compiler_params=pltpu.CompilerParams(vmem_limit_bytes=32 * 1024 * 1024),
    )(*[item.reshape(count, width) for item, (start, count, width) in zip(items, views)])


def unpack_small(own, came, places, extra_rows):
    views, total = small_views()
    dp = own.shape[0]
    share = total * 128 // dp
    half = small_half_rows(share)

    def kernel(place_ref, own_ref, came_ref, *refs):
        targets, extra_ref, flat, turned = refs[:-3], refs[-3], refs[-2], refs[-1]
        mine = [(place_ref[dp] == side).astype(jnp.float32) for side in range(2)]
        for number in range(dp):
            start, shift = number * share // 128, number * share % 128
            rows = -(-(share + shift) // 128)
            slot = place_ref[number]
            for side in range(2):
                both = own_ref[slot].astype(jnp.float32), came_ref[slot].astype(jnp.float32)
                whole = jnp.where(mine[side] > 0.5, *both)
                extra_ref[side, number] = whole[half : half + extra_rows].astype(extra_ref.dtype)
                part = whole[:half]
                turned[pl.ds(8 + side * half, half), :] = (
                    pltpu.roll(part, shift, 1) if shift else part
                )
            block = turned[pl.ds(8, rows), :]
            if shift:
                turned[7:8, :] = flat[pl.ds(start, 1), :]
                column = lax.broadcasted_iota(jnp.int32, (rows, 128), 1)
                block = jnp.where(column >= shift, block, turned[pl.ds(7, rows), :])
            flat[pl.ds(start, rows), :] = block
        for target, (start, count, width) in zip(targets, views):
            per = width // 128
            for part in range(per):
                target[:, part * 128 : (part + 1) * 128] = flat[
                    pl.ds(start + part, count, stride=per), :
                ]

    whole = pl.BlockSpec(memory_space=pltpu.VMEM)
    *outs, extra = pl.pallas_call(
        kernel,
        out_shape=[
            jax.ShapeDtypeStruct((count, width), jnp.float32) for start, count, width in views
        ]
        + [jax.ShapeDtypeStruct((2, dp, extra_rows, 128), jnp.bfloat16)],
        in_specs=[pl.BlockSpec(memory_space=pltpu.SMEM), whole, whole],
        out_specs=[whole] * (len(views) + 1),
        scratch_shapes=[
            pltpu.VMEM((total + 8, 128), jnp.float32),
            pltpu.VMEM((2 * half + 16, 128), jnp.float32),
        ],
        cost_estimate=pl.CostEstimate(flops=0, bytes_accessed=2000000, transcendentals=0),
        compiler_params=pltpu.CompilerParams(vmem_limit_bytes=32 * 1024 * 1024),
    )(places, own, came)
    return [item.reshape(piece_dims) for item, piece_dims in zip(outs, small_shapes())], extra


def norm_apply(values, gain_row, bias_row):
    centre = values - jnp.mean(values, axis=-1, keepdims=True)
    spread = jnp.mean(centre * centre, axis=-1, keepdims=True)
    return centre * lax.rsqrt(spread + EPSILON) * gain_row + bias_row


def norm_back(values, gain_row, bias_row, grad_out):
    unused, pullback = jax.vjp(norm_apply, values, gain_row, bias_row)
    return pullback(grad_out)


def gelu_exact(values):
    return jax.nn.gelu(values, approximate=False)


def contract_rows(left, right):
    return lax.dot_general(
        left, right, (((0,), (0,)), ((), ())), preferred_element_type=jnp.float32
    )


def contract_cols(left, right):
    return lax.dot_general(
        left, right, (((1,), (1,)), ((), ())), preferred_element_type=jnp.float32
    )


def heads_view(values, pages):
    return values.reshape(pages, PAGE_SLOTS, HEADS, values.shape[-1] // HEADS)


ROUND_ROWS = 32


def bits_of(size):
    return list(reversed(range(size.bit_length() - 1)))


def hop(values, axis, bit):
    pairs = [(spot, spot ^ (1 << bit)) for spot in range(lax.axis_size(axis))]
    return lax.ppermute(values, axis, pairs)


def own_bit(axis, bit):
    return (lax.axis_index(axis) >> bit) & 1


def routes():
    far = [("dp", bit) for bit in bits_of(lax.axis_size("dp"))]
    high = [("mp", bit) for bit in bits_of(lax.axis_size("mp"))[:-1]]
    core = ("mp", 0)
    return (far[:-1], far[-1], high, core)


def add_low(kept, came):
    return (kept.astype(jnp.float32) + came.astype(jnp.float32)).astype(jnp.bfloat16)


def tie(value, *waits):
    def kernel(*refs):
        pass

    spec = pl.BlockSpec(memory_space=pl.ANY)
    return pl.pallas_call(
        kernel,
        out_shape=jax.ShapeDtypeStruct(value.shape, value.dtype),
        in_specs=[spec] * (1 + len(waits)),
        out_specs=spec,
        input_output_aliases={0: 0},
        cost_estimate=pl.CostEstimate(flops=0, bytes_accessed=0, transcendentals=0),
    )(value, *waits)


def put_in_order(own, came, places):
    slots, rows, width = own.shape

    def kernel(place_ref, own_ref, came_ref, out_ref, sems):
        side = place_ref[slots]

        def copies(half, source):
            return [
                pltpu.make_async_copy(
                    source.at[place_ref[spot]],
                    out_ref.at[half, pl.ds(spot * rows, rows)],
                    sems.at[half, spot],
                )
                for spot in range(slots)
            ]

        for half in range(2):
            for mine, source in ((True, own_ref), (False, came_ref)):

                @pl.when((side == half) == mine)
                def _(half=half, source=source):
                    for copy in copies(half, source):
                        copy.start()

        for half in range(2):
            for copy in copies(half, own_ref):
                copy.wait()

    anywhere = pl.BlockSpec(memory_space=pl.ANY)
    return pl.pallas_call(
        kernel,
        out_shape=jax.ShapeDtypeStruct((2, slots * rows, width), own.dtype),
        in_specs=[pl.BlockSpec(memory_space=pltpu.SMEM), anywhere, anywhere],
        out_specs=pl.BlockSpec(memory_space=pltpu.VMEM),
        scratch_shapes=[pltpu.SemaphoreType.DMA((2, slots))],
        cost_estimate=pl.CostEstimate(
            flops=0, bytes_accessed=2 * slots * rows * width, transcendentals=0
        ),
        compiler_params=pltpu.CompilerParams(vmem_limit_bytes=16 * 1024 * 1024),
    )(places, own, came)


def embed_kernel(
    coords, embedded, text_pos, layout_pos, tables, text_emb, layout_emb, *outs
):
    text_pre, layout_pre, text, layout = outs
    quarter = LAYOUT_WIDTH // 4
    low = jnp.bfloat16
    row = lax.broadcasted_iota(jnp.int32, (PAGE_SLOTS, BOXES // 8), 1)
    lanes = lax.broadcasted_iota(jnp.int32, (PAGE_SLOTS, 8 * quarter), 1) // quarter
    fold_in = lax.broadcasted_iota(jnp.int32, (8 * quarter, LAYOUT_WIDTH), 0) % quarter
    fold_out = lax.broadcasted_iota(jnp.int32, (8 * quarter, LAYOUT_WIDTH), 1)
    looked = jnp.zeros((PAGE_SLOTS, LAYOUT_WIDTH), jnp.float32)
    for number in range(4):
        spot = coords[:, number : number + 1]
        marks = (spot // 8 == row).astype(jnp.float32).astype(low)
        wide = jnp.dot(
            marks, tables[number % 2].astype(low), preferred_element_type=jnp.float32
        )
        kept = jnp.where(spot % 8 == lanes, wide, 0.0).astype(low)
        fold = (fold_in + number * quarter == fold_out).astype(jnp.float32).astype(low)
        looked = looked + jnp.dot(kept, fold, preferred_element_type=jnp.float32)
    layout_pre[...] = looked + layout_pos[...]
    text_pre[...] = embedded[...] + text_pos[...]
    text[...] = norm_apply(text_pre[...], text_emb[0:1, :], text_emb[1:2, :])
    layout[...] = norm_apply(layout_pre[...], layout_emb[0:1, :], layout_emb[1:2, :])


def embed_streams(*operands):
    whole = pl.BlockSpec(memory_space=pltpu.VMEM)
    return pl.pallas_call(
        embed_kernel,
        out_shape=[
            jax.ShapeDtypeStruct((PAGE_SLOTS, width), jnp.float32)
            for width in (WIDTH, LAYOUT_WIDTH) * 2
        ],
        in_specs=[whole] * len(operands),
        out_specs=[whole] * 4,
        cost_estimate=pl.CostEstimate(flops=0, bytes_accessed=2000000, transcendentals=0),
        compiler_params=pltpu.CompilerParams(vmem_limit_bytes=24 * 1024 * 1024),
    )(*operands)


def mats_kernel(side, rows, query, keys, values, att, first, sent_ref, kept_ref, result):
    step = pl.program_id(0)
    half = jnp.where(step < 2, 1 - side[0], side[0])
    cases = ((rows, query), (rows, keys), (rows, values), (att, first))
    for number, (left, right) in enumerate(cases):

        @pl.when(half * 2 + step % 2 == number)
        def _(left=left, right=right):
            result[...] = contract_rows(left[...], right[...])

    def store(target):
        blocks = result[...].astype(target.dtype).reshape(target.shape[0], -1, WIDTH)
        target[:, : blocks.shape[1], :] = blocks

    @pl.when(step < 2)
    def _():
        store(sent_ref)

    @pl.when(step >= 2)
    def _():
        store(kept_ref)


def mats_sums(side, operands, padded):
    dp = lax.axis_size("dp")
    whole = pl.BlockSpec((PAGE_SLOTS, WIDTH), lambda step: (0, 0))
    shape = jax.ShapeDtypeStruct((dp, padded, 2 * WIDTH), jnp.bfloat16)
    return pl.pallas_call(
        mats_kernel,
        grid=(4,),
        in_specs=[pl.BlockSpec(memory_space=pltpu.SMEM)] + [whole] * 6,
        out_specs=[
            pl.BlockSpec((dp, padded, WIDTH), lambda step: (0, 0, jnp.minimum(step, 1))),
            pl.BlockSpec((dp, padded, WIDTH), lambda step: (0, 0, jnp.maximum(step - 2, 0))),
        ],
        out_shape=[shape, shape],
        scratch_shapes=[pltpu.VMEM((WIDTH, WIDTH), jnp.float32)],
        cost_estimate=pl.CostEstimate(
            flops=2 * PAGE_SLOTS * WIDTH * WIDTH, bytes_accessed=4000000, transcendentals=0
        ),
        compiler_params=pltpu.CompilerParams(vmem_limit_bytes=32 * 1024 * 1024),
    )(side, *operands)


def take_extra(pieces, rows):
    slots, total, width = pieces[0].shape

    def kernel(*refs):
        out_ref, sems = refs[-2], refs[-1]
        copies = [
            pltpu.make_async_copy(
                ref.at[:, pl.ds(rows, total - rows)],
                out_ref.at[pl.ds(number * slots, slots)],
                sems.at[number],
            )
            for number, ref in enumerate(refs[:-2])
        ]
        for copy in copies:
            copy.start()
        for copy in copies:
            copy.wait()

    return pl.pallas_call(
        kernel,
        out_shape=jax.ShapeDtypeStruct((slots * len(pieces), total - rows, width), pieces[0].dtype),
        in_specs=[pl.BlockSpec(memory_space=pl.ANY)] * len(pieces),
        out_specs=pl.BlockSpec(memory_space=pltpu.VMEM),
        scratch_shapes=[pltpu.SemaphoreType.DMA((len(pieces),))],
        cost_estimate=pl.CostEstimate(flops=0, bytes_accessed=500000, transcendentals=0),
    )(*pieces)


HEAD_PAIRS = HEADS // 2
TEXT_HEAD = WIDTH // HEADS
LAYOUT_HEAD = LAYOUT_WIDTH // HEADS


def head_of(text_ref, layout_ref, head, scaled=False):
    text = text_ref[:, head * TEXT_HEAD : (head + 1) * TEXT_HEAD]
    layout = layout_ref[:, head * LAYOUT_HEAD : (head + 1) * LAYOUT_HEAD]
    if scaled:
        text_scale, layout_scale = scale_pair()
        text = (text.astype(jnp.float32) * text_scale).astype(text.dtype)
        layout = (layout.astype(jnp.float32) * layout_scale).astype(layout.dtype)
    return jnp.concatenate([text, layout], 1)


def store_heads(text_ref, layout_ref, both):
    text_ref[...] = jnp.concatenate([item[:, :TEXT_HEAD] for item in both], 1).astype(
        text_ref.dtype
    )
    layout = jnp.concatenate([item[:, TEXT_HEAD:] for item in both], 1).astype(layout_ref.dtype)
    width = layout.shape[1]
    for pair in range(HEAD_PAIRS):

        @pl.when(pl.program_id(0) == pair)
        def _(pair=pair):
            layout_ref[:, pair * width : (pair + 1) * width] = layout


def own_pair(sources, targets):
    width = targets[0].shape[1]
    for pair in range(HEAD_PAIRS):

        @pl.when(pl.program_id(0) == pair)
        def _(pair=pair):
            for source, target in zip(sources, targets):
                target[...] = source[:, pair * width : (pair + 1) * width]


def attend_kernel(length, qt, kt, vt, *refs):
    out_t, out_l, lse, ql, kl, vl = refs[3:]
    own_pair(refs[:3], (ql, kl, vl))
    live = lax.broadcasted_iota(jnp.int32, (PAGE_SLOTS, PAGE_SLOTS), 1) < length[0]
    outs = []
    for head in range(2):
        query, keys = head_of(qt, ql, head, True), head_of(kt, kl, head)
        scores = jnp.where(live, contract_cols(query, keys), MASK_FILL)
        peak = jnp.max(scores, 1, keepdims=True)
        expo = jnp.exp(scores - peak)
        total = jnp.sum(expo, 1, keepdims=True)
        probs = (expo * (1.0 / total)).astype(jnp.bfloat16)
        outs.append(
            jnp.dot(probs, head_of(vt, vl, head), preferred_element_type=jnp.float32)
        )
        lse[0, :, head : head + 1] = peak + jnp.log(total)
    store_heads(out_t, out_l, outs)


def attend_back_kernel(length, qt, kt, vt, got, *refs):
    lse, dqt, dkt, dvt, dql, dkl, dvl, ql, kl, vl, gol = refs[4:]
    own_pair(refs[:4], (ql, kl, vl, gol))
    text_scale, layout_scale = scale_pair()
    live = lax.broadcasted_iota(jnp.int32, (PAGE_SLOTS, PAGE_SLOTS), 0) < length[0]
    column = lax.broadcasted_iota(jnp.int32, (1, TEXT_HEAD + LAYOUT_HEAD), 1)
    scales = jnp.where(column < TEXT_HEAD, text_scale, layout_scale)
    grads_q, grads_k, grads_v = [], [], []
    for head in range(2):
        query, keys = head_of(qt, ql, head, True), head_of(kt, kl, head)
        values, grad = head_of(vt, vl, head), head_of(got, gol, head)
        scores = jnp.where(live, contract_cols(keys, query), MASK_FILL)
        probs = jnp.exp(scores - lse[0, head : head + 1, :])
        grad_probs = contract_cols(values, grad)
        shift = jnp.sum(probs * grad_probs, 0, keepdims=True)
        grad_scores = (probs * (grad_probs - shift)).astype(jnp.bfloat16)
        grads_v.append(
            jnp.dot(probs.astype(jnp.bfloat16), grad, preferred_element_type=jnp.float32)
        )
        grads_k.append(jnp.dot(grad_scores, query, preferred_element_type=jnp.float32))
        grads_q.append(contract_rows(grad_scores, keys) * scales)
    store_heads(dqt, dql, grads_q)
    store_heads(dkt, dkl, grads_k)
    store_heads(dvt, dvl, grads_v)


def pair_specs():
    text = pl.BlockSpec((PAGE_SLOTS, 2 * TEXT_HEAD), lambda step: (0, step))
    layout = pl.BlockSpec((PAGE_SLOTS, LAYOUT_WIDTH), lambda step: (0, 0))
    return text, layout, pltpu.VMEM((PAGE_SLOTS, 2 * LAYOUT_HEAD), jnp.bfloat16)


def attend(text_qkv, layout_qkv, lengths):
    text, layout, pair = pair_specs()
    low = jnp.bfloat16
    out_t, out_l, lse = pl.pallas_call(
        attend_kernel,
        grid=(HEAD_PAIRS,),
        in_specs=[pl.BlockSpec(memory_space=pltpu.SMEM)] + [text] * 3 + [layout] * 3,
        out_specs=[text, layout, pl.BlockSpec((1, PAGE_SLOTS, 2), lambda step: (step, 0, 0))],
        out_shape=[
            jax.ShapeDtypeStruct((PAGE_SLOTS, WIDTH), low),
            jax.ShapeDtypeStruct((PAGE_SLOTS, LAYOUT_WIDTH), low),
            jax.ShapeDtypeStruct((HEAD_PAIRS, PAGE_SLOTS, 2), jnp.float32),
        ],
        scratch_shapes=[pair] * 3,
        cost_estimate=pl.CostEstimate(
            flops=4000000000, bytes_accessed=2000000, transcendentals=100000
        ),
        compiler_params=pltpu.CompilerParams(vmem_limit_bytes=24 * 1024 * 1024),
    )(lengths, *text_qkv, *layout_qkv)
    return (out_t, out_l, lse.transpose(0, 2, 1))


def attend_back(text_qkv, layout_qkv, lengths, lse, text_grad, layout_grad):
    text, layout, pair = pair_specs()
    low = jnp.bfloat16
    text_out = jax.ShapeDtypeStruct((PAGE_SLOTS, WIDTH), low)
    layout_out = jax.ShapeDtypeStruct((PAGE_SLOTS, LAYOUT_WIDTH), low)
    outs = pl.pallas_call(
        attend_back_kernel,
        grid=(HEAD_PAIRS,),
        in_specs=[pl.BlockSpec(memory_space=pltpu.SMEM)]
        + [text] * 4
        + [layout] * 4
        + [pl.BlockSpec((1, 2, PAGE_SLOTS), lambda step: (step, 0, 0))],
        out_specs=[text] * 3 + [layout] * 3,
        out_shape=[text_out] * 3 + [layout_out] * 3,
        scratch_shapes=[pair] * 4,
        cost_estimate=pl.CostEstimate(
            flops=5000000000, bytes_accessed=3000000, transcendentals=100000
        ),
        compiler_params=pltpu.CompilerParams(vmem_limit_bytes=32 * 1024 * 1024),
    )(lengths, *text_qkv, text_grad, *layout_qkv, layout_grad, lse)
    return (list(outs[:3]), list(outs[3:]))


ERF_TERMS = (0.254829592, -0.284496736, 1.421413741, -1.453152027, 1.061405429)


def gelu_pair(values):
    size = jnp.abs(values)
    base = 1.0 / (1.0 + (0.3275911 / math.sqrt(2.0)) * size)
    series = ERF_TERMS[4]
    for term in reversed(ERF_TERMS[:4]):
        series = series * base + term
    bell = jnp.exp(values * values * -0.5)
    tail = 0.5 * series * base * bell
    share = jnp.where(values < 0.0, tail, 1.0 - tail)
    return (values * share, share + values * bell * (1.0 / math.sqrt(2.0 * math.pi)))


def load_units(pieces_in, pieces_out, rows, buffers, sems, chunks):
    per = len(pieces_in) // chunks
    slots = pieces_in[0].shape[0]
    step = pl.program_id(0)

    def copies(turn):
        made = []
        for number in range(per):
            for side, pieces in enumerate((pieces_in, pieces_out)):
                made.append(
                    pltpu.make_async_copy(
                        pieces[turn * per + number].at[:, pl.ds(0, rows)],
                        buffers[side].at[turn % 2, pl.ds(number * slots, slots)],
                        sems.at[turn % 2, 2 * number + side],
                    )
                )
        return made

    for turn in range(chunks):

        @pl.when(step == turn)
        def _(turn=turn):
            if turn == 0:
                for copy in copies(0):
                    copy.start()
            if turn + 1 < chunks:
                for copy in copies(turn + 1):
                    copy.start()
            for copy in copies(turn):
                copy.wait()

    slot = step % 2
    return [buffer[slot].reshape(-1, buffer.shape[-1]) for buffer in buffers]


def unit_plan(units, chunk, rows, chunks):
    width = units[0][0].shape[-1] if rows else units[0].shape[-1]
    if not rows:
        unit = pl.BlockSpec((chunk, width), lambda step: (step, 0))
        return list(units), [unit, unit], []
    anywhere = pl.BlockSpec(memory_space=pl.ANY)
    operands = list(units[0]) + list(units[1])
    buffer = pltpu.VMEM((2, chunk // rows, rows, width), jnp.bfloat16)
    sems = pltpu.SemaphoreType.DMA((2, len(operands) // chunks))
    return operands, [anywhere] * len(operands), [buffer, buffer, sems]


def take_units(refs, scratch, rows, chunks):
    if not rows:
        return [ref[...] for ref in refs]
    half = len(refs) // 2
    return load_units(refs[:half], refs[half:], rows, scratch[:2], scratch[2], chunks)


def ffn_kernel(rows, chunks, count, rows_ref, bias_ref, *refs):
    hidden_ref, slope_ref, part_ref = refs[count : count + 3]
    units_in, units_out = take_units(refs[:count], refs[count + 3 :], rows, chunks)

    @pl.when(pl.program_id(0) == 0)
    def _():
        part_ref[...] = jnp.zeros_like(part_ref)

    step = PAGE_SLOTS // 2
    for number in range(2):
        span = pl.ds(number * step, step)
        pre_act = contract_cols(rows_ref[span, :], units_in) + bias_ref[...]
        hidden, slope = gelu_pair(pre_act)
        hidden = hidden.astype(jnp.bfloat16)
        hidden_ref[span, :] = hidden
        slope_ref[span, :] = slope.astype(jnp.bfloat16)
        part_ref[span, :] += jnp.dot(hidden, units_out, preferred_element_type=jnp.float32)


def ffn_front(rows_in, units, bias_in, chunks, rows):
    slots, width = rows_in.shape
    total = bias_in.shape[0]
    chunk = total // chunks
    whole = pl.BlockSpec((slots, width), lambda step: (0, 0))
    piece = pl.BlockSpec((slots, chunk), lambda step: (0, step))
    operands, specs, scratch = unit_plan(units, chunk, rows, chunks)
    return pl.pallas_call(
        functools.partial(ffn_kernel, rows, chunks, len(operands)),
        grid=(chunks,),
        in_specs=[whole, pl.BlockSpec((1, chunk), lambda step: (0, step))] + specs,
        out_specs=[piece, piece, whole],
        out_shape=[
            jax.ShapeDtypeStruct((slots, total), jnp.bfloat16),
            jax.ShapeDtypeStruct((slots, total), jnp.bfloat16),
            jax.ShapeDtypeStruct((slots, width), jnp.float32),
        ],
        scratch_shapes=scratch,
        cost_estimate=pl.CostEstimate(
            flops=slots * width * total,
            bytes_accessed=total * (width + slots),
            transcendentals=0,
        ),
        compiler_params=pltpu.CompilerParams(vmem_limit_bytes=40 * 1024 * 1024),
    )(rows_in, bias_in[None], *operands)


def tail_route(flip):
    far, near, high, core = routes()
    return (high + [near] if flip else [near] + high) + [core]


def key_mask(key, axis):
    return sum(1 << bit for name, bit in key if name == axis)


class Spread:
    def __init__(self, block, joined, apart):
        self.joined, self.apart = list(joined), list(apart)
        self.masks = [frozenset()]
        self.pieces = {frozenset(): block[None]}

    def advance(self, wait=None):
        if self.joined:
            step = self.joined.pop(0)
            (held,) = self.pieces.values()
            held = held if wait is None else tie(held, wait)
            self.sent = [held]
            came = hop(held, *step)
            self.pieces = {frozenset(): jnp.concatenate([held, came], 0)}
            self.masks = self.masks + [mask | {step} for mask in self.masks]
            return came
        step = self.apart.pop(0)
        self.sent = []
        for key, piece in list(self.pieces.items()):
            piece = piece if wait is None else tie(piece, wait)
            self.sent.append(piece)
            came = hop(piece, *step)
            self.pieces[key] = piece
            self.pieces[key | {step}] = came
        return came


def half_spread(own, near_first=False):
    far, near, high, core = routes()
    return Spread(own, [near] + far if near_first else far + [near], [core])


def half_parts(chain):
    core = routes()[3]
    spot = lax.axis_index("dp")
    masks = [key_mask(mask, "dp") for mask in chain.masks]
    slot_of = {mask: number for number, mask in enumerate(masks)}
    table = jnp.array([slot_of[number] for number in range(len(masks))], jnp.int32)
    numbers = jnp.arange(len(masks))
    marks = (spot ^ numbers)[:, None] == numbers[None, :]
    places = jnp.sum(jnp.where(marks, table[None, :], 0), 1, dtype=jnp.int32)
    places = jnp.concatenate([places, own_bit(*core).astype(jnp.int32)[None]])
    return chain.pieces[frozenset()], chain.pieces[frozenset([core])], places


def unit_spread(block, flip):
    return Spread(block, routes()[0], tail_route(flip))


def unit_keys():
    far, near, high, core = routes()
    keys = [frozenset()]
    for step in [near] + list(reversed(high)) + [core]:
        keys = keys + [key | {step} for key in keys]
    return keys


def unit_result(chain):
    return [chain.pieces[key] for key in unit_keys()]


def unit_blocks():
    far = [frozenset()]
    for step in routes()[0]:
        far = far + [mask | {step} for mask in far]
    masks = [key | mask for key in unit_keys() for mask in far]
    spots = jnp.array([key_mask(mask, "dp") for mask in masks], jnp.int32)
    lanes = jnp.array([key_mask(mask, "mp") for mask in masks], jnp.int32)
    lanes, spots = lanes ^ lax.axis_index("mp"), spots ^ lax.axis_index("dp")
    return lanes * lax.axis_size("dp") + spots


class UnitSum:
    def __init__(self, kept, sent, flip):
        far, near, high, core = routes()
        self.order = high + [near]
        self.left = list(reversed(tail_route(flip)[:-1])) + list(reversed(far))
        shape = (2,) * len(self.order) + (lax.axis_size("dp") // 2,) + kept.shape[1:]
        self.sent = sent
        self.kept, self.came = kept.reshape(shape), hop(sent, *core).reshape(shape)

    def half(self, values, side, where):
        if where is not None:
            return lax.index_in_dim(values, side, where, keepdims=False)
        size = values.shape[0] // 2
        return values[side * size : (side + 1) * size]

    def advance(self):
        step = self.left.pop(0)
        where = self.order.index(step) if step in self.order else None
        if where is not None:
            self.order.remove(step)
        sent, kept = [
            add_low(self.half(self.kept, side, where), self.half(self.came, side, where))
            for side in (1, 0)
        ]
        self.sent = sent
        self.kept, self.came = kept, hop(sent, *step)
        return self.sent

    def finish(self):
        while self.left:
            self.advance()
        return (self.kept.astype(jnp.float32) + self.came.astype(jnp.float32))[0]


def to_rows(values):
    flat = values.reshape(values.shape[0], -1)
    flat = jnp.pad(flat, ((0, 0), (0, -flat.shape[1] % WIDTH)))
    return flat.reshape(values.shape[0], -1, WIDTH)


def from_rows(values, units):
    flat = values.reshape(values.shape[0], -1)[:, : units * 2 * LAYOUT_WIDTH]
    return flat.reshape(-1, 2 * LAYOUT_WIDTH)


class HalfSum:
    def __init__(self, sent, kept):
        far, near, high, core = routes()
        self.order = far + [near]
        self.left = [near] + list(reversed(far)) + high + [core]
        shape = (2,) * len(self.order) + sent.shape[1:]
        self.sent = sent
        self.kept, self.came = kept.reshape(shape), hop(sent, *core).reshape(shape)

    def advance(self):
        far, near, high, core = routes()
        step = self.left.pop(0)
        if step == core or step in high:
            self.kept = self.sent = add_low(self.kept, self.came)
            self.came = hop(self.kept, *step)
        else:
            where = self.order.index(step)
            self.order.remove(step)
            mine = own_bit(*step)

            def side(values, number):
                return lax.dynamic_index_in_dim(values, number, where, keepdims=False)

            sent = add_low(side(self.kept, 1 - mine), side(self.came, 1 - mine))
            kept = add_low(side(self.kept, mine), side(self.came, mine))
            self.sent = sent
            self.kept, self.came = kept, hop(sent, *step)
        return self.sent

    def finish(self):
        while self.left:
            self.advance()
        first = own_bit(*routes()[3]) == 0
        own, other = self.kept, self.came
        return jnp.stack([jnp.where(first, own, other), jnp.where(first, other, own)]).astype(
            jnp.float32
        )


def own_half(values):
    half = values.shape[-1] // 2
    return jnp.where(own_bit("mp", 0) == 0, values[..., :half], values[..., half:])


def sum_everywhere(values):
    far, near, high, core = routes()
    for step in [core] + high + [near] + far:
        values = values + hop(values, *step)
    return values


def show_all(values):
    everywhere = ("dp", "mp")
    count = lax.axis_size("dp") * lax.axis_size("mp")
    return lax.all_to_all(
        jnp.broadcast_to(values[None], (count,) + values.shape), everywhere, 0, 0, tiled=True
    )


def trade(values):
    return lax.all_to_all(values, ("dp", "mp"), 0, 0, tiled=True)


def project_qkv(rows_low, mats, vectors, width):
    joined = jnp.dot(rows_low, mats[0], preferred_element_type=jnp.float32)
    query = (joined[:, :width] + vectors[0]).astype(jnp.bfloat16)
    keys = joined[:, width:].astype(jnp.bfloat16)
    values = jnp.dot(rows_low, mats[1][:, :width], preferred_element_type=jnp.float32)
    return (query, keys, (values + vectors[1]).astype(jnp.bfloat16))


def scale_pair():
    return (1.0 / math.sqrt(WIDTH // HEADS), 1.0 / math.sqrt(LAYOUT_WIDTH // HEADS))


def project_back(mats, grads, width):
    first = jnp.concatenate(grads[:2], 1)
    rows_grad = contract_cols(first, mats[0]) + contract_cols(grads[2], mats[1][:, :width])
    return (
        rows_grad,
        jnp.sum(grads[0], 0, dtype=jnp.float32),
        jnp.sum(grads[2], 0, dtype=jnp.float32),
    )


def ffn_back_kernel(
    rows_of, chunks, count, rows_ref, grad_ref, hidden_ref, slope_ref, extra_ref, *refs
):
    part_ref, bias_ref, *sums = refs[count : count + 6]
    units_in, units_out = take_units(refs[:count], refs[count + 6 :], rows_of, chunks)
    step, last = pl.program_id(0), chunks // 2
    rows, grad = rows_ref[...], grad_ref[...]
    grad_hidden = contract_cols(grad, units_out)
    grad_pre = grad_hidden * slope_ref[...].astype(jnp.float32)
    grad_low = grad_pre.astype(jnp.bfloat16)
    bias_ref[...] = jnp.sum(grad_low.astype(jnp.float32), 0, keepdims=True)

    @pl.when(step == 0)
    def _():
        part_ref[...] = jnp.zeros_like(part_ref)

    part_ref[...] += jnp.dot(grad_low, units_in, preferred_element_type=jnp.float32)
    results = [contract_rows(grad_low, rows), contract_rows(hidden_ref[...], grad)]

    def store(targets):
        for target, result in zip(targets, results):
            if len(target.shape) == 2:
                target[...] = result.astype(target.dtype)
            else:
                blocks = result.astype(target.dtype).reshape(target.shape[0], -1, rows.shape[1])
                target[:, : blocks.shape[1], :] = blocks
                if target.shape[1] > blocks.shape[1]:
                    target[:, blocks.shape[1] :, :] = extra_ref[...]

    @pl.when(step < last)
    def _():
        store(sums[:2])

    @pl.when(step >= last)
    def _():
        store(sums[2:])


def ffn_back(rows_in, units, slope, hidden, grad_rows, chunks, slot_rows, extra):
    slots, width = rows_in.shape
    total = hidden.shape[1]
    chunk, half = total // chunks, chunks // 2
    whole = pl.BlockSpec((slots, width), lambda step: (0, 0))
    piece = pl.BlockSpec((slots, chunk), lambda step: (0, step))
    operands, specs, scratch = unit_plan(
        units, chunk, slot_rows[0] if slot_rows else None, chunks
    )

    def first(step):
        return jnp.minimum(step, half - 1)

    def second(step):
        return jnp.maximum(step - half, 0)

    turns = (first, first, second, second)
    if slot_rows is None:
        shapes = [(total // 2, width)] * 4
        sum_specs = [
            pl.BlockSpec((chunk, width), lambda step, turn=turn: (turn(step), 0)) for turn in turns
        ]
        extra_spec = pl.BlockSpec(memory_space=pltpu.VMEM)
    else:
        rows, padded = slot_rows
        heights = [padded, rows] * 2
        shapes = [(total // (2 * rows), height, width) for height in heights]
        sum_specs = [
            pl.BlockSpec((chunk // rows, height, width), lambda step, turn=turn: (turn(step), 0, 0))
            for height, turn in zip(heights, turns)
        ]
        extra_spec = pl.BlockSpec((chunk // rows, padded - rows, width), lambda step: (step, 0, 0))
    return pl.pallas_call(
        functools.partial(
            ffn_back_kernel, slot_rows[0] if slot_rows else None, chunks, len(operands)
        ),
        grid=(chunks,),
        in_specs=[whole, whole, piece, piece, extra_spec] + specs,
        out_specs=[whole, pl.BlockSpec((1, chunk), lambda step: (0, step))] + sum_specs,
        out_shape=[
            jax.ShapeDtypeStruct((slots, width), jnp.float32),
            jax.ShapeDtypeStruct((1, total), jnp.float32),
        ]
        + [jax.ShapeDtypeStruct(shape, jnp.bfloat16) for shape in shapes],
        scratch_shapes=scratch,
        cost_estimate=pl.CostEstimate(
            flops=2 * slots * width * total,
            bytes_accessed=2 * total * (width + slots),
            transcendentals=0,
        ),
        compiler_params=pltpu.CompilerParams(vmem_limit_bytes=48 * 1024 * 1024),
    )(rows_in, grad_rows, hidden, slope, extra, *operands)


def stream_forward(rows, att, mats, units, bias_in, vec, unit_rows, hook):
    width = rows.shape[1]
    first = (
        rows + jnp.dot(att, mats[1][:, width:], preferred_element_type=jnp.float32) + vec[2]
    )
    mid = norm_apply(first, vec[3], vec[4])
    mid_low = hook(mid.astype(jnp.bfloat16))
    chunks = 4 if width == WIDTH else 1
    hidden, slope, part = ffn_front(mid_low, units, bias_in, chunks, unit_rows)
    last = mid + part + vec[5]
    return (norm_apply(last, vec[6], vec[7]), (first, mid_low, slope, hidden, last))


def layer_forward(text, layout, weights, lengths, hooks):
    (tm, lm, tb, lb, tv, lv) = weights
    text_low = hooks["low"](text.astype(jnp.bfloat16))
    layout_low = layout.astype(jnp.bfloat16)
    text_qkv = list(project_qkv(text_low, tm, tv, WIDTH))
    layout_qkv = project_qkv(layout_low, lm, lv, LAYOUT_WIDTH)
    text_qkv[0] = hooks["query"](text_qkv[0])
    text_att, layout_att, log_total = attend(text_qkv, layout_qkv, lengths)
    text_att = hooks["att"](text_att)
    tu, lu = hooks["units"]()
    count = lax.axis_size("dp") * lax.axis_size("mp")
    text_new, text_kept = stream_forward(
        text, text_att, tm, tu, tb, tv, FFN_UNITS // count, hooks["mid"]
    )
    layout_new, layout_kept = stream_forward(
        layout, layout_att, lm, lu, lb, lv, None, lambda value: value
    )
    cache = (
        text_low,
        layout_low,
        text_qkv,
        layout_qkv,
        log_total,
        text_att,
        layout_att,
        text_kept,
        layout_kept,
    )
    return (text_new, layout_new, cache, (tu, lu))


def stream_back(kept, att, mats, units, vec, grad, slot_rows, hook, extra):
    first, mid_low, slope, hidden, last = kept
    width = first.shape[1]
    last_g, gain2, bias2 = norm_back(last, vec[6], vec[7], grad)
    in_grad, bias_in_g, *unit_grads = ffn_back(
        mid_low,
        units,
        slope,
        hidden,
        hook(last_g.astype(jnp.bfloat16)),
        4 if width == WIDTH else 2,
        slot_rows,
        extra,
    )
    first_g, gain1, bias1 = norm_back(first, vec[3], vec[4], last_g + in_grad)
    first_low = first_g.astype(jnp.bfloat16)
    att_grad = contract_cols(first_low, mats[1][:, width:]).astype(jnp.bfloat16)
    vec_tail = [jnp.sum(first_g, 0), gain1, bias1, jnp.sum(last_g, 0), gain2, bias2]
    return (first_g, att_grad, first_low, unit_grads, bias_in_g[0], vec_tail)


def layer_backward(cache, grad_text, grad_layout, weights, lengths, plan):
    (
        text_low,
        layout_low,
        text_qkv,
        layout_qkv,
        log_total,
        text_att,
        layout_att,
        text_kept,
        layout_kept,
    ) = cache
    (tm, lm, tu, lu, tb, lb, tv, lv) = weights
    count = lax.axis_size("dp") * lax.axis_size("mp")
    rows = FFN_UNITS // count
    none = jnp.zeros((8, 128), jnp.float32)
    first_l, att_l, out_l, lu_g, lb_g, tail_l = stream_back(
        layout_kept, layout_att, lm, lu, lv, grad_layout, None, lambda value: value, none
    )
    halves = [jnp.concatenate(lu_g[2 * side : 2 * side + 2], 1) for side in range(2)]
    extra = to_rows(jnp.concatenate(halves, 0).reshape(count, -1, 2 * LAYOUT_WIDTH))
    extra = jnp.pad(extra, ((0, 0), (0, -extra.shape[1] % 16), (0, 0)))
    slot_rows = (rows, rows + extra.shape[1])
    first_t, att_t, out_t, tu_g, tb_g, tail_t = stream_back(
        text_kept, text_att, tm, tu, tv, grad_text, slot_rows, plan.before_units, extra
    )
    att_t = plan.after_units(att_t, tu_g)
    text_dqkv, layout_dqkv = attend_back(
        text_qkv, layout_qkv, lengths, log_total, att_t, att_l
    )
    text_dqkv[0] = plan.after_attend(text_dqkv[0])
    plan.after_mats(
        (text_low, *text_dqkv, text_att, out_t), (layout_low, *layout_dqkv, layout_att, out_l)
    )
    rows_t, q_bias_t, v_bias_t = project_back(tm, text_dqkv, WIDTH)
    rows_l, q_bias_l, v_bias_l = project_back(lm, layout_dqkv, LAYOUT_WIDTH)
    grads = (
        tb_g,
        lb_g,
        jnp.stack([q_bias_t, v_bias_t] + tail_t),
        jnp.stack([q_bias_l, v_bias_l] + tail_l),
    )
    return (first_t + rows_t, first_l + rows_l, grads)


class Plan:
    def __init__(self):
        self.units = []
        self.mats = []

    def step(self, value, items):
        return tie(value, *[item.advance() for item in items])

    def before_units(self, value):
        return self.step(value, self.mats[:1]) if self.mats else value

    def after_units(self, value, grads):
        keep_in, keep_out, send_in, send_out = grads
        self.units.append([UnitSum(keep_in, send_in, False), UnitSum(keep_out, send_out, True)])
        if self.mats:
            return self.step(value, self.units[0] + self.mats[:1])
        return self.step(value, self.units[0])

    def after_attend(self, value):
        if self.mats:
            return self.step(value, self.units[0] + self.mats[:1] + self.units[1])
        return value

    def after_mats(self, text, layout):
        dp = lax.axis_size("dp")
        low = jnp.bfloat16
        side = own_bit("mp", 0).astype(jnp.int32)
        rows, query, keys, values, att, first = layout
        first_half = contract_rows(rows, jnp.concatenate([query, keys], 1)).astype(low)
        second_half = jnp.concatenate(
            [contract_rows(rows, values), contract_rows(att, first)], 1
        ).astype(low)
        text_rows = WIDTH // dp
        extras = [
            jnp.where(side == number, second_half, first_half).reshape(dp, -1, 2 * WIDTH)
            for number in range(2)
        ]
        padded = -(-(text_rows + extras[0].shape[1]) // 8) * 8
        pad = ((0, 0), (0, padded - text_rows - extras[0].shape[1]), (0, 0))
        sums = mats_sums(side[None], text, padded)
        sent, kept = [
            lax.dynamic_update_slice(item, jnp.pad(extra, pad), (0, text_rows, 0))
            for item, extra in zip(sums, extras)
        ]
        self.mats.append(HalfSum(sent, kept))

    def between(self, value):
        if len(self.mats) == 1:
            return self.step(tie(value, self.mats[0].sent), self.units[0])
        return self.step(tie(value, self.mats[1].sent), self.mats[:1])


def split_high(values):
    high = values.astype(jnp.bfloat16)
    return (high, (values - high.astype(jnp.float32)).astype(jnp.bfloat16))


def add_rows(marks, values):
    high, low = split_high(values)
    return contract_rows(marks, high) + contract_rows(marks, low)


def apply_update(master, grad, moment, average, loss_count, factor):
    clipped = grad / loss_count * factor
    moment_new = MOMENTUM * moment + clipped
    master_new = master - LEARN_RATE * (clipped + MOMENTUM * moment_new)
    return (master_new, moment_new, AVERAGE_DECAY * average + (1.0 - AVERAGE_DECAY) * master_new)


def on_device(
    token_ids,
    mlm_targets,
    page_lengths,
    box_coords,
    mlm_positions,
    align_pairs,
    align_labels,
    table,
    text_mats,
    layout_mats,
    text_ffn,
    layout_ffn,
    small_params,
    table_momentum,
    text_mats_momentum,
    layout_mats_momentum,
    text_ffn_momentum,
    layout_ffn_momentum,
    small_momentum,
    table_average,
    text_mats_average,
    layout_mats_average,
    text_ffn_average,
    layout_ffn_average,
    small_average,
):
    lane, spot = lax.axis_index("mp"), lax.axis_index("dp")
    dp, mp = lax.axis_size("dp"), lax.axis_size("mp")
    count = dp * mp
    slots = PAGE_SLOTS
    mask_slots = mlm_positions.shape[1]
    pages = 1
    vocab_rows = table.shape[0]
    low = jnp.bfloat16

    own_ids = lax.dynamic_index_in_dim(token_ids, lane, 0, keepdims=False)
    own_targets = lax.dynamic_index_in_dim(mlm_targets, lane, 0, keepdims=False)
    shown = show_all(
        jnp.concatenate([own_ids, own_targets, jnp.broadcast_to(page_lengths, (mask_slots,))])
    )
    all_ids = shown[:, :slots]
    all_targets = shown[:, slots : slots + mask_slots].reshape(-1)
    all_lengths = shown[:, slots + mask_slots]
    table_low = table.astype(low)
    own_block = lane * dp + spot
    steps = jnp.arange(slots)
    earlier = steps[None, :] < steps[:, None]
    all_first = ~jnp.any((all_ids[:, :, None] == all_ids[:, None, :]) & earlier[None], -1)
    all_blocks = all_ids // vocab_rows
    counts = jnp.sum(
        (all_blocks[:, None, :] == jnp.arange(count)[None, :, None]) & all_first[:, None, :],
        -1,
        dtype=jnp.int32,
    )
    rounds = (jnp.max(counts) + ROUND_ROWS - 1) // ROUND_ROWS
    mine = all_first & (all_blocks == own_block)
    order = contract_cols(mine.astype(low), earlier.astype(low)).astype(jnp.int32)
    local = all_ids - own_block * vocab_rows
    page_first = lax.dynamic_index_in_dim(all_first, spot * mp + lane, 0, keepdims=False)
    same = own_ids[:, None] == own_ids[None, :]
    first_at = jnp.min(jnp.where(same, steps[None, :], slots), 1)
    block_own = own_ids // vocab_rows
    rank = jnp.sum(
        page_first[None, :]
        & (block_own[:, None] == block_own[None, :])
        & (steps[None, :] < first_at[:, None]),
        1,
        dtype=jnp.int32,
    )
    source = (block_own % dp) * mp + block_own // dp

    def asked_marks(turn):
        turn_rank = order - turn * ROUND_ROWS
        chosen = mine[:, None, :] & (turn_rank[:, None, :] == jnp.arange(ROUND_ROWS)[None, :, None])
        rows = jnp.sum(jnp.where(chosen, local[:, None, :] + 1, 0), -1).reshape(-1) - 1
        return (rows[:, None] == jnp.arange(vocab_rows)[None, :]).astype(low)

    def held_marks(turn):
        turn_rank = rank - turn * ROUND_ROWS
        inside = (turn_rank >= 0) & (turn_rank < ROUND_ROWS)
        place = jnp.where(inside, source * ROUND_ROWS + turn_rank, -1)
        return (place[:, None] == jnp.arange(count * ROUND_ROWS)[None, :]).astype(low)

    def fetch(turn, so_far):
        rows = jnp.dot(asked_marks(turn), table_low, preferred_element_type=jnp.float32)
        sent = rows.astype(low)
        came = trade(sent)
        return (
            so_far + jnp.dot(held_marks(turn), came, preferred_element_type=jnp.float32),
            came,
            sent,
        )

    share = small_params.shape[0]
    line = 2 * WIDTH
    half_rows = small_half_rows(share)
    small_pad = jnp.pad(small_params.astype(low), (0, 2 * half_rows * 128 - share))
    small_half = lax.dynamic_slice_in_dim(
        small_pad.reshape(2 * half_rows, 128), (lane & 1) * half_rows, half_rows
    )
    tmats_half = own_half(text_mats.astype(low))
    lmats_half = own_half(layout_mats.astype(low)).reshape(-1, 128)
    extra = jnp.concatenate(
        [small_half, lmats_half, jnp.zeros((-lmats_half.shape[0] % 16, 128), low)], 0
    )
    unit_rows = text_ffn.shape[1]
    layout_units = layout_ffn.shape[1]
    layout_unit_rows = -(-(2 * layout_units * LAYOUT_WIDTH) // WIDTH)
    unit_pad = -layout_unit_rows % 16

    def unit_block(layer_no, part):
        text_part = text_ffn[layer_no, :, part * WIDTH : (part + 1) * WIDTH].astype(low)
        if part:
            return text_part
        return jnp.concatenate(
            [
                text_part,
                to_rows(layout_ffn[layer_no : layer_no + 1].astype(low))[0],
                jnp.zeros((unit_pad, WIDTH), low),
            ],
            0,
        )

    mats_chains = [half_spread(tmats_half[layer_no]) for layer_no in range(LAYERS)]
    extra_chain = half_spread(extra, True)
    unit_chains = [
        [unit_spread(unit_block(layer_no, part), part == 1) for part in range(2)]
        for layer_no in range(LAYERS)
    ]
    far_steps = len(routes()[0])
    embedded, came_first, rows_first = fetch(0, jnp.zeros((slots, WIDTH), jnp.float32))
    embedded = lax.fori_loop(
        1, rounds, lambda turn, so_far: fetch(turn, so_far)[0], embedded
    )
    for number in range(far_steps + 1):
        extra_wait = extra_chain.advance()
        if number < far_steps:
            mats_chains[0].advance()
    mats_chains[0].advance()
    extra_chain.advance(rows_first)
    mats_chains[0].advance()
    for number in range(far_steps):
        for chain in unit_chains[0]:
            chain.advance(extra_wait)
        extra_wait = unit_chains[0][1].sent[0]
    core_key = frozenset([routes()[3]])
    extra_chain.pieces[core_key] = tie(extra_chain.pieces[core_key], came_first)
    small_parts, lmats_all = unpack_small(*half_parts(extra_chain), lmats_half.shape[0])
    lmats_all = lmats_all.reshape(2, dp, LAYERS, -1, 2 * LAYOUT_WIDTH)
    tmats_first = put_in_order(*half_parts(mats_chains[0]))
    (
        text_vec,
        layout_vec,
        text_bias,
        layout_bias,
        text_emb,
        layout_emb,
        text_pos,
        layout_pos,
        box_table,
        align_mat,
    ) = small_parts

    quarter = LAYOUT_WIDTH // 4
    lanes = jnp.arange(8 * quarter)
    fold = (lanes[:, None] % quarter == jnp.arange(quarter)[None, :]).astype(low)
    box_marks, box_masks = [], []
    for number in range(4):
        coords = box_coords[number, 0][:, None]
        box_marks.append((coords // 8 == jnp.arange(BOXES // 8)[None, :]).astype(low))
        box_masks.append(coords % 8 == lanes[None, :] // quarter)
    text_pre, layout_pre, text, layout = embed_streams(
        box_coords[:, 0].T, embedded, text_pos, layout_pos, box_table, text_emb, layout_emb
    )
    caches = []
    layer_weights = []

    def push(value, chains):
        waits = []
        for chain in chains:
            chain.advance()
            waits = waits + chain.sent
        return tie(value, *waits)

    def settle(chains, left):
        for chain in chains:
            while len(chain.joined) + len(chain.apart) > left:
                chain.advance()

    def after(chains, wait):
        for chain in chains:
            chain.advance(wait)

    def hooks_of(layer_no):
        units = unit_chains[layer_no]
        later = layer_no + 1 < LAYERS
        if later:
            next_mats, next_units = mats_chains[layer_no + 1], unit_chains[layer_no + 1]

        def at_low(value):
            if layer_no == 0:
                value = push(value, units)
            if later:
                value = push(value, [next_mats])
            return value

        def at_query(value):
            if layer_no:
                value = push(value, units)
            if later:
                value = push(value, [next_mats])
            return value

        def at_att(value):
            settle(units, 2)
            value = push(value, units + ([next_mats] if later else []))
            after(units, value)
            return value

        def at_mid(value):
            return push(value, next_units) if later else value

        return {
            "low": at_low,
            "query": at_query,
            "att": at_att,
            "mid": at_mid,
            "units": lambda: units_of(layer_no),
        }

    def units_of(layer_no):
        results = [unit_result(chain) for chain in unit_chains[layer_no]]
        layout_both = from_rows(
            take_extra(results[0], unit_rows)[:, :layout_unit_rows], layout_units
        )
        return (results, [layout_both[:, :LAYOUT_WIDTH], layout_both[:, LAYOUT_WIDTH:]])

    slot_marks = (unit_blocks()[:, None] == jnp.arange(count)[None, :]).astype(jnp.float32)
    for layer_no in range(LAYERS):
        if layer_no:
            settle([mats_chains[layer_no]], 1)
            text = push(text, unit_chains[layer_no] + [mats_chains[layer_no]])
            tmats = put_in_order(*half_parts(mats_chains[layer_no]))
        else:
            tmats = tmats_first
        weights = [
            tmats,
            lmats_all[:, :, layer_no].reshape(2, LAYOUT_WIDTH, -1),
            jnp.dot(
                slot_marks, text_bias[layer_no].reshape(count, -1), precision=PRECISE
            ).reshape(-1),
            jnp.dot(
                slot_marks, layout_bias[layer_no].reshape(count, -1), precision=PRECISE
            ).reshape(-1),
            text_vec[layer_no],
            layout_vec[layer_no],
        ]
        text, layout, cache, units = layer_forward(
            text, layout, weights, page_lengths, hooks_of(layer_no)
        )
        weights = weights[:2] + list(units) + weights[2:]
        caches.append(cache)
        layer_weights.append(weights)

    row_index = mlm_positions.reshape(-1)
    live_all = (
        (jnp.arange(mask_slots)[None, :] * slots < mask_slots * all_lengths[:, None])
        .astype(jnp.float32)
        .reshape(-1)
    )
    chosen_marks = (row_index[:, None] == steps[None, :]).astype(low)
    chosen_own = jnp.dot(
        chosen_marks, text.astype(low), preferred_element_type=jnp.float32
    ).astype(low)
    chosen_all = show_all(chosen_own).reshape(count * mask_slots, WIDTH)
    logits = contract_cols(chosen_all, table_low)
    target_local = all_targets - own_block * vocab_rows
    target_in = target_local[:, None] == jnp.arange(vocab_rows)[None, :]
    target_logit = jnp.sum(jnp.where(target_in, logits, 0.0), 1)
    row_peak = jnp.max(logits, axis=1)
    row_total = jnp.sum(jnp.exp(logits - row_peak[:, None]), axis=1)
    stats = show_all(jnp.stack([row_peak, row_total, target_logit]))
    all_peak = jnp.max(stats[:, 0], 0)
    all_total = jnp.sum(stats[:, 1] * jnp.exp(stats[:, 0] - all_peak[None]), 0)
    all_target = jnp.sum(stats[:, 2], 0)
    log_total = all_peak + jnp.log(all_total)
    own_start = (spot * mp + lane) * mask_slots
    live_own = lax.dynamic_slice_in_dim(live_all, own_start, mask_slots)
    own_loss = jnp.sum(
        lax.dynamic_slice_in_dim((log_total - all_target) * live_all, own_start, mask_slots)
    )
    grad_low = (
        (jnp.exp(logits - log_total[:, None]) - target_in.astype(jnp.float32)) * live_all[:, None]
    ).astype(low)
    table_grad = contract_rows(grad_low, chosen_all)
    chosen_parts = trade(jnp.dot(grad_low, table_low, preferred_element_type=jnp.float32).astype(low))
    chosen_grad = jnp.sum(
        chosen_parts.reshape(count, mask_slots, WIDTH).astype(jnp.float32), 0
    )

    first_marks = (align_pairs[0, :, 0][:, None] == steps[None, :]).astype(jnp.float32)
    second_marks = (align_pairs[0, :, 1][:, None] == steps[None, :]).astype(jnp.float32)
    answer = align_labels.reshape(-1).astype(jnp.float32)
    first_rows = jnp.dot(first_marks, text, precision=PRECISE)
    second_rows = jnp.dot(second_marks, layout, precision=PRECISE)

    def pair_loss(text_rows, layout_rows, align_weight):
        right = jnp.dot(layout_rows, align_weight, precision=PRECISE)
        logit = jnp.sum(text_rows * right, axis=-1) / math.sqrt(WIDTH)
        return jnp.sum(jax.nn.softplus(logit) - answer * logit)

    align_part, align_pull = jax.vjp(pair_loss, first_rows, second_rows, align_mat)
    first_back, second_back, align_grad = align_pull(jnp.ones((), jnp.float32))
    grad_text = add_rows(
        jnp.concatenate([first_marks.astype(low), chosen_marks], 0),
        jnp.concatenate([first_back, chosen_grad], 0),
    )
    grad_layout = add_rows(second_marks.astype(low), second_back)

    plan = Plan()
    layer_grads = [None] * LAYERS
    for layer_no in reversed(range(LAYERS)):
        grad_text, grad_layout, layer_grads[layer_no] = layer_backward(
            caches[layer_no], grad_text, grad_layout, layer_weights[layer_no], page_lengths, plan
        )
        grad_text = plan.between(grad_text)

    embed_grad, *text_emb_grad = norm_back(text_pre, text_emb[0], text_emb[1], grad_text)
    looked_grad, *layout_emb_grad = norm_back(
        layout_pre,
        layout_emb[0],
        layout_emb[1],
        tie(grad_layout, plan.mats[1].advance()),
    )
    text_emb_grad, layout_emb_grad = jnp.stack(text_emb_grad), jnp.stack(layout_emb_grad)
    box_parts = []
    for number in range(4):
        high, rest = split_high(looked_grad[:, number * quarter : (number + 1) * quarter])
        wide = contract_cols(high, fold) + contract_cols(rest, fold)
        box_parts.append(jnp.where(box_masks[number], wide, 0.0))
    box_grad = jnp.stack(
        [
            add_rows(
                jnp.concatenate([box_marks[side], box_marks[side + 2]], 0),
                jnp.concatenate([box_parts[side], box_parts[side + 2]], 0),
            )
            for side in range(2)
        ]
    )
    embed_low = embed_grad.astype(low)

    def give(turn, so_far):
        sent = contract_rows(held_marks(turn), embed_low).astype(low)
        return (so_far + contract_rows(asked_marks(turn), trade(sent)), sent)

    table_sum, gave_rows = give(0, table_grad)
    table_sum = lax.fori_loop(1, rounds, lambda turn, so_far: give(turn, so_far)[0], table_sum)

    def stacked(member):
        return jnp.stack([layer_grads[layer_no][member] for layer_no in range(LAYERS)])

    def in_order(member):
        return jnp.stack(
            [
                lax.dot_general(
                    slot_marks,
                    layer_grads[layer_no][member].reshape(count, -1),
                    (((0,), (0,)), ((), ())),
                    precision=PRECISE,
                )
                for layer_no in range(LAYERS)
            ]
        )

    small_items = [
        stacked(2),
        stacked(3),
        in_order(0),
        in_order(1),
        text_emb_grad,
        layout_emb_grad,
        embed_grad,
        looked_grad,
        box_grad,
        align_grad,
    ]
    small_items[6] = tie(
        embed_grad, gave_rows, *[item.advance() for item in plan.units[1]]
    )
    small_blocks = pack_small(small_items, dp).reshape(dp, 2, half_rows, 128)
    first = own_bit("mp", 0) == 0
    small_total = HalfSum(
        jnp.where(first, small_blocks[:, 1], small_blocks[:, 0]),
        jnp.where(first, small_blocks[:, 0], small_blocks[:, 1]),
    )
    chains = [plan.mats[1], small_total] + plan.units[1] + plan.units[0] + plan.mats[:1]
    while any(chain.left for chain in chains):
        for chain in chains:
            if chain.left:
                chain.advance()
    small_sum = small_total.finish().reshape(-1)[:share]
    plan.units.reverse()
    plan.mats.reverse()
    mats_sums = [item.finish() for item in plan.mats]
    mats_rows = text_mats.shape[1]
    extra_rows = layout_mats.shape[1] * LAYOUT_WIDTH * 2 // line
    tmats_sum = jnp.stack(
        [jnp.concatenate([item[0, :mats_rows], item[1, :mats_rows]], 1) for item in mats_sums]
    )
    lmats_sum = jnp.stack(
        [
            jnp.concatenate(
                [
                    item[side, mats_rows : mats_rows + extra_rows].reshape(-1, 2 * LAYOUT_WIDTH)
                    for side in range(2)
                ],
                1,
            )
            for item in mats_sums
        ]
    )
    unit_sums = [
        [item.finish() for item in plan.units[layer_no]] for layer_no in range(LAYERS)
    ]
    tffn_sum = jnp.stack(
        [jnp.concatenate([item[:unit_rows] for item in pair], 1) for pair in unit_sums]
    )
    lffn_sum = jnp.stack(
        [
            from_rows(pair[0][None, unit_rows : unit_rows + layout_unit_rows], layout_units)
            for pair in unit_sums
        ]
    )
    final_grads = (table_sum, tmats_sum, lmats_sum, tffn_sum, lffn_sum, small_sum)
    lane_first = (lane == 0).astype(jnp.float32)
    squares = (
        jnp.sum(table_sum * table_sum) + jnp.sum(tffn_sum * tffn_sum) + jnp.sum(lffn_sum * lffn_sum)
    )
    squares = squares + lane_first * (
        jnp.sum(tmats_sum * tmats_sum)
        + jnp.sum(lmats_sum * lmats_sum)
        + jnp.sum(small_sum * small_sum)
    )
    count_part = jnp.sum(live_own) + jnp.float32(pages * PAIRS)
    sums = sum_everywhere(
        jnp.broadcast_to(
            jnp.stack([squares, own_loss + align_part, count_part, squares])[:, None], (4, 128)
        )
    )
    total_squares, loss_sum, loss_count = sums[0, 0], sums[1, 0], sums[2, 0]
    grad_norm = jnp.sqrt(total_squares) / loss_count
    factor = jnp.minimum(1.0, CLIP_NORM / grad_norm)
    masters = (table, text_mats, layout_mats, text_ffn, layout_ffn, small_params)
    moments = (
        table_momentum,
        text_mats_momentum,
        layout_mats_momentum,
        text_ffn_momentum,
        layout_ffn_momentum,
        small_momentum,
    )
    averages = (
        table_average,
        text_mats_average,
        layout_mats_average,
        text_ffn_average,
        layout_ffn_average,
        small_average,
    )
    updated = [
        apply_update(
            masters[number],
            final_grads[number],
            moments[number],
            averages[number],
            loss_count,
            factor,
        )
        for number in range(6)
    ]
    new_masters = [item[0] for item in updated]
    new_moments = [item[1] for item in updated]
    new_averages = [item[2] for item in updated]
    copies = [item.astype(jnp.bfloat16) for item in new_masters[:5]]
    return (
        loss_sum,
        loss_count,
        grad_norm,
        new_masters[0],
        new_masters[1],
        new_masters[2],
        new_masters[3],
        new_masters[4],
        new_masters[5],
        copies[0],
        copies[1],
        copies[2],
        copies[3],
        copies[4],
        new_moments[0],
        new_moments[1],
        new_moments[2],
        new_moments[3],
        new_moments[4],
        new_moments[5],
        new_averages[0],
        new_averages[1],
        new_averages[2],
        new_averages[3],
        new_averages[4],
        new_averages[5],
    )


def solution(mesh):
    return jax.shard_map(
        on_device,
        mesh=mesh,
        in_specs=(
            P("dp", None),
            P("dp", None),
            P(("dp", "mp")),
            P(None, ("dp", "mp"), None),
            P(("dp", "mp"), None),
            P(("dp", "mp"), None, None),
            P(("dp", "mp"), None),
            P(("mp", "dp"), None),
            P(None, "dp", None),
            P(None, "dp", None),
            P(None, ("mp", "dp"), None),
            P(None, ("mp", "dp"), None),
            P("dp"),
            P(("mp", "dp"), None),
            P(None, "dp", None),
            P(None, "dp", None),
            P(None, ("mp", "dp"), None),
            P(None, ("mp", "dp"), None),
            P("dp"),
            P(("mp", "dp"), None),
            P(None, "dp", None),
            P(None, "dp", None),
            P(None, ("mp", "dp"), None),
            P(None, ("mp", "dp"), None),
            P("dp"),
        ),
        out_specs=(
            P(),
            P(),
            P(),
            P(("mp", "dp"), None),
            P(None, "dp", None),
            P(None, "dp", None),
            P(None, ("mp", "dp"), None),
            P(None, ("mp", "dp"), None),
            P("dp"),
            P(("mp", "dp"), None),
            P(None, "dp", None),
            P(None, "dp", None),
            P(None, ("mp", "dp"), None),
            P(None, ("mp", "dp"), None),
            P(("mp", "dp"), None),
            P(None, "dp", None),
            P(None, "dp", None),
            P(None, ("mp", "dp"), None),
            P(None, ("mp", "dp"), None),
            P("dp"),
            P(("mp", "dp"), None),
            P(None, "dp", None),
            P(None, "dp", None),
            P(None, ("mp", "dp"), None),
            P(None, ("mp", "dp"), None),
            P("dp"),
        ),
        check_vma=False,
    )
```

```python
import functools
import math

import jax
import jax.numpy as jnp
from jax import lax
from jax.experimental import pallas as pl
from jax.experimental.pallas import tpu as pltpu
from jax.sharding import PartitionSpec as P

WIDTH = 768
HEADS = 12
FFN_UNITS = 3072
LAYOUT_WIDTH = 192
LAYOUT_UNITS = 768
BOXES = 1024
PAGE_SLOTS = 512
PAIRS = 32
LAYERS = 2


EPSILON = 1e-05
CLIP_NORM = 0.01
LEARN_RATE = 10000.0
MOMENTUM = 0.5
AVERAGE_DECAY = 0.5
MASK_FILL = -1e30
PRECISE = lax.Precision.HIGHEST


def small_shapes():
    return [
        (LAYERS, 8, WIDTH),
        (LAYERS, 8, LAYOUT_WIDTH),
        (LAYERS, FFN_UNITS),
        (LAYERS, LAYOUT_UNITS),
        (2, WIDTH),
        (2, LAYOUT_WIDTH),
        (PAGE_SLOTS, WIDTH),
        (PAGE_SLOTS, LAYOUT_WIDTH),
        (2, BOXES // 8, 2 * LAYOUT_WIDTH),
        (LAYOUT_WIDTH, WIDTH),
    ]


def small_views():
    views = []
    offset = 0
    for piece_dims in small_shapes():
        amount = math.prod(piece_dims)
        width = piece_dims[-1] if piece_dims[-1] % 128 == 0 else 2 * piece_dims[-1]
        views.append((offset // 128, amount // width, width))
        offset = offset + amount
    return views, offset // 128


def small_half_rows(share):
    return -(-share // (128 * 32)) * 16


def pack_small(items, dp):
    views, total = small_views()
    share = total * 128 // dp
    rows = 2 * small_half_rows(share)

    def kernel(*refs):
        sources, out_ref, flat = refs[: len(items)], refs[len(items)], refs[len(items) + 1]
        flat[total:, :] = jnp.zeros((flat.shape[0] - total, 128), jnp.float32)
        for source, (start, count, width) in zip(sources, views):
            per = width // 128
            for part in range(per):
                flat[pl.ds(start + part, count, stride=per), :] = source[
                    :, part * 128 : (part + 1) * 128
                ]
        column = lax.broadcasted_iota(jnp.int32, (rows, 128), 1)
        for number in range(dp):
            start, shift = number * share // 128, number * share % 128
            block = flat[pl.ds(start, rows), :]
            if shift:
                after = flat[pl.ds(start + 1, rows), :]
                block = jnp.where(
                    column < 128 - shift,
                    pltpu.roll(block, 128 - shift, 1),
                    pltpu.roll(after, 128 - shift, 1),
                )
            out_ref[number] = block.astype(out_ref.dtype)

    whole = pl.BlockSpec(memory_space=pltpu.VMEM)
    return pl.pallas_call(
        kernel,
        out_shape=jax.ShapeDtypeStruct((dp, rows, 128), jnp.bfloat16),
        in_specs=[whole] * len(items),
        out_specs=whole,
        scratch_shapes=[pltpu.VMEM((total + rows + 8, 128), jnp.float32)],
        cost_estimate=pl.CostEstimate(flops=0, bytes_accessed=2000000, transcendentals=0),
        compiler_params=pltpu.CompilerParams(vmem_limit_bytes=32 * 1024 * 1024),
    )(*[item.reshape(count, width) for item, (start, count, width) in zip(items, views)])


def unpack_small(own, came, places, extra_rows):
    views, total = small_views()
    dp = own.shape[0]
    share = total * 128 // dp
    half = small_half_rows(share)

    def kernel(place_ref, own_ref, came_ref, *refs):
        targets, extra_ref, flat, turned = refs[:-3], refs[-3], refs[-2], refs[-1]
        mine = [(place_ref[dp] == side).astype(jnp.float32) for side in range(2)]
        for number in range(dp):
            start, shift = number * share // 128, number * share % 128
            rows = -(-(share + shift) // 128)
            slot = place_ref[number]
            for side in range(2):
                both = own_ref[slot].astype(jnp.float32), came_ref[slot].astype(jnp.float32)
                whole = jnp.where(mine[side] > 0.5, *both)
                extra_ref[side, number] = whole[half : half + extra_rows].astype(extra_ref.dtype)
                part = whole[:half]
                turned[pl.ds(8 + side * half, half), :] = (
                    pltpu.roll(part, shift, 1) if shift else part
                )
            block = turned[pl.ds(8, rows), :]
            if shift:
                turned[7:8, :] = flat[pl.ds(start, 1), :]
                column = lax.broadcasted_iota(jnp.int32, (rows, 128), 1)
                block = jnp.where(column >= shift, block, turned[pl.ds(7, rows), :])
            flat[pl.ds(start, rows), :] = block
        for target, (start, count, width) in zip(targets, views):
            per = width // 128
            for part in range(per):
                target[:, part * 128 : (part + 1) * 128] = flat[
                    pl.ds(start + part, count, stride=per), :
                ]

    whole = pl.BlockSpec(memory_space=pltpu.VMEM)
    *outs, extra = pl.pallas_call(
        kernel,
        out_shape=[
            jax.ShapeDtypeStruct((count, width), jnp.float32) for start, count, width in views
        ]
        + [jax.ShapeDtypeStruct((2, dp, extra_rows, 128), jnp.bfloat16)],
        in_specs=[pl.BlockSpec(memory_space=pltpu.SMEM), whole, whole],
        out_specs=[whole] * (len(views) + 1),
        scratch_shapes=[
            pltpu.VMEM((total + 8, 128), jnp.float32),
            pltpu.VMEM((2 * half + 16, 128), jnp.float32),
        ],
        cost_estimate=pl.CostEstimate(flops=0, bytes_accessed=2000000, transcendentals=0),
        compiler_params=pltpu.CompilerParams(vmem_limit_bytes=32 * 1024 * 1024),
    )(places, own, came)
    return [item.reshape(piece_dims) for item, piece_dims in zip(outs, small_shapes())], extra


def norm_apply(values, gain_row, bias_row):
    centre = values - jnp.mean(values, axis=-1, keepdims=True)
    spread = jnp.mean(centre * centre, axis=-1, keepdims=True)
    return centre * lax.rsqrt(spread + EPSILON) * gain_row + bias_row


def norm_back(values, gain_row, bias_row, grad_out):
    unused, pullback = jax.vjp(norm_apply, values, gain_row, bias_row)
    return pullback(grad_out)


def gelu_exact(values):
    return jax.nn.gelu(values, approximate=False)


def contract_rows(left, right):
    return lax.dot_general(
        left, right, (((0,), (0,)), ((), ())), preferred_element_type=jnp.float32
    )


def contract_cols(left, right):
    return lax.dot_general(
        left, right, (((1,), (1,)), ((), ())), preferred_element_type=jnp.float32
    )


def heads_view(values, pages):
    return values.reshape(pages, PAGE_SLOTS, HEADS, values.shape[-1] // HEADS)


ROUND_ROWS = 32


def bits_of(size):
    return list(reversed(range(size.bit_length() - 1)))


def hop(values, axis, bit):
    pairs = [(spot, spot ^ (1 << bit)) for spot in range(lax.axis_size(axis))]
    return lax.ppermute(values, axis, pairs)


def own_bit(axis, bit):
    return (lax.axis_index(axis) >> bit) & 1


def routes():
    far = [("dp", bit) for bit in bits_of(lax.axis_size("dp"))]
    high = [("mp", bit) for bit in bits_of(lax.axis_size("mp"))[:-1]]
    core = ("mp", 0)
    return (far[:-1], far[-1], high, core)


def add_low(kept, came):
    return (kept.astype(jnp.float32) + came.astype(jnp.float32)).astype(jnp.bfloat16)


def tie(value, *waits):
    def kernel(*refs):
        pass

    spec = pl.BlockSpec(memory_space=pl.ANY)
    return pl.pallas_call(
        kernel,
        out_shape=jax.ShapeDtypeStruct(value.shape, value.dtype),
        in_specs=[spec] * (1 + len(waits)),
        out_specs=spec,
        input_output_aliases={0: 0},
        cost_estimate=pl.CostEstimate(flops=0, bytes_accessed=0, transcendentals=0),
    )(value, *waits)


def put_in_order(own, came, places):
    slots, rows, width = own.shape

    def kernel(place_ref, own_ref, came_ref, out_ref, sems):
        side = place_ref[slots]

        def copies(half, source):
            return [
                pltpu.make_async_copy(
                    source.at[place_ref[spot]],
                    out_ref.at[half, pl.ds(spot * rows, rows)],
                    sems.at[half, spot],
                )
                for spot in range(slots)
            ]

        for half in range(2):
            for mine, source in ((True, own_ref), (False, came_ref)):

                @pl.when((side == half) == mine)
                def _(half=half, source=source):
                    for copy in copies(half, source):
                        copy.start()

        for half in range(2):
            for copy in copies(half, own_ref):
                copy.wait()

    anywhere = pl.BlockSpec(memory_space=pl.ANY)
    return pl.pallas_call(
        kernel,
        out_shape=jax.ShapeDtypeStruct((2, slots * rows, width), own.dtype),
        in_specs=[pl.BlockSpec(memory_space=pltpu.SMEM), anywhere, anywhere],
        out_specs=pl.BlockSpec(memory_space=pltpu.VMEM),
        scratch_shapes=[pltpu.SemaphoreType.DMA((2, slots))],
        cost_estimate=pl.CostEstimate(
            flops=0, bytes_accessed=2 * slots * rows * width, transcendentals=0
        ),
        compiler_params=pltpu.CompilerParams(vmem_limit_bytes=16 * 1024 * 1024),
    )(places, own, came)


def embed_kernel(
    coords, embedded, text_pos, layout_pos, tables, text_emb, layout_emb, *outs
):
    text_pre, layout_pre, text, layout = outs
    quarter = LAYOUT_WIDTH // 4
    low = jnp.bfloat16
    row = lax.broadcasted_iota(jnp.int32, (PAGE_SLOTS, BOXES // 8), 1)
    lanes = lax.broadcasted_iota(jnp.int32, (PAGE_SLOTS, 8 * quarter), 1) // quarter
    fold_in = lax.broadcasted_iota(jnp.int32, (8 * quarter, LAYOUT_WIDTH), 0) % quarter
    fold_out = lax.broadcasted_iota(jnp.int32, (8 * quarter, LAYOUT_WIDTH), 1)
    looked = jnp.zeros((PAGE_SLOTS, LAYOUT_WIDTH), jnp.float32)
    for number in range(4):
        spot = coords[:, number : number + 1]
        marks = (spot // 8 == row).astype(jnp.float32).astype(low)
        wide = jnp.dot(
            marks, tables[number % 2].astype(low), preferred_element_type=jnp.float32
        )
        kept = jnp.where(spot % 8 == lanes, wide, 0.0).astype(low)
        fold = (fold_in + number * quarter == fold_out).astype(jnp.float32).astype(low)
        looked = looked + jnp.dot(kept, fold, preferred_element_type=jnp.float32)
    layout_pre[...] = looked + layout_pos[...]
    text_pre[...] = embedded[...] + text_pos[...]
    text[...] = norm_apply(text_pre[...], text_emb[0:1, :], text_emb[1:2, :])
    layout[...] = norm_apply(layout_pre[...], layout_emb[0:1, :], layout_emb[1:2, :])


def norm_grads(values, gain, grad):
    centre = values - jnp.mean(values, axis=-1, keepdims=True)
    scale = lax.rsqrt(jnp.mean(centre * centre, axis=-1, keepdims=True) + EPSILON)
    unit = centre * scale
    lifted = grad * gain
    inner = jnp.mean(lifted * unit, axis=-1, keepdims=True)
    back = scale * (lifted - jnp.mean(lifted, axis=-1, keepdims=True) - unit * inner)
    sums = [jnp.sum(item, 0, keepdims=True) for item in (grad * unit, grad)]
    return back, jnp.concatenate(sums, 0)


def embed_back_kernel(coords, text_pre, layout_pre, text_emb, layout_emb, *refs):
    grad_text, grad_layout, text_back, layout_back, text_sums, layout_sums, boxes = refs
    low = jnp.bfloat16
    quarter = LAYOUT_WIDTH // 4
    text_back[...], text_sums[...] = norm_grads(text_pre[...], text_emb[0:1, :], grad_text[...])
    looked, layout_sums[...] = norm_grads(
        layout_pre[...], layout_emb[0:1, :], grad_layout[...]
    )
    layout_back[...] = looked
    high, rest = split_high(looked)
    row = lax.broadcasted_iota(jnp.int32, (PAGE_SLOTS, BOXES // 8), 1)
    lanes = lax.broadcasted_iota(jnp.int32, (PAGE_SLOTS, 8 * quarter), 1) // quarter
    fold_in = lax.broadcasted_iota(jnp.int32, (8 * quarter, LAYOUT_WIDTH), 0) % quarter
    fold_out = lax.broadcasted_iota(jnp.int32, (8 * quarter, LAYOUT_WIDTH), 1)
    boxes[...] = jnp.zeros_like(boxes)
    for number in range(4):
        spot = coords[:, number : number + 1]
        marks = (spot // 8 == row).astype(jnp.float32).astype(low)
        fold = (fold_in + number * quarter == fold_out).astype(jnp.float32).astype(low)
        wide = contract_cols(high, fold) + contract_cols(rest, fold)
        kept = jnp.where(spot % 8 == lanes, wide, 0.0)
        boxes[number % 2] += add_rows(marks, kept)


def embed_back(*operands):
    whole = pl.BlockSpec(memory_space=pltpu.VMEM)
    shapes = [
        (PAGE_SLOTS, WIDTH),
        (PAGE_SLOTS, LAYOUT_WIDTH),
        (2, WIDTH),
        (2, LAYOUT_WIDTH),
        (2, BOXES // 8, 2 * LAYOUT_WIDTH),
    ]
    return pl.pallas_call(
        embed_back_kernel,
        out_shape=[jax.ShapeDtypeStruct(shape, jnp.float32) for shape in shapes],
        in_specs=[whole] * len(operands),
        out_specs=[whole] * len(shapes),
        cost_estimate=pl.CostEstimate(flops=0, bytes_accessed=2000000, transcendentals=0),
        compiler_params=pltpu.CompilerParams(vmem_limit_bytes=32 * 1024 * 1024),
    )(*operands)


def embed_streams(*operands):
    whole = pl.BlockSpec(memory_space=pltpu.VMEM)
    return pl.pallas_call(
        embed_kernel,
        out_shape=[
            jax.ShapeDtypeStruct((PAGE_SLOTS, width), jnp.float32)
            for width in (WIDTH, LAYOUT_WIDTH) * 2
        ],
        in_specs=[whole] * len(operands),
        out_specs=[whole] * 4,
        cost_estimate=pl.CostEstimate(flops=0, bytes_accessed=2000000, transcendentals=0),
        compiler_params=pltpu.CompilerParams(vmem_limit_bytes=24 * 1024 * 1024),
    )(*operands)


def mats_kernel(side, rows, query, keys, values, att, first, sent_ref, kept_ref, result):
    step = pl.program_id(0)
    half = jnp.where(step < 2, 1 - side[0], side[0])
    cases = ((rows, query), (rows, keys), (rows, values), (att, first))
    for number, (left, right) in enumerate(cases):

        @pl.when(half * 2 + step % 2 == number)
        def _(left=left, right=right):
            result[...] = contract_rows(left[...], right[...])

    def store(target):
        blocks = result[...].astype(target.dtype).reshape(target.shape[0], -1, WIDTH)
        target[:, : blocks.shape[1], :] = blocks

    @pl.when(step < 2)
    def _():
        store(sent_ref)

    @pl.when(step >= 2)
    def _():
        store(kept_ref)


def mats_sums(side, operands, padded):
    dp = lax.axis_size("dp")
    whole = pl.BlockSpec((PAGE_SLOTS, WIDTH), lambda step: (0, 0))
    shape = jax.ShapeDtypeStruct((dp, padded, 2 * WIDTH), jnp.bfloat16)
    return pl.pallas_call(
        mats_kernel,
        grid=(4,),
        in_specs=[pl.BlockSpec(memory_space=pltpu.SMEM)] + [whole] * 6,
        out_specs=[
            pl.BlockSpec((dp, padded, WIDTH), lambda step: (0, 0, jnp.minimum(step, 1))),
            pl.BlockSpec((dp, padded, WIDTH), lambda step: (0, 0, jnp.maximum(step - 2, 0))),
        ],
        out_shape=[shape, shape],
        scratch_shapes=[pltpu.VMEM((WIDTH, WIDTH), jnp.float32)],
        cost_estimate=pl.CostEstimate(
            flops=2 * PAGE_SLOTS * WIDTH * WIDTH, bytes_accessed=4000000, transcendentals=0
        ),
        compiler_params=pltpu.CompilerParams(vmem_limit_bytes=32 * 1024 * 1024),
    )(side, *operands)


def take_extra(pieces, rows):
    slots, total, width = pieces[0].shape

    def kernel(*refs):
        out_ref, sems = refs[-2], refs[-1]
        copies = [
            pltpu.make_async_copy(
                ref.at[:, pl.ds(rows, total - rows)],
                out_ref.at[pl.ds(number * slots, slots)],
                sems.at[number],
            )
            for number, ref in enumerate(refs[:-2])
        ]
        for copy in copies:
            copy.start()
        for copy in copies:
            copy.wait()

    return pl.pallas_call(
        kernel,
        out_shape=jax.ShapeDtypeStruct((slots * len(pieces), total - rows, width), pieces[0].dtype),
        in_specs=[pl.BlockSpec(memory_space=pl.ANY)] * len(pieces),
        out_specs=pl.BlockSpec(memory_space=pltpu.VMEM),
        scratch_shapes=[pltpu.SemaphoreType.DMA((len(pieces),))],
        cost_estimate=pl.CostEstimate(flops=0, bytes_accessed=500000, transcendentals=0),
    )(*pieces)


HEAD_PAIRS = HEADS // 2
TEXT_HEAD = WIDTH // HEADS
LAYOUT_HEAD = LAYOUT_WIDTH // HEADS


def head_of(text_ref, layout_ref, head, scaled=False):
    text = text_ref[:, head * TEXT_HEAD : (head + 1) * TEXT_HEAD]
    layout = layout_ref[:, head * LAYOUT_HEAD : (head + 1) * LAYOUT_HEAD]
    if scaled:
        text_scale, layout_scale = scale_pair()
        text = (text.astype(jnp.float32) * text_scale).astype(text.dtype)
        layout = (layout.astype(jnp.float32) * layout_scale).astype(layout.dtype)
    return jnp.concatenate([text, layout], 1)


def store_heads(text_ref, layout_ref, both):
    text_ref[...] = jnp.concatenate([item[:, :TEXT_HEAD] for item in both], 1).astype(
        text_ref.dtype
    )
    layout = jnp.concatenate([item[:, TEXT_HEAD:] for item in both], 1).astype(layout_ref.dtype)
    width = layout.shape[1]
    for pair in range(HEAD_PAIRS):

        @pl.when(pl.program_id(0) == pair)
        def _(pair=pair):
            layout_ref[:, pair * width : (pair + 1) * width] = layout


def own_pair(sources, targets):
    width = targets[0].shape[1]
    for pair in range(HEAD_PAIRS):

        @pl.when(pl.program_id(0) == pair)
        def _(pair=pair):
            for source, target in zip(sources, targets):
                target[...] = source[:, pair * width : (pair + 1) * width]


def attend_kernel(length, qt, kt, vt, *refs):
    out_t, out_l, lse, ql, kl, vl = refs[3:]
    own_pair(refs[:3], (ql, kl, vl))
    live = lax.broadcasted_iota(jnp.int32, (PAGE_SLOTS, PAGE_SLOTS), 1) < length[0]
    outs = []
    for head in range(2):
        query, keys = head_of(qt, ql, head, True), head_of(kt, kl, head)
        scores = jnp.where(live, contract_cols(query, keys), MASK_FILL)
        peak = jnp.max(scores, 1, keepdims=True)
        expo = jnp.exp(scores - peak)
        total = jnp.sum(expo, 1, keepdims=True)
        probs = (expo * (1.0 / total)).astype(jnp.bfloat16)
        outs.append(
            jnp.dot(probs, head_of(vt, vl, head), preferred_element_type=jnp.float32)
        )
        lse[0, :, head : head + 1] = peak + jnp.log(total)
    store_heads(out_t, out_l, outs)


def attend_back_kernel(length, qt, kt, vt, got, *refs):
    lse, dqt, dkt, dvt, dql, dkl, dvl, ql, kl, vl, gol = refs[4:]
    own_pair(refs[:4], (ql, kl, vl, gol))
    text_scale, layout_scale = scale_pair()
    live = lax.broadcasted_iota(jnp.int32, (PAGE_SLOTS, PAGE_SLOTS), 0) < length[0]
    column = lax.broadcasted_iota(jnp.int32, (1, TEXT_HEAD + LAYOUT_HEAD), 1)
    scales = jnp.where(column < TEXT_HEAD, text_scale, layout_scale)
    grads_q, grads_k, grads_v = [], [], []
    for head in range(2):
        query, keys = head_of(qt, ql, head, True), head_of(kt, kl, head)
        values, grad = head_of(vt, vl, head), head_of(got, gol, head)
        scores = jnp.where(live, contract_cols(keys, query), MASK_FILL)
        probs = jnp.exp(scores - lse[0, head : head + 1, :])
        grad_probs = contract_cols(values, grad)
        shift = jnp.sum(probs * grad_probs, 0, keepdims=True)
        grad_scores = (probs * (grad_probs - shift)).astype(jnp.bfloat16)
        grads_v.append(
            jnp.dot(probs.astype(jnp.bfloat16), grad, preferred_element_type=jnp.float32)
        )
        grads_k.append(jnp.dot(grad_scores, query, preferred_element_type=jnp.float32))
        grads_q.append(contract_rows(grad_scores, keys) * scales)
    store_heads(dqt, dql, grads_q)
    store_heads(dkt, dkl, grads_k)
    store_heads(dvt, dvl, grads_v)


def pair_specs():
    text = pl.BlockSpec((PAGE_SLOTS, 2 * TEXT_HEAD), lambda step: (0, step))
    layout = pl.BlockSpec((PAGE_SLOTS, LAYOUT_WIDTH), lambda step: (0, 0))
    return text, layout, pltpu.VMEM((PAGE_SLOTS, 2 * LAYOUT_HEAD), jnp.bfloat16)


def attend(text_qkv, layout_qkv, lengths):
    text, layout, pair = pair_specs()
    low = jnp.bfloat16
    out_t, out_l, lse = pl.pallas_call(
        attend_kernel,
        grid=(HEAD_PAIRS,),
        in_specs=[pl.BlockSpec(memory_space=pltpu.SMEM)] + [text] * 3 + [layout] * 3,
        out_specs=[text, layout, pl.BlockSpec((1, PAGE_SLOTS, 2), lambda step: (step, 0, 0))],
        out_shape=[
            jax.ShapeDtypeStruct((PAGE_SLOTS, WIDTH), low),
            jax.ShapeDtypeStruct((PAGE_SLOTS, LAYOUT_WIDTH), low),
            jax.ShapeDtypeStruct((HEAD_PAIRS, PAGE_SLOTS, 2), jnp.float32),
        ],
        scratch_shapes=[pair] * 3,
        cost_estimate=pl.CostEstimate(
            flops=4000000000, bytes_accessed=2000000, transcendentals=100000
        ),
        compiler_params=pltpu.CompilerParams(vmem_limit_bytes=24 * 1024 * 1024),
    )(lengths, *text_qkv, *layout_qkv)
    return (out_t, out_l, lse.transpose(0, 2, 1))


def attend_back(text_qkv, layout_qkv, lengths, lse, text_grad, layout_grad):
    text, layout, pair = pair_specs()
    low = jnp.bfloat16
    text_out = jax.ShapeDtypeStruct((PAGE_SLOTS, WIDTH), low)
    layout_out = jax.ShapeDtypeStruct((PAGE_SLOTS, LAYOUT_WIDTH), low)
    outs = pl.pallas_call(
        attend_back_kernel,
        grid=(HEAD_PAIRS,),
        in_specs=[pl.BlockSpec(memory_space=pltpu.SMEM)]
        + [text] * 4
        + [layout] * 4
        + [pl.BlockSpec((1, 2, PAGE_SLOTS), lambda step: (step, 0, 0))],
        out_specs=[text] * 3 + [layout] * 3,
        out_shape=[text_out] * 3 + [layout_out] * 3,
        scratch_shapes=[pair] * 4,
        cost_estimate=pl.CostEstimate(
            flops=5000000000, bytes_accessed=3000000, transcendentals=100000
        ),
        compiler_params=pltpu.CompilerParams(vmem_limit_bytes=32 * 1024 * 1024),
    )(lengths, *text_qkv, text_grad, *layout_qkv, layout_grad, lse)
    return (list(outs[:3]), list(outs[3:]))


ERF_TERMS = (0.254829592, -0.284496736, 1.421413741, -1.453152027, 1.061405429)


def gelu_pair(values):
    size = jnp.abs(values)
    base = 1.0 / (1.0 + (0.3275911 / math.sqrt(2.0)) * size)
    series = ERF_TERMS[4]
    for term in reversed(ERF_TERMS[:4]):
        series = series * base + term
    bell = jnp.exp(values * values * -0.5)
    tail = 0.5 * series * base * bell
    share = jnp.where(values < 0.0, tail, 1.0 - tail)
    return (values * share, share + values * bell * (1.0 / math.sqrt(2.0 * math.pi)))


def load_units(pieces_in, pieces_out, rows, buffers, sems, chunks):
    per = len(pieces_in) // chunks
    slots = pieces_in[0].shape[0]
    step = pl.program_id(0)

    def copies(turn):
        made = []
        for number in range(per):
            for side, pieces in enumerate((pieces_in, pieces_out)):
                made.append(
                    pltpu.make_async_copy(
                        pieces[turn * per + number].at[:, pl.ds(0, rows)],
                        buffers[side].at[turn % 2, pl.ds(number * slots, slots)],
                        sems.at[turn % 2, 2 * number + side],
                    )
                )
        return made

    for turn in range(chunks):

        @pl.when(step == turn)
        def _(turn=turn):
            if turn == 0:
                for copy in copies(0):
                    copy.start()
            if turn + 1 < chunks:
                for copy in copies(turn + 1):
                    copy.start()
            for copy in copies(turn):
                copy.wait()

    slot = step % 2
    return [buffer[slot].reshape(-1, buffer.shape[-1]) for buffer in buffers]


def unit_plan(units, chunk, rows, chunks):
    width = units[0][0].shape[-1] if rows else units[0].shape[-1]
    if not rows:
        unit = pl.BlockSpec((chunk, width), lambda step: (step, 0))
        return list(units), [unit, unit], []
    anywhere = pl.BlockSpec(memory_space=pl.ANY)
    operands = list(units[0]) + list(units[1])
    buffer = pltpu.VMEM((2, chunk // rows, rows, width), jnp.bfloat16)
    sems = pltpu.SemaphoreType.DMA((2, len(operands) // chunks))
    return operands, [anywhere] * len(operands), [buffer, buffer, sems]


def take_units(refs, scratch, rows, chunks):
    if not rows:
        return [ref[...] for ref in refs]
    half = len(refs) // 2
    return load_units(refs[:half], refs[half:], rows, scratch[:2], scratch[2], chunks)


def ffn_kernel(rows, chunks, count, rows_ref, bias_ref, *refs):
    hidden_ref, slope_ref, part_ref = refs[count : count + 3]
    units_in, units_out = take_units(refs[:count], refs[count + 3 :], rows, chunks)

    @pl.when(pl.program_id(0) == 0)
    def _():
        part_ref[...] = jnp.zeros_like(part_ref)

    step = PAGE_SLOTS // 2
    for number in range(2):
        span = pl.ds(number * step, step)
        pre_act = contract_cols(rows_ref[span, :], units_in) + bias_ref[...]
        hidden, slope = gelu_pair(pre_act)
        hidden = hidden.astype(jnp.bfloat16)
        hidden_ref[span, :] = hidden
        slope_ref[span, :] = slope.astype(jnp.bfloat16)
        part_ref[span, :] += jnp.dot(hidden, units_out, preferred_element_type=jnp.float32)


def ffn_front(rows_in, units, bias_in, chunks, rows):
    slots, width = rows_in.shape
    total = bias_in.shape[0]
    chunk = total // chunks
    whole = pl.BlockSpec((slots, width), lambda step: (0, 0))
    piece = pl.BlockSpec((slots, chunk), lambda step: (0, step))
    operands, specs, scratch = unit_plan(units, chunk, rows, chunks)
    return pl.pallas_call(
        functools.partial(ffn_kernel, rows, chunks, len(operands)),
        grid=(chunks,),
        in_specs=[whole, pl.BlockSpec((1, chunk), lambda step: (0, step))] + specs,
        out_specs=[piece, piece, whole],
        out_shape=[
            jax.ShapeDtypeStruct((slots, total), jnp.bfloat16),
            jax.ShapeDtypeStruct((slots, total), jnp.bfloat16),
            jax.ShapeDtypeStruct((slots, width), jnp.float32),
        ],
        scratch_shapes=scratch,
        cost_estimate=pl.CostEstimate(
            flops=slots * width * total,
            bytes_accessed=total * (width + slots),
            transcendentals=0,
        ),
        compiler_params=pltpu.CompilerParams(vmem_limit_bytes=40 * 1024 * 1024),
    )(rows_in, bias_in[None], *operands)


def tail_route(flip):
    far, near, high, core = routes()
    return (high + [near] if flip else [near] + high) + [core]


def key_mask(key, axis):
    return sum(1 << bit for name, bit in key if name == axis)


class Spread:
    def __init__(self, block, joined, apart):
        self.joined, self.apart = list(joined), list(apart)
        self.masks = [frozenset()]
        self.pieces = {frozenset(): block[None]}

    def advance(self, wait=None):
        if self.joined:
            step = self.joined.pop(0)
            (held,) = self.pieces.values()
            held = held if wait is None else tie(held, wait)
            self.sent = [held]
            came = hop(held, *step)
            self.pieces = {frozenset(): jnp.concatenate([held, came], 0)}
            self.masks = self.masks + [mask | {step} for mask in self.masks]
            return came
        step = self.apart.pop(0)
        self.sent = []
        for key, piece in list(self.pieces.items()):
            piece = piece if wait is None else tie(piece, wait)
            self.sent.append(piece)
            came = hop(piece, *step)
            self.pieces[key] = piece
            self.pieces[key | {step}] = came
        return came


def half_spread(own, near_first=False):
    far, near, high, core = routes()
    return Spread(own, [near] + far if near_first else far + [near], [core])


def half_parts(chain):
    core = routes()[3]
    spot = lax.axis_index("dp")
    masks = [key_mask(mask, "dp") for mask in chain.masks]
    slot_of = {mask: number for number, mask in enumerate(masks)}
    table = jnp.array([slot_of[number] for number in range(len(masks))], jnp.int32)
    numbers = jnp.arange(len(masks))
    marks = (spot ^ numbers)[:, None] == numbers[None, :]
    places = jnp.sum(jnp.where(marks, table[None, :], 0), 1, dtype=jnp.int32)
    places = jnp.concatenate([places, own_bit(*core).astype(jnp.int32)[None]])
    return chain.pieces[frozenset()], chain.pieces[frozenset([core])], places


def unit_spread(block, flip):
    return Spread(block, routes()[0], tail_route(flip))


def unit_keys():
    far, near, high, core = routes()
    keys = [frozenset()]
    for step in [near] + list(reversed(high)) + [core]:
        keys = keys + [key | {step} for key in keys]
    return keys


def unit_result(chain):
    return [chain.pieces[key] for key in unit_keys()]


def unit_blocks():
    far = [frozenset()]
    for step in routes()[0]:
        far = far + [mask | {step} for mask in far]
    masks = [key | mask for key in unit_keys() for mask in far]
    spots = jnp.array([key_mask(mask, "dp") for mask in masks], jnp.int32)
    lanes = jnp.array([key_mask(mask, "mp") for mask in masks], jnp.int32)
    lanes, spots = lanes ^ lax.axis_index("mp"), spots ^ lax.axis_index("dp")
    return lanes * lax.axis_size("dp") + spots


class UnitSum:
    def __init__(self, kept, sent, flip):
        far, near, high, core = routes()
        self.order = high + [near]
        self.left = list(reversed(tail_route(flip)[:-1])) + list(reversed(far))
        shape = (2,) * len(self.order) + (lax.axis_size("dp") // 2,) + kept.shape[1:]
        self.sent = sent
        self.kept, self.came = kept.reshape(shape), hop(sent, *core).reshape(shape)

    def half(self, values, side, where):
        if where is not None:
            return lax.index_in_dim(values, side, where, keepdims=False)
        size = values.shape[0] // 2
        return values[side * size : (side + 1) * size]

    def advance(self):
        step = self.left.pop(0)
        where = self.order.index(step) if step in self.order else None
        if where is not None:
            self.order.remove(step)
        sent, kept = [
            add_low(self.half(self.kept, side, where), self.half(self.came, side, where))
            for side in (1, 0)
        ]
        self.sent = sent
        self.kept, self.came = kept, hop(sent, *step)
        return self.sent

    def finish(self):
        while self.left:
            self.advance()
        return (self.kept.astype(jnp.float32) + self.came.astype(jnp.float32))[0]


def to_rows(values):
    flat = values.reshape(values.shape[0], -1)
    flat = jnp.pad(flat, ((0, 0), (0, -flat.shape[1] % WIDTH)))
    return flat.reshape(values.shape[0], -1, WIDTH)


def from_rows(values, units):
    flat = values.reshape(values.shape[0], -1)[:, : units * 2 * LAYOUT_WIDTH]
    return flat.reshape(-1, 2 * LAYOUT_WIDTH)


class HalfSum:
    def __init__(self, sent, kept):
        far, near, high, core = routes()
        self.order = far + [near]
        self.left = [near] + list(reversed(far)) + high + [core]
        shape = (2,) * len(self.order) + sent.shape[1:]
        self.sent = sent
        self.kept, self.came = kept.reshape(shape), hop(sent, *core).reshape(shape)

    def advance(self):
        far, near, high, core = routes()
        step = self.left.pop(0)
        if step == core or step in high:
            self.kept = self.sent = add_low(self.kept, self.came)
            self.came = hop(self.kept, *step)
        else:
            where = self.order.index(step)
            self.order.remove(step)
            mine = own_bit(*step)

            def side(values, number):
                return lax.dynamic_index_in_dim(values, number, where, keepdims=False)

            sent = add_low(side(self.kept, 1 - mine), side(self.came, 1 - mine))
            kept = add_low(side(self.kept, mine), side(self.came, mine))
            self.sent = sent
            self.kept, self.came = kept, hop(sent, *step)
        return self.sent

    def finish(self):
        while self.left:
            self.advance()
        first = own_bit(*routes()[3]) == 0
        own, other = self.kept, self.came
        return jnp.stack([jnp.where(first, own, other), jnp.where(first, other, own)]).astype(
            jnp.float32
        )


def own_half(values):
    half = values.shape[-1] // 2
    return jnp.where(own_bit("mp", 0) == 0, values[..., :half], values[..., half:])


def sum_everywhere(values):
    far, near, high, core = routes()
    for step in [core] + high + [near] + far:
        values = values + hop(values, *step)
    return values


def show_all(values):
    everywhere = ("dp", "mp")
    count = lax.axis_size("dp") * lax.axis_size("mp")
    return lax.all_to_all(
        jnp.broadcast_to(values[None], (count,) + values.shape), everywhere, 0, 0, tiled=True
    )


def trade(values):
    return lax.all_to_all(values, ("dp", "mp"), 0, 0, tiled=True)


def project_qkv(rows_low, mats, vectors, width):
    joined = jnp.dot(rows_low, mats[0], preferred_element_type=jnp.float32)
    query = (joined[:, :width] + vectors[0]).astype(jnp.bfloat16)
    keys = joined[:, width:].astype(jnp.bfloat16)
    values = jnp.dot(rows_low, mats[1][:, :width], preferred_element_type=jnp.float32)
    return (query, keys, (values + vectors[1]).astype(jnp.bfloat16))


def scale_pair():
    return (1.0 / math.sqrt(WIDTH // HEADS), 1.0 / math.sqrt(LAYOUT_WIDTH // HEADS))


def project_back(mats, grads, width):
    first = jnp.concatenate(grads[:2], 1)
    rows_grad = contract_cols(first, mats[0]) + contract_cols(grads[2], mats[1][:, :width])
    return (
        rows_grad,
        jnp.sum(grads[0], 0, dtype=jnp.float32),
        jnp.sum(grads[2], 0, dtype=jnp.float32),
    )


def ffn_back_kernel(
    rows_of, chunks, count, rows_ref, grad_ref, hidden_ref, slope_ref, extra_ref, *refs
):
    part_ref, bias_ref, *sums = refs[count : count + 6]
    units_in, units_out = take_units(refs[:count], refs[count + 6 :], rows_of, chunks)
    step, last = pl.program_id(0), chunks // 2
    rows, grad = rows_ref[...], grad_ref[...]
    grad_hidden = contract_cols(grad, units_out)
    grad_pre = grad_hidden * slope_ref[...].astype(jnp.float32)
    grad_low = grad_pre.astype(jnp.bfloat16)
    bias_ref[...] = jnp.sum(grad_low.astype(jnp.float32), 0, keepdims=True)

    @pl.when(step == 0)
    def _():
        part_ref[...] = jnp.zeros_like(part_ref)

    part_ref[...] += jnp.dot(grad_low, units_in, preferred_element_type=jnp.float32)
    results = [contract_rows(grad_low, rows), contract_rows(hidden_ref[...], grad)]

    def store(targets):
        for target, result in zip(targets, results):
            if len(target.shape) == 2:
                target[...] = result.astype(target.dtype)
            else:
                blocks = result.astype(target.dtype).reshape(target.shape[0], -1, rows.shape[1])
                target[:, : blocks.shape[1], :] = blocks
                if target.shape[1] > blocks.shape[1]:
                    target[:, blocks.shape[1] :, :] = extra_ref[...]

    @pl.when(step < last)
    def _():
        store(sums[:2])

    @pl.when(step >= last)
    def _():
        store(sums[2:])


def ffn_back(rows_in, units, slope, hidden, grad_rows, chunks, slot_rows, extra):
    slots, width = rows_in.shape
    total = hidden.shape[1]
    chunk, half = total // chunks, chunks // 2
    whole = pl.BlockSpec((slots, width), lambda step: (0, 0))
    piece = pl.BlockSpec((slots, chunk), lambda step: (0, step))
    operands, specs, scratch = unit_plan(
        units, chunk, slot_rows[0] if slot_rows else None, chunks
    )

    def first(step):
        return jnp.minimum(step, half - 1)

    def second(step):
        return jnp.maximum(step - half, 0)

    turns = (first, first, second, second)
    if slot_rows is None:
        shapes = [(total // 2, width)] * 4
        sum_specs = [
            pl.BlockSpec((chunk, width), lambda step, turn=turn: (turn(step), 0)) for turn in turns
        ]
        extra_spec = pl.BlockSpec(memory_space=pltpu.VMEM)
    else:
        rows, padded = slot_rows
        heights = [padded, rows] * 2
        shapes = [(total // (2 * rows), height, width) for height in heights]
        sum_specs = [
            pl.BlockSpec((chunk // rows, height, width), lambda step, turn=turn: (turn(step), 0, 0))
            for height, turn in zip(heights, turns)
        ]
        extra_spec = pl.BlockSpec((chunk // rows, padded - rows, width), lambda step: (step, 0, 0))
    return pl.pallas_call(
        functools.partial(
            ffn_back_kernel, slot_rows[0] if slot_rows else None, chunks, len(operands)
        ),
        grid=(chunks,),
        in_specs=[whole, whole, piece, piece, extra_spec] + specs,
        out_specs=[whole, pl.BlockSpec((1, chunk), lambda step: (0, step))] + sum_specs,
        out_shape=[
            jax.ShapeDtypeStruct((slots, width), jnp.float32),
            jax.ShapeDtypeStruct((1, total), jnp.float32),
        ]
        + [jax.ShapeDtypeStruct(shape, jnp.bfloat16) for shape in shapes],
        scratch_shapes=scratch,
        cost_estimate=pl.CostEstimate(
            flops=2 * slots * width * total,
            bytes_accessed=2 * total * (width + slots),
            transcendentals=0,
        ),
        compiler_params=pltpu.CompilerParams(vmem_limit_bytes=48 * 1024 * 1024),
    )(rows_in, grad_rows, hidden, slope, extra, *operands)


def stream_forward(rows, att, mats, units, bias_in, vec, unit_rows, hook):
    width = rows.shape[1]
    first = (
        rows + jnp.dot(att, mats[1][:, width:], preferred_element_type=jnp.float32) + vec[2]
    )
    mid = norm_apply(first, vec[3], vec[4])
    mid_low = hook(mid.astype(jnp.bfloat16))
    chunks = 4 if width == WIDTH else 1
    hidden, slope, part = ffn_front(mid_low, units, bias_in, chunks, unit_rows)
    last = mid + part + vec[5]
    return (norm_apply(last, vec[6], vec[7]), (first, mid_low, slope, hidden, last))


def layer_forward(text, layout, weights, lengths, hooks):
    (tm, lm, tb, lb, tv, lv) = weights
    text_low = hooks["low"](text.astype(jnp.bfloat16))
    layout_low = layout.astype(jnp.bfloat16)
    text_qkv = list(project_qkv(text_low, tm, tv, WIDTH))
    layout_qkv = project_qkv(layout_low, lm, lv, LAYOUT_WIDTH)
    text_qkv[0] = hooks["query"](text_qkv[0])
    text_att, layout_att, log_total = attend(text_qkv, layout_qkv, lengths)
    text_att = hooks["att"](text_att)
    tu, lu = hooks["units"]()
    count = lax.axis_size("dp") * lax.axis_size("mp")
    text_new, text_kept = stream_forward(
        text, text_att, tm, tu, tb, tv, FFN_UNITS // count, hooks["mid"]
    )
    layout_new, layout_kept = stream_forward(
        layout, layout_att, lm, lu, lb, lv, None, lambda value: value
    )
    cache = (
        text_low,
        layout_low,
        text_qkv,
        layout_qkv,
        log_total,
        text_att,
        layout_att,
        text_kept,
        layout_kept,
    )
    return (text_new, layout_new, cache, (tu, lu))


def stream_back(kept, att, mats, units, vec, grad, slot_rows, hook, extra):
    first, mid_low, slope, hidden, last = kept
    width = first.shape[1]
    last_g, gain2, bias2 = norm_back(last, vec[6], vec[7], grad)
    in_grad, bias_in_g, *unit_grads = ffn_back(
        mid_low,
        units,
        slope,
        hidden,
        hook(last_g.astype(jnp.bfloat16)),
        4 if width == WIDTH else 2,
        slot_rows,
        extra,
    )
    first_g, gain1, bias1 = norm_back(first, vec[3], vec[4], last_g + in_grad)
    first_low = first_g.astype(jnp.bfloat16)
    att_grad = contract_cols(first_low, mats[1][:, width:]).astype(jnp.bfloat16)
    vec_tail = [jnp.sum(first_g, 0), gain1, bias1, jnp.sum(last_g, 0), gain2, bias2]
    return (first_g, att_grad, first_low, unit_grads, bias_in_g[0], vec_tail)


def layer_backward(cache, grad_text, grad_layout, weights, lengths, plan):
    (
        text_low,
        layout_low,
        text_qkv,
        layout_qkv,
        log_total,
        text_att,
        layout_att,
        text_kept,
        layout_kept,
    ) = cache
    (tm, lm, tu, lu, tb, lb, tv, lv) = weights
    count = lax.axis_size("dp") * lax.axis_size("mp")
    rows = FFN_UNITS // count
    none = jnp.zeros((8, 128), jnp.float32)
    first_l, att_l, out_l, lu_g, lb_g, tail_l = stream_back(
        layout_kept, layout_att, lm, lu, lv, grad_layout, None, lambda value: value, none
    )
    halves = [jnp.concatenate(lu_g[2 * side : 2 * side + 2], 1) for side in range(2)]
    extra = to_rows(jnp.concatenate(halves, 0).reshape(count, -1, 2 * LAYOUT_WIDTH))
    extra = jnp.pad(extra, ((0, 0), (0, -extra.shape[1] % 16), (0, 0)))
    slot_rows = (rows, rows + extra.shape[1])
    first_t, att_t, out_t, tu_g, tb_g, tail_t = stream_back(
        text_kept, text_att, tm, tu, tv, grad_text, slot_rows, plan.before_units, extra
    )
    att_t = plan.after_units(att_t, tu_g)
    text_dqkv, layout_dqkv = attend_back(
        text_qkv, layout_qkv, lengths, log_total, att_t, att_l
    )
    text_dqkv[0] = plan.after_attend(text_dqkv[0])
    plan.after_mats(
        (text_low, *text_dqkv, text_att, out_t), (layout_low, *layout_dqkv, layout_att, out_l)
    )
    rows_t, q_bias_t, v_bias_t = project_back(tm, text_dqkv, WIDTH)
    rows_l, q_bias_l, v_bias_l = project_back(lm, layout_dqkv, LAYOUT_WIDTH)
    grads = (
        tb_g,
        lb_g,
        jnp.stack([q_bias_t, v_bias_t] + tail_t),
        jnp.stack([q_bias_l, v_bias_l] + tail_l),
    )
    return (first_t + rows_t, first_l + rows_l, grads)


class Plan:
    def __init__(self):
        self.units = []
        self.mats = []

    def step(self, value, items):
        return tie(value, *[item.advance() for item in items])

    def before_units(self, value):
        return self.step(value, self.mats[:1]) if self.mats else value

    def after_units(self, value, grads):
        keep_in, keep_out, send_in, send_out = grads
        self.units.append([UnitSum(keep_in, send_in, False), UnitSum(keep_out, send_out, True)])
        if self.mats:
            return self.step(value, self.units[0] + self.mats[:1])
        return self.step(value, self.units[0])

    def after_attend(self, value):
        if self.mats:
            return self.step(value, self.units[1])
        return value

    def after_mats(self, text, layout):
        dp = lax.axis_size("dp")
        low = jnp.bfloat16
        side = own_bit("mp", 0).astype(jnp.int32)
        rows, query, keys, values, att, first = layout
        first_half = contract_rows(rows, jnp.concatenate([query, keys], 1)).astype(low)
        second_half = jnp.concatenate(
            [contract_rows(rows, values), contract_rows(att, first)], 1
        ).astype(low)
        text_rows = WIDTH // dp
        extras = [
            jnp.where(side == number, second_half, first_half).reshape(dp, -1, 2 * WIDTH)
            for number in range(2)
        ]
        padded = -(-(text_rows + extras[0].shape[1]) // 8) * 8
        pad = ((0, 0), (0, padded - text_rows - extras[0].shape[1]), (0, 0))
        sums = mats_sums(side[None], text, padded)
        sent, kept = [
            lax.dynamic_update_slice(item, jnp.pad(extra, pad), (0, text_rows, 0))
            for item, extra in zip(sums, extras)
        ]
        self.mats.append(HalfSum(sent, kept))

    def between(self, value):
        if len(self.mats) == 1:
            return self.step(tie(value, self.mats[0].sent), self.units[0])
        return self.step(tie(value, self.mats[1].sent), self.units[0] + self.mats[:1])


def split_high(values):
    high = values.astype(jnp.bfloat16)
    return (high, (values - high.astype(jnp.float32)).astype(jnp.bfloat16))


def add_rows(marks, values):
    high, low = split_high(values)
    return contract_rows(marks, high) + contract_rows(marks, low)


def apply_update(master, grad, moment, average, loss_count, factor):
    clipped = grad / loss_count * factor
    moment_new = MOMENTUM * moment + clipped
    master_new = master - LEARN_RATE * (clipped + MOMENTUM * moment_new)
    return (master_new, moment_new, AVERAGE_DECAY * average + (1.0 - AVERAGE_DECAY) * master_new)


def on_device(
    token_ids,
    mlm_targets,
    page_lengths,
    box_coords,
    mlm_positions,
    align_pairs,
    align_labels,
    table,
    text_mats,
    layout_mats,
    text_ffn,
    layout_ffn,
    small_params,
    table_momentum,
    text_mats_momentum,
    layout_mats_momentum,
    text_ffn_momentum,
    layout_ffn_momentum,
    small_momentum,
    table_average,
    text_mats_average,
    layout_mats_average,
    text_ffn_average,
    layout_ffn_average,
    small_average,
):
    lane, spot = lax.axis_index("mp"), lax.axis_index("dp")
    dp, mp = lax.axis_size("dp"), lax.axis_size("mp")
    count = dp * mp
    slots = PAGE_SLOTS
    mask_slots = mlm_positions.shape[1]
    pages = 1
    vocab_rows = table.shape[0]
    low = jnp.bfloat16

    own_ids = lax.dynamic_index_in_dim(token_ids, lane, 0, keepdims=False)
    own_targets = lax.dynamic_index_in_dim(mlm_targets, lane, 0, keepdims=False)
    table_low = table.astype(low)
    own_block = lane * dp + spot
    steps = jnp.arange(slots)
    first_at = jnp.min(
        jnp.where(own_ids[:, None] == own_ids[None, :], steps[None, :], slots), 1
    )
    page_first = first_at == steps
    block_own = own_ids // vocab_rows
    rank = jnp.sum(
        page_first[None, :]
        & (block_own[:, None] == block_own[None, :])
        & (steps[None, :] < first_at[:, None]),
        1,
        dtype=jnp.int32,
    )
    source = (block_own % dp) * mp + block_own // dp
    local_own = own_ids - block_own * vocab_rows
    places = jnp.arange(count * ROUND_ROWS)

    def place_of(turn):
        turn_rank = rank - turn * ROUND_ROWS
        inside = (turn_rank >= 0) & (turn_rank < ROUND_ROWS)
        return jnp.where(inside, source * ROUND_ROWS + turn_rank, -1)

    def requests(turn):
        asked = (place_of(turn)[None, :] == places[:, None]) & page_first[None, :]
        rows = jnp.sum(jnp.where(asked, local_own[None, :] + 1, 0), 1, dtype=jnp.int32) - 1
        return rows.reshape(count, ROUND_ROWS)

    def settle(chains, left):
        for chain in chains:
            while len(chain.joined) + len(chain.apart) > left:
                chain.advance()

    def marks_of(rows):
        return (rows.reshape(-1)[:, None] == jnp.arange(vocab_rows)[None, :]).astype(low)


    def held_marks(turn):
        return (place_of(turn)[:, None] == places[None, :]).astype(low)

    def fetch(turn, marks, so_far):
        sent = jnp.dot(marks, table_low, preferred_element_type=jnp.float32).astype(low)
        came = trade(sent)
        return (
            so_far + jnp.dot(held_marks(turn), came, preferred_element_type=jnp.float32),
            came,
            sent,
        )

    share = small_params.shape[0]
    line = 2 * WIDTH
    half_rows = small_half_rows(share)
    small_pad = jnp.pad(small_params.astype(low), (0, 2 * half_rows * 128 - share))
    small_half = lax.dynamic_slice_in_dim(
        small_pad.reshape(2 * half_rows, 128), (lane & 1) * half_rows, half_rows
    )
    tmats_half = own_half(text_mats.astype(low))
    lmats_half = own_half(layout_mats.astype(low)).reshape(-1, 128)
    extra = jnp.concatenate(
        [small_half, lmats_half, jnp.zeros((-lmats_half.shape[0] % 16, 128), low)], 0
    )
    unit_rows = text_ffn.shape[1]
    layout_units = layout_ffn.shape[1]
    layout_unit_rows = -(-(2 * layout_units * LAYOUT_WIDTH) // WIDTH)
    unit_pad = -layout_unit_rows % 16

    def unit_block(layer_no, part):
        text_part = text_ffn[layer_no, :, part * WIDTH : (part + 1) * WIDTH].astype(low)
        if part:
            return text_part
        return jnp.concatenate(
            [
                text_part,
                to_rows(layout_ffn[layer_no : layer_no + 1].astype(low))[0],
                jnp.zeros((unit_pad, WIDTH), low),
            ],
            0,
        )

    mats_chains = [half_spread(tmats_half[layer_no]) for layer_no in range(LAYERS)]
    extra_chain = half_spread(extra, True)
    unit_chains = [
        [unit_spread(unit_block(layer_no, part), part == 1) for part in range(2)]
        for layer_no in range(LAYERS)
    ]
    far_steps = len(routes()[0])
    told = jnp.concatenate(
        [
            jnp.max(rank, keepdims=True) // ROUND_ROWS + 1,
            page_lengths,
            own_targets,
        ]
    )
    told = jnp.broadcast_to(told[None], (count, mask_slots + 2))
    spare = jnp.zeros((count, -(ROUND_ROWS + mask_slots + 2) % 128), jnp.int32)
    message = jnp.concatenate([requests(0), told, spare], 1)
    mats_chains[0].advance()
    extra_chain.advance()
    extra_chain.advance()
    shown = trade(tie(message, *extra_chain.sent))
    mats_chains[0].advance()
    extra_chain.advance()
    shown = tie(shown, *mats_chains[0].sent, *extra_chain.sent)
    rounds = jnp.max(shown[:, ROUND_ROWS])
    all_lengths = shown[:, ROUND_ROWS + 1]
    all_targets = shown[:, ROUND_ROWS + 2 : ROUND_ROWS + 2 + mask_slots].reshape(-1)

    asked_first = marks_of(shown[:, :ROUND_ROWS])
    embedded, came_first, rows_first = fetch(
        0, asked_first, jnp.zeros((slots, WIDTH), jnp.float32)
    )
    embedded = lax.fori_loop(
        1,
        rounds,
        lambda turn, so_far: fetch(turn, marks_of(trade(requests(turn))), so_far)[0],
        embedded,
    )
    settle(mats_chains[:1], 2)
    mats_chains[0].advance(rows_first)
    settle([extra_chain], 1)
    extra_chain.advance(mats_chains[0].sent[0])
    wait = extra_chain.sent[0]
    for chain in unit_chains[0]:
        chain.advance(wait)
    core_key = frozenset([routes()[3]])
    extra_chain.pieces[core_key] = tie(
        extra_chain.pieces[core_key], *[chain.sent[0] for chain in unit_chains[0]]
    )
    small_parts, lmats_all = unpack_small(*half_parts(extra_chain), lmats_half.shape[0])
    lmats_all = lmats_all.reshape(2, dp, LAYERS, -1, 2 * LAYOUT_WIDTH)
    mats_chains[0].advance(tie(came_first, small_parts[6]))
    for number in range(1, far_steps):
        for chain in unit_chains[0]:
            chain.advance(mats_chains[0].sent[0])
    tmats_first = put_in_order(*half_parts(mats_chains[0]))
    (
        text_vec,
        layout_vec,
        text_bias,
        layout_bias,
        text_emb,
        layout_emb,
        text_pos,
        layout_pos,
        box_table,
        align_mat,
    ) = small_parts

    coords = box_coords[:, 0].T
    text_pre, layout_pre, text, layout = embed_streams(
        coords, embedded, text_pos, layout_pos, box_table, text_emb, layout_emb
    )
    caches = []
    layer_weights = []

    def push(value, chains):
        waits = []
        for chain in chains:
            chain.advance()
            waits = waits + chain.sent
        return tie(value, *waits)

    def after(chains, wait):
        for chain in chains:
            chain.advance(wait)

    def hooks_of(layer_no):
        units = unit_chains[layer_no]
        later = layer_no + 1 < LAYERS
        if later:
            next_mats, next_units = mats_chains[layer_no + 1], unit_chains[layer_no + 1]

        def at_low(value):
            if layer_no == 0:
                value = push(value, units)
            if later:
                next_mats.advance(units[1].sent[0])
            return value

        def at_query(value):
            return push(value, units) if layer_no else value

        def at_att(value):
            settle(units, 2)
            pending = [chain for chain in units if len(chain.joined) + len(chain.apart) > 1]
            if pending or later:
                value = push(value, pending + ([next_mats] if later else []))
            after(units, value)
            if later:
                after(next_units, next_mats.sent[0])
            return value

        def at_mid(value):
            return push(value, [next_mats] + next_units) if later else value

        return {
            "low": at_low,
            "query": at_query,
            "att": at_att,
            "mid": at_mid,
            "units": lambda: units_of(layer_no),
        }

    def units_of(layer_no):
        results = [unit_result(chain) for chain in unit_chains[layer_no]]
        layout_both = from_rows(
            take_extra(results[0], unit_rows)[:, :layout_unit_rows], layout_units
        )
        return (results, [layout_both[:, :LAYOUT_WIDTH], layout_both[:, LAYOUT_WIDTH:]])

    slot_marks = (unit_blocks()[:, None] == jnp.arange(count)[None, :]).astype(jnp.float32)
    for layer_no in range(LAYERS):
        if layer_no:
            settle([mats_chains[layer_no]], 1)
            text = push(text, unit_chains[layer_no] + [mats_chains[layer_no]])
            tmats = put_in_order(*half_parts(mats_chains[layer_no]))
        else:
            tmats = tmats_first
        weights = [
            tmats,
            lmats_all[:, :, layer_no].reshape(2, LAYOUT_WIDTH, -1),
            jnp.dot(
                slot_marks, text_bias[layer_no].reshape(count, -1), precision=PRECISE
            ).reshape(-1),
            jnp.dot(
                slot_marks, layout_bias[layer_no].reshape(count, -1), precision=PRECISE
            ).reshape(-1),
            text_vec[layer_no],
            layout_vec[layer_no],
        ]
        text, layout, cache, units = layer_forward(
            text, layout, weights, page_lengths, hooks_of(layer_no)
        )
        weights = weights[:2] + list(units) + weights[2:]
        caches.append(cache)
        layer_weights.append(weights)

    row_index = mlm_positions.reshape(-1)
    live_all = (
        (jnp.arange(mask_slots)[None, :] * slots < mask_slots * all_lengths[:, None])
        .astype(jnp.float32)
        .reshape(-1)
    )
    chosen_marks = (row_index[:, None] == steps[None, :]).astype(low)
    chosen_own = jnp.dot(
        chosen_marks, text.astype(low), preferred_element_type=jnp.float32
    ).astype(low)
    chosen_all = show_all(chosen_own).reshape(count * mask_slots, WIDTH)
    logits = contract_cols(chosen_all, table_low)
    target_local = all_targets - own_block * vocab_rows
    target_in = target_local[:, None] == jnp.arange(vocab_rows)[None, :]
    target_logit = jnp.sum(jnp.where(target_in, logits, 0.0), 1)
    row_peak = jnp.max(logits, axis=1)
    row_total = jnp.sum(jnp.exp(logits - row_peak[:, None]), axis=1)
    stats = show_all(jnp.stack([row_peak, row_total, target_logit]))
    all_peak = jnp.max(stats[:, 0], 0)
    all_total = jnp.sum(stats[:, 1] * jnp.exp(stats[:, 0] - all_peak[None]), 0)
    all_target = jnp.sum(stats[:, 2], 0)
    log_total = all_peak + jnp.log(all_total)
    own_start = (spot * mp + lane) * mask_slots
    live_own = lax.dynamic_slice_in_dim(live_all, own_start, mask_slots)
    own_loss = jnp.sum(
        lax.dynamic_slice_in_dim((log_total - all_target) * live_all, own_start, mask_slots)
    )
    grad_low = (
        (jnp.exp(logits - log_total[:, None]) - target_in.astype(jnp.float32)) * live_all[:, None]
    ).astype(low)
    table_grad = contract_rows(grad_low, chosen_all)
    chosen_parts = trade(jnp.dot(grad_low, table_low, preferred_element_type=jnp.float32).astype(low))
    chosen_grad = jnp.sum(
        chosen_parts.reshape(count, mask_slots, WIDTH).astype(jnp.float32), 0
    )

    first_marks = (align_pairs[0, :, 0][:, None] == steps[None, :]).astype(jnp.float32)
    second_marks = (align_pairs[0, :, 1][:, None] == steps[None, :]).astype(jnp.float32)
    answer = align_labels.reshape(-1).astype(jnp.float32)
    first_rows = jnp.dot(first_marks, text, precision=PRECISE)
    second_rows = jnp.dot(second_marks, layout, precision=PRECISE)

    def pair_loss(text_rows, layout_rows, align_weight):
        right = jnp.dot(layout_rows, align_weight, precision=PRECISE)
        logit = jnp.sum(text_rows * right, axis=-1) / math.sqrt(WIDTH)
        return jnp.sum(jax.nn.softplus(logit) - answer * logit)

    align_part, align_pull = jax.vjp(pair_loss, first_rows, second_rows, align_mat)
    first_back, second_back, align_grad = align_pull(jnp.ones((), jnp.float32))
    grad_text = add_rows(
        jnp.concatenate([first_marks.astype(low), chosen_marks], 0),
        jnp.concatenate([first_back, chosen_grad], 0),
    )
    grad_layout = add_rows(second_marks.astype(low), second_back)

    plan = Plan()
    layer_grads = [None] * LAYERS
    for layer_no in reversed(range(LAYERS)):
        grad_text, grad_layout, layer_grads[layer_no] = layer_backward(
            caches[layer_no], grad_text, grad_layout, layer_weights[layer_no], page_lengths, plan
        )
        grad_text = plan.between(grad_text)

    embed_grad, looked_grad, text_emb_grad, layout_emb_grad, box_grad = embed_back(
        coords, text_pre, layout_pre, text_emb, layout_emb, grad_text, grad_layout
    )
    embed_low = embed_grad.astype(low)

    def give(turn, marks, so_far):
        sent = contract_rows(held_marks(turn), embed_low).astype(low)
        came = trade(sent)
        return (so_far + contract_rows(marks, came), sent, came)

    table_sum, gave_rows, gave_came = give(0, asked_first, table_grad)
    table_sum = lax.fori_loop(
        1,
        rounds,
        lambda turn, so_far: give(turn, marks_of(trade(requests(turn))), so_far)[0],
        table_sum,
    )

    def stacked(member):
        return jnp.stack([layer_grads[layer_no][member] for layer_no in range(LAYERS)])

    def in_order(member):
        return jnp.stack(
            [
                lax.dot_general(
                    slot_marks,
                    layer_grads[layer_no][member].reshape(count, -1),
                    (((0,), (0,)), ((), ())),
                    precision=PRECISE,
                )
                for layer_no in range(LAYERS)
            ]
        )

    small_items = [
        stacked(2),
        stacked(3),
        in_order(0),
        in_order(1),
        text_emb_grad,
        layout_emb_grad,
        embed_grad,
        looked_grad,
        box_grad,
        align_grad,
    ]
    plan.mats[1].advance()
    token = plan.mats[1].sent
    small_items[6] = tie(embed_grad, token, gave_rows)
    small_blocks = pack_small(small_items, dp).reshape(dp, 2, half_rows, 128)
    first = own_bit("mp", 0) == 0
    small_total = HalfSum(
        jnp.where(first, small_blocks[:, 1], small_blocks[:, 0]),
        jnp.where(first, small_blocks[:, 0], small_blocks[:, 1]),
    )
    token = small_total.sent
    turns = plan.units[1] + [small_total] + plan.units[1] + [plan.mats[1], small_total]
    turns = turns + plan.units[1] + [plan.mats[1], small_total] * 4
    for number, chain in enumerate(turns):
        if chain.left:
            chain.came = tie(chain.came, token)
            chain.advance()
            token = chain.sent
        if number == 6:
            token = tie(gave_came, token)
    small_sum = small_total.finish().reshape(-1)[:share]
    plan.units.reverse()
    plan.mats.reverse()
    mats_sums = [item.finish() for item in plan.mats]
    mats_rows = text_mats.shape[1]
    extra_rows = layout_mats.shape[1] * LAYOUT_WIDTH * 2 // line
    tmats_sum = jnp.stack(
        [jnp.concatenate([item[0, :mats_rows], item[1, :mats_rows]], 1) for item in mats_sums]
    )
    lmats_sum = jnp.stack(
        [
            jnp.concatenate(
                [
                    item[side, mats_rows : mats_rows + extra_rows].reshape(-1, 2 * LAYOUT_WIDTH)
                    for side in range(2)
                ],
                1,
            )
            for item in mats_sums
        ]
    )
    unit_sums = [
        [item.finish() for item in plan.units[layer_no]] for layer_no in range(LAYERS)
    ]
    tffn_sum = jnp.stack(
        [jnp.concatenate([item[:unit_rows] for item in pair], 1) for pair in unit_sums]
    )
    lffn_sum = jnp.stack(
        [
            from_rows(pair[0][None, unit_rows : unit_rows + layout_unit_rows], layout_units)
            for pair in unit_sums
        ]
    )
    final_grads = (table_sum, tmats_sum, lmats_sum, tffn_sum, lffn_sum, small_sum)
    lane_first = (lane == 0).astype(jnp.float32)
    squares = (
        jnp.sum(table_sum * table_sum) + jnp.sum(tffn_sum * tffn_sum) + jnp.sum(lffn_sum * lffn_sum)
    )
    squares = squares + lane_first * (
        jnp.sum(tmats_sum * tmats_sum)
        + jnp.sum(lmats_sum * lmats_sum)
        + jnp.sum(small_sum * small_sum)
    )
    count_part = jnp.sum(live_own) + jnp.float32(pages * PAIRS)
    sums = sum_everywhere(
        jnp.broadcast_to(
            jnp.stack([squares, own_loss + align_part, count_part, squares])[:, None], (4, 128)
        )
    )
    total_squares, loss_sum, loss_count = sums[0, 0], sums[1, 0], sums[2, 0]
    grad_norm = jnp.sqrt(total_squares) / loss_count
    factor = jnp.minimum(1.0, CLIP_NORM / grad_norm)
    masters = (table, text_mats, layout_mats, text_ffn, layout_ffn, small_params)
    moments = (
        table_momentum,
        text_mats_momentum,
        layout_mats_momentum,
        text_ffn_momentum,
        layout_ffn_momentum,
        small_momentum,
    )
    averages = (
        table_average,
        text_mats_average,
        layout_mats_average,
        text_ffn_average,
        layout_ffn_average,
        small_average,
    )
    updated = [
        apply_update(
            masters[number],
            final_grads[number],
            moments[number],
            averages[number],
            loss_count,
            factor,
        )
        for number in range(6)
    ]
    new_masters = [item[0] for item in updated]
    new_moments = [item[1] for item in updated]
    new_averages = [item[2] for item in updated]
    copies = [item.astype(jnp.bfloat16) for item in new_masters[:5]]
    return (
        loss_sum,
        loss_count,
        grad_norm,
        new_masters[0],
        new_masters[1],
        new_masters[2],
        new_masters[3],
        new_masters[4],
        new_masters[5],
        copies[0],
        copies[1],
        copies[2],
        copies[3],
        copies[4],
        new_moments[0],
        new_moments[1],
        new_moments[2],
        new_moments[3],
        new_moments[4],
        new_moments[5],
        new_averages[0],
        new_averages[1],
        new_averages[2],
        new_averages[3],
        new_averages[4],
        new_averages[5],
    )


def solution(mesh):
    return jax.shard_map(
        on_device,
        mesh=mesh,
        in_specs=(
            P("dp", None),
            P("dp", None),
            P(("dp", "mp")),
            P(None, ("dp", "mp"), None),
            P(("dp", "mp"), None),
            P(("dp", "mp"), None, None),
            P(("dp", "mp"), None),
            P(("mp", "dp"), None),
            P(None, "dp", None),
            P(None, "dp", None),
            P(None, ("mp", "dp"), None),
            P(None, ("mp", "dp"), None),
            P("dp"),
            P(("mp", "dp"), None),
            P(None, "dp", None),
            P(None, "dp", None),
            P(None, ("mp", "dp"), None),
            P(None, ("mp", "dp"), None),
            P("dp"),
            P(("mp", "dp"), None),
            P(None, "dp", None),
            P(None, "dp", None),
            P(None, ("mp", "dp"), None),
            P(None, ("mp", "dp"), None),
            P("dp"),
        ),
        out_specs=(
            P(),
            P(),
            P(),
            P(("mp", "dp"), None),
            P(None, "dp", None),
            P(None, "dp", None),
            P(None, ("mp", "dp"), None),
            P(None, ("mp", "dp"), None),
            P("dp"),
            P(("mp", "dp"), None),
            P(None, "dp", None),
            P(None, "dp", None),
            P(None, ("mp", "dp"), None),
            P(None, ("mp", "dp"), None),
            P(("mp", "dp"), None),
            P(None, "dp", None),
            P(None, "dp", None),
            P(None, ("mp", "dp"), None),
            P(None, ("mp", "dp"), None),
            P("dp"),
            P(("mp", "dp"), None),
            P(None, "dp", None),
            P(None, "dp", None),
            P(None, ("mp", "dp"), None),
            P(None, ("mp", "dp"), None),
            P("dp"),
        ),
        check_vma=False,
    )
```

```python
import functools
import math

import jax
import jax.numpy as jnp
from jax import lax
from jax.experimental import pallas as pl
from jax.experimental.pallas import tpu as pltpu
from jax.sharding import PartitionSpec as P

WIDTH = 768
HEADS = 12
FFN_UNITS = 3072
LAYOUT_WIDTH = 192
LAYOUT_UNITS = 768
BOXES = 1024
PAGE_SLOTS = 512
PAIRS = 32
LAYERS = 2


EPSILON = 1e-05
CLIP_NORM = 0.01
LEARN_RATE = 10000.0
MOMENTUM = 0.5
AVERAGE_DECAY = 0.5
MASK_FILL = -1e30
PRECISE = lax.Precision.HIGHEST


def small_shapes():
    return [
        (LAYERS, 8, WIDTH),
        (LAYERS, 8, LAYOUT_WIDTH),
        (LAYERS, FFN_UNITS),
        (LAYERS, LAYOUT_UNITS),
        (2, WIDTH),
        (2, LAYOUT_WIDTH),
        (PAGE_SLOTS, WIDTH),
        (PAGE_SLOTS, LAYOUT_WIDTH),
        (2, BOXES // 8, 2 * LAYOUT_WIDTH),
        (LAYOUT_WIDTH, WIDTH),
    ]


def small_views():
    views = []
    offset = 0
    for piece_dims in small_shapes():
        amount = math.prod(piece_dims)
        width = piece_dims[-1] if piece_dims[-1] % 128 == 0 else 2 * piece_dims[-1]
        views.append((offset // 128, amount // width, width))
        offset = offset + amount
    return views, offset // 128


def small_half_rows(share):
    return -(-share // (128 * 32)) * 16


def pack_small(items, dp):
    views, total = small_views()
    share = total * 128 // dp
    rows = 2 * small_half_rows(share)

    def kernel(*refs):
        sources, out_ref, flat = refs[: len(items)], refs[len(items)], refs[len(items) + 1]
        flat[total:, :] = jnp.zeros((flat.shape[0] - total, 128), jnp.float32)
        for source, (start, count, width) in zip(sources, views):
            per = width // 128
            for part in range(per):
                flat[pl.ds(start + part, count, stride=per), :] = source[
                    :, part * 128 : (part + 1) * 128
                ]
        column = lax.broadcasted_iota(jnp.int32, (rows, 128), 1)
        for number in range(dp):
            start, shift = number * share // 128, number * share % 128
            block = flat[pl.ds(start, rows), :]
            if shift:
                after = flat[pl.ds(start + 1, rows), :]
                block = jnp.where(
                    column < 128 - shift,
                    pltpu.roll(block, 128 - shift, 1),
                    pltpu.roll(after, 128 - shift, 1),
                )
            out_ref[number] = block.astype(out_ref.dtype)

    whole = pl.BlockSpec(memory_space=pltpu.VMEM)
    return pl.pallas_call(
        kernel,
        out_shape=jax.ShapeDtypeStruct((dp, rows, 128), jnp.bfloat16),
        in_specs=[whole] * len(items),
        out_specs=whole,
        scratch_shapes=[pltpu.VMEM((total + rows + 8, 128), jnp.float32)],
        cost_estimate=pl.CostEstimate(flops=0, bytes_accessed=2000000, transcendentals=0),
        compiler_params=pltpu.CompilerParams(vmem_limit_bytes=32 * 1024 * 1024),
    )(*[item.reshape(count, width) for item, (start, count, width) in zip(items, views)])


def unpack_small(own, came, places, extra_rows):
    views, total = small_views()
    dp = own.shape[0]
    share = total * 128 // dp
    half = small_half_rows(share)

    def kernel(place_ref, own_ref, came_ref, *refs):
        targets, extra_ref, flat, turned = refs[:-3], refs[-3], refs[-2], refs[-1]
        mine = [(place_ref[dp] == side).astype(jnp.float32) for side in range(2)]
        for number in range(dp):
            start, shift = number * share // 128, number * share % 128
            rows = -(-(share + shift) // 128)
            slot = place_ref[number]
            for side in range(2):
                both = own_ref[slot].astype(jnp.float32), came_ref[slot].astype(jnp.float32)
                whole = jnp.where(mine[side] > 0.5, *both)
                extra_ref[side, number] = whole[half : half + extra_rows].astype(extra_ref.dtype)
                part = whole[:half]
                turned[pl.ds(8 + side * half, half), :] = (
                    pltpu.roll(part, shift, 1) if shift else part
                )
            block = turned[pl.ds(8, rows), :]
            if shift:
                turned[7:8, :] = flat[pl.ds(start, 1), :]
                column = lax.broadcasted_iota(jnp.int32, (rows, 128), 1)
                block = jnp.where(column >= shift, block, turned[pl.ds(7, rows), :])
            flat[pl.ds(start, rows), :] = block
        for target, (start, count, width) in zip(targets, views):
            per = width // 128
            for part in range(per):
                target[:, part * 128 : (part + 1) * 128] = flat[
                    pl.ds(start + part, count, stride=per), :
                ]

    whole = pl.BlockSpec(memory_space=pltpu.VMEM)
    *outs, extra = pl.pallas_call(
        kernel,
        out_shape=[
            jax.ShapeDtypeStruct((count, width), jnp.float32) for start, count, width in views
        ]
        + [jax.ShapeDtypeStruct((2, dp, extra_rows, 128), jnp.bfloat16)],
        in_specs=[pl.BlockSpec(memory_space=pltpu.SMEM), whole, whole],
        out_specs=[whole] * (len(views) + 1),
        scratch_shapes=[
            pltpu.VMEM((total + 8, 128), jnp.float32),
            pltpu.VMEM((2 * half + 16, 128), jnp.float32),
        ],
        cost_estimate=pl.CostEstimate(flops=0, bytes_accessed=2000000, transcendentals=0),
        compiler_params=pltpu.CompilerParams(vmem_limit_bytes=32 * 1024 * 1024),
    )(places, own, came)
    return [item.reshape(piece_dims) for item, piece_dims in zip(outs, small_shapes())], extra


def norm_apply(values, gain_row, bias_row):
    centre = values - jnp.mean(values, axis=-1, keepdims=True)
    spread = jnp.mean(centre * centre, axis=-1, keepdims=True)
    return centre * lax.rsqrt(spread + EPSILON) * gain_row + bias_row


def norm_back(values, gain_row, bias_row, grad_out):
    unused, pullback = jax.vjp(norm_apply, values, gain_row, bias_row)
    return pullback(grad_out)


def gelu_exact(values):
    return jax.nn.gelu(values, approximate=False)


def contract_rows(left, right):
    return lax.dot_general(
        left, right, (((0,), (0,)), ((), ())), preferred_element_type=jnp.float32
    )


def contract_cols(left, right):
    return lax.dot_general(
        left, right, (((1,), (1,)), ((), ())), preferred_element_type=jnp.float32
    )


def heads_view(values, pages):
    return values.reshape(pages, PAGE_SLOTS, HEADS, values.shape[-1] // HEADS)


ROUND_ROWS = 32


def bits_of(size):
    return list(reversed(range(size.bit_length() - 1)))


def hop(values, axis, bit):
    pairs = [(spot, spot ^ (1 << bit)) for spot in range(lax.axis_size(axis))]
    return lax.ppermute(values, axis, pairs)


def own_bit(axis, bit):
    return (lax.axis_index(axis) >> bit) & 1


def routes():
    far = [("dp", bit) for bit in bits_of(lax.axis_size("dp"))]
    high = [("mp", bit) for bit in bits_of(lax.axis_size("mp"))[:-1]]
    core = ("mp", 0)
    return (far[:-1], far[-1], high, core)


def add_low(kept, came):
    return (kept.astype(jnp.float32) + came.astype(jnp.float32)).astype(jnp.bfloat16)


def tie(value, *waits):
    def kernel(*refs):
        pass

    spec = pl.BlockSpec(memory_space=pl.ANY)
    return pl.pallas_call(
        kernel,
        out_shape=jax.ShapeDtypeStruct(value.shape, value.dtype),
        in_specs=[spec] * (1 + len(waits)),
        out_specs=spec,
        input_output_aliases={0: 0},
        cost_estimate=pl.CostEstimate(flops=0, bytes_accessed=0, transcendentals=0),
    )(value, *waits)


def put_in_order(own, came, places):
    slots, rows, width = own.shape

    def kernel(place_ref, own_ref, came_ref, out_ref, sems):
        side = place_ref[slots]

        def copies(half, source):
            return [
                pltpu.make_async_copy(
                    source.at[place_ref[spot]],
                    out_ref.at[half, pl.ds(spot * rows, rows)],
                    sems.at[half, spot],
                )
                for spot in range(slots)
            ]

        for half in range(2):
            for mine, source in ((True, own_ref), (False, came_ref)):

                @pl.when((side == half) == mine)
                def _(half=half, source=source):
                    for copy in copies(half, source):
                        copy.start()

        for half in range(2):
            for copy in copies(half, own_ref):
                copy.wait()

    anywhere = pl.BlockSpec(memory_space=pl.ANY)
    return pl.pallas_call(
        kernel,
        out_shape=jax.ShapeDtypeStruct((2, slots * rows, width), own.dtype),
        in_specs=[pl.BlockSpec(memory_space=pltpu.SMEM), anywhere, anywhere],
        out_specs=pl.BlockSpec(memory_space=pltpu.VMEM),
        scratch_shapes=[pltpu.SemaphoreType.DMA((2, slots))],
        cost_estimate=pl.CostEstimate(
            flops=0, bytes_accessed=2 * slots * rows * width, transcendentals=0
        ),
        compiler_params=pltpu.CompilerParams(vmem_limit_bytes=16 * 1024 * 1024),
    )(places, own, came)


def embed_kernel(
    coords, embedded, text_pos, layout_pos, tables, text_emb, layout_emb, *outs
):
    text_pre, layout_pre, text, layout = outs
    quarter = LAYOUT_WIDTH // 4
    low = jnp.bfloat16
    row = lax.broadcasted_iota(jnp.int32, (PAGE_SLOTS, BOXES // 8), 1)
    lanes = lax.broadcasted_iota(jnp.int32, (PAGE_SLOTS, 8 * quarter), 1) // quarter
    fold_in = lax.broadcasted_iota(jnp.int32, (8 * quarter, LAYOUT_WIDTH), 0) % quarter
    fold_out = lax.broadcasted_iota(jnp.int32, (8 * quarter, LAYOUT_WIDTH), 1)
    looked = jnp.zeros((PAGE_SLOTS, LAYOUT_WIDTH), jnp.float32)
    for number in range(4):
        spot = coords[:, number : number + 1]
        marks = (spot // 8 == row).astype(jnp.float32).astype(low)
        wide = jnp.dot(
            marks, tables[number % 2].astype(low), preferred_element_type=jnp.float32
        )
        kept = jnp.where(spot % 8 == lanes, wide, 0.0).astype(low)
        fold = (fold_in + number * quarter == fold_out).astype(jnp.float32).astype(low)
        looked = looked + jnp.dot(kept, fold, preferred_element_type=jnp.float32)
    layout_pre[...] = looked + layout_pos[...]
    text_pre[...] = embedded[...] + text_pos[...]
    text[...] = norm_apply(text_pre[...], text_emb[0:1, :], text_emb[1:2, :])
    layout[...] = norm_apply(layout_pre[...], layout_emb[0:1, :], layout_emb[1:2, :])


def norm_grads(values, gain, grad):
    centre = values - jnp.mean(values, axis=-1, keepdims=True)
    scale = lax.rsqrt(jnp.mean(centre * centre, axis=-1, keepdims=True) + EPSILON)
    unit = centre * scale
    lifted = grad * gain
    inner = jnp.mean(lifted * unit, axis=-1, keepdims=True)
    back = scale * (lifted - jnp.mean(lifted, axis=-1, keepdims=True) - unit * inner)
    sums = [jnp.sum(item, 0, keepdims=True) for item in (grad * unit, grad)]
    return back, jnp.concatenate(sums, 0)


def embed_back_kernel(coords, text_pre, layout_pre, text_emb, layout_emb, *refs):
    grad_text, grad_layout, text_back, layout_back, text_sums, layout_sums, boxes = refs
    low = jnp.bfloat16
    quarter = LAYOUT_WIDTH // 4
    text_back[...], text_sums[...] = norm_grads(text_pre[...], text_emb[0:1, :], grad_text[...])
    looked, layout_sums[...] = norm_grads(
        layout_pre[...], layout_emb[0:1, :], grad_layout[...]
    )
    layout_back[...] = looked
    high, rest = split_high(looked)
    row = lax.broadcasted_iota(jnp.int32, (PAGE_SLOTS, BOXES // 8), 1)
    lanes = lax.broadcasted_iota(jnp.int32, (PAGE_SLOTS, 8 * quarter), 1) // quarter
    fold_in = lax.broadcasted_iota(jnp.int32, (8 * quarter, LAYOUT_WIDTH), 0) % quarter
    fold_out = lax.broadcasted_iota(jnp.int32, (8 * quarter, LAYOUT_WIDTH), 1)
    boxes[...] = jnp.zeros_like(boxes)
    for number in range(4):
        spot = coords[:, number : number + 1]
        marks = (spot // 8 == row).astype(jnp.float32).astype(low)
        fold = (fold_in + number * quarter == fold_out).astype(jnp.float32).astype(low)
        wide = contract_cols(high, fold) + contract_cols(rest, fold)
        kept = jnp.where(spot % 8 == lanes, wide, 0.0)
        boxes[number % 2] += add_rows(marks, kept)


def embed_back(*operands):
    whole = pl.BlockSpec(memory_space=pltpu.VMEM)
    shapes = [
        (PAGE_SLOTS, WIDTH),
        (PAGE_SLOTS, LAYOUT_WIDTH),
        (2, WIDTH),
        (2, LAYOUT_WIDTH),
        (2, BOXES // 8, 2 * LAYOUT_WIDTH),
    ]
    return pl.pallas_call(
        embed_back_kernel,
        out_shape=[jax.ShapeDtypeStruct(shape, jnp.float32) for shape in shapes],
        in_specs=[whole] * len(operands),
        out_specs=[whole] * len(shapes),
        cost_estimate=pl.CostEstimate(flops=0, bytes_accessed=2000000, transcendentals=0),
        compiler_params=pltpu.CompilerParams(vmem_limit_bytes=32 * 1024 * 1024),
    )(*operands)


def embed_streams(*operands):
    whole = pl.BlockSpec(memory_space=pltpu.VMEM)
    return pl.pallas_call(
        embed_kernel,
        out_shape=[
            jax.ShapeDtypeStruct((PAGE_SLOTS, width), jnp.float32)
            for width in (WIDTH, LAYOUT_WIDTH) * 2
        ],
        in_specs=[whole] * len(operands),
        out_specs=[whole] * 4,
        cost_estimate=pl.CostEstimate(flops=0, bytes_accessed=2000000, transcendentals=0),
        compiler_params=pltpu.CompilerParams(vmem_limit_bytes=24 * 1024 * 1024),
    )(*operands)


def mats_kernel(side, rows, query, keys, values, att, first, sent_ref, kept_ref, result):
    step = pl.program_id(0)
    half = jnp.where(step < 2, 1 - side[0], side[0])
    cases = ((rows, query), (rows, keys), (rows, values), (att, first))
    for number, (left, right) in enumerate(cases):

        @pl.when(half * 2 + step % 2 == number)
        def _(left=left, right=right):
            result[...] = contract_rows(left[...], right[...])

    def store(target):
        blocks = result[...].astype(target.dtype).reshape(target.shape[0], -1, WIDTH)
        target[:, : blocks.shape[1], :] = blocks

    @pl.when(step < 2)
    def _():
        store(sent_ref)

    @pl.when(step >= 2)
    def _():
        store(kept_ref)


def mats_sums(side, operands, padded):
    dp = lax.axis_size("dp")
    whole = pl.BlockSpec((PAGE_SLOTS, WIDTH), lambda step: (0, 0))
    shape = jax.ShapeDtypeStruct((dp, padded, 2 * WIDTH), jnp.bfloat16)
    return pl.pallas_call(
        mats_kernel,
        grid=(4,),
        in_specs=[pl.BlockSpec(memory_space=pltpu.SMEM)] + [whole] * 6,
        out_specs=[
            pl.BlockSpec((dp, padded, WIDTH), lambda step: (0, 0, jnp.minimum(step, 1))),
            pl.BlockSpec((dp, padded, WIDTH), lambda step: (0, 0, jnp.maximum(step - 2, 0))),
        ],
        out_shape=[shape, shape],
        scratch_shapes=[pltpu.VMEM((WIDTH, WIDTH), jnp.float32)],
        cost_estimate=pl.CostEstimate(
            flops=2 * PAGE_SLOTS * WIDTH * WIDTH, bytes_accessed=4000000, transcendentals=0
        ),
        compiler_params=pltpu.CompilerParams(vmem_limit_bytes=32 * 1024 * 1024),
    )(side, *operands)


def take_extra(pieces, rows):
    slots, total, width = pieces[0].shape

    def kernel(*refs):
        out_ref, sems = refs[-2], refs[-1]
        copies = [
            pltpu.make_async_copy(
                ref.at[:, pl.ds(rows, total - rows)],
                out_ref.at[pl.ds(number * slots, slots)],
                sems.at[number],
            )
            for number, ref in enumerate(refs[:-2])
        ]
        for copy in copies:
            copy.start()
        for copy in copies:
            copy.wait()

    return pl.pallas_call(
        kernel,
        out_shape=jax.ShapeDtypeStruct((slots * len(pieces), total - rows, width), pieces[0].dtype),
        in_specs=[pl.BlockSpec(memory_space=pl.ANY)] * len(pieces),
        out_specs=pl.BlockSpec(memory_space=pltpu.VMEM),
        scratch_shapes=[pltpu.SemaphoreType.DMA((len(pieces),))],
        cost_estimate=pl.CostEstimate(flops=0, bytes_accessed=500000, transcendentals=0),
    )(*pieces)


HEAD_PAIRS = HEADS // 2
TEXT_HEAD = WIDTH // HEADS
LAYOUT_HEAD = LAYOUT_WIDTH // HEADS


def head_of(text_ref, layout_ref, head, scaled=False):
    text = text_ref[:, head * TEXT_HEAD : (head + 1) * TEXT_HEAD]
    layout = layout_ref[:, head * LAYOUT_HEAD : (head + 1) * LAYOUT_HEAD]
    if scaled:
        text_scale, layout_scale = scale_pair()
        text = (text.astype(jnp.float32) * text_scale).astype(text.dtype)
        layout = (layout.astype(jnp.float32) * layout_scale).astype(layout.dtype)
    return jnp.concatenate([text, layout], 1)


def store_heads(text_ref, layout_ref, both):
    text_ref[...] = jnp.concatenate([item[:, :TEXT_HEAD] for item in both], 1).astype(
        text_ref.dtype
    )
    layout = jnp.concatenate([item[:, TEXT_HEAD:] for item in both], 1).astype(layout_ref.dtype)
    width = layout.shape[1]
    for pair in range(HEAD_PAIRS):

        @pl.when(pl.program_id(0) == pair)
        def _(pair=pair):
            layout_ref[:, pair * width : (pair + 1) * width] = layout


def own_pair(sources, targets):
    width = targets[0].shape[1]
    for pair in range(HEAD_PAIRS):

        @pl.when(pl.program_id(0) == pair)
        def _(pair=pair):
            for source, target in zip(sources, targets):
                target[...] = source[:, pair * width : (pair + 1) * width]


def attend_kernel(length, qt, kt, vt, *refs):
    out_t, out_l, lse, ql, kl, vl = refs[3:]
    own_pair(refs[:3], (ql, kl, vl))
    live = lax.broadcasted_iota(jnp.int32, (PAGE_SLOTS, PAGE_SLOTS), 1) < length[0]
    outs = []
    for head in range(2):
        query, keys = head_of(qt, ql, head, True), head_of(kt, kl, head)
        scores = jnp.where(live, contract_cols(query, keys), MASK_FILL)
        peak = jnp.max(scores, 1, keepdims=True)
        expo = jnp.exp(scores - peak)
        total = jnp.sum(expo, 1, keepdims=True)
        probs = (expo * (1.0 / total)).astype(jnp.bfloat16)
        outs.append(
            jnp.dot(probs, head_of(vt, vl, head), preferred_element_type=jnp.float32)
        )
        lse[0, :, head : head + 1] = peak + jnp.log(total)
    store_heads(out_t, out_l, outs)


def attend_back_kernel(length, qt, kt, vt, got, *refs):
    lse, dqt, dkt, dvt, dql, dkl, dvl, ql, kl, vl, gol = refs[4:]
    own_pair(refs[:4], (ql, kl, vl, gol))
    text_scale, layout_scale = scale_pair()
    live = lax.broadcasted_iota(jnp.int32, (PAGE_SLOTS, PAGE_SLOTS), 0) < length[0]
    column = lax.broadcasted_iota(jnp.int32, (1, TEXT_HEAD + LAYOUT_HEAD), 1)
    scales = jnp.where(column < TEXT_HEAD, text_scale, layout_scale)
    grads_q, grads_k, grads_v = [], [], []
    for head in range(2):
        query, keys = head_of(qt, ql, head, True), head_of(kt, kl, head)
        values, grad = head_of(vt, vl, head), head_of(got, gol, head)
        scores = jnp.where(live, contract_cols(keys, query), MASK_FILL)
        probs = jnp.exp(scores - lse[0, head : head + 1, :])
        grad_probs = contract_cols(values, grad)
        shift = jnp.sum(probs * grad_probs, 0, keepdims=True)
        grad_scores = (probs * (grad_probs - shift)).astype(jnp.bfloat16)
        grads_v.append(
            jnp.dot(probs.astype(jnp.bfloat16), grad, preferred_element_type=jnp.float32)
        )
        grads_k.append(jnp.dot(grad_scores, query, preferred_element_type=jnp.float32))
        grads_q.append(contract_rows(grad_scores, keys) * scales)
    store_heads(dqt, dql, grads_q)
    store_heads(dkt, dkl, grads_k)
    store_heads(dvt, dvl, grads_v)


def pair_specs():
    text = pl.BlockSpec((PAGE_SLOTS, 2 * TEXT_HEAD), lambda step: (0, step))
    layout = pl.BlockSpec((PAGE_SLOTS, LAYOUT_WIDTH), lambda step: (0, 0))
    return text, layout, pltpu.VMEM((PAGE_SLOTS, 2 * LAYOUT_HEAD), jnp.bfloat16)


def attend(text_qkv, layout_qkv, lengths):
    text, layout, pair = pair_specs()
    low = jnp.bfloat16
    out_t, out_l, lse = pl.pallas_call(
        attend_kernel,
        grid=(HEAD_PAIRS,),
        in_specs=[pl.BlockSpec(memory_space=pltpu.SMEM)] + [text] * 3 + [layout] * 3,
        out_specs=[text, layout, pl.BlockSpec((1, PAGE_SLOTS, 2), lambda step: (step, 0, 0))],
        out_shape=[
            jax.ShapeDtypeStruct((PAGE_SLOTS, WIDTH), low),
            jax.ShapeDtypeStruct((PAGE_SLOTS, LAYOUT_WIDTH), low),
            jax.ShapeDtypeStruct((HEAD_PAIRS, PAGE_SLOTS, 2), jnp.float32),
        ],
        scratch_shapes=[pair] * 3,
        cost_estimate=pl.CostEstimate(
            flops=4000000000, bytes_accessed=2000000, transcendentals=100000
        ),
        compiler_params=pltpu.CompilerParams(vmem_limit_bytes=24 * 1024 * 1024),
    )(lengths, *text_qkv, *layout_qkv)
    return (out_t, out_l, lse.transpose(0, 2, 1))


def attend_back(text_qkv, layout_qkv, lengths, lse, text_grad, layout_grad):
    text, layout, pair = pair_specs()
    low = jnp.bfloat16
    text_out = jax.ShapeDtypeStruct((PAGE_SLOTS, WIDTH), low)
    layout_out = jax.ShapeDtypeStruct((PAGE_SLOTS, LAYOUT_WIDTH), low)
    outs = pl.pallas_call(
        attend_back_kernel,
        grid=(HEAD_PAIRS,),
        in_specs=[pl.BlockSpec(memory_space=pltpu.SMEM)]
        + [text] * 4
        + [layout] * 4
        + [pl.BlockSpec((1, 2, PAGE_SLOTS), lambda step: (step, 0, 0))],
        out_specs=[text] * 3 + [layout] * 3,
        out_shape=[text_out] * 3 + [layout_out] * 3,
        scratch_shapes=[pair] * 4,
        cost_estimate=pl.CostEstimate(
            flops=5000000000, bytes_accessed=3000000, transcendentals=100000
        ),
        compiler_params=pltpu.CompilerParams(vmem_limit_bytes=32 * 1024 * 1024),
    )(lengths, *text_qkv, text_grad, *layout_qkv, layout_grad, lse)
    return (list(outs[:3]), list(outs[3:]))


ERF_TERMS = (0.254829592, -0.284496736, 1.421413741, -1.453152027, 1.061405429)


def gelu_pair(values):
    size = jnp.abs(values)
    base = 1.0 / (1.0 + (0.3275911 / math.sqrt(2.0)) * size)
    series = ERF_TERMS[4]
    for term in reversed(ERF_TERMS[:4]):
        series = series * base + term
    bell = jnp.exp(values * values * -0.5)
    tail = 0.5 * series * base * bell
    share = jnp.where(values < 0.0, tail, 1.0 - tail)
    return (values * share, share + values * bell * (1.0 / math.sqrt(2.0 * math.pi)))


def load_units(pieces_in, pieces_out, rows, buffers, sems, chunks):
    per = len(pieces_in) // chunks
    slots = pieces_in[0].shape[0]
    step = pl.program_id(0)

    def copies(turn):
        made = []
        for number in range(per):
            for side, pieces in enumerate((pieces_in, pieces_out)):
                made.append(
                    pltpu.make_async_copy(
                        pieces[turn * per + number].at[:, pl.ds(0, rows)],
                        buffers[side].at[turn % 2, pl.ds(number * slots, slots)],
                        sems.at[turn % 2, 2 * number + side],
                    )
                )
        return made

    for turn in range(chunks):

        @pl.when(step == turn)
        def _(turn=turn):
            if turn == 0:
                for copy in copies(0):
                    copy.start()
            if turn + 1 < chunks:
                for copy in copies(turn + 1):
                    copy.start()
            for copy in copies(turn):
                copy.wait()

    slot = step % 2
    return [buffer[slot].reshape(-1, buffer.shape[-1]) for buffer in buffers]


def unit_plan(units, chunk, rows, chunks):
    width = units[0][0].shape[-1] if rows else units[0].shape[-1]
    if not rows:
        unit = pl.BlockSpec((chunk, width), lambda step: (step, 0))
        return list(units), [unit, unit], []
    anywhere = pl.BlockSpec(memory_space=pl.ANY)
    operands = list(units[0]) + list(units[1])
    buffer = pltpu.VMEM((2, chunk // rows, rows, width), jnp.bfloat16)
    sems = pltpu.SemaphoreType.DMA((2, len(operands) // chunks))
    return operands, [anywhere] * len(operands), [buffer, buffer, sems]


def take_units(refs, scratch, rows, chunks):
    if not rows:
        return [ref[...] for ref in refs]
    half = len(refs) // 2
    return load_units(refs[:half], refs[half:], rows, scratch[:2], scratch[2], chunks)


def ffn_kernel(rows, chunks, count, rows_ref, bias_ref, *refs):
    hidden_ref, slope_ref, part_ref = refs[count : count + 3]
    units_in, units_out = take_units(refs[:count], refs[count + 3 :], rows, chunks)

    @pl.when(pl.program_id(0) == 0)
    def _():
        part_ref[...] = jnp.zeros_like(part_ref)

    step = PAGE_SLOTS // 2
    for number in range(2):
        span = pl.ds(number * step, step)
        pre_act = contract_cols(rows_ref[span, :], units_in) + bias_ref[...]
        hidden, slope = gelu_pair(pre_act)
        hidden = hidden.astype(jnp.bfloat16)
        hidden_ref[span, :] = hidden
        slope_ref[span, :] = slope.astype(jnp.bfloat16)
        part_ref[span, :] += jnp.dot(hidden, units_out, preferred_element_type=jnp.float32)


def ffn_front(rows_in, units, bias_in, chunks, rows):
    slots, width = rows_in.shape
    total = bias_in.shape[0]
    chunk = total // chunks
    whole = pl.BlockSpec((slots, width), lambda step: (0, 0))
    piece = pl.BlockSpec((slots, chunk), lambda step: (0, step))
    operands, specs, scratch = unit_plan(units, chunk, rows, chunks)
    return pl.pallas_call(
        functools.partial(ffn_kernel, rows, chunks, len(operands)),
        grid=(chunks,),
        in_specs=[whole, pl.BlockSpec((1, chunk), lambda step: (0, step))] + specs,
        out_specs=[piece, piece, whole],
        out_shape=[
            jax.ShapeDtypeStruct((slots, total), jnp.bfloat16),
            jax.ShapeDtypeStruct((slots, total), jnp.bfloat16),
            jax.ShapeDtypeStruct((slots, width), jnp.float32),
        ],
        scratch_shapes=scratch,
        cost_estimate=pl.CostEstimate(
            flops=slots * width * total,
            bytes_accessed=total * (width + slots),
            transcendentals=0,
        ),
        compiler_params=pltpu.CompilerParams(vmem_limit_bytes=40 * 1024 * 1024),
    )(rows_in, bias_in[None], *operands)


def tail_route(flip):
    far, near, high, core = routes()
    return (high + [near] if flip else [near] + high) + [core]


def key_mask(key, axis):
    return sum(1 << bit for name, bit in key if name == axis)


class Spread:
    def __init__(self, block, joined, apart):
        self.joined, self.apart = list(joined), list(apart)
        self.masks = [frozenset()]
        self.held, self.came = block[None], None
        self.pieces = None

    def join(self, wait):
        if self.came is None:
            self.held = self.held if wait is None else tie(self.held, wait)
        else:
            came = self.came if wait is None else tie(self.came, wait)
            self.held = jnp.concatenate([self.held, came], 0)
        return self.held

    def advance(self, wait=None):
        if self.joined:
            step = self.joined.pop(0)
            held = self.join(wait)
            self.sent = [held]
            self.came = hop(held, *step)
            self.masks = self.masks + [mask | {step} for mask in self.masks]
            return self.came
        step = self.apart.pop(0)
        if self.pieces is None:
            self.pieces = {frozenset(): self.join(wait)}
            wait = None
        self.sent = []
        for key, piece in list(self.pieces.items()):
            piece = piece if wait is None else tie(piece, wait)
            self.sent.append(piece)
            came = hop(piece, *step)
            self.pieces[key] = piece
            self.pieces[key | {step}] = came
        return came


def half_spread(own, near_first=False):
    far, near, high, core = routes()
    return Spread(own, [near] + far if near_first else far + [near], [core])


def half_parts(chain):
    core = routes()[3]
    spot = lax.axis_index("dp")
    masks = [key_mask(mask, "dp") for mask in chain.masks]
    slot_of = {mask: number for number, mask in enumerate(masks)}
    table = jnp.array([slot_of[number] for number in range(len(masks))], jnp.int32)
    numbers = jnp.arange(len(masks))
    marks = (spot ^ numbers)[:, None] == numbers[None, :]
    places = jnp.sum(jnp.where(marks, table[None, :], 0), 1, dtype=jnp.int32)
    places = jnp.concatenate([places, own_bit(*core).astype(jnp.int32)[None]])
    return chain.pieces[frozenset()], chain.pieces[frozenset([core])], places


def unit_spread(block, flip):
    return Spread(block, routes()[0], tail_route(flip))


def unit_keys():
    far, near, high, core = routes()
    keys = [frozenset()]
    for step in [near] + list(reversed(high)) + [core]:
        keys = keys + [key | {step} for key in keys]
    return keys


def unit_result(chain):
    return [chain.pieces[key] for key in unit_keys()]


def unit_blocks():
    far = [frozenset()]
    for step in routes()[0]:
        far = far + [mask | {step} for mask in far]
    masks = [key | mask for key in unit_keys() for mask in far]
    spots = jnp.array([key_mask(mask, "dp") for mask in masks], jnp.int32)
    lanes = jnp.array([key_mask(mask, "mp") for mask in masks], jnp.int32)
    lanes, spots = lanes ^ lax.axis_index("mp"), spots ^ lax.axis_index("dp")
    return lanes * lax.axis_size("dp") + spots


class UnitSum:
    def __init__(self, kept, sent, flip):
        far, near, high, core = routes()
        self.order = high + [near]
        self.left = list(reversed(tail_route(flip)[:-1])) + list(reversed(far))
        shape = (2,) * len(self.order) + (lax.axis_size("dp") // 2,) + kept.shape[1:]
        self.sent = sent
        self.kept, self.came = kept.reshape(shape), hop(sent, *core).reshape(shape)

    def half(self, values, side, where):
        if where is not None:
            return lax.index_in_dim(values, side, where, keepdims=False)
        size = values.shape[0] // 2
        return values[side * size : (side + 1) * size]

    def advance(self):
        step = self.left.pop(0)
        where = self.order.index(step) if step in self.order else None
        if where is not None:
            self.order.remove(step)
        sent, kept = [
            add_low(self.half(self.kept, side, where), self.half(self.came, side, where))
            for side in (1, 0)
        ]
        self.sent = sent
        self.kept, self.came = kept, hop(sent, *step)
        return self.sent

    def finish(self):
        while self.left:
            self.advance()
        return (self.kept.astype(jnp.float32) + self.came.astype(jnp.float32))[0]


def to_rows(values):
    flat = values.reshape(values.shape[0], -1)
    flat = jnp.pad(flat, ((0, 0), (0, -flat.shape[1] % WIDTH)))
    return flat.reshape(values.shape[0], -1, WIDTH)


def from_rows(values, units):
    flat = values.reshape(values.shape[0], -1)[:, : units * 2 * LAYOUT_WIDTH]
    return flat.reshape(-1, 2 * LAYOUT_WIDTH)


class HalfSum:
    def __init__(self, sent, kept):
        far, near, high, core = routes()
        self.order = far + [near]
        self.left = [near] + list(reversed(far)) + high + [core]
        shape = (2,) * len(self.order) + sent.shape[1:]
        self.sent = sent
        self.kept, self.came = kept.reshape(shape), hop(sent, *core).reshape(shape)

    def advance(self):
        far, near, high, core = routes()
        step = self.left.pop(0)
        if step == core or step in high:
            self.kept = self.sent = add_low(self.kept, self.came)
            self.came = hop(self.kept, *step)
        else:
            where = self.order.index(step)
            self.order.remove(step)
            mine = own_bit(*step)

            def side(values, number):
                return lax.dynamic_index_in_dim(values, number, where, keepdims=False)

            sent = add_low(side(self.kept, 1 - mine), side(self.came, 1 - mine))
            kept = add_low(side(self.kept, mine), side(self.came, mine))
            self.sent = sent
            self.kept, self.came = kept, hop(sent, *step)
        return self.sent

    def finish(self):
        while self.left:
            self.advance()
        first = own_bit(*routes()[3]) == 0
        own, other = self.kept, self.came
        return jnp.stack([jnp.where(first, own, other), jnp.where(first, other, own)]).astype(
            jnp.float32
        )


def own_half(values):
    half = values.shape[-1] // 2
    return jnp.where(own_bit("mp", 0) == 0, values[..., :half], values[..., half:])


def sum_everywhere(values):
    far, near, high, core = routes()
    for step in [core] + high + [near] + far:
        values = values + hop(values, *step)
    return values


def show_all(values):
    everywhere = ("dp", "mp")
    count = lax.axis_size("dp") * lax.axis_size("mp")
    return lax.all_to_all(
        jnp.broadcast_to(values[None], (count,) + values.shape), everywhere, 0, 0, tiled=True
    )


def trade(values):
    return lax.all_to_all(values, ("dp", "mp"), 0, 0, tiled=True)


def project_qkv(rows_low, mats, vectors, width):
    joined = jnp.dot(rows_low, mats[0], preferred_element_type=jnp.float32)
    query = (joined[:, :width] + vectors[0]).astype(jnp.bfloat16)
    keys = joined[:, width:].astype(jnp.bfloat16)
    values = jnp.dot(rows_low, mats[1][:, :width], preferred_element_type=jnp.float32)
    return (query, keys, (values + vectors[1]).astype(jnp.bfloat16))


def scale_pair():
    return (1.0 / math.sqrt(WIDTH // HEADS), 1.0 / math.sqrt(LAYOUT_WIDTH // HEADS))


def project_back(mats, grads, width):
    first = jnp.concatenate(grads[:2], 1)
    rows_grad = contract_cols(first, mats[0]) + contract_cols(grads[2], mats[1][:, :width])
    return (
        rows_grad,
        jnp.sum(grads[0], 0, dtype=jnp.float32),
        jnp.sum(grads[2], 0, dtype=jnp.float32),
    )


def ffn_back_kernel(
    rows_of, chunks, count, rows_ref, grad_ref, hidden_ref, slope_ref, extra_ref, *refs
):
    part_ref, bias_ref, *sums = refs[count : count + 6]
    units_in, units_out = take_units(refs[:count], refs[count + 6 :], rows_of, chunks)
    step, last = pl.program_id(0), chunks // 2
    rows, grad = rows_ref[...], grad_ref[...]
    grad_hidden = contract_cols(grad, units_out)
    grad_pre = grad_hidden * slope_ref[...].astype(jnp.float32)
    grad_low = grad_pre.astype(jnp.bfloat16)
    bias_ref[...] = jnp.sum(grad_low.astype(jnp.float32), 0, keepdims=True)

    @pl.when(step == 0)
    def _():
        part_ref[...] = jnp.zeros_like(part_ref)

    part_ref[...] += jnp.dot(grad_low, units_in, preferred_element_type=jnp.float32)
    results = [contract_rows(grad_low, rows), contract_rows(hidden_ref[...], grad)]

    def store(targets):
        for target, result in zip(targets, results):
            if len(target.shape) == 2:
                target[...] = result.astype(target.dtype)
            else:
                blocks = result.astype(target.dtype).reshape(target.shape[0], -1, rows.shape[1])
                target[:, : blocks.shape[1], :] = blocks
                if target.shape[1] > blocks.shape[1]:
                    target[:, blocks.shape[1] :, :] = extra_ref[...]

    @pl.when(step < last)
    def _():
        store(sums[:2])

    @pl.when(step >= last)
    def _():
        store(sums[2:])


def ffn_back(rows_in, units, slope, hidden, grad_rows, chunks, slot_rows, extra):
    slots, width = rows_in.shape
    total = hidden.shape[1]
    chunk, half = total // chunks, chunks // 2
    whole = pl.BlockSpec((slots, width), lambda step: (0, 0))
    piece = pl.BlockSpec((slots, chunk), lambda step: (0, step))
    operands, specs, scratch = unit_plan(
        units, chunk, slot_rows[0] if slot_rows else None, chunks
    )

    def first(step):
        return jnp.minimum(step, half - 1)

    def second(step):
        return jnp.maximum(step - half, 0)

    turns = (first, first, second, second)
    if slot_rows is None:
        shapes = [(total // 2, width)] * 4
        sum_specs = [
            pl.BlockSpec((chunk, width), lambda step, turn=turn: (turn(step), 0)) for turn in turns
        ]
        extra_spec = pl.BlockSpec(memory_space=pltpu.VMEM)
    else:
        rows, padded = slot_rows
        heights = [padded, rows] * 2
        shapes = [(total // (2 * rows), height, width) for height in heights]
        sum_specs = [
            pl.BlockSpec((chunk // rows, height, width), lambda step, turn=turn: (turn(step), 0, 0))
            for height, turn in zip(heights, turns)
        ]
        extra_spec = pl.BlockSpec((chunk // rows, padded - rows, width), lambda step: (step, 0, 0))
    return pl.pallas_call(
        functools.partial(
            ffn_back_kernel, slot_rows[0] if slot_rows else None, chunks, len(operands)
        ),
        grid=(chunks,),
        in_specs=[whole, whole, piece, piece, extra_spec] + specs,
        out_specs=[whole, pl.BlockSpec((1, chunk), lambda step: (0, step))] + sum_specs,
        out_shape=[
            jax.ShapeDtypeStruct((slots, width), jnp.float32),
            jax.ShapeDtypeStruct((1, total), jnp.float32),
        ]
        + [jax.ShapeDtypeStruct(shape, jnp.bfloat16) for shape in shapes],
        scratch_shapes=scratch,
        cost_estimate=pl.CostEstimate(
            flops=2 * slots * width * total,
            bytes_accessed=2 * total * (width + slots),
            transcendentals=0,
        ),
        compiler_params=pltpu.CompilerParams(vmem_limit_bytes=48 * 1024 * 1024),
    )(rows_in, grad_rows, hidden, slope, extra, *operands)


def stream_forward(rows, att, mats, units, bias_in, vec, unit_rows, hook):
    width = rows.shape[1]
    first = (
        rows + jnp.dot(att, mats[1][:, width:], preferred_element_type=jnp.float32) + vec[2]
    )
    mid = norm_apply(first, vec[3], vec[4])
    mid_low = hook(mid.astype(jnp.bfloat16))
    chunks = 4 if width == WIDTH else 1
    hidden, slope, part = ffn_front(mid_low, units, bias_in, chunks, unit_rows)
    last = mid + part + vec[5]
    return (norm_apply(last, vec[6], vec[7]), (first, mid_low, slope, hidden, last))


def layer_forward(text, layout, weights, lengths, hooks):
    (tm, lm, tb, lb, tv, lv) = weights
    text_low = hooks["low"](text.astype(jnp.bfloat16))
    layout_low = layout.astype(jnp.bfloat16)
    text_qkv = list(project_qkv(text_low, tm, tv, WIDTH))
    layout_qkv = project_qkv(layout_low, lm, lv, LAYOUT_WIDTH)
    text_qkv[0] = hooks["query"](text_qkv[0])
    text_att, layout_att, log_total = attend(text_qkv, layout_qkv, lengths)
    text_att = hooks["att"](text_att)
    tu, lu = hooks["units"]()
    count = lax.axis_size("dp") * lax.axis_size("mp")
    text_new, text_kept = stream_forward(
        text, text_att, tm, tu, tb, tv, FFN_UNITS // count, hooks["mid"]
    )
    layout_new, layout_kept = stream_forward(
        layout, layout_att, lm, lu, lb, lv, None, lambda value: value
    )
    cache = (
        text_low,
        layout_low,
        text_qkv,
        layout_qkv,
        log_total,
        text_att,
        layout_att,
        text_kept,
        layout_kept,
    )
    return (text_new, layout_new, cache, (tu, lu))


def stream_back(kept, att, mats, units, vec, grad, slot_rows, hook, extra):
    first, mid_low, slope, hidden, last = kept
    width = first.shape[1]
    last_g, gain2, bias2 = norm_back(last, vec[6], vec[7], grad)
    in_grad, bias_in_g, *unit_grads = ffn_back(
        mid_low,
        units,
        slope,
        hidden,
        hook(last_g.astype(jnp.bfloat16)),
        4 if width == WIDTH else 2,
        slot_rows,
        extra,
    )
    first_g, gain1, bias1 = norm_back(first, vec[3], vec[4], last_g + in_grad)
    first_low = first_g.astype(jnp.bfloat16)
    att_grad = contract_cols(first_low, mats[1][:, width:]).astype(jnp.bfloat16)
    vec_tail = [jnp.sum(first_g, 0), gain1, bias1, jnp.sum(last_g, 0), gain2, bias2]
    return (first_g, att_grad, first_low, unit_grads, bias_in_g[0], vec_tail)


def layer_backward(cache, grad_text, grad_layout, weights, lengths, plan):
    (
        text_low,
        layout_low,
        text_qkv,
        layout_qkv,
        log_total,
        text_att,
        layout_att,
        text_kept,
        layout_kept,
    ) = cache
    (tm, lm, tu, lu, tb, lb, tv, lv) = weights
    count = lax.axis_size("dp") * lax.axis_size("mp")
    rows = FFN_UNITS // count
    none = jnp.zeros((8, 128), jnp.float32)
    first_l, att_l, out_l, lu_g, lb_g, tail_l = stream_back(
        layout_kept, layout_att, lm, lu, lv, grad_layout, None, lambda value: value, none
    )
    halves = [jnp.concatenate(lu_g[2 * side : 2 * side + 2], 1) for side in range(2)]
    extra = to_rows(jnp.concatenate(halves, 0).reshape(count, -1, 2 * LAYOUT_WIDTH))
    extra = jnp.pad(extra, ((0, 0), (0, -extra.shape[1] % 16), (0, 0)))
    slot_rows = (rows, rows + extra.shape[1])
    first_t, att_t, out_t, tu_g, tb_g, tail_t = stream_back(
        text_kept, text_att, tm, tu, tv, grad_text, slot_rows, plan.before_units, extra
    )
    att_t = plan.after_units(att_t, tu_g)
    text_dqkv, layout_dqkv = attend_back(
        text_qkv, layout_qkv, lengths, log_total, att_t, att_l
    )
    text_dqkv[0] = plan.after_attend(text_dqkv[0])
    plan.after_mats(
        (text_low, *text_dqkv, text_att, out_t), (layout_low, *layout_dqkv, layout_att, out_l)
    )
    rows_t, q_bias_t, v_bias_t = project_back(tm, text_dqkv, WIDTH)
    rows_l, q_bias_l, v_bias_l = project_back(lm, layout_dqkv, LAYOUT_WIDTH)
    grads = (
        tb_g,
        lb_g,
        jnp.stack([q_bias_t, v_bias_t] + tail_t),
        jnp.stack([q_bias_l, v_bias_l] + tail_l),
    )
    return (first_t + rows_t, first_l + rows_l, grads)


class Plan:
    def __init__(self):
        self.units = []
        self.mats = []

    def step(self, value, items):
        for item in items:
            item.came = tie(item.came, value)
        return tie(value, *[item.advance() for item in items])

    def before_units(self, value):
        return self.step(value, self.mats[:1]) if self.mats else value

    def after_units(self, value, grads):
        keep_in, keep_out, send_in, send_out = grads
        self.units.append([UnitSum(keep_in, send_in, False), UnitSum(keep_out, send_out, True)])
        if self.mats:
            return self.step(value, self.units[0] + self.mats[:1])
        return self.step(value, self.units[0])

    def after_attend(self, value):
        if self.mats:
            return self.step(value, self.units[1])
        return value

    def after_mats(self, text, layout):
        dp = lax.axis_size("dp")
        low = jnp.bfloat16
        side = own_bit("mp", 0).astype(jnp.int32)
        rows, query, keys, values, att, first = layout
        first_half = contract_rows(rows, jnp.concatenate([query, keys], 1)).astype(low)
        second_half = jnp.concatenate(
            [contract_rows(rows, values), contract_rows(att, first)], 1
        ).astype(low)
        text_rows = WIDTH // dp
        extras = [
            jnp.where(side == number, second_half, first_half).reshape(dp, -1, 2 * WIDTH)
            for number in range(2)
        ]
        padded = -(-(text_rows + extras[0].shape[1]) // 8) * 8
        pad = ((0, 0), (0, padded - text_rows - extras[0].shape[1]), (0, 0))
        sums = mats_sums(side[None], text, padded)
        sent, kept = [
            lax.dynamic_update_slice(item, jnp.pad(extra, pad), (0, text_rows, 0))
            for item, extra in zip(sums, extras)
        ]
        self.mats.append(HalfSum(sent, kept))

    def between(self, value):
        if len(self.mats) == 1:
            return self.step(tie(value, self.mats[0].sent), self.units[0])
        return self.step(tie(value, self.mats[1].sent), self.units[0] + self.mats[:1])


def split_high(values):
    high = values.astype(jnp.bfloat16)
    return (high, (values - high.astype(jnp.float32)).astype(jnp.bfloat16))


def add_rows(marks, values):
    high, low = split_high(values)
    return contract_rows(marks, high) + contract_rows(marks, low)


def apply_update(master, grad, moment, average, loss_count, factor):
    clipped = grad / loss_count * factor
    moment_new = MOMENTUM * moment + clipped
    master_new = master - LEARN_RATE * (clipped + MOMENTUM * moment_new)
    return (master_new, moment_new, AVERAGE_DECAY * average + (1.0 - AVERAGE_DECAY) * master_new)


def on_device(
    token_ids,
    mlm_targets,
    page_lengths,
    box_coords,
    mlm_positions,
    align_pairs,
    align_labels,
    table,
    text_mats,
    layout_mats,
    text_ffn,
    layout_ffn,
    small_params,
    table_momentum,
    text_mats_momentum,
    layout_mats_momentum,
    text_ffn_momentum,
    layout_ffn_momentum,
    small_momentum,
    table_average,
    text_mats_average,
    layout_mats_average,
    text_ffn_average,
    layout_ffn_average,
    small_average,
):
    lane, spot = lax.axis_index("mp"), lax.axis_index("dp")
    dp, mp = lax.axis_size("dp"), lax.axis_size("mp")
    count = dp * mp
    slots = PAGE_SLOTS
    mask_slots = mlm_positions.shape[1]
    pages = 1
    vocab_rows = table.shape[0]
    low = jnp.bfloat16

    own_ids = lax.dynamic_index_in_dim(token_ids, lane, 0, keepdims=False)
    own_targets = lax.dynamic_index_in_dim(mlm_targets, lane, 0, keepdims=False)
    table_low = table.astype(low)
    own_block = lane * dp + spot
    steps = jnp.arange(slots)
    first_at = jnp.min(
        jnp.where(own_ids[:, None] == own_ids[None, :], steps[None, :], slots), 1
    )
    page_first = first_at == steps
    block_own = own_ids // vocab_rows
    rank = jnp.sum(
        page_first[None, :]
        & (block_own[:, None] == block_own[None, :])
        & (steps[None, :] < first_at[:, None]),
        1,
        dtype=jnp.int32,
    )
    source = (block_own % dp) * mp + block_own // dp
    local_own = own_ids - block_own * vocab_rows
    places = jnp.arange(count * ROUND_ROWS)

    def place_of(turn):
        turn_rank = rank - turn * ROUND_ROWS
        inside = (turn_rank >= 0) & (turn_rank < ROUND_ROWS)
        return jnp.where(inside, source * ROUND_ROWS + turn_rank, -1)

    def requests(turn):
        asked = (place_of(turn)[None, :] == places[:, None]) & page_first[None, :]
        rows = jnp.sum(jnp.where(asked, local_own[None, :] + 1, 0), 1, dtype=jnp.int32) - 1
        return rows.reshape(count, ROUND_ROWS)

    def settle(chains, left):
        for chain in chains:
            while len(chain.joined) + len(chain.apart) > left:
                chain.advance()

    def marks_of(rows):
        return (rows.reshape(-1)[:, None] == jnp.arange(vocab_rows)[None, :]).astype(low)


    def held_marks(turn):
        return (place_of(turn)[:, None] == places[None, :]).astype(low)

    def fetch(turn, marks, so_far):
        sent = jnp.dot(marks, table_low, preferred_element_type=jnp.float32).astype(low)
        came = trade(sent)
        return (
            so_far + jnp.dot(held_marks(turn), came, preferred_element_type=jnp.float32),
            came,
            sent,
        )

    share = small_params.shape[0]
    line = 2 * WIDTH
    half_rows = small_half_rows(share)
    small_pad = jnp.pad(small_params.astype(low), (0, 2 * half_rows * 128 - share))
    small_half = lax.dynamic_slice_in_dim(
        small_pad.reshape(2 * half_rows, 128), (lane & 1) * half_rows, half_rows
    )
    tmats_half = own_half(text_mats.astype(low))
    lmats_half = own_half(layout_mats.astype(low)).reshape(-1, 128)
    extra = jnp.concatenate(
        [small_half, lmats_half, jnp.zeros((-lmats_half.shape[0] % 16, 128), low)], 0
    )
    unit_rows = text_ffn.shape[1]
    layout_units = layout_ffn.shape[1]
    layout_unit_rows = -(-(2 * layout_units * LAYOUT_WIDTH) // WIDTH)
    unit_pad = -layout_unit_rows % 16

    def unit_block(layer_no, part):
        text_part = text_ffn[layer_no, :, part * WIDTH : (part + 1) * WIDTH].astype(low)
        if part:
            return text_part
        return jnp.concatenate(
            [
                text_part,
                to_rows(layout_ffn[layer_no : layer_no + 1].astype(low))[0],
                jnp.zeros((unit_pad, WIDTH), low),
            ],
            0,
        )

    mats_chains = [half_spread(tmats_half[layer_no]) for layer_no in range(LAYERS)]
    extra_chain = half_spread(extra, True)
    unit_chains = [
        [unit_spread(unit_block(layer_no, part), part == 1) for part in range(2)]
        for layer_no in range(LAYERS)
    ]
    far_steps = len(routes()[0])
    told = jnp.concatenate(
        [
            jnp.max(rank, keepdims=True) // ROUND_ROWS + 1,
            page_lengths,
            own_targets,
        ]
    )
    told = jnp.broadcast_to(told[None], (count, mask_slots + 2))
    spare = jnp.zeros((count, -(ROUND_ROWS + mask_slots + 2) % 128), jnp.int32)
    message = jnp.concatenate([requests(0), told, spare], 1)
    mats_chains[0].advance()
    extra_chain.advance()
    extra_chain.advance()
    shown = trade(tie(message, *extra_chain.sent))
    mats_chains[0].advance()
    extra_chain.advance()
    shown = tie(shown, *mats_chains[0].sent, *extra_chain.sent)
    rounds = jnp.max(shown[:, ROUND_ROWS])
    all_lengths = shown[:, ROUND_ROWS + 1]
    all_targets = shown[:, ROUND_ROWS + 2 : ROUND_ROWS + 2 + mask_slots].reshape(-1)

    asked_first = marks_of(shown[:, :ROUND_ROWS])
    embedded, came_first, rows_first = fetch(
        0, asked_first, jnp.zeros((slots, WIDTH), jnp.float32)
    )
    embedded = lax.fori_loop(
        1,
        rounds,
        lambda turn, so_far: fetch(turn, marks_of(trade(requests(turn))), so_far)[0],
        embedded,
    )
    settle(mats_chains[:1], 2)
    mats_chains[0].advance(rows_first)
    settle([extra_chain], 1)
    extra_chain.advance(mats_chains[0].sent[0])
    wait = extra_chain.sent[0]
    for chain in unit_chains[0]:
        chain.advance(wait)
    core_key = frozenset([routes()[3]])
    extra_chain.pieces[core_key] = tie(
        extra_chain.pieces[core_key], *[chain.sent[0] for chain in unit_chains[0]]
    )
    small_parts, lmats_all = unpack_small(*half_parts(extra_chain), lmats_half.shape[0])
    lmats_all = lmats_all.reshape(2, dp, LAYERS, -1, 2 * LAYOUT_WIDTH)
    mats_chains[0].advance(tie(came_first, small_parts[6]))
    for number in range(1, far_steps):
        for chain in unit_chains[0]:
            chain.advance(mats_chains[0].sent[0])
    tmats_first = put_in_order(*half_parts(mats_chains[0]))
    (
        text_vec,
        layout_vec,
        text_bias,
        layout_bias,
        text_emb,
        layout_emb,
        text_pos,
        layout_pos,
        box_table,
        align_mat,
    ) = small_parts

    coords = box_coords[:, 0].T
    text_pre, layout_pre, text, layout = embed_streams(
        coords, embedded, text_pos, layout_pos, box_table, text_emb, layout_emb
    )
    caches = []
    layer_weights = []

    def push(value, chains):
        waits = []
        for chain in chains:
            chain.advance(value)
            waits = waits + chain.sent
        return tie(value, *waits)

    def after(chains, wait):
        for chain in chains:
            chain.advance(wait)

    def hooks_of(layer_no):
        units = unit_chains[layer_no]
        later = layer_no + 1 < LAYERS
        if later:
            next_mats, next_units = mats_chains[layer_no + 1], unit_chains[layer_no + 1]

        def at_low(value):
            if layer_no == 0:
                value = push(value, units)
            if later:
                next_mats.advance(units[1].sent[0])
            return value

        def at_query(value):
            return push(value, units) if layer_no else value

        def at_att(value):
            settle(units, 2)
            pending = [chain for chain in units if len(chain.joined) + len(chain.apart) > 1]
            if pending or later:
                value = push(value, pending + ([next_mats] if later else []))
            after(units, value)
            if later:
                after(next_units, next_mats.sent[0])
            return value

        def at_mid(value):
            return push(value, [next_mats] + next_units) if later else value

        return {
            "low": at_low,
            "query": at_query,
            "att": at_att,
            "mid": at_mid,
            "units": lambda: units_of(layer_no),
        }

    def units_of(layer_no):
        results = [unit_result(chain) for chain in unit_chains[layer_no]]
        layout_both = from_rows(
            take_extra(results[0], unit_rows)[:, :layout_unit_rows], layout_units
        )
        return (results, [layout_both[:, :LAYOUT_WIDTH], layout_both[:, LAYOUT_WIDTH:]])

    slot_marks = (unit_blocks()[:, None] == jnp.arange(count)[None, :]).astype(jnp.float32)
    for layer_no in range(LAYERS):
        if layer_no:
            settle([mats_chains[layer_no]], 1)
            text = push(text, unit_chains[layer_no] + [mats_chains[layer_no]])
            tmats = put_in_order(*half_parts(mats_chains[layer_no]))
        else:
            tmats = tmats_first
        weights = [
            tmats,
            lmats_all[:, :, layer_no].reshape(2, LAYOUT_WIDTH, -1),
            jnp.dot(
                slot_marks, text_bias[layer_no].reshape(count, -1), precision=PRECISE
            ).reshape(-1),
            jnp.dot(
                slot_marks, layout_bias[layer_no].reshape(count, -1), precision=PRECISE
            ).reshape(-1),
            text_vec[layer_no],
            layout_vec[layer_no],
        ]
        text, layout, cache, units = layer_forward(
            text, layout, weights, page_lengths, hooks_of(layer_no)
        )
        weights = weights[:2] + list(units) + weights[2:]
        caches.append(cache)
        layer_weights.append(weights)

    row_index = mlm_positions.reshape(-1)
    live_all = (
        (jnp.arange(mask_slots)[None, :] * slots < mask_slots * all_lengths[:, None])
        .astype(jnp.float32)
        .reshape(-1)
    )
    chosen_marks = (row_index[:, None] == steps[None, :]).astype(low)
    chosen_own = jnp.dot(
        chosen_marks, text.astype(low), preferred_element_type=jnp.float32
    ).astype(low)
    chosen_all = show_all(chosen_own).reshape(count * mask_slots, WIDTH)
    logits = contract_cols(chosen_all, table_low)
    target_local = all_targets - own_block * vocab_rows
    target_in = target_local[:, None] == jnp.arange(vocab_rows)[None, :]
    target_logit = jnp.sum(jnp.where(target_in, logits, 0.0), 1)
    row_peak = jnp.max(logits, axis=1)
    row_total = jnp.sum(jnp.exp(logits - row_peak[:, None]), axis=1)
    stats = show_all(jnp.stack([row_peak, row_total, target_logit]))
    all_peak = jnp.max(stats[:, 0], 0)
    all_total = jnp.sum(stats[:, 1] * jnp.exp(stats[:, 0] - all_peak[None]), 0)
    all_target = jnp.sum(stats[:, 2], 0)
    log_total = all_peak + jnp.log(all_total)
    own_start = (spot * mp + lane) * mask_slots
    live_own = lax.dynamic_slice_in_dim(live_all, own_start, mask_slots)
    own_loss = jnp.sum(
        lax.dynamic_slice_in_dim((log_total - all_target) * live_all, own_start, mask_slots)
    )
    grad_low = (
        (jnp.exp(logits - log_total[:, None]) - target_in.astype(jnp.float32)) * live_all[:, None]
    ).astype(low)
    table_grad = contract_rows(grad_low, chosen_all)
    chosen_parts = trade(jnp.dot(grad_low, table_low, preferred_element_type=jnp.float32).astype(low))
    chosen_grad = jnp.sum(
        chosen_parts.reshape(count, mask_slots, WIDTH).astype(jnp.float32), 0
    )

    first_marks = (align_pairs[0, :, 0][:, None] == steps[None, :]).astype(jnp.float32)
    second_marks = (align_pairs[0, :, 1][:, None] == steps[None, :]).astype(jnp.float32)
    answer = align_labels.reshape(-1).astype(jnp.float32)
    first_rows = jnp.dot(first_marks, text, precision=PRECISE)
    second_rows = jnp.dot(second_marks, layout, precision=PRECISE)

    def pair_loss(text_rows, layout_rows, align_weight):
        right = jnp.dot(layout_rows, align_weight, precision=PRECISE)
        logit = jnp.sum(text_rows * right, axis=-1) / math.sqrt(WIDTH)
        return jnp.sum(jax.nn.softplus(logit) - answer * logit)

    align_part, align_pull = jax.vjp(pair_loss, first_rows, second_rows, align_mat)
    first_back, second_back, align_grad = align_pull(jnp.ones((), jnp.float32))
    grad_text = add_rows(
        jnp.concatenate([first_marks.astype(low), chosen_marks], 0),
        jnp.concatenate([first_back, chosen_grad], 0),
    )
    grad_layout = add_rows(second_marks.astype(low), second_back)

    plan = Plan()
    layer_grads = [None] * LAYERS
    for layer_no in reversed(range(LAYERS)):
        grad_text, grad_layout, layer_grads[layer_no] = layer_backward(
            caches[layer_no], grad_text, grad_layout, layer_weights[layer_no], page_lengths, plan
        )
        grad_text = plan.between(grad_text)

    embed_grad, looked_grad, text_emb_grad, layout_emb_grad, box_grad = embed_back(
        coords, text_pre, layout_pre, text_emb, layout_emb, grad_text, grad_layout
    )
    embed_low = embed_grad.astype(low)

    def give(turn, marks, so_far):
        sent = contract_rows(held_marks(turn), embed_low).astype(low)
        came = trade(sent)
        return (so_far + contract_rows(marks, came), sent, came)

    table_sum, gave_rows, gave_came = give(0, asked_first, table_grad)
    table_sum = lax.fori_loop(
        1,
        rounds,
        lambda turn, so_far: give(turn, marks_of(trade(requests(turn))), so_far)[0],
        table_sum,
    )

    def stacked(member):
        return jnp.stack([layer_grads[layer_no][member] for layer_no in range(LAYERS)])

    def in_order(member):
        return jnp.stack(
            [
                lax.dot_general(
                    slot_marks,
                    layer_grads[layer_no][member].reshape(count, -1),
                    (((0,), (0,)), ((), ())),
                    precision=PRECISE,
                )
                for layer_no in range(LAYERS)
            ]
        )

    small_items = [
        stacked(2),
        stacked(3),
        in_order(0),
        in_order(1),
        text_emb_grad,
        layout_emb_grad,
        embed_grad,
        looked_grad,
        box_grad,
        align_grad,
    ]
    plan.mats[1].advance()
    token = plan.mats[1].sent
    small_items[6] = tie(embed_grad, token, gave_rows)
    small_blocks = pack_small(small_items, dp).reshape(dp, 2, half_rows, 128)
    first = own_bit("mp", 0) == 0
    small_total = HalfSum(
        jnp.where(first, small_blocks[:, 1], small_blocks[:, 0]),
        jnp.where(first, small_blocks[:, 0], small_blocks[:, 1]),
    )
    token = small_total.sent
    outer = plan.units[1]
    turns = outer + [plan.mats[1]] + outer + [small_total, plan.mats[1]] + outer
    turns = turns + [small_total, plan.mats[1]] * 5
    for number, chain in enumerate(turns):
        if chain.left:
            chain.came = tie(chain.came, token)
            chain.advance()
            token = chain.sent
        if number == 2:
            token = tie(gave_came, token)
    small_sum = small_total.finish().reshape(-1)[:share]
    plan.units.reverse()
    plan.mats.reverse()
    mats_sums = [item.finish() for item in plan.mats]
    mats_rows = text_mats.shape[1]
    extra_rows = layout_mats.shape[1] * LAYOUT_WIDTH * 2 // line
    tmats_sum = jnp.stack(
        [jnp.concatenate([item[0, :mats_rows], item[1, :mats_rows]], 1) for item in mats_sums]
    )
    lmats_sum = jnp.stack(
        [
            jnp.concatenate(
                [
                    item[side, mats_rows : mats_rows + extra_rows].reshape(-1, 2 * LAYOUT_WIDTH)
                    for side in range(2)
                ],
                1,
            )
            for item in mats_sums
        ]
    )
    unit_sums = [
        [item.finish() for item in plan.units[layer_no]] for layer_no in range(LAYERS)
    ]
    tffn_sum = jnp.stack(
        [jnp.concatenate([item[:unit_rows] for item in pair], 1) for pair in unit_sums]
    )
    lffn_sum = jnp.stack(
        [
            from_rows(pair[0][None, unit_rows : unit_rows + layout_unit_rows], layout_units)
            for pair in unit_sums
        ]
    )
    final_grads = (table_sum, tmats_sum, lmats_sum, tffn_sum, lffn_sum, small_sum)
    lane_first = (lane == 0).astype(jnp.float32)
    squares = (
        jnp.sum(table_sum * table_sum) + jnp.sum(tffn_sum * tffn_sum) + jnp.sum(lffn_sum * lffn_sum)
    )
    squares = squares + lane_first * (
        jnp.sum(tmats_sum * tmats_sum)
        + jnp.sum(lmats_sum * lmats_sum)
        + jnp.sum(small_sum * small_sum)
    )
    count_part = jnp.sum(live_own) + jnp.float32(pages * PAIRS)
    sums = sum_everywhere(
        jnp.broadcast_to(
            jnp.stack([squares, own_loss + align_part, count_part, squares])[:, None], (4, 128)
        )
    )
    total_squares, loss_sum, loss_count = sums[0, 0], sums[1, 0], sums[2, 0]
    grad_norm = jnp.sqrt(total_squares) / loss_count
    factor = jnp.minimum(1.0, CLIP_NORM / grad_norm)
    masters = (table, text_mats, layout_mats, text_ffn, layout_ffn, small_params)
    moments = (
        table_momentum,
        text_mats_momentum,
        layout_mats_momentum,
        text_ffn_momentum,
        layout_ffn_momentum,
        small_momentum,
    )
    averages = (
        table_average,
        text_mats_average,
        layout_mats_average,
        text_ffn_average,
        layout_ffn_average,
        small_average,
    )
    updated = [
        apply_update(
            masters[number],
            final_grads[number],
            moments[number],
            averages[number],
            loss_count,
            factor,
        )
        for number in range(6)
    ]
    new_masters = [item[0] for item in updated]
    new_moments = [item[1] for item in updated]
    new_averages = [item[2] for item in updated]
    copies = [item.astype(jnp.bfloat16) for item in new_masters[:5]]
    return (
        loss_sum,
        loss_count,
        grad_norm,
        new_masters[0],
        new_masters[1],
        new_masters[2],
        new_masters[3],
        new_masters[4],
        new_masters[5],
        copies[0],
        copies[1],
        copies[2],
        copies[3],
        copies[4],
        new_moments[0],
        new_moments[1],
        new_moments[2],
        new_moments[3],
        new_moments[4],
        new_moments[5],
        new_averages[0],
        new_averages[1],
        new_averages[2],
        new_averages[3],
        new_averages[4],
        new_averages[5],
    )


def solution(mesh):
    return jax.shard_map(
        on_device,
        mesh=mesh,
        in_specs=(
            P("dp", None),
            P("dp", None),
            P(("dp", "mp")),
            P(None, ("dp", "mp"), None),
            P(("dp", "mp"), None),
            P(("dp", "mp"), None, None),
            P(("dp", "mp"), None),
            P(("mp", "dp"), None),
            P(None, "dp", None),
            P(None, "dp", None),
            P(None, ("mp", "dp"), None),
            P(None, ("mp", "dp"), None),
            P("dp"),
            P(("mp", "dp"), None),
            P(None, "dp", None),
            P(None, "dp", None),
            P(None, ("mp", "dp"), None),
            P(None, ("mp", "dp"), None),
            P("dp"),
            P(("mp", "dp"), None),
            P(None, "dp", None),
            P(None, "dp", None),
            P(None, ("mp", "dp"), None),
            P(None, ("mp", "dp"), None),
            P("dp"),
        ),
        out_specs=(
            P(),
            P(),
            P(),
            P(("mp", "dp"), None),
            P(None, "dp", None),
            P(None, "dp", None),
            P(None, ("mp", "dp"), None),
            P(None, ("mp", "dp"), None),
            P("dp"),
            P(("mp", "dp"), None),
            P(None, "dp", None),
            P(None, "dp", None),
            P(None, ("mp", "dp"), None),
            P(None, ("mp", "dp"), None),
            P(("mp", "dp"), None),
            P(None, "dp", None),
            P(None, "dp", None),
            P(None, ("mp", "dp"), None),
            P(None, ("mp", "dp"), None),
            P("dp"),
            P(("mp", "dp"), None),
            P(None, "dp", None),
            P(None, "dp", None),
            P(None, ("mp", "dp"), None),
            P(None, ("mp", "dp"), None),
            P("dp"),
        ),
        check_vma=False,
    )
```

```python
import functools
import math

import jax
import jax.numpy as jnp
from jax import lax
from jax.experimental import pallas as pl
from jax.experimental.pallas import tpu as pltpu
from jax.sharding import PartitionSpec as P

WIDTH = 768
HEADS = 12
FFN_UNITS = 3072
LAYOUT_WIDTH = 192
LAYOUT_UNITS = 768
BOXES = 1024
PAGE_SLOTS = 512
PAIRS = 32
LAYERS = 2


EPSILON = 1e-05
CLIP_NORM = 0.01
LEARN_RATE = 10000.0
MOMENTUM = 0.5
AVERAGE_DECAY = 0.5
MASK_FILL = -1e30
PRECISE = lax.Precision.HIGHEST


def small_shapes():
    return [
        (LAYERS, 8, WIDTH),
        (LAYERS, 8, LAYOUT_WIDTH),
        (LAYERS, FFN_UNITS),
        (LAYERS, LAYOUT_UNITS),
        (2, WIDTH),
        (2, LAYOUT_WIDTH),
        (PAGE_SLOTS, WIDTH),
        (PAGE_SLOTS, LAYOUT_WIDTH),
        (2, BOXES // 8, 2 * LAYOUT_WIDTH),
        (LAYOUT_WIDTH, WIDTH),
    ]


def small_views():
    views = []
    offset = 0
    for piece_dims in small_shapes():
        amount = math.prod(piece_dims)
        width = piece_dims[-1] if piece_dims[-1] % 128 == 0 else 2 * piece_dims[-1]
        views.append((offset // 128, amount // width, width))
        offset = offset + amount
    return views, offset // 128


def small_half_rows(share):
    return -(-share // (128 * 32)) * 16


def pack_small(items, dp):
    views, total = small_views()
    share = total * 128 // dp
    rows = 2 * small_half_rows(share)

    def kernel(*refs):
        sources, out_ref, flat = refs[: len(items)], refs[len(items)], refs[len(items) + 1]
        flat[total:, :] = jnp.zeros((flat.shape[0] - total, 128), jnp.float32)
        for source, (start, count, width) in zip(sources, views):
            per = width // 128
            for part in range(per):
                flat[pl.ds(start + part, count, stride=per), :] = source[
                    :, part * 128 : (part + 1) * 128
                ]
        column = lax.broadcasted_iota(jnp.int32, (rows, 128), 1)
        for number in range(dp):
            start, shift = number * share // 128, number * share % 128
            block = flat[pl.ds(start, rows), :]
            if shift:
                after = flat[pl.ds(start + 1, rows), :]
                block = jnp.where(
                    column < 128 - shift,
                    pltpu.roll(block, 128 - shift, 1),
                    pltpu.roll(after, 128 - shift, 1),
                )
            out_ref[number] = block.astype(out_ref.dtype)

    whole = pl.BlockSpec(memory_space=pltpu.VMEM)
    return pl.pallas_call(
        kernel,
        out_shape=jax.ShapeDtypeStruct((dp, rows, 128), jnp.bfloat16),
        in_specs=[whole] * len(items),
        out_specs=whole,
        scratch_shapes=[pltpu.VMEM((total + rows + 8, 128), jnp.float32)],
        cost_estimate=pl.CostEstimate(flops=0, bytes_accessed=2000000, transcendentals=0),
        compiler_params=pltpu.CompilerParams(vmem_limit_bytes=32 * 1024 * 1024),
    )(*[item.reshape(count, width) for item, (start, count, width) in zip(items, views)])


def unpack_small(own, came, places, extra_rows):
    views, total = small_views()
    dp = own.shape[0]
    share = total * 128 // dp
    half = small_half_rows(share)

    def kernel(place_ref, own_ref, came_ref, *refs):
        targets, extra_ref, flat, turned = refs[:-3], refs[-3], refs[-2], refs[-1]
        mine = [(place_ref[dp] == side).astype(jnp.float32) for side in range(2)]
        for number in range(dp):
            start, shift = number * share // 128, number * share % 128
            rows = -(-(share + shift) // 128)
            slot = place_ref[number]
            for side in range(2):
                both = own_ref[slot].astype(jnp.float32), came_ref[slot].astype(jnp.float32)
                whole = jnp.where(mine[side] > 0.5, *both)
                extra_ref[side, number] = whole[half : half + extra_rows].astype(extra_ref.dtype)
                part = whole[:half]
                turned[pl.ds(8 + side * half, half), :] = (
                    pltpu.roll(part, shift, 1) if shift else part
                )
            block = turned[pl.ds(8, rows), :]
            if shift:
                turned[7:8, :] = flat[pl.ds(start, 1), :]
                column = lax.broadcasted_iota(jnp.int32, (rows, 128), 1)
                block = jnp.where(column >= shift, block, turned[pl.ds(7, rows), :])
            flat[pl.ds(start, rows), :] = block
        for target, (start, count, width) in zip(targets, views):
            per = width // 128
            for part in range(per):
                target[:, part * 128 : (part + 1) * 128] = flat[
                    pl.ds(start + part, count, stride=per), :
                ]

    whole = pl.BlockSpec(memory_space=pltpu.VMEM)
    *outs, extra = pl.pallas_call(
        kernel,
        out_shape=[
            jax.ShapeDtypeStruct((count, width), jnp.float32) for start, count, width in views
        ]
        + [jax.ShapeDtypeStruct((2, dp, extra_rows, 128), jnp.bfloat16)],
        in_specs=[pl.BlockSpec(memory_space=pltpu.SMEM), whole, whole],
        out_specs=[whole] * (len(views) + 1),
        scratch_shapes=[
            pltpu.VMEM((total + 8, 128), jnp.float32),
            pltpu.VMEM((2 * half + 16, 128), jnp.float32),
        ],
        cost_estimate=pl.CostEstimate(flops=0, bytes_accessed=2000000, transcendentals=0),
        compiler_params=pltpu.CompilerParams(vmem_limit_bytes=32 * 1024 * 1024),
    )(places, own, came)
    return [item.reshape(piece_dims) for item, piece_dims in zip(outs, small_shapes())], extra


def norm_apply(values, gain_row, bias_row):
    centre = values - jnp.mean(values, axis=-1, keepdims=True)
    spread = jnp.mean(centre * centre, axis=-1, keepdims=True)
    return centre * lax.rsqrt(spread + EPSILON) * gain_row + bias_row


def norm_back(values, gain_row, bias_row, grad_out):
    unused, pullback = jax.vjp(norm_apply, values, gain_row, bias_row)
    return pullback(grad_out)


def gelu_exact(values):
    return jax.nn.gelu(values, approximate=False)


def contract_rows(left, right):
    return lax.dot_general(
        left, right, (((0,), (0,)), ((), ())), preferred_element_type=jnp.float32
    )


def contract_cols(left, right):
    return lax.dot_general(
        left, right, (((1,), (1,)), ((), ())), preferred_element_type=jnp.float32
    )


def heads_view(values, pages):
    return values.reshape(pages, PAGE_SLOTS, HEADS, values.shape[-1] // HEADS)


ROUND_ROWS = 32


def bits_of(size):
    return list(reversed(range(size.bit_length() - 1)))


def hop(values, axis, bit):
    pairs = [(spot, spot ^ (1 << bit)) for spot in range(lax.axis_size(axis))]
    return lax.ppermute(values, axis, pairs)


def own_bit(axis, bit):
    return (lax.axis_index(axis) >> bit) & 1


def routes():
    far = [("dp", bit) for bit in bits_of(lax.axis_size("dp"))]
    high = [("mp", bit) for bit in bits_of(lax.axis_size("mp"))[:-1]]
    core = ("mp", 0)
    return (far[:-1], far[-1], high, core)


def add_low(kept, came):
    return (kept.astype(jnp.float32) + came.astype(jnp.float32)).astype(jnp.bfloat16)


def tie(value, *waits):
    def kernel(*refs):
        pass

    spec = pl.BlockSpec(memory_space=pl.ANY)
    return pl.pallas_call(
        kernel,
        out_shape=jax.ShapeDtypeStruct(value.shape, value.dtype),
        in_specs=[spec] * (1 + len(waits)),
        out_specs=spec,
        input_output_aliases={0: 0},
        cost_estimate=pl.CostEstimate(flops=0, bytes_accessed=0, transcendentals=0),
    )(value, *waits)


def put_in_order(own, came, places):
    slots, rows, width = own.shape

    def kernel(place_ref, own_ref, came_ref, out_ref, sems):
        side = place_ref[slots]

        def copies(half, source):
            return [
                pltpu.make_async_copy(
                    source.at[place_ref[spot]],
                    out_ref.at[half, pl.ds(spot * rows, rows)],
                    sems.at[half, spot],
                )
                for spot in range(slots)
            ]

        for half in range(2):
            for mine, source in ((True, own_ref), (False, came_ref)):

                @pl.when((side == half) == mine)
                def _(half=half, source=source):
                    for copy in copies(half, source):
                        copy.start()

        for half in range(2):
            for copy in copies(half, own_ref):
                copy.wait()

    anywhere = pl.BlockSpec(memory_space=pl.ANY)
    return pl.pallas_call(
        kernel,
        out_shape=jax.ShapeDtypeStruct((2, slots * rows, width), own.dtype),
        in_specs=[pl.BlockSpec(memory_space=pltpu.SMEM), anywhere, anywhere],
        out_specs=pl.BlockSpec(memory_space=pltpu.VMEM),
        scratch_shapes=[pltpu.SemaphoreType.DMA((2, slots))],
        cost_estimate=pl.CostEstimate(
            flops=0, bytes_accessed=2 * slots * rows * width, transcendentals=0
        ),
        compiler_params=pltpu.CompilerParams(vmem_limit_bytes=16 * 1024 * 1024),
    )(places, own, came)


def embed_kernel(
    coords, embedded, text_pos, layout_pos, tables, text_emb, layout_emb, *outs
):
    text_pre, layout_pre, text, layout = outs
    quarter = LAYOUT_WIDTH // 4
    low = jnp.bfloat16
    row = lax.broadcasted_iota(jnp.int32, (PAGE_SLOTS, BOXES // 8), 1)
    lanes = lax.broadcasted_iota(jnp.int32, (PAGE_SLOTS, 8 * quarter), 1) // quarter
    fold_in = lax.broadcasted_iota(jnp.int32, (8 * quarter, LAYOUT_WIDTH), 0) % quarter
    fold_out = lax.broadcasted_iota(jnp.int32, (8 * quarter, LAYOUT_WIDTH), 1)
    looked = jnp.zeros((PAGE_SLOTS, LAYOUT_WIDTH), jnp.float32)
    for number in range(4):
        spot = coords[:, number : number + 1]
        marks = (spot // 8 == row).astype(jnp.float32).astype(low)
        wide = jnp.dot(
            marks, tables[number % 2].astype(low), preferred_element_type=jnp.float32
        )
        kept = jnp.where(spot % 8 == lanes, wide, 0.0).astype(low)
        fold = (fold_in + number * quarter == fold_out).astype(jnp.float32).astype(low)
        looked = looked + jnp.dot(kept, fold, preferred_element_type=jnp.float32)
    layout_pre[...] = looked + layout_pos[...]
    text_pre[...] = embedded[...] + text_pos[...]
    text[...] = norm_apply(text_pre[...], text_emb[0:1, :], text_emb[1:2, :])
    layout[...] = norm_apply(layout_pre[...], layout_emb[0:1, :], layout_emb[1:2, :])


def norm_grads(values, gain, grad):
    centre = values - jnp.mean(values, axis=-1, keepdims=True)
    scale = lax.rsqrt(jnp.mean(centre * centre, axis=-1, keepdims=True) + EPSILON)
    unit = centre * scale
    lifted = grad * gain
    inner = jnp.mean(lifted * unit, axis=-1, keepdims=True)
    back = scale * (lifted - jnp.mean(lifted, axis=-1, keepdims=True) - unit * inner)
    sums = [jnp.sum(item, 0, keepdims=True) for item in (grad * unit, grad)]
    return back, jnp.concatenate(sums, 0)


def embed_back_kernel(coords, text_pre, layout_pre, text_emb, layout_emb, *refs):
    grad_text, grad_layout, text_back, layout_back, text_sums, layout_sums, boxes = refs
    low = jnp.bfloat16
    quarter = LAYOUT_WIDTH // 4
    text_back[...], text_sums[...] = norm_grads(text_pre[...], text_emb[0:1, :], grad_text[...])
    looked, layout_sums[...] = norm_grads(
        layout_pre[...], layout_emb[0:1, :], grad_layout[...]
    )
    layout_back[...] = looked
    high, rest = split_high(looked)
    row = lax.broadcasted_iota(jnp.int32, (PAGE_SLOTS, BOXES // 8), 1)
    lanes = lax.broadcasted_iota(jnp.int32, (PAGE_SLOTS, 8 * quarter), 1) // quarter
    fold_in = lax.broadcasted_iota(jnp.int32, (8 * quarter, LAYOUT_WIDTH), 0) % quarter
    fold_out = lax.broadcasted_iota(jnp.int32, (8 * quarter, LAYOUT_WIDTH), 1)
    boxes[...] = jnp.zeros_like(boxes)
    for number in range(4):
        spot = coords[:, number : number + 1]
        marks = (spot // 8 == row).astype(jnp.float32).astype(low)
        fold = (fold_in + number * quarter == fold_out).astype(jnp.float32).astype(low)
        wide = contract_cols(high, fold) + contract_cols(rest, fold)
        kept = jnp.where(spot % 8 == lanes, wide, 0.0)
        boxes[number % 2] += add_rows(marks, kept)


def embed_back(*operands):
    whole = pl.BlockSpec(memory_space=pltpu.VMEM)
    shapes = [
        (PAGE_SLOTS, WIDTH),
        (PAGE_SLOTS, LAYOUT_WIDTH),
        (2, WIDTH),
        (2, LAYOUT_WIDTH),
        (2, BOXES // 8, 2 * LAYOUT_WIDTH),
    ]
    return pl.pallas_call(
        embed_back_kernel,
        out_shape=[jax.ShapeDtypeStruct(shape, jnp.float32) for shape in shapes],
        in_specs=[whole] * len(operands),
        out_specs=[whole] * len(shapes),
        cost_estimate=pl.CostEstimate(flops=0, bytes_accessed=2000000, transcendentals=0),
        compiler_params=pltpu.CompilerParams(vmem_limit_bytes=32 * 1024 * 1024),
    )(*operands)


def embed_streams(*operands):
    whole = pl.BlockSpec(memory_space=pltpu.VMEM)
    return pl.pallas_call(
        embed_kernel,
        out_shape=[
            jax.ShapeDtypeStruct((PAGE_SLOTS, width), jnp.float32)
            for width in (WIDTH, LAYOUT_WIDTH) * 2
        ],
        in_specs=[whole] * len(operands),
        out_specs=[whole] * 4,
        cost_estimate=pl.CostEstimate(flops=0, bytes_accessed=2000000, transcendentals=0),
        compiler_params=pltpu.CompilerParams(vmem_limit_bytes=24 * 1024 * 1024),
    )(*operands)


def mats_kernel(side, rows, query, keys, values, att, first, sent_ref, kept_ref, result):
    step = pl.program_id(0)
    half = jnp.where(step < 2, 1 - side[0], side[0])
    cases = ((rows, query), (rows, keys), (rows, values), (att, first))
    for number, (left, right) in enumerate(cases):

        @pl.when(half * 2 + step % 2 == number)
        def _(left=left, right=right):
            result[...] = contract_rows(left[...], right[...])

    def store(target):
        blocks = result[...].astype(target.dtype).reshape(target.shape[0], -1, WIDTH)
        target[:, : blocks.shape[1], :] = blocks

    @pl.when(step < 2)
    def _():
        store(sent_ref)

    @pl.when(step >= 2)
    def _():
        store(kept_ref)


def mats_sums(side, operands, padded):
    dp = lax.axis_size("dp")
    whole = pl.BlockSpec((PAGE_SLOTS, WIDTH), lambda step: (0, 0))
    shape = jax.ShapeDtypeStruct((dp, padded, 2 * WIDTH), jnp.bfloat16)
    return pl.pallas_call(
        mats_kernel,
        grid=(4,),
        in_specs=[pl.BlockSpec(memory_space=pltpu.SMEM)] + [whole] * 6,
        out_specs=[
            pl.BlockSpec((dp, padded, WIDTH), lambda step: (0, 0, jnp.minimum(step, 1))),
            pl.BlockSpec((dp, padded, WIDTH), lambda step: (0, 0, jnp.maximum(step - 2, 0))),
        ],
        out_shape=[shape, shape],
        scratch_shapes=[pltpu.VMEM((WIDTH, WIDTH), jnp.float32)],
        cost_estimate=pl.CostEstimate(
            flops=2 * PAGE_SLOTS * WIDTH * WIDTH, bytes_accessed=4000000, transcendentals=0
        ),
        compiler_params=pltpu.CompilerParams(vmem_limit_bytes=32 * 1024 * 1024),
    )(side, *operands)


def take_extra(pieces, rows):
    slots, total, width = pieces[0].shape

    def kernel(*refs):
        out_ref, sems = refs[-2], refs[-1]
        copies = [
            pltpu.make_async_copy(
                ref.at[:, pl.ds(rows, total - rows)],
                out_ref.at[pl.ds(number * slots, slots)],
                sems.at[number],
            )
            for number, ref in enumerate(refs[:-2])
        ]
        for copy in copies:
            copy.start()
        for copy in copies:
            copy.wait()

    return pl.pallas_call(
        kernel,
        out_shape=jax.ShapeDtypeStruct((slots * len(pieces), total - rows, width), pieces[0].dtype),
        in_specs=[pl.BlockSpec(memory_space=pl.ANY)] * len(pieces),
        out_specs=pl.BlockSpec(memory_space=pltpu.VMEM),
        scratch_shapes=[pltpu.SemaphoreType.DMA((len(pieces),))],
        cost_estimate=pl.CostEstimate(flops=0, bytes_accessed=500000, transcendentals=0),
    )(*pieces)


HEAD_PAIRS = HEADS // 2
TEXT_HEAD = WIDTH // HEADS
LAYOUT_HEAD = LAYOUT_WIDTH // HEADS


def head_of(text_ref, layout_ref, head, scaled=False):
    text = text_ref[:, head * TEXT_HEAD : (head + 1) * TEXT_HEAD]
    layout = layout_ref[:, head * LAYOUT_HEAD : (head + 1) * LAYOUT_HEAD]
    if scaled:
        text_scale, layout_scale = scale_pair()
        text = (text.astype(jnp.float32) * text_scale).astype(text.dtype)
        layout = (layout.astype(jnp.float32) * layout_scale).astype(layout.dtype)
    return jnp.concatenate([text, layout], 1)


def store_heads(text_ref, layout_ref, both):
    text_ref[...] = jnp.concatenate([item[:, :TEXT_HEAD] for item in both], 1).astype(
        text_ref.dtype
    )
    layout = jnp.concatenate([item[:, TEXT_HEAD:] for item in both], 1).astype(layout_ref.dtype)
    width = layout.shape[1]
    for pair in range(HEAD_PAIRS):

        @pl.when(pl.program_id(0) == pair)
        def _(pair=pair):
            layout_ref[:, pair * width : (pair + 1) * width] = layout


def own_pair(sources, targets):
    width = targets[0].shape[1]
    for pair in range(HEAD_PAIRS):

        @pl.when(pl.program_id(0) == pair)
        def _(pair=pair):
            for source, target in zip(sources, targets):
                target[...] = source[:, pair * width : (pair + 1) * width]


def attend_kernel(length, qt, kt, vt, *refs):
    out_t, out_l, lse, ql, kl, vl = refs[3:]
    own_pair(refs[:3], (ql, kl, vl))
    live = lax.broadcasted_iota(jnp.int32, (PAGE_SLOTS, PAGE_SLOTS), 1) < length[0]
    outs = []
    for head in range(2):
        query, keys = head_of(qt, ql, head, True), head_of(kt, kl, head)
        scores = jnp.where(live, contract_cols(query, keys), MASK_FILL)
        peak = jnp.max(scores, 1, keepdims=True)
        expo = jnp.exp(scores - peak)
        total = jnp.sum(expo, 1, keepdims=True)
        probs = (expo * (1.0 / total)).astype(jnp.bfloat16)
        outs.append(
            jnp.dot(probs, head_of(vt, vl, head), preferred_element_type=jnp.float32)
        )
        lse[0, :, head : head + 1] = peak + jnp.log(total)
    store_heads(out_t, out_l, outs)


def attend_back_kernel(length, qt, kt, vt, got, *refs):
    lse, dqt, dkt, dvt, dql, dkl, dvl, ql, kl, vl, gol = refs[4:]
    own_pair(refs[:4], (ql, kl, vl, gol))
    text_scale, layout_scale = scale_pair()
    live = lax.broadcasted_iota(jnp.int32, (PAGE_SLOTS, PAGE_SLOTS), 0) < length[0]
    column = lax.broadcasted_iota(jnp.int32, (1, TEXT_HEAD + LAYOUT_HEAD), 1)
    scales = jnp.where(column < TEXT_HEAD, text_scale, layout_scale)
    grads_q, grads_k, grads_v = [], [], []
    for head in range(2):
        query, keys = head_of(qt, ql, head, True), head_of(kt, kl, head)
        values, grad = head_of(vt, vl, head), head_of(got, gol, head)
        scores = jnp.where(live, contract_cols(keys, query), MASK_FILL)
        probs = jnp.exp(scores - lse[0, head : head + 1, :])
        grad_probs = contract_cols(values, grad)
        shift = jnp.sum(probs * grad_probs, 0, keepdims=True)
        grad_scores = (probs * (grad_probs - shift)).astype(jnp.bfloat16)
        grads_v.append(
            jnp.dot(probs.astype(jnp.bfloat16), grad, preferred_element_type=jnp.float32)
        )
        grads_k.append(jnp.dot(grad_scores, query, preferred_element_type=jnp.float32))
        grads_q.append(contract_rows(grad_scores, keys) * scales)
    store_heads(dqt, dql, grads_q)
    store_heads(dkt, dkl, grads_k)
    store_heads(dvt, dvl, grads_v)


def pair_specs():
    text = pl.BlockSpec((PAGE_SLOTS, 2 * TEXT_HEAD), lambda step: (0, step))
    layout = pl.BlockSpec((PAGE_SLOTS, LAYOUT_WIDTH), lambda step: (0, 0))
    return text, layout, pltpu.VMEM((PAGE_SLOTS, 2 * LAYOUT_HEAD), jnp.bfloat16)


def attend(text_qkv, layout_qkv, lengths):
    text, layout, pair = pair_specs()
    low = jnp.bfloat16
    out_t, out_l, lse = pl.pallas_call(
        attend_kernel,
        grid=(HEAD_PAIRS,),
        in_specs=[pl.BlockSpec(memory_space=pltpu.SMEM)] + [text] * 3 + [layout] * 3,
        out_specs=[text, layout, pl.BlockSpec((1, PAGE_SLOTS, 2), lambda step: (step, 0, 0))],
        out_shape=[
            jax.ShapeDtypeStruct((PAGE_SLOTS, WIDTH), low),
            jax.ShapeDtypeStruct((PAGE_SLOTS, LAYOUT_WIDTH), low),
            jax.ShapeDtypeStruct((HEAD_PAIRS, PAGE_SLOTS, 2), jnp.float32),
        ],
        scratch_shapes=[pair] * 3,
        cost_estimate=pl.CostEstimate(
            flops=4000000000, bytes_accessed=2000000, transcendentals=100000
        ),
        compiler_params=pltpu.CompilerParams(vmem_limit_bytes=24 * 1024 * 1024),
    )(lengths, *text_qkv, *layout_qkv)
    return (out_t, out_l, lse.transpose(0, 2, 1))


def attend_back(text_qkv, layout_qkv, lengths, lse, text_grad, layout_grad):
    text, layout, pair = pair_specs()
    low = jnp.bfloat16
    text_out = jax.ShapeDtypeStruct((PAGE_SLOTS, WIDTH), low)
    layout_out = jax.ShapeDtypeStruct((PAGE_SLOTS, LAYOUT_WIDTH), low)
    outs = pl.pallas_call(
        attend_back_kernel,
        grid=(HEAD_PAIRS,),
        in_specs=[pl.BlockSpec(memory_space=pltpu.SMEM)]
        + [text] * 4
        + [layout] * 4
        + [pl.BlockSpec((1, 2, PAGE_SLOTS), lambda step: (step, 0, 0))],
        out_specs=[text] * 3 + [layout] * 3,
        out_shape=[text_out] * 3 + [layout_out] * 3,
        scratch_shapes=[pair] * 4,
        cost_estimate=pl.CostEstimate(
            flops=5000000000, bytes_accessed=3000000, transcendentals=100000
        ),
        compiler_params=pltpu.CompilerParams(vmem_limit_bytes=32 * 1024 * 1024),
    )(lengths, *text_qkv, text_grad, *layout_qkv, layout_grad, lse)
    return (list(outs[:3]), list(outs[3:]))


ERF_TERMS = (0.254829592, -0.284496736, 1.421413741, -1.453152027, 1.061405429)


def gelu_pair(values):
    size = jnp.abs(values)
    base = 1.0 / (1.0 + (0.3275911 / math.sqrt(2.0)) * size)
    series = ERF_TERMS[4]
    for term in reversed(ERF_TERMS[:4]):
        series = series * base + term
    bell = jnp.exp(values * values * -0.5)
    tail = 0.5 * series * base * bell
    share = jnp.where(values < 0.0, tail, 1.0 - tail)
    return (values * share, share + values * bell * (1.0 / math.sqrt(2.0 * math.pi)))


def load_units(pieces_in, pieces_out, rows, buffers, sems, chunks):
    per = len(pieces_in) // chunks
    slots = pieces_in[0].shape[0]
    step = pl.program_id(0)

    def copies(turn):
        made = []
        for number in range(per):
            for side, pieces in enumerate((pieces_in, pieces_out)):
                made.append(
                    pltpu.make_async_copy(
                        pieces[turn * per + number].at[:, pl.ds(0, rows)],
                        buffers[side].at[turn % 2, pl.ds(number * slots, slots)],
                        sems.at[turn % 2, 2 * number + side],
                    )
                )
        return made

    for turn in range(chunks):

        @pl.when(step == turn)
        def _(turn=turn):
            if turn == 0:
                for copy in copies(0):
                    copy.start()
            if turn + 1 < chunks:
                for copy in copies(turn + 1):
                    copy.start()
            for copy in copies(turn):
                copy.wait()

    slot = step % 2
    return [buffer[slot].reshape(-1, buffer.shape[-1]) for buffer in buffers]


def unit_plan(units, chunk, rows, chunks):
    width = units[0][0].shape[-1] if rows else units[0].shape[-1]
    if not rows:
        unit = pl.BlockSpec((chunk, width), lambda step: (step, 0))
        return list(units), [unit, unit], []
    anywhere = pl.BlockSpec(memory_space=pl.ANY)
    operands = list(units[0]) + list(units[1])
    buffer = pltpu.VMEM((2, chunk // rows, rows, width), jnp.bfloat16)
    sems = pltpu.SemaphoreType.DMA((2, len(operands) // chunks))
    return operands, [anywhere] * len(operands), [buffer, buffer, sems]


def take_units(refs, scratch, rows, chunks):
    if not rows:
        return [ref[...] for ref in refs]
    half = len(refs) // 2
    return load_units(refs[:half], refs[half:], rows, scratch[:2], scratch[2], chunks)


def ffn_kernel(rows, chunks, count, rows_ref, bias_ref, *refs):
    hidden_ref, slope_ref, part_ref = refs[count : count + 3]
    units_in, units_out = take_units(refs[:count], refs[count + 3 :], rows, chunks)

    @pl.when(pl.program_id(0) == 0)
    def _():
        part_ref[...] = jnp.zeros_like(part_ref)

    step = PAGE_SLOTS // 2
    for number in range(2):
        span = pl.ds(number * step, step)
        pre_act = contract_cols(rows_ref[span, :], units_in) + bias_ref[...]
        hidden, slope = gelu_pair(pre_act)
        hidden = hidden.astype(jnp.bfloat16)
        hidden_ref[span, :] = hidden
        slope_ref[span, :] = slope.astype(jnp.bfloat16)
        part_ref[span, :] += jnp.dot(hidden, units_out, preferred_element_type=jnp.float32)


def ffn_front(rows_in, units, bias_in, chunks, rows):
    slots, width = rows_in.shape
    total = bias_in.shape[0]
    chunk = total // chunks
    whole = pl.BlockSpec((slots, width), lambda step: (0, 0))
    piece = pl.BlockSpec((slots, chunk), lambda step: (0, step))
    operands, specs, scratch = unit_plan(units, chunk, rows, chunks)
    return pl.pallas_call(
        functools.partial(ffn_kernel, rows, chunks, len(operands)),
        grid=(chunks,),
        in_specs=[whole, pl.BlockSpec((1, chunk), lambda step: (0, step))] + specs,
        out_specs=[piece, piece, whole],
        out_shape=[
            jax.ShapeDtypeStruct((slots, total), jnp.bfloat16),
            jax.ShapeDtypeStruct((slots, total), jnp.bfloat16),
            jax.ShapeDtypeStruct((slots, width), jnp.float32),
        ],
        scratch_shapes=scratch,
        cost_estimate=pl.CostEstimate(
            flops=slots * width * total,
            bytes_accessed=total * (width + slots),
            transcendentals=0,
        ),
        compiler_params=pltpu.CompilerParams(vmem_limit_bytes=40 * 1024 * 1024),
    )(rows_in, bias_in[None], *operands)


def tail_route(flip):
    far, near, high, core = routes()
    return (high + [near] if flip else [near] + high) + [core]


def key_mask(key, axis):
    return sum(1 << bit for name, bit in key if name == axis)


class Spread:
    def __init__(self, block, joined, apart):
        self.joined, self.apart = list(joined), list(apart)
        self.masks = [frozenset()]
        self.held, self.came = block[None], None
        self.pieces = None

    def join(self, wait):
        if self.came is None:
            self.held = self.held if wait is None else tie(self.held, wait)
        else:
            came = self.came if wait is None else tie(self.came, wait)
            self.held = jnp.concatenate([self.held, came], 0)
        return self.held

    def advance(self, wait=None):
        if self.joined:
            step = self.joined.pop(0)
            held = self.join(wait)
            self.sent = [held]
            self.came = hop(held, *step)
            self.masks = self.masks + [mask | {step} for mask in self.masks]
            return self.came
        step = self.apart.pop(0)
        if self.pieces is None:
            self.pieces = {frozenset(): self.join(wait)}
            wait = None
        self.sent = []
        for key, piece in list(self.pieces.items()):
            piece = piece if wait is None else tie(piece, wait)
            self.sent.append(piece)
            came = hop(piece, *step)
            self.pieces[key] = piece
            self.pieces[key | {step}] = came
        return came


def half_spread(own, near_first=False):
    far, near, high, core = routes()
    return Spread(own, [near] + far if near_first else far + [near], [core])


def half_parts(chain):
    core = routes()[3]
    spot = lax.axis_index("dp")
    masks = [key_mask(mask, "dp") for mask in chain.masks]
    slot_of = {mask: number for number, mask in enumerate(masks)}
    table = jnp.array([slot_of[number] for number in range(len(masks))], jnp.int32)
    numbers = jnp.arange(len(masks))
    marks = (spot ^ numbers)[:, None] == numbers[None, :]
    places = jnp.sum(jnp.where(marks, table[None, :], 0), 1, dtype=jnp.int32)
    places = jnp.concatenate([places, own_bit(*core).astype(jnp.int32)[None]])
    return chain.pieces[frozenset()], chain.pieces[frozenset([core])], places


def unit_spread(block, flip):
    return Spread(block, routes()[0], tail_route(flip))


def unit_keys():
    far, near, high, core = routes()
    keys = [frozenset()]
    for step in [near] + list(reversed(high)) + [core]:
        keys = keys + [key | {step} for key in keys]
    return keys


def unit_result(chain):
    return [chain.pieces[key] for key in unit_keys()]


def unit_blocks():
    far = [frozenset()]
    for step in routes()[0]:
        far = far + [mask | {step} for mask in far]
    masks = [key | mask for key in unit_keys() for mask in far]
    spots = jnp.array([key_mask(mask, "dp") for mask in masks], jnp.int32)
    lanes = jnp.array([key_mask(mask, "mp") for mask in masks], jnp.int32)
    lanes, spots = lanes ^ lax.axis_index("mp"), spots ^ lax.axis_index("dp")
    return lanes * lax.axis_size("dp") + spots


class UnitSum:
    def __init__(self, kept, sent, flip):
        far, near, high, core = routes()
        self.order = high + [near]
        self.left = list(reversed(tail_route(flip)[:-1])) + list(reversed(far))
        shape = (2,) * len(self.order) + (lax.axis_size("dp") // 2,) + kept.shape[1:]
        self.sent = sent
        self.kept, self.came = kept.reshape(shape), hop(sent, *core).reshape(shape)

    def half(self, values, side, where):
        if where is not None:
            return lax.index_in_dim(values, side, where, keepdims=False)
        size = values.shape[0] // 2
        return values[side * size : (side + 1) * size]

    def advance(self):
        step = self.left.pop(0)
        where = self.order.index(step) if step in self.order else None
        if where is not None:
            self.order.remove(step)
        sent, kept = [
            add_low(self.half(self.kept, side, where), self.half(self.came, side, where))
            for side in (1, 0)
        ]
        self.sent = sent
        self.kept, self.came = kept, hop(sent, *step)
        return self.sent

    def finish(self):
        while self.left:
            self.advance()
        return (self.kept.astype(jnp.float32) + self.came.astype(jnp.float32))[0]


def to_rows(values):
    flat = values.reshape(values.shape[0], -1)
    flat = jnp.pad(flat, ((0, 0), (0, -flat.shape[1] % WIDTH)))
    return flat.reshape(values.shape[0], -1, WIDTH)


def from_rows(values, units):
    flat = values.reshape(values.shape[0], -1)[:, : units * 2 * LAYOUT_WIDTH]
    return flat.reshape(-1, 2 * LAYOUT_WIDTH)


class HalfSum:
    def __init__(self, sent, kept):
        far, near, high, core = routes()
        self.order = far + [near]
        self.left = [near] + list(reversed(far)) + high + [core]
        shape = (2,) * len(self.order) + sent.shape[1:]
        self.sent = sent
        self.kept, self.came = kept.reshape(shape), hop(sent, *core).reshape(shape)

    def advance(self):
        far, near, high, core = routes()
        step = self.left.pop(0)
        if step == core or step in high:
            self.kept = self.sent = add_low(self.kept, self.came)
            self.came = hop(self.kept, *step)
        else:
            where = self.order.index(step)
            self.order.remove(step)
            mine = own_bit(*step)

            def side(values, number):
                return lax.dynamic_index_in_dim(values, number, where, keepdims=False)

            sent = add_low(side(self.kept, 1 - mine), side(self.came, 1 - mine))
            kept = add_low(side(self.kept, mine), side(self.came, mine))
            self.sent = sent
            self.kept, self.came = kept, hop(sent, *step)
        return self.sent

    def finish(self):
        while self.left:
            self.advance()
        first = own_bit(*routes()[3]) == 0
        own, other = self.kept, self.came
        return jnp.stack([jnp.where(first, own, other), jnp.where(first, other, own)]).astype(
            jnp.float32
        )


def own_half(values):
    half = values.shape[-1] // 2
    return jnp.where(own_bit("mp", 0) == 0, values[..., :half], values[..., half:])


def sum_everywhere(values):
    for axis in ("mp", "dp"):
        size = lax.axis_size(axis)

        def jump(mask):
            pairs = [(spot, spot ^ mask) for spot in range(size)]
            return lax.ppermute(values, axis, pairs)

        steps = [1 << bit for bit in bits_of(size)]
        for number in range(0, len(steps), 2):
            pair = steps[number : number + 2]
            if len(pair) == 2:
                near, far, both = jump(pair[0]), jump(pair[1]), jump(pair[0] | pair[1])
                values = (values + near) + (far + both)
            else:
                values = values + jump(pair[0])
    return values


def show_all(values):
    everywhere = ("dp", "mp")
    count = lax.axis_size("dp") * lax.axis_size("mp")
    return lax.all_to_all(
        jnp.broadcast_to(values[None], (count,) + values.shape), everywhere, 0, 0, tiled=True
    )


def trade(values):
    return lax.all_to_all(values, ("dp", "mp"), 0, 0, tiled=True)


def project_qkv(rows_low, mats, vectors, width):
    joined = jnp.dot(rows_low, mats[0], preferred_element_type=jnp.float32)
    query = (joined[:, :width] + vectors[0]).astype(jnp.bfloat16)
    keys = joined[:, width:].astype(jnp.bfloat16)
    values = jnp.dot(rows_low, mats[1][:, :width], preferred_element_type=jnp.float32)
    return (query, keys, (values + vectors[1]).astype(jnp.bfloat16))


def scale_pair():
    return (1.0 / math.sqrt(WIDTH // HEADS), 1.0 / math.sqrt(LAYOUT_WIDTH // HEADS))


def project_back(mats, grads, width):
    first = jnp.concatenate(grads[:2], 1)
    rows_grad = contract_cols(first, mats[0]) + contract_cols(grads[2], mats[1][:, :width])
    return (
        rows_grad,
        jnp.sum(grads[0], 0, dtype=jnp.float32),
        jnp.sum(grads[2], 0, dtype=jnp.float32),
    )


def ffn_back_kernel(
    rows_of, chunks, count, rows_ref, grad_ref, hidden_ref, slope_ref, extra_ref, *refs
):
    part_ref, bias_ref, *sums = refs[count : count + 6]
    units_in, units_out = take_units(refs[:count], refs[count + 6 :], rows_of, chunks)
    step, last = pl.program_id(0), chunks // 2
    rows, grad = rows_ref[...], grad_ref[...]
    grad_hidden = contract_cols(grad, units_out)
    grad_pre = grad_hidden * slope_ref[...].astype(jnp.float32)
    grad_low = grad_pre.astype(jnp.bfloat16)
    bias_ref[...] = jnp.sum(grad_low.astype(jnp.float32), 0, keepdims=True)

    @pl.when(step == 0)
    def _():
        part_ref[...] = jnp.zeros_like(part_ref)

    part_ref[...] += jnp.dot(grad_low, units_in, preferred_element_type=jnp.float32)
    results = [contract_rows(grad_low, rows), contract_rows(hidden_ref[...], grad)]

    def store(targets):
        for target, result in zip(targets, results):
            if len(target.shape) == 2:
                target[...] = result.astype(target.dtype)
            else:
                blocks = result.astype(target.dtype).reshape(target.shape[0], -1, rows.shape[1])
                target[:, : blocks.shape[1], :] = blocks
                if target.shape[1] > blocks.shape[1]:
                    target[:, blocks.shape[1] :, :] = extra_ref[...]

    @pl.when(step < last)
    def _():
        store(sums[:2])

    @pl.when(step >= last)
    def _():
        store(sums[2:])


def ffn_back(rows_in, units, slope, hidden, grad_rows, chunks, slot_rows, extra):
    slots, width = rows_in.shape
    total = hidden.shape[1]
    chunk, half = total // chunks, chunks // 2
    whole = pl.BlockSpec((slots, width), lambda step: (0, 0))
    piece = pl.BlockSpec((slots, chunk), lambda step: (0, step))
    operands, specs, scratch = unit_plan(
        units, chunk, slot_rows[0] if slot_rows else None, chunks
    )

    def first(step):
        return jnp.minimum(step, half - 1)

    def second(step):
        return jnp.maximum(step - half, 0)

    turns = (first, first, second, second)
    if slot_rows is None:
        shapes = [(total // 2, width)] * 4
        sum_specs = [
            pl.BlockSpec((chunk, width), lambda step, turn=turn: (turn(step), 0)) for turn in turns
        ]
        extra_spec = pl.BlockSpec(memory_space=pltpu.VMEM)
    else:
        rows, padded = slot_rows
        heights = [padded, rows] * 2
        shapes = [(total // (2 * rows), height, width) for height in heights]
        sum_specs = [
            pl.BlockSpec((chunk // rows, height, width), lambda step, turn=turn: (turn(step), 0, 0))
            for height, turn in zip(heights, turns)
        ]
        extra_spec = pl.BlockSpec((chunk // rows, padded - rows, width), lambda step: (step, 0, 0))
    return pl.pallas_call(
        functools.partial(
            ffn_back_kernel, slot_rows[0] if slot_rows else None, chunks, len(operands)
        ),
        grid=(chunks,),
        in_specs=[whole, whole, piece, piece, extra_spec] + specs,
        out_specs=[whole, pl.BlockSpec((1, chunk), lambda step: (0, step))] + sum_specs,
        out_shape=[
            jax.ShapeDtypeStruct((slots, width), jnp.float32),
            jax.ShapeDtypeStruct((1, total), jnp.float32),
        ]
        + [jax.ShapeDtypeStruct(shape, jnp.bfloat16) for shape in shapes],
        scratch_shapes=scratch,
        cost_estimate=pl.CostEstimate(
            flops=2 * slots * width * total,
            bytes_accessed=2 * total * (width + slots),
            transcendentals=0,
        ),
        compiler_params=pltpu.CompilerParams(vmem_limit_bytes=48 * 1024 * 1024),
    )(rows_in, grad_rows, hidden, slope, extra, *operands)


def stream_forward(rows, att, mats, units, bias_in, vec, unit_rows, hook):
    width = rows.shape[1]
    first = (
        rows + jnp.dot(att, mats[1][:, width:], preferred_element_type=jnp.float32) + vec[2]
    )
    mid = norm_apply(first, vec[3], vec[4])
    mid_low = hook(mid.astype(jnp.bfloat16))
    chunks = 4 if width == WIDTH else 1
    hidden, slope, part = ffn_front(mid_low, units, bias_in, chunks, unit_rows)
    last = mid + part + vec[5]
    return (norm_apply(last, vec[6], vec[7]), (first, mid_low, slope, hidden, last))


def layer_forward(text, layout, weights, lengths, hooks):
    (tm, lm, tb, lb, tv, lv) = weights
    text_low = hooks["low"](text.astype(jnp.bfloat16))
    layout_low = layout.astype(jnp.bfloat16)
    text_qkv = list(project_qkv(text_low, tm, tv, WIDTH))
    layout_qkv = project_qkv(layout_low, lm, lv, LAYOUT_WIDTH)
    text_qkv[0] = hooks["query"](text_qkv[0])
    text_att, layout_att, log_total = attend(text_qkv, layout_qkv, lengths)
    text_att = hooks["att"](text_att)
    tu, lu = hooks["units"]()
    count = lax.axis_size("dp") * lax.axis_size("mp")
    text_new, text_kept = stream_forward(
        text, text_att, tm, tu, tb, tv, FFN_UNITS // count, hooks["mid"]
    )
    layout_new, layout_kept = stream_forward(
        layout, layout_att, lm, lu, lb, lv, None, lambda value: value
    )
    cache = (
        text_low,
        layout_low,
        text_qkv,
        layout_qkv,
        log_total,
        text_att,
        layout_att,
        text_kept,
        layout_kept,
    )
    return (text_new, layout_new, cache, (tu, lu))


def stream_back(kept, att, mats, units, vec, grad, slot_rows, hook, extra):
    first, mid_low, slope, hidden, last = kept
    width = first.shape[1]
    last_g, gain2, bias2 = norm_back(last, vec[6], vec[7], grad)
    in_grad, bias_in_g, *unit_grads = ffn_back(
        mid_low,
        units,
        slope,
        hidden,
        hook(last_g.astype(jnp.bfloat16)),
        4 if width == WIDTH else 2,
        slot_rows,
        extra,
    )
    first_g, gain1, bias1 = norm_back(first, vec[3], vec[4], last_g + in_grad)
    first_low = first_g.astype(jnp.bfloat16)
    att_grad = contract_cols(first_low, mats[1][:, width:]).astype(jnp.bfloat16)
    vec_tail = [jnp.sum(first_g, 0), gain1, bias1, jnp.sum(last_g, 0), gain2, bias2]
    return (first_g, att_grad, first_low, unit_grads, bias_in_g[0], vec_tail)


def layer_backward(cache, grad_text, grad_layout, weights, lengths, plan):
    (
        text_low,
        layout_low,
        text_qkv,
        layout_qkv,
        log_total,
        text_att,
        layout_att,
        text_kept,
        layout_kept,
    ) = cache
    (tm, lm, tu, lu, tb, lb, tv, lv) = weights
    count = lax.axis_size("dp") * lax.axis_size("mp")
    rows = FFN_UNITS // count
    none = jnp.zeros((8, 128), jnp.float32)
    first_l, att_l, out_l, lu_g, lb_g, tail_l = stream_back(
        layout_kept, layout_att, lm, lu, lv, grad_layout, None, lambda value: value, none
    )
    halves = [jnp.concatenate(lu_g[2 * side : 2 * side + 2], 1) for side in range(2)]
    extra = to_rows(jnp.concatenate(halves, 0).reshape(count, -1, 2 * LAYOUT_WIDTH))
    extra = jnp.pad(extra, ((0, 0), (0, -extra.shape[1] % 16), (0, 0)))
    slot_rows = (rows, rows + extra.shape[1])
    first_t, att_t, out_t, tu_g, tb_g, tail_t = stream_back(
        text_kept, text_att, tm, tu, tv, grad_text, slot_rows, plan.before_units, extra
    )
    att_t = plan.after_units(att_t, tu_g)
    text_dqkv, layout_dqkv = attend_back(
        text_qkv, layout_qkv, lengths, log_total, att_t, att_l
    )
    text_dqkv[0] = plan.after_attend(text_dqkv[0])
    plan.after_mats(
        (text_low, *text_dqkv, text_att, out_t), (layout_low, *layout_dqkv, layout_att, out_l)
    )
    rows_t, q_bias_t, v_bias_t = project_back(tm, text_dqkv, WIDTH)
    rows_l, q_bias_l, v_bias_l = project_back(lm, layout_dqkv, LAYOUT_WIDTH)
    grads = (
        tb_g,
        lb_g,
        jnp.stack([q_bias_t, v_bias_t] + tail_t),
        jnp.stack([q_bias_l, v_bias_l] + tail_l),
    )
    return (first_t + rows_t, first_l + rows_l, grads)


class Plan:
    def __init__(self):
        self.units = []
        self.mats = []

    def step(self, value, items):
        for item in items:
            item.came = tie(item.came, value)
        return tie(value, *[item.advance() for item in items])

    def before_units(self, value):
        return self.step(value, self.mats[:1]) if self.mats else value

    def after_units(self, value, grads):
        keep_in, keep_out, send_in, send_out = grads
        self.units.append([UnitSum(keep_in, send_in, False), UnitSum(keep_out, send_out, True)])
        if self.mats:
            return self.step(value, self.units[0] + self.mats[:1])
        return self.step(value, self.units[0])

    def after_attend(self, value):
        if self.mats:
            return self.step(value, self.units[1] + self.mats[:1])
        return value

    def after_mats(self, text, layout):
        dp = lax.axis_size("dp")
        low = jnp.bfloat16
        side = own_bit("mp", 0).astype(jnp.int32)
        rows, query, keys, values, att, first = layout
        first_half = contract_rows(rows, jnp.concatenate([query, keys], 1)).astype(low)
        second_half = jnp.concatenate(
            [contract_rows(rows, values), contract_rows(att, first)], 1
        ).astype(low)
        text_rows = WIDTH // dp
        extras = [
            jnp.where(side == number, second_half, first_half).reshape(dp, -1, 2 * WIDTH)
            for number in range(2)
        ]
        padded = -(-(text_rows + extras[0].shape[1]) // 8) * 8
        pad = ((0, 0), (0, padded - text_rows - extras[0].shape[1]), (0, 0))
        sums = mats_sums(side[None], text, padded)
        sent, kept = [
            lax.dynamic_update_slice(item, jnp.pad(extra, pad), (0, text_rows, 0))
            for item, extra in zip(sums, extras)
        ]
        self.mats.append(HalfSum(sent, kept))

    def between(self, value):
        if len(self.mats) == 1:
            return self.step(tie(value, self.mats[0].sent), self.units[0])
        return self.step(tie(value, self.mats[1].sent), self.units[0] + self.mats[:1])


def split_high(values):
    high = values.astype(jnp.bfloat16)
    return (high, (values - high.astype(jnp.float32)).astype(jnp.bfloat16))


def add_rows(marks, values):
    high, low = split_high(values)
    return contract_rows(marks, high) + contract_rows(marks, low)


def apply_update(master, grad, moment, average, loss_count, factor):
    clipped = grad / loss_count * factor
    moment_new = MOMENTUM * moment + clipped
    master_new = master - LEARN_RATE * (clipped + MOMENTUM * moment_new)
    return (master_new, moment_new, AVERAGE_DECAY * average + (1.0 - AVERAGE_DECAY) * master_new)


def on_device(
    token_ids,
    mlm_targets,
    page_lengths,
    box_coords,
    mlm_positions,
    align_pairs,
    align_labels,
    table,
    text_mats,
    layout_mats,
    text_ffn,
    layout_ffn,
    small_params,
    table_momentum,
    text_mats_momentum,
    layout_mats_momentum,
    text_ffn_momentum,
    layout_ffn_momentum,
    small_momentum,
    table_average,
    text_mats_average,
    layout_mats_average,
    text_ffn_average,
    layout_ffn_average,
    small_average,
):
    lane, spot = lax.axis_index("mp"), lax.axis_index("dp")
    dp, mp = lax.axis_size("dp"), lax.axis_size("mp")
    count = dp * mp
    slots = PAGE_SLOTS
    mask_slots = mlm_positions.shape[1]
    pages = 1
    vocab_rows = table.shape[0]
    low = jnp.bfloat16

    own_ids = lax.dynamic_index_in_dim(token_ids, lane, 0, keepdims=False)
    own_targets = lax.dynamic_index_in_dim(mlm_targets, lane, 0, keepdims=False)
    table_low = table.astype(low)
    own_block = lane * dp + spot
    steps = jnp.arange(slots)
    first_at = jnp.min(
        jnp.where(own_ids[:, None] == own_ids[None, :], steps[None, :], slots), 1
    )
    page_first = first_at == steps
    block_own = own_ids // vocab_rows
    rank = jnp.sum(
        page_first[None, :]
        & (block_own[:, None] == block_own[None, :])
        & (steps[None, :] < first_at[:, None]),
        1,
        dtype=jnp.int32,
    )
    source = (block_own % dp) * mp + block_own // dp
    local_own = own_ids - block_own * vocab_rows
    places = jnp.arange(count * ROUND_ROWS)

    def place_of(turn):
        turn_rank = rank - turn * ROUND_ROWS
        inside = (turn_rank >= 0) & (turn_rank < ROUND_ROWS)
        return jnp.where(inside, source * ROUND_ROWS + turn_rank, -1)

    def requests(turn):
        asked = (place_of(turn)[None, :] == places[:, None]) & page_first[None, :]
        rows = jnp.sum(jnp.where(asked, local_own[None, :] + 1, 0), 1, dtype=jnp.int32) - 1
        return rows.reshape(count, ROUND_ROWS)

    def settle(chains, left):
        for chain in chains:
            while len(chain.joined) + len(chain.apart) > left:
                chain.advance()

    def marks_of(rows):
        return (rows.reshape(-1)[:, None] == jnp.arange(vocab_rows)[None, :]).astype(low)


    def held_marks(turn):
        return (place_of(turn)[:, None] == places[None, :]).astype(low)

    def fetch(turn, marks, so_far):
        sent = jnp.dot(marks, table_low, preferred_element_type=jnp.float32).astype(low)
        came = trade(sent)
        return (
            so_far + jnp.dot(held_marks(turn), came, preferred_element_type=jnp.float32),
            came,
            sent,
        )

    share = small_params.shape[0]
    line = 2 * WIDTH
    half_rows = small_half_rows(share)
    small_pad = jnp.pad(small_params.astype(low), (0, 2 * half_rows * 128 - share))
    small_half = lax.dynamic_slice_in_dim(
        small_pad.reshape(2 * half_rows, 128), (lane & 1) * half_rows, half_rows
    )
    tmats_half = own_half(text_mats.astype(low))
    lmats_half = own_half(layout_mats.astype(low)).reshape(-1, 128)
    extra = jnp.concatenate(
        [small_half, lmats_half, jnp.zeros((-lmats_half.shape[0] % 16, 128), low)], 0
    )
    unit_rows = text_ffn.shape[1]
    layout_units = layout_ffn.shape[1]
    layout_unit_rows = -(-(2 * layout_units * LAYOUT_WIDTH) // WIDTH)
    unit_pad = -layout_unit_rows % 16

    def unit_block(layer_no, part):
        text_part = text_ffn[layer_no, :, part * WIDTH : (part + 1) * WIDTH].astype(low)
        if part:
            return text_part
        return jnp.concatenate(
            [
                text_part,
                to_rows(layout_ffn[layer_no : layer_no + 1].astype(low))[0],
                jnp.zeros((unit_pad, WIDTH), low),
            ],
            0,
        )

    mats_chains = [half_spread(tmats_half[layer_no]) for layer_no in range(LAYERS)]
    extra_chain = half_spread(extra, True)
    unit_chains = [
        [unit_spread(unit_block(layer_no, part), part == 1) for part in range(2)]
        for layer_no in range(LAYERS)
    ]
    far_steps = len(routes()[0])
    told = jnp.concatenate(
        [
            jnp.max(rank, keepdims=True) // ROUND_ROWS + 1,
            page_lengths,
            own_targets,
        ]
    )
    told = jnp.broadcast_to(told[None], (count, mask_slots + 2))
    spare = jnp.zeros((count, -(ROUND_ROWS + mask_slots + 2) % 128), jnp.int32)
    message = jnp.concatenate([requests(0), told, spare], 1)
    mats_chains[0].advance()
    extra_chain.advance()
    extra_chain.advance()
    shown = trade(tie(message, *extra_chain.sent))
    mats_chains[0].advance()
    extra_chain.advance()
    shown = tie(shown, *mats_chains[0].sent, *extra_chain.sent)
    rounds = jnp.max(shown[:, ROUND_ROWS])
    all_lengths = shown[:, ROUND_ROWS + 1]
    all_targets = shown[:, ROUND_ROWS + 2 : ROUND_ROWS + 2 + mask_slots].reshape(-1)

    asked_first = marks_of(shown[:, :ROUND_ROWS])
    embedded, came_first, rows_first = fetch(
        0, asked_first, jnp.zeros((slots, WIDTH), jnp.float32)
    )
    embedded = lax.fori_loop(
        1,
        rounds,
        lambda turn, so_far: fetch(turn, marks_of(trade(requests(turn))), so_far)[0],
        embedded,
    )
    settle(mats_chains[:1], 2)
    mats_chains[0].advance(rows_first)
    settle([extra_chain], 1)
    extra_chain.advance(mats_chains[0].sent[0])
    wait = extra_chain.sent[0]
    for chain in unit_chains[0]:
        chain.advance(wait)
    core_key = frozenset([routes()[3]])
    extra_chain.pieces[core_key] = tie(
        extra_chain.pieces[core_key], *[chain.sent[0] for chain in unit_chains[0]]
    )
    small_parts, lmats_all = unpack_small(*half_parts(extra_chain), lmats_half.shape[0])
    lmats_all = lmats_all.reshape(2, dp, LAYERS, -1, 2 * LAYOUT_WIDTH)
    mats_chains[0].advance(tie(came_first, small_parts[6]))
    for number in range(1, far_steps):
        for chain in unit_chains[0]:
            chain.advance(mats_chains[0].sent[0])
    tmats_first = put_in_order(*half_parts(mats_chains[0]))
    (
        text_vec,
        layout_vec,
        text_bias,
        layout_bias,
        text_emb,
        layout_emb,
        text_pos,
        layout_pos,
        box_table,
        align_mat,
    ) = small_parts

    coords = box_coords[:, 0].T
    text_pre, layout_pre, text, layout = embed_streams(
        coords, embedded, text_pos, layout_pos, box_table, text_emb, layout_emb
    )
    caches = []
    layer_weights = []

    def push(value, chains):
        waits = []
        for chain in chains:
            chain.advance(value)
            waits = waits + chain.sent
        return tie(value, *waits)

    def after(chains, wait):
        for chain in chains:
            chain.advance(wait)

    def hooks_of(layer_no):
        units = unit_chains[layer_no]
        later = layer_no + 1 < LAYERS
        if later:
            next_mats, next_units = mats_chains[layer_no + 1], unit_chains[layer_no + 1]

        def at_low(value):
            if layer_no == 0:
                value = push(value, units)
            if later:
                next_mats.advance(units[1].sent[0])
            return value

        def at_query(value):
            return push(value, units) if layer_no else value

        def at_att(value):
            settle(units, 2)
            pending = [chain for chain in units if len(chain.joined) + len(chain.apart) > 1]
            if pending or later:
                value = push(value, pending + ([next_mats] if later else []))
            after(units, value)
            if later:
                after(next_units, next_mats.sent[0])
            return value

        def at_mid(value):
            return push(value, [next_mats] + next_units) if later else value

        return {
            "low": at_low,
            "query": at_query,
            "att": at_att,
            "mid": at_mid,
            "units": lambda: units_of(layer_no),
        }

    def units_of(layer_no):
        results = [unit_result(chain) for chain in unit_chains[layer_no]]
        layout_both = from_rows(
            take_extra(results[0], unit_rows)[:, :layout_unit_rows], layout_units
        )
        return (results, [layout_both[:, :LAYOUT_WIDTH], layout_both[:, LAYOUT_WIDTH:]])

    slot_marks = (unit_blocks()[:, None] == jnp.arange(count)[None, :]).astype(jnp.float32)
    for layer_no in range(LAYERS):
        if layer_no:
            settle([mats_chains[layer_no]], 1)
            text = push(text, unit_chains[layer_no] + [mats_chains[layer_no]])
            tmats = put_in_order(*half_parts(mats_chains[layer_no]))
        else:
            tmats = tmats_first
        weights = [
            tmats,
            lmats_all[:, :, layer_no].reshape(2, LAYOUT_WIDTH, -1),
            jnp.dot(
                slot_marks, text_bias[layer_no].reshape(count, -1), precision=PRECISE
            ).reshape(-1),
            jnp.dot(
                slot_marks, layout_bias[layer_no].reshape(count, -1), precision=PRECISE
            ).reshape(-1),
            text_vec[layer_no],
            layout_vec[layer_no],
        ]
        text, layout, cache, units = layer_forward(
            text, layout, weights, page_lengths, hooks_of(layer_no)
        )
        weights = weights[:2] + list(units) + weights[2:]
        caches.append(cache)
        layer_weights.append(weights)

    row_index = mlm_positions.reshape(-1)
    live_all = (
        (jnp.arange(mask_slots)[None, :] * slots < mask_slots * all_lengths[:, None])
        .astype(jnp.float32)
        .reshape(-1)
    )
    chosen_marks = (row_index[:, None] == steps[None, :]).astype(low)
    chosen_own = jnp.dot(
        chosen_marks, text.astype(low), preferred_element_type=jnp.float32
    ).astype(low)
    chosen_all = show_all(chosen_own).reshape(count * mask_slots, WIDTH)
    logits = contract_cols(chosen_all, table_low)
    target_local = all_targets - own_block * vocab_rows
    target_in = target_local[:, None] == jnp.arange(vocab_rows)[None, :]
    target_logit = jnp.sum(jnp.where(target_in, logits, 0.0), 1)
    row_peak = jnp.max(logits, axis=1)
    row_total = jnp.sum(jnp.exp(logits - row_peak[:, None]), axis=1)
    stats = show_all(jnp.stack([row_peak, row_total, target_logit]))
    all_peak = jnp.max(stats[:, 0], 0)
    all_total = jnp.sum(stats[:, 1] * jnp.exp(stats[:, 0] - all_peak[None]), 0)
    all_target = jnp.sum(stats[:, 2], 0)
    log_total = all_peak + jnp.log(all_total)
    own_start = (spot * mp + lane) * mask_slots
    live_own = lax.dynamic_slice_in_dim(live_all, own_start, mask_slots)
    own_loss = jnp.sum(
        lax.dynamic_slice_in_dim((log_total - all_target) * live_all, own_start, mask_slots)
    )
    grad_low = (
        (jnp.exp(logits - log_total[:, None]) - target_in.astype(jnp.float32)) * live_all[:, None]
    ).astype(low)
    table_grad = contract_rows(grad_low, chosen_all)
    chosen_parts = trade(jnp.dot(grad_low, table_low, preferred_element_type=jnp.float32).astype(low))
    chosen_grad = jnp.sum(
        chosen_parts.reshape(count, mask_slots, WIDTH).astype(jnp.float32), 0
    )

    first_marks = (align_pairs[0, :, 0][:, None] == steps[None, :]).astype(jnp.float32)
    second_marks = (align_pairs[0, :, 1][:, None] == steps[None, :]).astype(jnp.float32)
    answer = align_labels.reshape(-1).astype(jnp.float32)
    first_rows = jnp.dot(first_marks, text, precision=PRECISE)
    second_rows = jnp.dot(second_marks, layout, precision=PRECISE)

    def pair_loss(text_rows, layout_rows, align_weight):
        right = jnp.dot(layout_rows, align_weight, precision=PRECISE)
        logit = jnp.sum(text_rows * right, axis=-1) / math.sqrt(WIDTH)
        return jnp.sum(jax.nn.softplus(logit) - answer * logit)

    align_part, align_pull = jax.vjp(pair_loss, first_rows, second_rows, align_mat)
    first_back, second_back, align_grad = align_pull(jnp.ones((), jnp.float32))
    grad_text = add_rows(
        jnp.concatenate([first_marks.astype(low), chosen_marks], 0),
        jnp.concatenate([first_back, chosen_grad], 0),
    )
    grad_layout = add_rows(second_marks.astype(low), second_back)

    plan = Plan()
    layer_grads = [None] * LAYERS
    for layer_no in reversed(range(LAYERS)):
        grad_text, grad_layout, layer_grads[layer_no] = layer_backward(
            caches[layer_no], grad_text, grad_layout, layer_weights[layer_no], page_lengths, plan
        )
        grad_text = plan.between(grad_text)

    embed_grad, looked_grad, text_emb_grad, layout_emb_grad, box_grad = embed_back(
        coords, text_pre, layout_pre, text_emb, layout_emb, grad_text, grad_layout
    )
    embed_low = embed_grad.astype(low)

    def give(turn, marks, so_far):
        sent = contract_rows(held_marks(turn), embed_low).astype(low)
        came = trade(sent)
        return (so_far + contract_rows(marks, came), sent, came)

    table_sum, gave_rows, gave_came = give(0, asked_first, table_grad)
    table_sum = lax.fori_loop(
        1,
        rounds,
        lambda turn, so_far: give(turn, marks_of(trade(requests(turn))), so_far)[0],
        table_sum,
    )

    def stacked(member):
        return jnp.stack([layer_grads[layer_no][member] for layer_no in range(LAYERS)])

    def in_order(member):
        return jnp.stack(
            [
                lax.dot_general(
                    slot_marks,
                    layer_grads[layer_no][member].reshape(count, -1),
                    (((0,), (0,)), ((), ())),
                    precision=PRECISE,
                )
                for layer_no in range(LAYERS)
            ]
        )

    small_items = [
        stacked(2),
        stacked(3),
        in_order(0),
        in_order(1),
        text_emb_grad,
        layout_emb_grad,
        embed_grad,
        looked_grad,
        box_grad,
        align_grad,
    ]
    plan.mats[1].advance()
    token = plan.mats[1].sent
    small_items[6] = tie(embed_grad, token, gave_rows)
    small_blocks = pack_small(small_items, dp).reshape(dp, 2, half_rows, 128)
    first = own_bit("mp", 0) == 0
    small_total = HalfSum(
        jnp.where(first, small_blocks[:, 1], small_blocks[:, 0]),
        jnp.where(first, small_blocks[:, 0], small_blocks[:, 1]),
    )
    token = small_total.sent
    outer = plan.units[1]
    turns = outer + [plan.mats[1]] + outer + [small_total, plan.mats[1]] + outer
    turns = turns + [small_total, plan.mats[1]] * 5
    for number, chain in enumerate(turns):
        if chain.left:
            chain.came = tie(chain.came, token)
            chain.advance()
            token = chain.sent
        if number == 2:
            token = tie(gave_came, token)
    small_sum = small_total.finish().reshape(-1)[:share]
    plan.units.reverse()
    plan.mats.reverse()
    mats_sums = [item.finish() for item in plan.mats]
    mats_rows = text_mats.shape[1]
    extra_rows = layout_mats.shape[1] * LAYOUT_WIDTH * 2 // line
    tmats_sum = jnp.stack(
        [jnp.concatenate([item[0, :mats_rows], item[1, :mats_rows]], 1) for item in mats_sums]
    )
    lmats_sum = jnp.stack(
        [
            jnp.concatenate(
                [
                    item[side, mats_rows : mats_rows + extra_rows].reshape(-1, 2 * LAYOUT_WIDTH)
                    for side in range(2)
                ],
                1,
            )
            for item in mats_sums
        ]
    )
    unit_sums = [
        [item.finish() for item in plan.units[layer_no]] for layer_no in range(LAYERS)
    ]
    tffn_sum = jnp.stack(
        [jnp.concatenate([item[:unit_rows] for item in pair], 1) for pair in unit_sums]
    )
    lffn_sum = jnp.stack(
        [
            from_rows(pair[0][None, unit_rows : unit_rows + layout_unit_rows], layout_units)
            for pair in unit_sums
        ]
    )
    final_grads = (table_sum, tmats_sum, lmats_sum, tffn_sum, lffn_sum, small_sum)
    lane_first = (lane == 0).astype(jnp.float32)
    squares = (
        jnp.sum(table_sum * table_sum) + jnp.sum(tffn_sum * tffn_sum) + jnp.sum(lffn_sum * lffn_sum)
    )
    squares = squares + lane_first * (
        jnp.sum(tmats_sum * tmats_sum)
        + jnp.sum(lmats_sum * lmats_sum)
        + jnp.sum(small_sum * small_sum)
    )
    count_part = jnp.sum(live_own) + jnp.float32(pages * PAIRS)
    sums = sum_everywhere(
        jnp.broadcast_to(
            jnp.stack([squares, own_loss + align_part, count_part, squares])[:, None], (4, 128)
        )
    )
    total_squares, loss_sum, loss_count = sums[0, 0], sums[1, 0], sums[2, 0]
    grad_norm = jnp.sqrt(total_squares) / loss_count
    factor = jnp.minimum(1.0, CLIP_NORM / grad_norm)
    masters = (table, text_mats, layout_mats, text_ffn, layout_ffn, small_params)
    moments = (
        table_momentum,
        text_mats_momentum,
        layout_mats_momentum,
        text_ffn_momentum,
        layout_ffn_momentum,
        small_momentum,
    )
    averages = (
        table_average,
        text_mats_average,
        layout_mats_average,
        text_ffn_average,
        layout_ffn_average,
        small_average,
    )
    updated = [
        apply_update(
            masters[number],
            final_grads[number],
            moments[number],
            averages[number],
            loss_count,
            factor,
        )
        for number in range(6)
    ]
    new_masters = [item[0] for item in updated]
    new_moments = [item[1] for item in updated]
    new_averages = [item[2] for item in updated]
    copies = [item.astype(jnp.bfloat16) for item in new_masters[:5]]
    return (
        loss_sum,
        loss_count,
        grad_norm,
        new_masters[0],
        new_masters[1],
        new_masters[2],
        new_masters[3],
        new_masters[4],
        new_masters[5],
        copies[0],
        copies[1],
        copies[2],
        copies[3],
        copies[4],
        new_moments[0],
        new_moments[1],
        new_moments[2],
        new_moments[3],
        new_moments[4],
        new_moments[5],
        new_averages[0],
        new_averages[1],
        new_averages[2],
        new_averages[3],
        new_averages[4],
        new_averages[5],
    )


def solution(mesh):
    return jax.shard_map(
        on_device,
        mesh=mesh,
        in_specs=(
            P("dp", None),
            P("dp", None),
            P(("dp", "mp")),
            P(None, ("dp", "mp"), None),
            P(("dp", "mp"), None),
            P(("dp", "mp"), None, None),
            P(("dp", "mp"), None),
            P(("mp", "dp"), None),
            P(None, "dp", None),
            P(None, "dp", None),
            P(None, ("mp", "dp"), None),
            P(None, ("mp", "dp"), None),
            P("dp"),
            P(("mp", "dp"), None),
            P(None, "dp", None),
            P(None, "dp", None),
            P(None, ("mp", "dp"), None),
            P(None, ("mp", "dp"), None),
            P("dp"),
            P(("mp", "dp"), None),
            P(None, "dp", None),
            P(None, "dp", None),
            P(None, ("mp", "dp"), None),
            P(None, ("mp", "dp"), None),
            P("dp"),
        ),
        out_specs=(
            P(),
            P(),
            P(),
            P(("mp", "dp"), None),
            P(None, "dp", None),
            P(None, "dp", None),
            P(None, ("mp", "dp"), None),
            P(None, ("mp", "dp"), None),
            P("dp"),
            P(("mp", "dp"), None),
            P(None, "dp", None),
            P(None, "dp", None),
            P(None, ("mp", "dp"), None),
            P(None, ("mp", "dp"), None),
            P(("mp", "dp"), None),
            P(None, "dp", None),
            P(None, "dp", None),
            P(None, ("mp", "dp"), None),
            P(None, ("mp", "dp"), None),
            P("dp"),
            P(("mp", "dp"), None),
            P(None, "dp", None),
            P(None, "dp", None),
            P(None, ("mp", "dp"), None),
            P(None, ("mp", "dp"), None),
            P("dp"),
        ),
        check_vma=False,
    )
```

```python
import functools
import math

import jax
import jax.numpy as jnp
from jax import lax
from jax.experimental import pallas as pl
from jax.experimental.pallas import tpu as pltpu
from jax.sharding import PartitionSpec as P

WIDTH = 768
HEADS = 12
FFN_UNITS = 3072
LAYOUT_WIDTH = 192
LAYOUT_UNITS = 768
BOXES = 1024
PAGE_SLOTS = 512
PAIRS = 32
LAYERS = 2


EPSILON = 1e-05
CLIP_NORM = 0.01
LEARN_RATE = 10000.0
MOMENTUM = 0.5
AVERAGE_DECAY = 0.5
MASK_FILL = -1e30
PRECISE = lax.Precision.HIGHEST


def small_shapes():
    return [
        (LAYERS, 8, WIDTH),
        (LAYERS, 8, LAYOUT_WIDTH),
        (LAYERS, FFN_UNITS),
        (LAYERS, LAYOUT_UNITS),
        (2, WIDTH),
        (2, LAYOUT_WIDTH),
        (PAGE_SLOTS, WIDTH),
        (PAGE_SLOTS, LAYOUT_WIDTH),
        (2, BOXES // 8, 2 * LAYOUT_WIDTH),
        (LAYOUT_WIDTH, WIDTH),
    ]


def small_views():
    views = []
    offset = 0
    for piece_dims in small_shapes():
        amount = math.prod(piece_dims)
        width = piece_dims[-1] if piece_dims[-1] % 128 == 0 else 2 * piece_dims[-1]
        views.append((offset // 128, amount // width, width))
        offset = offset + amount
    return views, offset // 128


def small_half_rows(share):
    return -(-share // (128 * 32)) * 16


def pack_small(items, dp):
    views, total = small_views()
    share = total * 128 // dp
    rows = 2 * small_half_rows(share)

    def kernel(*refs):
        sources, out_ref, flat = refs[: len(items)], refs[len(items)], refs[len(items) + 1]
        flat[total:, :] = jnp.zeros((flat.shape[0] - total, 128), jnp.float32)
        for source, (start, count, width) in zip(sources, views):
            per = width // 128
            for part in range(per):
                flat[pl.ds(start + part, count, stride=per), :] = source[
                    :, part * 128 : (part + 1) * 128
                ]
        column = lax.broadcasted_iota(jnp.int32, (rows, 128), 1)
        for number in range(dp):
            start, shift = number * share // 128, number * share % 128
            block = flat[pl.ds(start, rows), :]
            if shift:
                after = flat[pl.ds(start + 1, rows), :]
                block = jnp.where(
                    column < 128 - shift,
                    pltpu.roll(block, 128 - shift, 1),
                    pltpu.roll(after, 128 - shift, 1),
                )
            out_ref[number] = block.astype(out_ref.dtype)

    whole = pl.BlockSpec(memory_space=pltpu.VMEM)
    return pl.pallas_call(
        kernel,
        out_shape=jax.ShapeDtypeStruct((dp, rows, 128), jnp.bfloat16),
        in_specs=[whole] * len(items),
        out_specs=whole,
        scratch_shapes=[pltpu.VMEM((total + rows + 8, 128), jnp.float32)],
        cost_estimate=pl.CostEstimate(flops=0, bytes_accessed=2000000, transcendentals=0),
        compiler_params=pltpu.CompilerParams(vmem_limit_bytes=32 * 1024 * 1024),
    )(*[item.reshape(count, width) for item, (start, count, width) in zip(items, views)])


def unpack_small(own, came, places, extra_rows):
    views, total = small_views()
    dp = own.shape[0]
    share = total * 128 // dp
    half = small_half_rows(share)

    def kernel(place_ref, own_ref, came_ref, *refs):
        targets, extra_ref, flat, turned = refs[:-3], refs[-3], refs[-2], refs[-1]
        mine = [(place_ref[dp] == side).astype(jnp.float32) for side in range(2)]
        for number in range(dp):
            start, shift = number * share // 128, number * share % 128
            rows = -(-(share + shift) // 128)
            slot = place_ref[number]
            for side in range(2):
                both = own_ref[slot].astype(jnp.float32), came_ref[slot].astype(jnp.float32)
                whole = jnp.where(mine[side] > 0.5, *both)
                extra_ref[side, number] = whole[half : half + extra_rows].astype(extra_ref.dtype)
                part = whole[:half]
                turned[pl.ds(8 + side * half, half), :] = (
                    pltpu.roll(part, shift, 1) if shift else part
                )
            block = turned[pl.ds(8, rows), :]
            if shift:
                turned[7:8, :] = flat[pl.ds(start, 1), :]
                column = lax.broadcasted_iota(jnp.int32, (rows, 128), 1)
                block = jnp.where(column >= shift, block, turned[pl.ds(7, rows), :])
            flat[pl.ds(start, rows), :] = block
        for target, (start, count, width) in zip(targets, views):
            per = width // 128
            for part in range(per):
                target[:, part * 128 : (part + 1) * 128] = flat[
                    pl.ds(start + part, count, stride=per), :
                ]

    whole = pl.BlockSpec(memory_space=pltpu.VMEM)
    *outs, extra = pl.pallas_call(
        kernel,
        out_shape=[
            jax.ShapeDtypeStruct((count, width), jnp.float32) for start, count, width in views
        ]
        + [jax.ShapeDtypeStruct((2, dp, extra_rows, 128), jnp.bfloat16)],
        in_specs=[pl.BlockSpec(memory_space=pltpu.SMEM), whole, whole],
        out_specs=[whole] * (len(views) + 1),
        scratch_shapes=[
            pltpu.VMEM((total + 8, 128), jnp.float32),
            pltpu.VMEM((2 * half + 16, 128), jnp.float32),
        ],
        cost_estimate=pl.CostEstimate(flops=0, bytes_accessed=2000000, transcendentals=0),
        compiler_params=pltpu.CompilerParams(vmem_limit_bytes=32 * 1024 * 1024),
    )(places, own, came)
    return [item.reshape(piece_dims) for item, piece_dims in zip(outs, small_shapes())], extra


def norm_apply(values, gain_row, bias_row):
    centre = values - jnp.mean(values, axis=-1, keepdims=True)
    spread = jnp.mean(centre * centre, axis=-1, keepdims=True)
    return centre * lax.rsqrt(spread + EPSILON) * gain_row + bias_row


def norm_back(values, gain_row, bias_row, grad_out):
    unused, pullback = jax.vjp(norm_apply, values, gain_row, bias_row)
    return pullback(grad_out)


def gelu_exact(values):
    return jax.nn.gelu(values, approximate=False)


def contract_rows(left, right):
    return lax.dot_general(
        left, right, (((0,), (0,)), ((), ())), preferred_element_type=jnp.float32
    )


def contract_cols(left, right):
    return lax.dot_general(
        left, right, (((1,), (1,)), ((), ())), preferred_element_type=jnp.float32
    )


def heads_view(values, pages):
    return values.reshape(pages, PAGE_SLOTS, HEADS, values.shape[-1] // HEADS)


ROUND_ROWS = 32


def bits_of(size):
    return list(reversed(range(size.bit_length() - 1)))


def hop(values, axis, bit):
    pairs = [(spot, spot ^ (1 << bit)) for spot in range(lax.axis_size(axis))]
    return lax.ppermute(values, axis, pairs)


def own_bit(axis, bit):
    return (lax.axis_index(axis) >> bit) & 1


def routes():
    far = [("dp", bit) for bit in bits_of(lax.axis_size("dp"))]
    high = [("mp", bit) for bit in bits_of(lax.axis_size("mp"))[:-1]]
    core = ("mp", 0)
    return (far[:-1], far[-1], high, core)


def add_low(kept, came):
    return (kept.astype(jnp.float32) + came.astype(jnp.float32)).astype(jnp.bfloat16)


def tie(value, *waits):
    def kernel(*refs):
        pass

    spec = pl.BlockSpec(memory_space=pl.ANY)
    return pl.pallas_call(
        kernel,
        out_shape=jax.ShapeDtypeStruct(value.shape, value.dtype),
        in_specs=[spec] * (1 + len(waits)),
        out_specs=spec,
        input_output_aliases={0: 0},
        cost_estimate=pl.CostEstimate(flops=0, bytes_accessed=0, transcendentals=0),
    )(value, *waits)


def put_in_order(own, came, places):
    slots, rows, width = own.shape

    def kernel(place_ref, own_ref, came_ref, out_ref, sems):
        side = place_ref[slots]

        def copies(half, source):
            return [
                pltpu.make_async_copy(
                    source.at[place_ref[spot]],
                    out_ref.at[half, pl.ds(spot * rows, rows)],
                    sems.at[half, spot],
                )
                for spot in range(slots)
            ]

        for half in range(2):
            for mine, source in ((True, own_ref), (False, came_ref)):

                @pl.when((side == half) == mine)
                def _(half=half, source=source):
                    for copy in copies(half, source):
                        copy.start()

        for half in range(2):
            for copy in copies(half, own_ref):
                copy.wait()

    anywhere = pl.BlockSpec(memory_space=pl.ANY)
    return pl.pallas_call(
        kernel,
        out_shape=jax.ShapeDtypeStruct((2, slots * rows, width), own.dtype),
        in_specs=[pl.BlockSpec(memory_space=pltpu.SMEM), anywhere, anywhere],
        out_specs=pl.BlockSpec(memory_space=pltpu.VMEM),
        scratch_shapes=[pltpu.SemaphoreType.DMA((2, slots))],
        cost_estimate=pl.CostEstimate(
            flops=0, bytes_accessed=2 * slots * rows * width, transcendentals=0
        ),
        compiler_params=pltpu.CompilerParams(vmem_limit_bytes=16 * 1024 * 1024),
    )(places, own, came)


def embed_kernel(
    coords, embedded, text_pos, layout_pos, tables, text_emb, layout_emb, *outs
):
    text_pre, layout_pre, text, layout = outs
    quarter = LAYOUT_WIDTH // 4
    low = jnp.bfloat16
    row = lax.broadcasted_iota(jnp.int32, (PAGE_SLOTS, BOXES // 8), 1)
    lanes = lax.broadcasted_iota(jnp.int32, (PAGE_SLOTS, 8 * quarter), 1) // quarter
    fold_in = lax.broadcasted_iota(jnp.int32, (8 * quarter, LAYOUT_WIDTH), 0) % quarter
    fold_out = lax.broadcasted_iota(jnp.int32, (8 * quarter, LAYOUT_WIDTH), 1)
    looked = jnp.zeros((PAGE_SLOTS, LAYOUT_WIDTH), jnp.float32)
    for number in range(4):
        spot = coords[:, number : number + 1]
        marks = (spot // 8 == row).astype(jnp.float32).astype(low)
        wide = jnp.dot(
            marks, tables[number % 2].astype(low), preferred_element_type=jnp.float32
        )
        kept = jnp.where(spot % 8 == lanes, wide, 0.0).astype(low)
        fold = (fold_in + number * quarter == fold_out).astype(jnp.float32).astype(low)
        looked = looked + jnp.dot(kept, fold, preferred_element_type=jnp.float32)
    layout_pre[...] = looked + layout_pos[...]
    text_pre[...] = embedded[...] + text_pos[...]
    text[...] = norm_apply(text_pre[...], text_emb[0:1, :], text_emb[1:2, :])
    layout[...] = norm_apply(layout_pre[...], layout_emb[0:1, :], layout_emb[1:2, :])


def norm_grads(values, gain, grad):
    centre = values - jnp.mean(values, axis=-1, keepdims=True)
    scale = lax.rsqrt(jnp.mean(centre * centre, axis=-1, keepdims=True) + EPSILON)
    unit = centre * scale
    lifted = grad * gain
    inner = jnp.mean(lifted * unit, axis=-1, keepdims=True)
    back = scale * (lifted - jnp.mean(lifted, axis=-1, keepdims=True) - unit * inner)
    sums = [jnp.sum(item, 0, keepdims=True) for item in (grad * unit, grad)]
    return back, jnp.concatenate(sums, 0)


def embed_back_kernel(coords, text_pre, layout_pre, text_emb, layout_emb, *refs):
    grad_text, grad_layout, text_back, layout_back, text_sums, layout_sums, boxes = refs
    low = jnp.bfloat16
    quarter = LAYOUT_WIDTH // 4
    text_back[...], text_sums[...] = norm_grads(text_pre[...], text_emb[0:1, :], grad_text[...])
    looked, layout_sums[...] = norm_grads(
        layout_pre[...], layout_emb[0:1, :], grad_layout[...]
    )
    layout_back[...] = looked
    high, rest = split_high(looked)
    row = lax.broadcasted_iota(jnp.int32, (PAGE_SLOTS, BOXES // 8), 1)
    lanes = lax.broadcasted_iota(jnp.int32, (PAGE_SLOTS, 8 * quarter), 1) // quarter
    fold_in = lax.broadcasted_iota(jnp.int32, (8 * quarter, LAYOUT_WIDTH), 0) % quarter
    fold_out = lax.broadcasted_iota(jnp.int32, (8 * quarter, LAYOUT_WIDTH), 1)
    boxes[...] = jnp.zeros_like(boxes)
    for number in range(4):
        spot = coords[:, number : number + 1]
        marks = (spot // 8 == row).astype(jnp.float32).astype(low)
        fold = (fold_in + number * quarter == fold_out).astype(jnp.float32).astype(low)
        wide = contract_cols(high, fold) + contract_cols(rest, fold)
        kept = jnp.where(spot % 8 == lanes, wide, 0.0)
        boxes[number % 2] += add_rows(marks, kept)


def embed_back(*operands):
    whole = pl.BlockSpec(memory_space=pltpu.VMEM)
    shapes = [
        (PAGE_SLOTS, WIDTH),
        (PAGE_SLOTS, LAYOUT_WIDTH),
        (2, WIDTH),
        (2, LAYOUT_WIDTH),
        (2, BOXES // 8, 2 * LAYOUT_WIDTH),
    ]
    return pl.pallas_call(
        embed_back_kernel,
        out_shape=[jax.ShapeDtypeStruct(shape, jnp.float32) for shape in shapes],
        in_specs=[whole] * len(operands),
        out_specs=[whole] * len(shapes),
        cost_estimate=pl.CostEstimate(flops=0, bytes_accessed=2000000, transcendentals=0),
        compiler_params=pltpu.CompilerParams(vmem_limit_bytes=32 * 1024 * 1024),
    )(*operands)


def embed_streams(*operands):
    whole = pl.BlockSpec(memory_space=pltpu.VMEM)
    return pl.pallas_call(
        embed_kernel,
        out_shape=[
            jax.ShapeDtypeStruct((PAGE_SLOTS, width), jnp.float32)
            for width in (WIDTH, LAYOUT_WIDTH) * 2
        ],
        in_specs=[whole] * len(operands),
        out_specs=[whole] * 4,
        cost_estimate=pl.CostEstimate(flops=0, bytes_accessed=2000000, transcendentals=0),
        compiler_params=pltpu.CompilerParams(vmem_limit_bytes=24 * 1024 * 1024),
    )(*operands)


def mats_kernel(side, rows, query, keys, values, att, first, sent_ref, kept_ref, result):
    step = pl.program_id(0)
    half = jnp.where(step < 2, 1 - side[0], side[0])
    cases = ((rows, query), (rows, keys), (rows, values), (att, first))
    for number, (left, right) in enumerate(cases):

        @pl.when(half * 2 + step % 2 == number)
        def _(left=left, right=right):
            result[...] = contract_rows(left[...], right[...])

    def store(target):
        blocks = result[...].astype(target.dtype).reshape(target.shape[0], -1, WIDTH)
        target[:, : blocks.shape[1], :] = blocks

    @pl.when(step < 2)
    def _():
        store(sent_ref)

    @pl.when(step >= 2)
    def _():
        store(kept_ref)


def mats_sums(side, operands, padded):
    dp = lax.axis_size("dp")
    whole = pl.BlockSpec((PAGE_SLOTS, WIDTH), lambda step: (0, 0))
    shape = jax.ShapeDtypeStruct((dp, padded, 2 * WIDTH), jnp.bfloat16)
    return pl.pallas_call(
        mats_kernel,
        grid=(4,),
        in_specs=[pl.BlockSpec(memory_space=pltpu.SMEM)] + [whole] * 6,
        out_specs=[
            pl.BlockSpec((dp, padded, WIDTH), lambda step: (0, 0, jnp.minimum(step, 1))),
            pl.BlockSpec((dp, padded, WIDTH), lambda step: (0, 0, jnp.maximum(step - 2, 0))),
        ],
        out_shape=[shape, shape],
        scratch_shapes=[pltpu.VMEM((WIDTH, WIDTH), jnp.float32)],
        cost_estimate=pl.CostEstimate(
            flops=2 * PAGE_SLOTS * WIDTH * WIDTH, bytes_accessed=4000000, transcendentals=0
        ),
        compiler_params=pltpu.CompilerParams(vmem_limit_bytes=32 * 1024 * 1024),
    )(side, *operands)


def take_extra(pieces, rows):
    slots, total, width = pieces[0].shape

    def kernel(*refs):
        out_ref, sems = refs[-2], refs[-1]
        copies = [
            pltpu.make_async_copy(
                ref.at[:, pl.ds(rows, total - rows)],
                out_ref.at[pl.ds(number * slots, slots)],
                sems.at[number],
            )
            for number, ref in enumerate(refs[:-2])
        ]
        for copy in copies:
            copy.start()
        for copy in copies:
            copy.wait()

    return pl.pallas_call(
        kernel,
        out_shape=jax.ShapeDtypeStruct((slots * len(pieces), total - rows, width), pieces[0].dtype),
        in_specs=[pl.BlockSpec(memory_space=pl.ANY)] * len(pieces),
        out_specs=pl.BlockSpec(memory_space=pltpu.VMEM),
        scratch_shapes=[pltpu.SemaphoreType.DMA((len(pieces),))],
        cost_estimate=pl.CostEstimate(flops=0, bytes_accessed=500000, transcendentals=0),
    )(*pieces)


HEAD_PAIRS = HEADS // 2
TEXT_HEAD = WIDTH // HEADS
LAYOUT_HEAD = LAYOUT_WIDTH // HEADS


def head_of(text_ref, layout_ref, head, scaled=False):
    text = text_ref[:, head * TEXT_HEAD : (head + 1) * TEXT_HEAD]
    layout = layout_ref[:, head * LAYOUT_HEAD : (head + 1) * LAYOUT_HEAD]
    if scaled:
        text_scale, layout_scale = scale_pair()
        text = (text.astype(jnp.float32) * text_scale).astype(text.dtype)
        layout = (layout.astype(jnp.float32) * layout_scale).astype(layout.dtype)
    return jnp.concatenate([text, layout], 1)


def store_heads(text_ref, layout_ref, both):
    text_ref[...] = jnp.concatenate([item[:, :TEXT_HEAD] for item in both], 1).astype(
        text_ref.dtype
    )
    layout = jnp.concatenate([item[:, TEXT_HEAD:] for item in both], 1).astype(layout_ref.dtype)
    width = layout.shape[1]
    for pair in range(HEAD_PAIRS):

        @pl.when(pl.program_id(0) == pair)
        def _(pair=pair):
            layout_ref[:, pair * width : (pair + 1) * width] = layout


def own_pair(sources, targets):
    width = targets[0].shape[1]
    for pair in range(HEAD_PAIRS):

        @pl.when(pl.program_id(0) == pair)
        def _(pair=pair):
            for source, target in zip(sources, targets):
                target[...] = source[:, pair * width : (pair + 1) * width]


def attend_kernel(length, qt, kt, vt, *refs):
    out_t, out_l, lse, ql, kl, vl = refs[3:]
    own_pair(refs[:3], (ql, kl, vl))
    live = lax.broadcasted_iota(jnp.int32, (PAGE_SLOTS, PAGE_SLOTS), 1) < length[0]
    outs = []
    for head in range(2):
        query, keys = head_of(qt, ql, head, True), head_of(kt, kl, head)
        scores = jnp.where(live, contract_cols(query, keys), MASK_FILL)
        peak = jnp.max(scores, 1, keepdims=True)
        expo = jnp.exp(scores - peak)
        total = jnp.sum(expo, 1, keepdims=True)
        probs = (expo * (1.0 / total)).astype(jnp.bfloat16)
        outs.append(
            jnp.dot(probs, head_of(vt, vl, head), preferred_element_type=jnp.float32)
        )
        lse[0, :, head : head + 1] = peak + jnp.log(total)
    store_heads(out_t, out_l, outs)


def attend_back_kernel(length, qt, kt, vt, got, *refs):
    lse, dqt, dkt, dvt, dql, dkl, dvl, ql, kl, vl, gol = refs[4:]
    own_pair(refs[:4], (ql, kl, vl, gol))
    text_scale, layout_scale = scale_pair()
    live = lax.broadcasted_iota(jnp.int32, (PAGE_SLOTS, PAGE_SLOTS), 0) < length[0]
    column = lax.broadcasted_iota(jnp.int32, (1, TEXT_HEAD + LAYOUT_HEAD), 1)
    scales = jnp.where(column < TEXT_HEAD, text_scale, layout_scale)
    grads_q, grads_k, grads_v = [], [], []
    for head in range(2):
        query, keys = head_of(qt, ql, head, True), head_of(kt, kl, head)
        values, grad = head_of(vt, vl, head), head_of(got, gol, head)
        scores = jnp.where(live, contract_cols(keys, query), MASK_FILL)
        probs = jnp.exp(scores - lse[0, head : head + 1, :])
        grad_probs = contract_cols(values, grad)
        shift = jnp.sum(probs * grad_probs, 0, keepdims=True)
        grad_scores = (probs * (grad_probs - shift)).astype(jnp.bfloat16)
        grads_v.append(
            jnp.dot(probs.astype(jnp.bfloat16), grad, preferred_element_type=jnp.float32)
        )
        grads_k.append(jnp.dot(grad_scores, query, preferred_element_type=jnp.float32))
        grads_q.append(contract_rows(grad_scores, keys) * scales)
    store_heads(dqt, dql, grads_q)
    store_heads(dkt, dkl, grads_k)
    store_heads(dvt, dvl, grads_v)


def pair_specs():
    text = pl.BlockSpec((PAGE_SLOTS, 2 * TEXT_HEAD), lambda step: (0, step))
    layout = pl.BlockSpec((PAGE_SLOTS, LAYOUT_WIDTH), lambda step: (0, 0))
    return text, layout, pltpu.VMEM((PAGE_SLOTS, 2 * LAYOUT_HEAD), jnp.bfloat16)


def attend(text_qkv, layout_qkv, lengths):
    text, layout, pair = pair_specs()
    low = jnp.bfloat16
    out_t, out_l, lse = pl.pallas_call(
        attend_kernel,
        grid=(HEAD_PAIRS,),
        in_specs=[pl.BlockSpec(memory_space=pltpu.SMEM)] + [text] * 3 + [layout] * 3,
        out_specs=[text, layout, pl.BlockSpec((1, PAGE_SLOTS, 2), lambda step: (step, 0, 0))],
        out_shape=[
            jax.ShapeDtypeStruct((PAGE_SLOTS, WIDTH), low),
            jax.ShapeDtypeStruct((PAGE_SLOTS, LAYOUT_WIDTH), low),
            jax.ShapeDtypeStruct((HEAD_PAIRS, PAGE_SLOTS, 2), jnp.float32),
        ],
        scratch_shapes=[pair] * 3,
        cost_estimate=pl.CostEstimate(
            flops=4000000000, bytes_accessed=2000000, transcendentals=100000
        ),
        compiler_params=pltpu.CompilerParams(vmem_limit_bytes=24 * 1024 * 1024),
    )(lengths, *text_qkv, *layout_qkv)
    return (out_t, out_l, lse.transpose(0, 2, 1))


def attend_back(text_qkv, layout_qkv, lengths, lse, text_grad, layout_grad):
    text, layout, pair = pair_specs()
    low = jnp.bfloat16
    text_out = jax.ShapeDtypeStruct((PAGE_SLOTS, WIDTH), low)
    layout_out = jax.ShapeDtypeStruct((PAGE_SLOTS, LAYOUT_WIDTH), low)
    outs = pl.pallas_call(
        attend_back_kernel,
        grid=(HEAD_PAIRS,),
        in_specs=[pl.BlockSpec(memory_space=pltpu.SMEM)]
        + [text] * 4
        + [layout] * 4
        + [pl.BlockSpec((1, 2, PAGE_SLOTS), lambda step: (step, 0, 0))],
        out_specs=[text] * 3 + [layout] * 3,
        out_shape=[text_out] * 3 + [layout_out] * 3,
        scratch_shapes=[pair] * 4,
        cost_estimate=pl.CostEstimate(
            flops=5000000000, bytes_accessed=3000000, transcendentals=100000
        ),
        compiler_params=pltpu.CompilerParams(vmem_limit_bytes=32 * 1024 * 1024),
    )(lengths, *text_qkv, text_grad, *layout_qkv, layout_grad, lse)
    return (list(outs[:3]), list(outs[3:]))


ERF_TERMS = (0.254829592, -0.284496736, 1.421413741, -1.453152027, 1.061405429)


def gelu_pair(values):
    size = jnp.abs(values)
    base = 1.0 / (1.0 + (0.3275911 / math.sqrt(2.0)) * size)
    series = ERF_TERMS[4]
    for term in reversed(ERF_TERMS[:4]):
        series = series * base + term
    bell = jnp.exp(values * values * -0.5)
    tail = 0.5 * series * base * bell
    share = jnp.where(values < 0.0, tail, 1.0 - tail)
    return (values * share, share + values * bell * (1.0 / math.sqrt(2.0 * math.pi)))


def load_units(pieces_in, pieces_out, rows, buffers, sems, chunks):
    per = len(pieces_in) // chunks
    slots = pieces_in[0].shape[0]
    step = pl.program_id(0)

    def copies(turn):
        made = []
        for number in range(per):
            for side, pieces in enumerate((pieces_in, pieces_out)):
                made.append(
                    pltpu.make_async_copy(
                        pieces[turn * per + number].at[:, pl.ds(0, rows)],
                        buffers[side].at[turn % 2, pl.ds(number * slots, slots)],
                        sems.at[turn % 2, 2 * number + side],
                    )
                )
        return made

    for turn in range(chunks):

        @pl.when(step == turn)
        def _(turn=turn):
            if turn == 0:
                for copy in copies(0):
                    copy.start()
            if turn + 1 < chunks:
                for copy in copies(turn + 1):
                    copy.start()
            for copy in copies(turn):
                copy.wait()

    slot = step % 2
    return [buffer[slot].reshape(-1, buffer.shape[-1]) for buffer in buffers]


def unit_plan(units, chunk, rows, chunks):
    width = units[0][0].shape[-1] if rows else units[0].shape[-1]
    if not rows:
        unit = pl.BlockSpec((chunk, width), lambda step: (step, 0))
        return list(units), [unit, unit], []
    anywhere = pl.BlockSpec(memory_space=pl.ANY)
    operands = list(units[0]) + list(units[1])
    buffer = pltpu.VMEM((2, chunk // rows, rows, width), jnp.bfloat16)
    sems = pltpu.SemaphoreType.DMA((2, len(operands) // chunks))
    return operands, [anywhere] * len(operands), [buffer, buffer, sems]


def take_units(refs, scratch, rows, chunks):
    if not rows:
        return [ref[...] for ref in refs]
    half = len(refs) // 2
    return load_units(refs[:half], refs[half:], rows, scratch[:2], scratch[2], chunks)


def ffn_kernel(rows, chunks, count, rows_ref, bias_ref, *refs):
    hidden_ref, slope_ref, part_ref = refs[count : count + 3]
    units_in, units_out = take_units(refs[:count], refs[count + 3 :], rows, chunks)

    @pl.when(pl.program_id(0) == 0)
    def _():
        part_ref[...] = jnp.zeros_like(part_ref)

    step = PAGE_SLOTS // 2
    for number in range(2):
        span = pl.ds(number * step, step)
        pre_act = contract_cols(rows_ref[span, :], units_in) + bias_ref[...]
        hidden, slope = gelu_pair(pre_act)
        hidden = hidden.astype(jnp.bfloat16)
        hidden_ref[span, :] = hidden
        slope_ref[span, :] = slope.astype(jnp.bfloat16)
        part_ref[span, :] += jnp.dot(hidden, units_out, preferred_element_type=jnp.float32)


def ffn_front(rows_in, units, bias_in, chunks, rows):
    slots, width = rows_in.shape
    total = bias_in.shape[0]
    chunk = total // chunks
    whole = pl.BlockSpec((slots, width), lambda step: (0, 0))
    piece = pl.BlockSpec((slots, chunk), lambda step: (0, step))
    operands, specs, scratch = unit_plan(units, chunk, rows, chunks)
    return pl.pallas_call(
        functools.partial(ffn_kernel, rows, chunks, len(operands)),
        grid=(chunks,),
        in_specs=[whole, pl.BlockSpec((1, chunk), lambda step: (0, step))] + specs,
        out_specs=[piece, piece, whole],
        out_shape=[
            jax.ShapeDtypeStruct((slots, total), jnp.bfloat16),
            jax.ShapeDtypeStruct((slots, total), jnp.bfloat16),
            jax.ShapeDtypeStruct((slots, width), jnp.float32),
        ],
        scratch_shapes=scratch,
        cost_estimate=pl.CostEstimate(
            flops=slots * width * total,
            bytes_accessed=total * (width + slots),
            transcendentals=0,
        ),
        compiler_params=pltpu.CompilerParams(vmem_limit_bytes=40 * 1024 * 1024),
    )(rows_in, bias_in[None], *operands)


def tail_route(flip):
    far, near, high, core = routes()
    return (high + [near] if flip else [near] + high) + [core]


def key_mask(key, axis):
    return sum(1 << bit for name, bit in key if name == axis)


class Spread:
    def __init__(self, block, joined, apart):
        self.joined, self.apart = list(joined), list(apart)
        self.masks = [frozenset()]
        self.held, self.came = block[None], None
        self.pieces = None

    def join(self, wait):
        if self.came is None:
            self.held = self.held if wait is None else tie(self.held, wait)
        else:
            came = self.came if wait is None else tie(self.came, wait)
            self.held = jnp.concatenate([self.held, came], 0)
        return self.held

    def advance(self, wait=None):
        if self.joined:
            step = self.joined.pop(0)
            held = self.join(wait)
            self.sent = [held]
            self.came = hop(held, *step)
            self.masks = self.masks + [mask | {step} for mask in self.masks]
            return self.came
        step = self.apart.pop(0)
        if self.pieces is None:
            self.pieces = {frozenset(): self.join(wait)}
            wait = None
        self.sent = []
        for key, piece in list(self.pieces.items()):
            piece = piece if wait is None else tie(piece, wait)
            self.sent.append(piece)
            came = hop(piece, *step)
            self.pieces[key] = piece
            self.pieces[key | {step}] = came
        return came


def half_spread(own, near_first=False):
    far, near, high, core = routes()
    return Spread(own, [near] + far if near_first else far + [near], [core])


def half_parts(chain):
    core = routes()[3]
    spot = lax.axis_index("dp")
    masks = [key_mask(mask, "dp") for mask in chain.masks]
    slot_of = {mask: number for number, mask in enumerate(masks)}
    table = jnp.array([slot_of[number] for number in range(len(masks))], jnp.int32)
    numbers = jnp.arange(len(masks))
    marks = (spot ^ numbers)[:, None] == numbers[None, :]
    places = jnp.sum(jnp.where(marks, table[None, :], 0), 1, dtype=jnp.int32)
    places = jnp.concatenate([places, own_bit(*core).astype(jnp.int32)[None]])
    return chain.pieces[frozenset()], chain.pieces[frozenset([core])], places


def unit_spread(block, flip):
    return Spread(block, routes()[0], tail_route(flip))


def unit_keys():
    far, near, high, core = routes()
    keys = [frozenset()]
    for step in [near] + list(reversed(high)) + [core]:
        keys = keys + [key | {step} for key in keys]
    return keys


def unit_result(chain):
    return [chain.pieces[key] for key in unit_keys()]


def unit_blocks():
    far = [frozenset()]
    for step in routes()[0]:
        far = far + [mask | {step} for mask in far]
    masks = [key | mask for key in unit_keys() for mask in far]
    spots = jnp.array([key_mask(mask, "dp") for mask in masks], jnp.int32)
    lanes = jnp.array([key_mask(mask, "mp") for mask in masks], jnp.int32)
    lanes, spots = lanes ^ lax.axis_index("mp"), spots ^ lax.axis_index("dp")
    return lanes * lax.axis_size("dp") + spots


class UnitSum:
    def __init__(self, kept, sent, flip):
        far, near, high, core = routes()
        self.order = high + [near]
        self.left = list(reversed(tail_route(flip)[:-1])) + list(reversed(far))
        shape = (2,) * len(self.order) + (lax.axis_size("dp") // 2,) + kept.shape[1:]
        self.sent = sent
        self.kept, self.came = kept.reshape(shape), hop(sent, *core).reshape(shape)

    def half(self, values, side, where):
        if where is not None:
            return lax.index_in_dim(values, side, where, keepdims=False)
        size = values.shape[0] // 2
        return values[side * size : (side + 1) * size]

    def advance(self):
        step = self.left.pop(0)
        where = self.order.index(step) if step in self.order else None
        if where is not None:
            self.order.remove(step)
        sent, kept = [
            add_low(self.half(self.kept, side, where), self.half(self.came, side, where))
            for side in (1, 0)
        ]
        self.sent = sent
        self.kept, self.came = kept, hop(sent, *step)
        return self.sent

    def finish(self):
        while self.left:
            self.advance()
        return (self.kept.astype(jnp.float32) + self.came.astype(jnp.float32))[0]


def to_rows(values):
    flat = values.reshape(values.shape[0], -1)
    flat = jnp.pad(flat, ((0, 0), (0, -flat.shape[1] % WIDTH)))
    return flat.reshape(values.shape[0], -1, WIDTH)


def from_rows(values, units):
    flat = values.reshape(values.shape[0], -1)[:, : units * 2 * LAYOUT_WIDTH]
    return flat.reshape(-1, 2 * LAYOUT_WIDTH)


class HalfSum:
    def __init__(self, sent, kept):
        far, near, high, core = routes()
        self.order = far + [near]
        self.left = [near] + list(reversed(far)) + high + [core]
        shape = (2,) * len(self.order) + sent.shape[1:]
        self.sent = sent
        self.kept, self.came = kept.reshape(shape), hop(sent, *core).reshape(shape)

    def advance(self):
        far, near, high, core = routes()
        step = self.left.pop(0)
        if step == core or step in high:
            self.kept = self.sent = add_low(self.kept, self.came)
            self.came = hop(self.kept, *step)
        else:
            where = self.order.index(step)
            self.order.remove(step)
            mine = own_bit(*step)

            def side(values, number):
                return lax.dynamic_index_in_dim(values, number, where, keepdims=False)

            sent = add_low(side(self.kept, 1 - mine), side(self.came, 1 - mine))
            kept = add_low(side(self.kept, mine), side(self.came, mine))
            self.sent = sent
            self.kept, self.came = kept, hop(sent, *step)
        return self.sent

    def finish(self):
        while self.left:
            self.advance()
        first = own_bit(*routes()[3]) == 0
        own, other = self.kept, self.came
        return jnp.stack([jnp.where(first, own, other), jnp.where(first, other, own)]).astype(
            jnp.float32
        )


def own_half(values):
    half = values.shape[-1] // 2
    return jnp.where(own_bit("mp", 0) == 0, values[..., :half], values[..., half:])


def sum_everywhere(values):
    for axis in ("mp", "dp"):
        size = lax.axis_size(axis)

        def jump(mask):
            pairs = [(spot, spot ^ mask) for spot in range(size)]
            return lax.ppermute(values, axis, pairs)

        steps = [1 << bit for bit in bits_of(size)]
        for number in range(0, len(steps), 2):
            pair = steps[number : number + 2]
            if len(pair) == 2:
                near, far, both = jump(pair[0]), jump(pair[1]), jump(pair[0] | pair[1])
                values = (values + near) + (far + both)
            else:
                values = values + jump(pair[0])
    return values


def show_all(values):
    everywhere = ("dp", "mp")
    count = lax.axis_size("dp") * lax.axis_size("mp")
    return lax.all_to_all(
        jnp.broadcast_to(values[None], (count,) + values.shape), everywhere, 0, 0, tiled=True
    )


def trade(values):
    return lax.all_to_all(values, ("dp", "mp"), 0, 0, tiled=True)


def project_qkv(rows_low, mats, vectors, width):
    joined = jnp.dot(rows_low, mats[0], preferred_element_type=jnp.float32)
    query = (joined[:, :width] + vectors[0]).astype(jnp.bfloat16)
    keys = joined[:, width:].astype(jnp.bfloat16)
    values = jnp.dot(rows_low, mats[1][:, :width], preferred_element_type=jnp.float32)
    return (query, keys, (values + vectors[1]).astype(jnp.bfloat16))


def scale_pair():
    return (1.0 / math.sqrt(WIDTH // HEADS), 1.0 / math.sqrt(LAYOUT_WIDTH // HEADS))


def project_back(mats, grads, width):
    first = jnp.concatenate(grads[:2], 1)
    rows_grad = contract_cols(first, mats[0]) + contract_cols(grads[2], mats[1][:, :width])
    return (
        rows_grad,
        jnp.sum(grads[0], 0, dtype=jnp.float32),
        jnp.sum(grads[2], 0, dtype=jnp.float32),
    )


def ffn_back_kernel(
    rows_of, chunks, count, rows_ref, grad_ref, hidden_ref, slope_ref, extra_ref, *refs
):
    part_ref, bias_ref, *sums = refs[count : count + 6]
    units_in, units_out = take_units(refs[:count], refs[count + 6 :], rows_of, chunks)
    step, last = pl.program_id(0), chunks // 2
    rows, grad = rows_ref[...], grad_ref[...]
    grad_hidden = contract_cols(grad, units_out)
    grad_pre = grad_hidden * slope_ref[...].astype(jnp.float32)
    grad_low = grad_pre.astype(jnp.bfloat16)
    bias_ref[...] = jnp.sum(grad_low.astype(jnp.float32), 0, keepdims=True)

    @pl.when(step == 0)
    def _():
        part_ref[...] = jnp.zeros_like(part_ref)

    part_ref[...] += jnp.dot(grad_low, units_in, preferred_element_type=jnp.float32)
    results = [contract_rows(grad_low, rows), contract_rows(hidden_ref[...], grad)]

    def store(targets):
        for target, result in zip(targets, results):
            if len(target.shape) == 2:
                target[...] = result.astype(target.dtype)
            else:
                blocks = result.astype(target.dtype).reshape(target.shape[0], -1, rows.shape[1])
                target[:, : blocks.shape[1], :] = blocks
                if target.shape[1] > blocks.shape[1]:
                    target[:, blocks.shape[1] :, :] = extra_ref[...]

    @pl.when(step < last)
    def _():
        store(sums[:2])

    @pl.when(step >= last)
    def _():
        store(sums[2:])


def ffn_back(rows_in, units, slope, hidden, grad_rows, chunks, slot_rows, extra):
    slots, width = rows_in.shape
    total = hidden.shape[1]
    chunk, half = total // chunks, chunks // 2
    whole = pl.BlockSpec((slots, width), lambda step: (0, 0))
    piece = pl.BlockSpec((slots, chunk), lambda step: (0, step))
    operands, specs, scratch = unit_plan(
        units, chunk, slot_rows[0] if slot_rows else None, chunks
    )

    def first(step):
        return jnp.minimum(step, half - 1)

    def second(step):
        return jnp.maximum(step - half, 0)

    turns = (first, first, second, second)
    if slot_rows is None:
        shapes = [(total // 2, width)] * 4
        sum_specs = [
            pl.BlockSpec((chunk, width), lambda step, turn=turn: (turn(step), 0)) for turn in turns
        ]
        extra_spec = pl.BlockSpec(memory_space=pltpu.VMEM)
    else:
        rows, padded = slot_rows
        heights = [padded, rows] * 2
        shapes = [(total // (2 * rows), height, width) for height in heights]
        sum_specs = [
            pl.BlockSpec((chunk // rows, height, width), lambda step, turn=turn: (turn(step), 0, 0))
            for height, turn in zip(heights, turns)
        ]
        extra_spec = pl.BlockSpec((chunk // rows, padded - rows, width), lambda step: (step, 0, 0))
    return pl.pallas_call(
        functools.partial(
            ffn_back_kernel, slot_rows[0] if slot_rows else None, chunks, len(operands)
        ),
        grid=(chunks,),
        in_specs=[whole, whole, piece, piece, extra_spec] + specs,
        out_specs=[whole, pl.BlockSpec((1, chunk), lambda step: (0, step))] + sum_specs,
        out_shape=[
            jax.ShapeDtypeStruct((slots, width), jnp.float32),
            jax.ShapeDtypeStruct((1, total), jnp.float32),
        ]
        + [jax.ShapeDtypeStruct(shape, jnp.bfloat16) for shape in shapes],
        scratch_shapes=scratch,
        cost_estimate=pl.CostEstimate(
            flops=2 * slots * width * total,
            bytes_accessed=2 * total * (width + slots),
            transcendentals=0,
        ),
        compiler_params=pltpu.CompilerParams(vmem_limit_bytes=48 * 1024 * 1024),
    )(rows_in, grad_rows, hidden, slope, extra, *operands)


def stream_forward(rows, att, mats, units, bias_in, vec, unit_rows, hook):
    width = rows.shape[1]
    first = (
        rows + jnp.dot(att, mats[1][:, width:], preferred_element_type=jnp.float32) + vec[2]
    )
    mid = norm_apply(first, vec[3], vec[4])
    mid_low = hook(mid.astype(jnp.bfloat16))
    chunks = 2 if width == WIDTH else 1
    hidden, slope, part = ffn_front(mid_low, units, bias_in, chunks, unit_rows)
    last = mid + part + vec[5]
    return (norm_apply(last, vec[6], vec[7]), (first, mid_low, slope, hidden, last))


def layer_forward(text, layout, weights, lengths, hooks):
    (tm, lm, tb, lb, tv, lv) = weights
    text_low = hooks["low"](text.astype(jnp.bfloat16))
    layout_low = layout.astype(jnp.bfloat16)
    text_qkv = list(project_qkv(text_low, tm, tv, WIDTH))
    layout_qkv = project_qkv(layout_low, lm, lv, LAYOUT_WIDTH)
    text_qkv[0] = hooks["query"](text_qkv[0])
    text_att, layout_att, log_total = attend(text_qkv, layout_qkv, lengths)
    text_att = hooks["att"](text_att)
    tu, lu = hooks["units"]()
    count = lax.axis_size("dp") * lax.axis_size("mp")
    text_new, text_kept = stream_forward(
        text, text_att, tm, tu, tb, tv, FFN_UNITS // count, hooks["mid"]
    )
    layout_new, layout_kept = stream_forward(
        layout, layout_att, lm, lu, lb, lv, None, lambda value: value
    )
    cache = (
        text_low,
        layout_low,
        text_qkv,
        layout_qkv,
        log_total,
        text_att,
        layout_att,
        text_kept,
        layout_kept,
    )
    return (text_new, layout_new, cache, (tu, lu))


def stream_back(kept, att, mats, units, vec, grad, slot_rows, hook, extra):
    first, mid_low, slope, hidden, last = kept
    width = first.shape[1]
    last_g, gain2, bias2 = norm_back(last, vec[6], vec[7], grad)
    in_grad, bias_in_g, *unit_grads = ffn_back(
        mid_low,
        units,
        slope,
        hidden,
        hook(last_g.astype(jnp.bfloat16)),
        4 if width == WIDTH else 2,
        slot_rows,
        extra,
    )
    first_g, gain1, bias1 = norm_back(first, vec[3], vec[4], last_g + in_grad)
    first_low = first_g.astype(jnp.bfloat16)
    att_grad = contract_cols(first_low, mats[1][:, width:]).astype(jnp.bfloat16)
    vec_tail = [jnp.sum(first_g, 0), gain1, bias1, jnp.sum(last_g, 0), gain2, bias2]
    return (first_g, att_grad, first_low, unit_grads, bias_in_g[0], vec_tail)


def layer_backward(cache, grad_text, grad_layout, weights, lengths, plan):
    (
        text_low,
        layout_low,
        text_qkv,
        layout_qkv,
        log_total,
        text_att,
        layout_att,
        text_kept,
        layout_kept,
    ) = cache
    (tm, lm, tu, lu, tb, lb, tv, lv) = weights
    count = lax.axis_size("dp") * lax.axis_size("mp")
    rows = FFN_UNITS // count
    none = jnp.zeros((8, 128), jnp.float32)
    first_l, att_l, out_l, lu_g, lb_g, tail_l = stream_back(
        layout_kept, layout_att, lm, lu, lv, grad_layout, None, lambda value: value, none
    )
    halves = [jnp.concatenate(lu_g[2 * side : 2 * side + 2], 1) for side in range(2)]
    extra = to_rows(jnp.concatenate(halves, 0).reshape(count, -1, 2 * LAYOUT_WIDTH))
    extra = jnp.pad(extra, ((0, 0), (0, -extra.shape[1] % 16), (0, 0)))
    slot_rows = (rows, rows + extra.shape[1])
    first_t, att_t, out_t, tu_g, tb_g, tail_t = stream_back(
        text_kept, text_att, tm, tu, tv, grad_text, slot_rows, plan.before_units, extra
    )
    att_t = plan.after_units(att_t, tu_g)
    text_dqkv, layout_dqkv = attend_back(
        text_qkv, layout_qkv, lengths, log_total, att_t, att_l
    )
    text_dqkv[0] = plan.after_attend(text_dqkv[0])
    plan.after_mats(
        (text_low, *text_dqkv, text_att, out_t), (layout_low, *layout_dqkv, layout_att, out_l)
    )
    rows_t, q_bias_t, v_bias_t = project_back(tm, text_dqkv, WIDTH)
    rows_l, q_bias_l, v_bias_l = project_back(lm, layout_dqkv, LAYOUT_WIDTH)
    grads = (
        tb_g,
        lb_g,
        jnp.stack([q_bias_t, v_bias_t] + tail_t),
        jnp.stack([q_bias_l, v_bias_l] + tail_l),
    )
    return (first_t + rows_t, first_l + rows_l, grads)


class Plan:
    def __init__(self):
        self.units = []
        self.mats = []

    def step(self, value, items):
        for item in items:
            item.came = tie(item.came, value)
        return tie(value, *[item.advance() for item in items])

    def before_units(self, value):
        return self.step(value, self.mats[:1]) if self.mats else value

    def after_units(self, value, grads):
        keep_in, keep_out, send_in, send_out = grads
        self.units.append([UnitSum(keep_in, send_in, False), UnitSum(keep_out, send_out, True)])
        if self.mats:
            return self.step(value, self.units[0] + self.mats[:1])
        return self.step(value, self.units[0])

    def after_attend(self, value):
        if self.mats:
            return self.step(value, self.units[1] + self.mats[:1])
        return value

    def after_mats(self, text, layout):
        dp = lax.axis_size("dp")
        low = jnp.bfloat16
        side = own_bit("mp", 0).astype(jnp.int32)
        rows, query, keys, values, att, first = layout
        first_half = contract_rows(rows, jnp.concatenate([query, keys], 1)).astype(low)
        second_half = jnp.concatenate(
            [contract_rows(rows, values), contract_rows(att, first)], 1
        ).astype(low)
        text_rows = WIDTH // dp
        extras = [
            jnp.where(side == number, second_half, first_half).reshape(dp, -1, 2 * WIDTH)
            for number in range(2)
        ]
        padded = -(-(text_rows + extras[0].shape[1]) // 8) * 8
        pad = ((0, 0), (0, padded - text_rows - extras[0].shape[1]), (0, 0))
        sums = mats_sums(side[None], text, padded)
        sent, kept = [
            lax.dynamic_update_slice(item, jnp.pad(extra, pad), (0, text_rows, 0))
            for item, extra in zip(sums, extras)
        ]
        self.mats.append(HalfSum(sent, kept))

    def between(self, value):
        if len(self.mats) == 1:
            return self.step(tie(value, self.mats[0].sent), self.units[0])
        return self.step(tie(value, self.mats[1].sent), self.units[0] + self.mats[:1])


def split_high(values):
    high = values.astype(jnp.bfloat16)
    return (high, (values - high.astype(jnp.float32)).astype(jnp.bfloat16))


def add_rows(marks, values):
    high, low = split_high(values)
    return contract_rows(marks, high) + contract_rows(marks, low)


def apply_update(master, grad, moment, average, loss_count, factor):
    clipped = grad / loss_count * factor
    moment_new = MOMENTUM * moment + clipped
    master_new = master - LEARN_RATE * (clipped + MOMENTUM * moment_new)
    return (master_new, moment_new, AVERAGE_DECAY * average + (1.0 - AVERAGE_DECAY) * master_new)


def on_device(
    token_ids,
    mlm_targets,
    page_lengths,
    box_coords,
    mlm_positions,
    align_pairs,
    align_labels,
    table,
    text_mats,
    layout_mats,
    text_ffn,
    layout_ffn,
    small_params,
    table_momentum,
    text_mats_momentum,
    layout_mats_momentum,
    text_ffn_momentum,
    layout_ffn_momentum,
    small_momentum,
    table_average,
    text_mats_average,
    layout_mats_average,
    text_ffn_average,
    layout_ffn_average,
    small_average,
):
    lane, spot = lax.axis_index("mp"), lax.axis_index("dp")
    dp, mp = lax.axis_size("dp"), lax.axis_size("mp")
    count = dp * mp
    slots = PAGE_SLOTS
    mask_slots = mlm_positions.shape[1]
    pages = 1
    vocab_rows = table.shape[0]
    low = jnp.bfloat16

    own_ids = lax.dynamic_index_in_dim(token_ids, lane, 0, keepdims=False)
    own_targets = lax.dynamic_index_in_dim(mlm_targets, lane, 0, keepdims=False)
    table_low = table.astype(low)
    own_block = lane * dp + spot
    steps = jnp.arange(slots)
    first_at = jnp.min(
        jnp.where(own_ids[:, None] == own_ids[None, :], steps[None, :], slots), 1
    )
    page_first = first_at == steps
    block_own = own_ids // vocab_rows
    rank = jnp.sum(
        page_first[None, :]
        & (block_own[:, None] == block_own[None, :])
        & (steps[None, :] < first_at[:, None]),
        1,
        dtype=jnp.int32,
    )
    source = (block_own % dp) * mp + block_own // dp
    local_own = own_ids - block_own * vocab_rows
    places = jnp.arange(count * ROUND_ROWS)

    def place_of(turn):
        turn_rank = rank - turn * ROUND_ROWS
        inside = (turn_rank >= 0) & (turn_rank < ROUND_ROWS)
        return jnp.where(inside, source * ROUND_ROWS + turn_rank, -1)

    def requests(turn):
        asked = (place_of(turn)[None, :] == places[:, None]) & page_first[None, :]
        rows = jnp.sum(jnp.where(asked, local_own[None, :] + 1, 0), 1, dtype=jnp.int32) - 1
        return rows.reshape(count, ROUND_ROWS)

    def settle(chains, left):
        for chain in chains:
            while len(chain.joined) + len(chain.apart) > left:
                chain.advance()

    def marks_of(rows):
        return (rows.reshape(-1)[:, None] == jnp.arange(vocab_rows)[None, :]).astype(low)


    def held_marks(turn):
        return (place_of(turn)[:, None] == places[None, :]).astype(low)

    def fetch(turn, marks, so_far):
        sent = jnp.dot(marks, table_low, preferred_element_type=jnp.float32).astype(low)
        came = trade(sent)
        return (
            so_far + jnp.dot(held_marks(turn), came, preferred_element_type=jnp.float32),
            came,
            sent,
        )

    share = small_params.shape[0]
    line = 2 * WIDTH
    half_rows = small_half_rows(share)
    small_pad = jnp.pad(small_params.astype(low), (0, 2 * half_rows * 128 - share))
    small_half = lax.dynamic_slice_in_dim(
        small_pad.reshape(2 * half_rows, 128), (lane & 1) * half_rows, half_rows
    )
    tmats_half = own_half(text_mats.astype(low))
    lmats_half = own_half(layout_mats.astype(low)).reshape(-1, 128)
    extra = jnp.concatenate(
        [small_half, lmats_half, jnp.zeros((-lmats_half.shape[0] % 16, 128), low)], 0
    )
    unit_rows = text_ffn.shape[1]
    layout_units = layout_ffn.shape[1]
    layout_unit_rows = -(-(2 * layout_units * LAYOUT_WIDTH) // WIDTH)
    unit_pad = -layout_unit_rows % 16

    def unit_block(layer_no, part):
        text_part = text_ffn[layer_no, :, part * WIDTH : (part + 1) * WIDTH].astype(low)
        if part:
            return text_part
        return jnp.concatenate(
            [
                text_part,
                to_rows(layout_ffn[layer_no : layer_no + 1].astype(low))[0],
                jnp.zeros((unit_pad, WIDTH), low),
            ],
            0,
        )

    mats_chains = [half_spread(tmats_half[layer_no]) for layer_no in range(LAYERS)]
    extra_chain = half_spread(extra, True)
    unit_chains = [
        [unit_spread(unit_block(layer_no, part), part == 1) for part in range(2)]
        for layer_no in range(LAYERS)
    ]
    far_steps = len(routes()[0])
    told = jnp.concatenate(
        [
            jnp.max(rank, keepdims=True) // ROUND_ROWS + 1,
            page_lengths,
            own_targets,
        ]
    )
    told = jnp.broadcast_to(told[None], (count, mask_slots + 2))
    spare = jnp.zeros((count, -(ROUND_ROWS + mask_slots + 2) % 128), jnp.int32)
    message = jnp.concatenate([requests(0), told, spare], 1)
    mats_chains[0].advance()
    extra_chain.advance()
    extra_chain.advance()
    shown = trade(tie(message, *extra_chain.sent))
    mats_chains[0].advance()
    extra_chain.advance()
    shown = tie(shown, *mats_chains[0].sent, *extra_chain.sent)
    rounds = jnp.max(shown[:, ROUND_ROWS])
    all_lengths = shown[:, ROUND_ROWS + 1]
    all_targets = shown[:, ROUND_ROWS + 2 : ROUND_ROWS + 2 + mask_slots].reshape(-1)

    asked_first = marks_of(shown[:, :ROUND_ROWS])
    embedded, came_first, rows_first = fetch(
        0, asked_first, jnp.zeros((slots, WIDTH), jnp.float32)
    )
    embedded = lax.fori_loop(
        1,
        rounds,
        lambda turn, so_far: fetch(turn, marks_of(trade(requests(turn))), so_far)[0],
        embedded,
    )
    settle(mats_chains[:1], 2)
    mats_chains[0].advance(rows_first)
    settle([extra_chain], 1)
    extra_chain.advance(mats_chains[0].sent[0])
    wait = extra_chain.sent[0]
    for chain in unit_chains[0]:
        chain.advance(wait)
    core_key = frozenset([routes()[3]])
    extra_chain.pieces[core_key] = tie(
        extra_chain.pieces[core_key], *[chain.sent[0] for chain in unit_chains[0]]
    )
    small_parts, lmats_all = unpack_small(*half_parts(extra_chain), lmats_half.shape[0])
    lmats_all = lmats_all.reshape(2, dp, LAYERS, -1, 2 * LAYOUT_WIDTH)
    mats_chains[0].advance(tie(came_first, small_parts[6]))
    for number in range(1, far_steps):
        for chain in unit_chains[0]:
            chain.advance(mats_chains[0].sent[0])
    tmats_first = put_in_order(*half_parts(mats_chains[0]))
    (
        text_vec,
        layout_vec,
        text_bias,
        layout_bias,
        text_emb,
        layout_emb,
        text_pos,
        layout_pos,
        box_table,
        align_mat,
    ) = small_parts

    coords = box_coords[:, 0].T
    text_pre, layout_pre, text, layout = embed_streams(
        coords, embedded, text_pos, layout_pos, box_table, text_emb, layout_emb
    )
    caches = []
    layer_weights = []

    def push(value, chains):
        waits = []
        for chain in chains:
            chain.advance(value)
            waits = waits + chain.sent
        return tie(value, *waits)

    def after(chains, wait):
        for chain in chains:
            chain.advance(wait)

    def hooks_of(layer_no):
        units = unit_chains[layer_no]
        later = layer_no + 1 < LAYERS
        if later:
            next_mats, next_units = mats_chains[layer_no + 1], unit_chains[layer_no + 1]

        def at_low(value):
            if layer_no == 0:
                value = push(value, units)
            if later:
                next_mats.advance(units[1].sent[0])
            return value

        def at_query(value):
            return push(value, units) if layer_no else value

        def at_att(value):
            settle(units, 2)
            pending = [chain for chain in units if len(chain.joined) + len(chain.apart) > 1]
            if pending or later:
                value = push(value, pending + ([next_mats] if later else []))
            after(units, value)
            if later:
                after(next_units, next_mats.sent[0])
            return value

        def at_mid(value):
            return push(value, [next_mats] + next_units) if later else value

        return {
            "low": at_low,
            "query": at_query,
            "att": at_att,
            "mid": at_mid,
            "units": lambda: units_of(layer_no),
        }

    def units_of(layer_no):
        results = [unit_result(chain) for chain in unit_chains[layer_no]]
        layout_both = from_rows(
            take_extra(results[0], unit_rows)[:, :layout_unit_rows], layout_units
        )
        return (results, [layout_both[:, :LAYOUT_WIDTH], layout_both[:, LAYOUT_WIDTH:]])

    slot_marks = (unit_blocks()[:, None] == jnp.arange(count)[None, :]).astype(jnp.float32)
    for layer_no in range(LAYERS):
        if layer_no:
            settle([mats_chains[layer_no]], 1)
            text = push(text, unit_chains[layer_no] + [mats_chains[layer_no]])
            tmats = put_in_order(*half_parts(mats_chains[layer_no]))
        else:
            tmats = tmats_first
        weights = [
            tmats,
            lmats_all[:, :, layer_no].reshape(2, LAYOUT_WIDTH, -1),
            jnp.dot(
                slot_marks, text_bias[layer_no].reshape(count, -1), precision=PRECISE
            ).reshape(-1),
            jnp.dot(
                slot_marks, layout_bias[layer_no].reshape(count, -1), precision=PRECISE
            ).reshape(-1),
            text_vec[layer_no],
            layout_vec[layer_no],
        ]
        text, layout, cache, units = layer_forward(
            text, layout, weights, page_lengths, hooks_of(layer_no)
        )
        weights = weights[:2] + list(units) + weights[2:]
        caches.append(cache)
        layer_weights.append(weights)

    row_index = mlm_positions.reshape(-1)
    live_all = (
        (jnp.arange(mask_slots)[None, :] * slots < mask_slots * all_lengths[:, None])
        .astype(jnp.float32)
        .reshape(-1)
    )
    chosen_marks = (row_index[:, None] == steps[None, :]).astype(low)
    chosen_own = jnp.dot(
        chosen_marks, text.astype(low), preferred_element_type=jnp.float32
    ).astype(low)
    chosen_all = show_all(chosen_own).reshape(count * mask_slots, WIDTH)
    logits = contract_cols(chosen_all, table_low)
    target_local = all_targets - own_block * vocab_rows
    target_in = target_local[:, None] == jnp.arange(vocab_rows)[None, :]
    target_logit = jnp.sum(jnp.where(target_in, logits, 0.0), 1)
    row_peak = jnp.max(logits, axis=1)
    row_total = jnp.sum(jnp.exp(logits - row_peak[:, None]), axis=1)
    stats = show_all(jnp.stack([row_peak, row_total, target_logit]))
    all_peak = jnp.max(stats[:, 0], 0)
    all_total = jnp.sum(stats[:, 1] * jnp.exp(stats[:, 0] - all_peak[None]), 0)
    all_target = jnp.sum(stats[:, 2], 0)
    log_total = all_peak + jnp.log(all_total)
    own_start = (spot * mp + lane) * mask_slots
    live_own = lax.dynamic_slice_in_dim(live_all, own_start, mask_slots)
    own_loss = jnp.sum(
        lax.dynamic_slice_in_dim((log_total - all_target) * live_all, own_start, mask_slots)
    )
    grad_low = (
        (jnp.exp(logits - log_total[:, None]) - target_in.astype(jnp.float32)) * live_all[:, None]
    ).astype(low)
    table_grad = contract_rows(grad_low, chosen_all)
    chosen_parts = trade(jnp.dot(grad_low, table_low, preferred_element_type=jnp.float32).astype(low))
    chosen_grad = jnp.sum(
        chosen_parts.reshape(count, mask_slots, WIDTH).astype(jnp.float32), 0
    )

    first_marks = (align_pairs[0, :, 0][:, None] == steps[None, :]).astype(jnp.float32)
    second_marks = (align_pairs[0, :, 1][:, None] == steps[None, :]).astype(jnp.float32)
    answer = align_labels.reshape(-1).astype(jnp.float32)
    first_rows = jnp.dot(first_marks, text, precision=PRECISE)
    second_rows = jnp.dot(second_marks, layout, precision=PRECISE)

    def pair_loss(text_rows, layout_rows, align_weight):
        right = jnp.dot(layout_rows, align_weight, precision=PRECISE)
        logit = jnp.sum(text_rows * right, axis=-1) / math.sqrt(WIDTH)
        return jnp.sum(jax.nn.softplus(logit) - answer * logit)

    align_part, align_pull = jax.vjp(pair_loss, first_rows, second_rows, align_mat)
    first_back, second_back, align_grad = align_pull(jnp.ones((), jnp.float32))
    grad_text = add_rows(
        jnp.concatenate([first_marks.astype(low), chosen_marks], 0),
        jnp.concatenate([first_back, chosen_grad], 0),
    )
    grad_layout = add_rows(second_marks.astype(low), second_back)

    plan = Plan()
    layer_grads = [None] * LAYERS
    for layer_no in reversed(range(LAYERS)):
        grad_text, grad_layout, layer_grads[layer_no] = layer_backward(
            caches[layer_no], grad_text, grad_layout, layer_weights[layer_no], page_lengths, plan
        )
        grad_text = plan.between(grad_text)

    embed_grad, looked_grad, text_emb_grad, layout_emb_grad, box_grad = embed_back(
        coords, text_pre, layout_pre, text_emb, layout_emb, grad_text, grad_layout
    )
    embed_low = embed_grad.astype(low)

    def give(turn, marks, so_far):
        sent = contract_rows(held_marks(turn), embed_low).astype(low)
        came = trade(sent)
        return (so_far + contract_rows(marks, came), sent, came)

    table_sum, gave_rows, gave_came = give(0, asked_first, table_grad)
    table_sum = lax.fori_loop(
        1,
        rounds,
        lambda turn, so_far: give(turn, marks_of(trade(requests(turn))), so_far)[0],
        table_sum,
    )

    def stacked(member):
        return jnp.stack([layer_grads[layer_no][member] for layer_no in range(LAYERS)])

    def in_order(member):
        return jnp.stack(
            [
                lax.dot_general(
                    slot_marks,
                    layer_grads[layer_no][member].reshape(count, -1),
                    (((0,), (0,)), ((), ())),
                    precision=PRECISE,
                )
                for layer_no in range(LAYERS)
            ]
        )

    small_items = [
        stacked(2),
        stacked(3),
        in_order(0),
        in_order(1),
        text_emb_grad,
        layout_emb_grad,
        embed_grad,
        looked_grad,
        box_grad,
        align_grad,
    ]
    plan.mats[1].advance()
    token = plan.mats[1].sent
    small_items[6] = tie(embed_grad, token, gave_rows)
    small_blocks = pack_small(small_items, dp).reshape(dp, 2, half_rows, 128)
    first = own_bit("mp", 0) == 0
    small_total = HalfSum(
        jnp.where(first, small_blocks[:, 1], small_blocks[:, 0]),
        jnp.where(first, small_blocks[:, 0], small_blocks[:, 1]),
    )
    token = small_total.sent
    outer = plan.units[1]
    turns = outer + [plan.mats[1]] + outer + [small_total, plan.mats[1]] + outer
    turns = turns + [small_total, plan.mats[1]] * 5
    for number, chain in enumerate(turns):
        if chain.left:
            chain.came = tie(chain.came, token)
            chain.advance()
            token = chain.sent
        if number == 2:
            token = tie(gave_came, token)
    small_sum = small_total.finish().reshape(-1)[:share]
    plan.units.reverse()
    plan.mats.reverse()
    mats_sums = [item.finish() for item in plan.mats]
    mats_rows = text_mats.shape[1]
    extra_rows = layout_mats.shape[1] * LAYOUT_WIDTH * 2 // line
    tmats_sum = jnp.stack(
        [jnp.concatenate([item[0, :mats_rows], item[1, :mats_rows]], 1) for item in mats_sums]
    )
    lmats_sum = jnp.stack(
        [
            jnp.concatenate(
                [
                    item[side, mats_rows : mats_rows + extra_rows].reshape(-1, 2 * LAYOUT_WIDTH)
                    for side in range(2)
                ],
                1,
            )
            for item in mats_sums
        ]
    )
    unit_sums = [
        [item.finish() for item in plan.units[layer_no]] for layer_no in range(LAYERS)
    ]
    tffn_sum = jnp.stack(
        [jnp.concatenate([item[:unit_rows] for item in pair], 1) for pair in unit_sums]
    )
    lffn_sum = jnp.stack(
        [
            from_rows(pair[0][None, unit_rows : unit_rows + layout_unit_rows], layout_units)
            for pair in unit_sums
        ]
    )
    final_grads = (table_sum, tmats_sum, lmats_sum, tffn_sum, lffn_sum, small_sum)
    lane_first = (lane == 0).astype(jnp.float32)
    squares = (
        jnp.sum(table_sum * table_sum) + jnp.sum(tffn_sum * tffn_sum) + jnp.sum(lffn_sum * lffn_sum)
    )
    squares = squares + lane_first * (
        jnp.sum(tmats_sum * tmats_sum)
        + jnp.sum(lmats_sum * lmats_sum)
        + jnp.sum(small_sum * small_sum)
    )
    count_part = jnp.sum(live_own) + jnp.float32(pages * PAIRS)
    sums = sum_everywhere(
        jnp.broadcast_to(
            jnp.stack([squares, own_loss + align_part, count_part, squares])[:, None], (4, 128)
        )
    )
    total_squares, loss_sum, loss_count = sums[0, 0], sums[1, 0], sums[2, 0]
    grad_norm = jnp.sqrt(total_squares) / loss_count
    factor = jnp.minimum(1.0, CLIP_NORM / grad_norm)
    masters = (table, text_mats, layout_mats, text_ffn, layout_ffn, small_params)
    moments = (
        table_momentum,
        text_mats_momentum,
        layout_mats_momentum,
        text_ffn_momentum,
        layout_ffn_momentum,
        small_momentum,
    )
    averages = (
        table_average,
        text_mats_average,
        layout_mats_average,
        text_ffn_average,
        layout_ffn_average,
        small_average,
    )
    updated = [
        apply_update(
            masters[number],
            final_grads[number],
            moments[number],
            averages[number],
            loss_count,
            factor,
        )
        for number in range(6)
    ]
    new_masters = [item[0] for item in updated]
    new_moments = [item[1] for item in updated]
    new_averages = [item[2] for item in updated]
    copies = [item.astype(jnp.bfloat16) for item in new_masters[:5]]
    return (
        loss_sum,
        loss_count,
        grad_norm,
        new_masters[0],
        new_masters[1],
        new_masters[2],
        new_masters[3],
        new_masters[4],
        new_masters[5],
        copies[0],
        copies[1],
        copies[2],
        copies[3],
        copies[4],
        new_moments[0],
        new_moments[1],
        new_moments[2],
        new_moments[3],
        new_moments[4],
        new_moments[5],
        new_averages[0],
        new_averages[1],
        new_averages[2],
        new_averages[3],
        new_averages[4],
        new_averages[5],
    )


def solution(mesh):
    return jax.shard_map(
        on_device,
        mesh=mesh,
        in_specs=(
            P("dp", None),
            P("dp", None),
            P(("dp", "mp")),
            P(None, ("dp", "mp"), None),
            P(("dp", "mp"), None),
            P(("dp", "mp"), None, None),
            P(("dp", "mp"), None),
            P(("mp", "dp"), None),
            P(None, "dp", None),
            P(None, "dp", None),
            P(None, ("mp", "dp"), None),
            P(None, ("mp", "dp"), None),
            P("dp"),
            P(("mp", "dp"), None),
            P(None, "dp", None),
            P(None, "dp", None),
            P(None, ("mp", "dp"), None),
            P(None, ("mp", "dp"), None),
            P("dp"),
            P(("mp", "dp"), None),
            P(None, "dp", None),
            P(None, "dp", None),
            P(None, ("mp", "dp"), None),
            P(None, ("mp", "dp"), None),
            P("dp"),
        ),
        out_specs=(
            P(),
            P(),
            P(),
            P(("mp", "dp"), None),
            P(None, "dp", None),
            P(None, "dp", None),
            P(None, ("mp", "dp"), None),
            P(None, ("mp", "dp"), None),
            P("dp"),
            P(("mp", "dp"), None),
            P(None, "dp", None),
            P(None, "dp", None),
            P(None, ("mp", "dp"), None),
            P(None, ("mp", "dp"), None),
            P(("mp", "dp"), None),
            P(None, "dp", None),
            P(None, "dp", None),
            P(None, ("mp", "dp"), None),
            P(None, ("mp", "dp"), None),
            P("dp"),
            P(("mp", "dp"), None),
            P(None, "dp", None),
            P(None, "dp", None),
            P(None, ("mp", "dp"), None),
            P(None, ("mp", "dp"), None),
            P("dp"),
        ),
        check_vma=False,
    )
```
